32 devices in a mesh: rep: 4 (over y, x), shard: 8 (over z, core).
Axes of the slice: x: 2, y: 2, z: 4, core: 2. Of those that a mesh axis runs over, the one named last changes fastest.
Arguments:
- block_input: bfloat16 [16384, 960], P(('rep', 'shard')), may hold values from -6 to 6
- block_cotangent: bfloat16 [16384, 960], P(('rep', 'shard')), may hold values from -6 to 6
- lengths: int32 [4, 3], P('rep'), may hold values from 1 to 2048, 4096 in all within a row
- attend_gain: bfloat16 [960], P('shard'), may hold values from 0.5 to 1.5
- attend_weight: bfloat16 [960, 1600], P('shard'), may hold values from -0.25 to 0.25
- output_weight: bfloat16 [960, 960], P(None, 'shard'), may hold values from -0.375 to 0.375
- expand_gain: bfloat16 [960], P('shard'), may hold values from 0.5 to 1.5
- expand_weight: bfloat16 [960, 5120], P('shard'), may hold values from -0.1875 to 0.1875
- shrink_weight: bfloat16 [2560, 960], P(None, 'shard'), may hold values from -0.125 to 0.125
- attend_gain_first: float32 [960], P('shard'), may hold values from -6 to 6
- attend_weight_first: float32 [960, 1600], P('shard'), may hold values from -6 to 6
- output_weight_first: float32 [960, 960], P(None, 'shard'), may hold values from -4 to 4
- expand_gain_first: float32 [960], P('shard'), may hold values from -5 to 5
- expand_weight_first: float32 [960, 5120], P('shard'), may hold values from -2.5 to 2.5
- shrink_weight_first: float32 [2560, 960], P(None, 'shard'), may hold values from -4 to 4
- attend_gain_second: float32 [960], P('shard'), may hold values from 10 to 40
- attend_weight_second: float32 [960, 1600], P('shard'), may hold values from 3 to 13
- output_weight_second: float32 [960, 960], P(None, 'shard'), may hold values from 0.3 to 1.2
- expand_gain_second: float32 [960], P('shard'), may hold values from 0.6 to 2.4
- expand_weight_second: float32 [960, 5120], P('shard'), may hold values from 0.12 to 0.5
- shrink_weight_second: float32 [2560, 960], P(None, 'shard'), may hold values from 0.3 to 1.2
Outputs:
- block_output: float32 [16384, 960], P(('rep', 'shard'))
- input_gradient: float32 [16384, 960], P(('rep', 'shard'))
- attend_gain_gradient: float32 [960], P('shard')
- attend_weight_gradient: float32 [960, 1600], P('shard')
- output_weight_gradient: float32 [960, 960], P(None, 'shard')
- expand_gain_gradient: float32 [960], P('shard')
- expand_weight_gradient: float32 [960, 5120], P('shard')
- shrink_weight_gradient: float32 [2560, 960], P(None, 'shard')
- attend_gain_moment: float32 [960], P('shard')
- attend_weight_moment: float32 [960, 1600], P('shard')
- output_weight_moment: float32 [960, 960], P(None, 'shard')
- expand_gain_moment: float32 [960], P('shard')
- expand_weight_moment: float32 [960, 5120], P('shard')
- shrink_weight_moment: float32 [2560, 960], P(None, 'shard')
- attend_gain_square: float32 [960], P('shard')
- attend_weight_square: float32 [960, 1600], P('shard')
- output_weight_square: float32 [960, 960], P(None, 'shard')
- expand_gain_square: float32 [960], P('shard')
- expand_weight_square: float32 [960, 5120], P('shard')
- shrink_weight_square: float32 [2560, 960], P(None, 'shard')
- attend_gain_update: float32 [960], P('shard')
- attend_weight_next: float32 [960, 1600], P('shard')
- output_weight_next: float32 [960, 960], P(None, 'shard')
- expand_gain_update: float32 [960], P('shard')
- expand_weight_next: float32 [960, 5120], P('shard')
- shrink_weight_next: float32 [2560, 960], P(None, 'shard')
The draws below stay inside these ranges and needn't reach their ends.
Inputs may be any that keep to these rules, and one draw needn't show every extreme that they name: In each replica group's row the 3 lengths sum to 4096 and the longest is exactly 2048; the sequences lie back to back, in this order, in the group's token rows.
All inputs are finite; a program needn't handle non-finite values.
Results may differ from the reference program's by a relative error of at most 0.015.
Values may be sent and summed in bfloat16 or wider, within the bound.
A program may use at most 136 MiB of HBM per device.

```python
import math
import jax
import jax.numpy as jnp
import numpy as np
from jax import lax

D = 960
HEADS = 15
KV_HEADS = 5
HEAD_DIM = 64
FF = 2560
TOK_DEV = 512
MAXLEN = 2048
STEP = 10
QW = 960
KW = 320
REACH = 4
GROUP_TOK = 4096
SEQS = 3
TOKENS = 16384
N_REP = 4
N_SHARD = 8


def steps_of(key, dims, cuts, smallest, largest):
    loudness, own = 1.0, jax.random.fold_in(key, 6)
    for dim, blocks in cuts:
        steps = jnp.exp(jax.random.uniform(jax.random.fold_in(own, dim), (blocks,), jnp.float32, smallest / len(cuts), largest / len(cuts)))
        loudness = loudness * jnp.repeat(steps, dims[dim] // blocks).reshape([-1 if axis == dim else 1 for axis in range(len(dims))])
    return loudness


def split_up(amount, total, limit, lean):
    weights = [(1 << 20) // math.isqrt(grade ** lean) + 1 for grade in range(2, amount + 1)]
    surplus, counts = total - limit - (amount - 1), [1] * (amount - 1)
    while surplus > 0:
        candidates = [i for i in range(amount - 1) if counts[i] < limit]
        whole, left = sum([weights[i] for i in candidates]), surplus
        for i in candidates:
            addition = min(limit - counts[i], max(1, left * weights[i] // whole), surplus)
            counts[i] = counts[i] + addition
            surplus = surplus - addition
    return np.array([limit] + counts)


def ragged_sizes(key, number_of, total, reach, slope):
    if number_of == 2:
        one = jax.random.randint(key, (), max(1, total - reach), min(reach, total - 1) + 1)
        return jnp.stack([one, total - one])
    sizes = jnp.asarray(split_up(number_of, total, reach, slope), jnp.int32)
    pairs = (number_of - 1) // 2
    donor, receiver = sizes[1:1 + 2 * pairs:2], sizes[2:2 + 2 * pairs:2]
    margin = jnp.minimum(donor - 1, reach - receiver)
    passed = jax.random.randint(jax.random.fold_in(key, 1), (pairs,), 0, 1 << 20) % (margin + 1)
    sizes = sizes.at[1:1 + 2 * pairs:2].set(donor - passed).at[2:2 + 2 * pairs:2].set(receiver + passed)
    return sizes[jax.random.permutation(jax.random.fold_in(key, 2), number_of)]


def centred(rng, dims, spread, reach, split=(), held_as=jnp.bfloat16):
    entries = jax.random.normal(rng, dims, jnp.float32) * spread
    if len(split) > 0:
        entries = steps_of(rng, dims, split, -0.22, 0.18) * entries
    return jnp.clip(entries, min=-reach, max=reach).astype(held_as)


def setup_inputs(seed: int = 0) -> dict:
    streams_of = jax.random.split(jax.random.key(seed), 22)
    return {
        "block_input": centred(streams_of[0], (TOKENS, D), 1.0, 6.0, ((0, 32),)),
        "block_cotangent": centred(streams_of[1], (TOKENS, D), 1.0, 6.0, ((0, 32),)),
        "lengths": jax.vmap(lambda own: ragged_sizes(own, SEQS, GROUP_TOK, MAXLEN, 2))(jax.random.split(streams_of[2], N_REP)).reshape((N_REP, SEQS)).astype(jnp.int32),
        "attend_gain": jnp.clip(1.0 + 0.1 * jax.random.normal(streams_of[3], (D,), jnp.float32), 0.5, 1.5).astype(jnp.bfloat16),
        "attend_weight": centred(streams_of[4], (D, QW + 2 * KW), (D // 2) ** -0.5, 0.25, ((0, 8),)),
        "output_weight": centred(streams_of[5], (QW, D), (QW // 4) ** -0.5, 0.375, ((1, 8),)),
        "expand_gain": jnp.clip(1.0 + 0.1 * jax.random.normal(streams_of[6], (D,), jnp.float32), 0.5, 1.5).astype(jnp.bfloat16),
        "expand_weight": centred(streams_of[7], (D, 2 * FF), D ** -0.5, 0.1875, ((0, 8),)),
        "shrink_weight": centred(streams_of[8], (FF, D), FF ** -0.5, 0.125, ((1, 8),)),
        "attend_gain_first": centred(streams_of[9], (D,), 1.5, 6.0, ((0, 8),), jnp.float32),
        "attend_weight_first": centred(streams_of[10], (D, QW + 2 * KW), 0.9, 6.0, ((0, 8),), jnp.float32),
        "output_weight_first": centred(streams_of[11], (QW, D), 0.27, 4.0, ((1, 8),), jnp.float32),
        "expand_gain_first": centred(streams_of[12], (D,), 0.37, 5.0, ((0, 8),), jnp.float32),
        "expand_weight_first": centred(streams_of[13], (D, 2 * FF), 0.17, 2.5, ((0, 8),), jnp.float32),
        "shrink_weight_first": centred(streams_of[14], (FF, D), 0.27, 4.0, ((1, 8),), jnp.float32),
        "attend_gain_second": jnp.clip(jnp.exp(math.log(40.0) - 1.3862944 * jax.random.uniform(streams_of[15], (D,), jnp.float32) ** steps_of(streams_of[15], (D,), ((0, 8),), -0.2, 0.2)), 10.0, 40.0),
        "attend_weight_second": jnp.clip(jnp.exp(math.log(13.0) - 1.4663371 * jax.random.uniform(streams_of[16], (D, QW + 2 * KW), jnp.float32) ** steps_of(streams_of[16], (D, QW + 2 * KW), ((0, 8),), -0.2, 0.2)), 3.0, 13.0),
        "output_weight_second": jnp.clip(jnp.exp(math.log(1.2) - 1.3862944 * jax.random.uniform(streams_of[17], (QW, D), jnp.float32) ** steps_of(streams_of[17], (QW, D), ((1, 8),), -0.2, 0.2)), 0.3, 1.2),
        "expand_gain_second": jnp.clip(jnp.exp(math.log(2.4) - 1.3862944 * jax.random.uniform(streams_of[18], (D,), jnp.float32) ** steps_of(streams_of[18], (D,), ((0, 8),), -0.2, 0.2)), 0.6, 2.4),
        "expand_weight_second": jnp.clip(jnp.exp(math.log(0.5) - 1.4271164 * jax.random.uniform(streams_of[19], (D, 2 * FF), jnp.float32) ** steps_of(streams_of[19], (D, 2 * FF), ((0, 8),), -0.2, 0.2)), 0.12, 0.5),
        "shrink_weight_second": jnp.clip(jnp.exp(math.log(1.2) - 1.3862944 * jax.random.uniform(streams_of[20], (FF, D), jnp.float32) ** steps_of(streams_of[20], (FF, D), ((1, 8),), -0.2, 0.2)), 0.3, 1.2),
    }


@jax.custom_vjp
def low(v):
    return lax.optimization_barrier(v.astype(jnp.bfloat16)).astype(jnp.float32)

@jax.custom_vjp
def low_back(v):
    return v

def low_keep(v):
    return (low(v), None)

def low_pass(kept, grad):
    return (grad,)

def back_keep(v):
    return (v, None)

def back_low(kept, grad):
    return (low(grad),)
low.defvjp(low_keep, low_pass)
low_back.defvjp(back_keep, back_low)
precise = lax.Precision.HIGHEST
eps_norm = 1e-05
rope_base = 100000.0
beta_one = 0.9
beta_two = 0.95
adam_eps = 1e-08
learn_rate = 0.05
decay_rate = 0.1
grad_factor = 4.0
masked_score = -1e+30

def sequence_starts(lengths, group_index):
    ends_at = jnp.cumsum(lengths, dtype=jnp.int32)
    before = (ends_at[None, :] <= group_index[:, None]).astype(jnp.int32)
    return lax.optimization_barrier(jnp.sum(before * lengths[None, :], axis=1, dtype=jnp.int32))

def angles(positions):
    half_dim = HEAD_DIM // 2
    inverse = rope_base ** (-(2.0 * jnp.arange(half_dim, dtype=jnp.float32) / HEAD_DIM))
    phases = positions.astype(jnp.float32)[:, None] * inverse[None, :]
    return (jnp.cos(phases)[:, None, :], jnp.sin(phases)[:, None, :])

def rotate(tensor, cosine_table, sine_table):
    half_dim = tensor.shape[-1] // 2
    front_half = tensor[..., :half_dim]
    back_half = tensor[..., half_dim:]
    return jnp.concatenate([front_half * cosine_table - back_half * sine_table, back_half * cosine_table + front_half * sine_table], axis=-1)

def normalize(tensor):
    return tensor * lax.rsqrt(lax.optimization_barrier(jnp.mean(tensor * tensor, axis=-1, keepdims=True)) + eps_norm)

def attend_block(element):
    query_block, key_block, value_block, query_index, start_index, key_index = element
    scores = jnp.einsum('qkgd,wkd->kgqw', query_block, key_block, precision=precise) * HEAD_DIM ** (-0.5)
    scores = low_back(scores)
    allowed = (key_index[None, :] >= start_index[:, None]) & (key_index[None, :] <= query_index[:, None])
    scores = jnp.where(allowed[None, None], scores, masked_score)
    weights = jax.nn.softmax(scores, axis=-1)
    return jnp.einsum('kgqw,wkd->qkgd', low(weights), value_block, precision=precise)

def attention(queries, key_rows, values, query_index, start_index):
    group_size = HEADS // KV_HEADS
    blocks = N_REP * N_SHARD
    window_rows = (REACH + 1) * TOK_DEV

    def windows(tensor):
        tail = tensor.shape[1:]
        shaped = tensor.reshape((N_REP, N_SHARD, TOK_DEV) + tail)
        padded = jnp.concatenate([jnp.zeros((N_REP, REACH, TOK_DEV) + tail, tensor.dtype), shaped], axis=1)
        joined = jnp.concatenate([padded[:, offset:offset + N_SHARD] for offset in range(REACH + 1)], axis=2)
        return joined.reshape((blocks, window_rows) + tail)
    key_index = (jnp.arange(blocks, dtype=jnp.int32) % N_SHARD * TOK_DEV - REACH * TOK_DEV)[:, None] + jnp.arange(window_rows, dtype=jnp.int32)[None, :]
    query_blocks = queries.reshape(blocks, TOK_DEV, KV_HEADS, group_size, HEAD_DIM)
    mixed_rows = lax.map(jax.checkpoint(attend_block), (query_blocks, windows(key_rows), windows(values), query_index.reshape(blocks, TOK_DEV), start_index.reshape(blocks, TOK_DEV), key_index))
    return mixed_rows.reshape(TOKENS, QW)

def layer(params, block_input, cosine_table, sine_table, query_index, start_index):
    attend_gain, attend_weight, output_weight, expand_gain, expand_weight, shrink_weight = params
    hidden_one = low(normalize(block_input) * attend_gain)
    joint_out = low_back(jnp.dot(hidden_one, attend_weight, precision=precise))
    queries = low(rotate(joint_out[:, :QW].reshape(TOKENS, HEADS, HEAD_DIM), cosine_table, sine_table))
    key_rows = low(rotate(joint_out[:, QW:QW + KW].reshape(TOKENS, KV_HEADS, HEAD_DIM), cosine_table, sine_table))
    values = low(joint_out[:, QW + KW:].reshape(TOKENS, KV_HEADS, HEAD_DIM))
    mixed_rows = low(low_back(attention(queries, key_rows, values, query_index, start_index)))
    middle = block_input + low_back(jnp.dot(mixed_rows, output_weight, precision=precise))
    hidden_two = low(normalize(middle) * expand_gain)
    gate_up = low_back(jnp.dot(hidden_two, expand_weight, precision=precise))
    inner_rows = low(jax.nn.silu(gate_up[:, :FF]) * gate_up[:, FF:])
    return middle + jnp.dot(inner_rows, shrink_weight, precision=precise)

def adam_step(weight_now, gradient, first, second, decay_factor):
    moment = beta_one * first + (1.0 - beta_one) * gradient
    square = beta_two * second + (1.0 - beta_two) * gradient * gradient
    corrected = moment / (1.0 - beta_one ** STEP)
    divisor = jnp.sqrt(square / (1.0 - beta_two ** STEP)) + adam_eps
    update = -learn_rate * (corrected / divisor + decay_factor * weight_now)
    return (gradient, moment, square, weight_now + update, update)

def reference(block_input, block_cotangent, lengths, attend_gain, attend_weight, output_weight, expand_gain, expand_weight, shrink_weight, attend_gain_first, attend_weight_first, output_weight_first, expand_gain_first, expand_weight_first, shrink_weight_first, attend_gain_second, attend_weight_second, output_weight_second, expand_gain_second, expand_weight_second, shrink_weight_second):
    params = (attend_gain, attend_weight, output_weight, expand_gain, expand_weight, shrink_weight)
    firsts = (attend_gain_first, attend_weight_first, output_weight_first, expand_gain_first, expand_weight_first, shrink_weight_first)
    seconds = (attend_gain_second, attend_weight_second, output_weight_second, expand_gain_second, expand_weight_second, shrink_weight_second)
    group_index = jnp.arange(GROUP_TOK, dtype=jnp.int32)
    start_index = jnp.concatenate([sequence_starts(lengths[group], group_index) for group in range(N_REP)])
    query_index = jnp.tile(group_index, N_REP)
    cosine_table, sine_table = angles(query_index - start_index)
    floats = tuple((weight_now.astype(jnp.float32) for weight_now in params))

    def forward(weights, inputs):
        return layer(weights, inputs, cosine_table, sine_table, query_index, start_index)
    output, pullback = jax.vjp(forward, floats, block_input.astype(jnp.float32))
    weight_sums, input_sum = pullback(block_cotangent.astype(jnp.float32))
    grad_scale = grad_factor * TOKENS ** (-0.5)
    decays = (0.0, decay_rate, decay_rate, 0.0, decay_rate, decay_rate)
    results = [adam_step(floats[number], weight_sums[number] * grad_scale, firsts[number], seconds[number], decays[number]) for number in range(6)]
    return (output.astype(jnp.float32), input_sum.astype(jnp.float32), results[0][0], results[1][0], results[2][0], results[3][0], results[4][0], results[5][0], results[0][1], results[1][1], results[2][1], results[3][1], results[4][1], results[5][1], results[0][2], results[1][2], results[2][2], results[3][2], results[4][2], results[5][2], results[0][4], results[1][3], results[2][3], results[3][4], results[4][3], results[5][3])
```

```python
import functools
import math

import jax
import jax.numpy as jnp
from jax import lax
from jax.experimental import pallas as pl
from jax.experimental.pallas import tpu as pltpu
from jax.sharding import PartitionSpec as P

HEADS = 15
KV_HEADS = 5
HEAD_DIM = 64
GROUP = HEADS // KV_HEADS
FF = 2560
MAXLEN = 2048
STEP = 10
QW = 960
KW = 320
JW = QW + 2 * KW
D = 960

eps_norm = 1e-05
rope_base = 100000.0
beta_one = 0.9
beta_two = 0.95
adam_eps = 1e-08
learn_rate = 0.05
decay_rate = 0.1
grad_factor = 4.0

F32 = jnp.float32
BF = jnp.bfloat16
MESH = pl.DeviceIdType.MESH
ANY = pl.ANY
VMEM = pltpu.VMEM
DMA = pltpu.SemaphoreType.DMA

QC = 256
KB = 768
HALF = 64
ONES = 112
NEG = -1e30
EXP_SCALE = HEAD_DIM**-0.5 * math.log2(math.e)
BIG_VMEM = 60 * 2**20


def dot(a, b, ca=1, cb=0):
    return lax.dot_general(a, b, (((ca,), (cb,)), ((), ())), preferred_element_type=F32)


def causal_tile():
    key = lax.broadcasted_iota(jnp.int32, (QC, QC), 0)
    query = lax.broadcasted_iota(jnp.int32, (QC, QC), 1)
    return key <= query


def mask_last(scores, causal):
    last = jnp.where(causal, scores[KB - QC :], NEG)
    return jnp.concatenate([scores[: KB - QC], last], axis=0)


def attend_forward_kernel(
    kv_ref, feat_ref, qt_ref, qfeat_ref, mixed_ref, lse_ref, kvf, vt, qa, sb
):
    blocks, kv_heads, rows, lanes = kv_ref.shape
    window = blocks * rows
    tokens = qt_ref.shape[1]
    span = window - (tokens - QC)
    steps = span // KB
    kvf[:, lanes:] = feat_ref[...]
    qa[HALF:lanes, :] = jnp.zeros((HALF, tokens), BF)
    qa[lanes:, :] = qfeat_ref[...]
    vt[HALF:, :] = jnp.ones((vt.shape[0] - HALF, window), BF)
    causal = causal_tile()

    def key_head(j, _):
        for block in range(blocks):
            part = kv_ref[block, j]
            kvf[block * rows : (block + 1) * rows, :lanes] = part
            vt[:HALF, block * rows : (block + 1) * rows] = part.T[HALF:, :]

        def head(g, _):
            h = j * GROUP + g
            row = pl.multiple_of(h * HEAD_DIM, HEAD_DIM)
            qa[:HALF, :] = qt_ref[pl.ds(row, HEAD_DIM), :]
            tops = []
            for chunk in range(tokens // QC):
                low = chunk * QC
                highest = None
                for b in range(steps):
                    first = low + b * KB
                    s = dot(kvf[first : first + KB, :], qa[:, low : low + QC])
                    if b == steps - 1:
                        s = mask_last(s, causal)
                    sb[chunk, b * KB : (b + 1) * KB, :] = s
                    peak = jnp.max(s.reshape(KB // 8, 8, QC), axis=0)
                    highest = peak if highest is None else jnp.maximum(highest, peak)
                tops.append(jnp.max(highest, axis=0, keepdims=True))
            for chunk in range(tokens // QC):
                low = chunk * QC
                shift = tops[chunk] * EXP_SCALE
                total = None
                for b in range(steps):
                    first = low + b * KB
                    s = sb[chunk, b * KB : (b + 1) * KB, :]
                    p = jnp.exp2(s * EXP_SCALE - shift).astype(BF)
                    term = dot(vt[:, first : first + KB], p)
                    total = term if total is None else total + term
                weight = total[HALF : HALF + 1, :]
                mixed_ref[pl.ds(row, HEAD_DIM), low : low + QC] = (
                    total[:HALF, :] * (1.0 / weight)
                ).astype(BF)
                lse_ref[pl.ds(h, 1), :, low : low + QC] = (
                    tops[chunk] * HEAD_DIM**-0.5 + jnp.log(weight)
                )[None]
            return 0

        lax.fori_loop(0, GROUP, head, 0)
        return 0

    lax.fori_loop(0, kv_heads, key_head, 0)


def attend_forward(window, feat, qt, qfeat):
    blocks, kv_heads, rows, lanes = window.shape
    keys = blocks * rows
    tokens = qt.shape[1]
    span = keys - (tokens - QC)
    return pl.pallas_call(
        attend_forward_kernel,
        out_shape=(
            jax.ShapeDtypeStruct(qt.shape, BF),
            jax.ShapeDtypeStruct((HEADS, 1, tokens), F32),
        ),
        scratch_shapes=[
            VMEM((keys, 2 * lanes), BF),
            VMEM((HALF + 16, keys), BF),
            VMEM((2 * lanes, tokens), BF),
            VMEM((tokens // QC, span, QC), F32),
        ],
        compiler_params=pltpu.CompilerParams(vmem_limit_bytes=BIG_VMEM),
        name="attend_forward",
    )(window, feat, qt, qfeat)


def three_parts(value, rows):
    one = value.astype(BF).astype(F32)
    two = (value - one).astype(BF).astype(F32)
    three = value - one - two
    shape = (rows, value.shape[1])
    place = lax.broadcasted_iota(jnp.int32, shape, 0)
    parts = [jnp.broadcast_to(part, shape) for part in (one, two, three)]
    chosen = jnp.where(
        place == 0, parts[0], jnp.where(place == 1, parts[1], jnp.where(place == 2, parts[2], 0.0))
    )
    return chosen.astype(BF)


def attend_backward_kernel(
    kv_ref,
    feat_ref,
    qt_ref,
    qfeat_ref,
    gradt_ref,
    mixed_ref,
    lse_ref,
    dq_ref,
    dkv_ref,
    kvf,
    kt,
    qa,
    da,
    acc,
    rhs,
):
    blocks, kv_heads, rows, lanes = kv_ref.shape
    window = blocks * rows
    tokens = qt_ref.shape[1]
    span = window - (tokens - QC)
    steps = span // KB
    kvf[:, lanes:] = feat_ref[...]
    qa[HALF:lanes, :] = jnp.zeros((HALF, tokens), BF)
    da[...] = jnp.zeros_like(da)
    rhs[...] = jnp.zeros_like(rhs)
    causal = causal_tile()
    extra = lanes - ONES

    def key_head(j, _):
        for block in range(blocks):
            part = kv_ref[block, j]
            kvf[block * rows : (block + 1) * rows, :lanes] = part
            kt[:, block * rows : (block + 1) * rows] = part.T[:HALF, :]
        acc[...] = jnp.zeros_like(acc)

        def head(g, _):
            h = j * GROUP + g
            row = pl.multiple_of(h * HEAD_DIM, HEAD_DIM)
            q = qt_ref[pl.ds(row, HEAD_DIM), :]
            grad = gradt_ref[pl.ds(row, HEAD_DIM), :]
            qa[:HALF, :] = q
            da[HALF:lanes, :] = grad
            mixed = mixed_ref[pl.ds(row, HEAD_DIM), :].astype(F32)
            row_total = jnp.sum(grad.astype(F32) * mixed, axis=0, keepdims=True)
            lse = lse_ref[pl.ds(h, 1), :, :][0]
            qa[lanes : lanes + ONES, :] = qfeat_ref[:ONES, :]
            qa[lanes + ONES :, :] = three_parts(-(HEAD_DIM**0.5) * lse, extra)
            da[lanes + ONES :, :] = three_parts(-row_total, extra)
            query_grads = [None] * (tokens // QC)
            for chunk in range(tokens // QC):
                low = chunk * QC
                rhs[chunk, :HALF, :QC] = q[:, low : low + QC]
                rhs[chunk, HALF:, QC:] = grad[:, low : low + QC]
            for b in range(steps):
                for chunk in range(tokens // QC):
                    low = chunk * QC
                    first = low + b * KB
                    keys = kvf[first : first + KB, :]
                    s = dot(keys, qa[:, low : low + QC])
                    if b == steps - 1:
                        s = mask_last(s, causal)
                    p = jnp.exp2(s * EXP_SCALE)
                    dp = dot(keys, da[:, low : low + QC])
                    ds = (p * dp).astype(BF)
                    both = jnp.concatenate([ds, p.astype(BF)], axis=1)
                    acc[first : first + KB, :] += dot(both, rhs[chunk], 1, 1)
                    term = dot(kt[:, first : first + KB], ds)
                    old = query_grads[chunk]
                    query_grads[chunk] = term if old is None else old + term
            for chunk in range(tokens // QC):
                low = chunk * QC
                dq_ref[pl.ds(row, HEAD_DIM), low : low + QC] = query_grads[chunk] * HEAD_DIM**-0.5
            return 0

        lax.fori_loop(0, GROUP, head, 0)
        lane = lax.broadcasted_iota(jnp.int32, (1, lanes), 1)
        factor = jnp.where(lane < HALF, HEAD_DIM**-0.5, 1.0)
        for block in range(blocks):
            part = acc[block * rows : (block + 1) * rows, :]
            dkv_ref[block, j] = (part * factor).astype(dkv_ref.dtype)
        return 0

    lax.fori_loop(0, kv_heads, key_head, 0)


def attend_backward(window, feat, qt, qfeat, gradt, mixed, lse):
    blocks, kv_heads, rows, lanes = window.shape
    keys = blocks * rows
    tokens = qt.shape[1]
    return pl.pallas_call(
        attend_backward_kernel,
        out_shape=(
            jax.ShapeDtypeStruct(qt.shape, F32),
            jax.ShapeDtypeStruct(window.shape, BF),
        ),
        scratch_shapes=[
            VMEM((keys, 2 * lanes), BF),
            VMEM((HALF, keys), BF),
            VMEM((2 * lanes, tokens), BF),
            VMEM((2 * lanes, tokens), BF),
            VMEM((keys, lanes), F32),
            VMEM((tokens // QC, lanes, 2 * QC), BF),
        ],
        compiler_params=pltpu.CompilerParams(vmem_limit_bytes=BIG_VMEM),
        name="attend_backward",
    )(window, feat, qt, qfeat, gradt, mixed, lse)


class Place:
    def __init__(self):
        self.r = lax.axis_index("rep")
        self.s = lax.axis_index("shard")
        self.x, self.y = lax.rem(self.r, 2), self.r // 2
        self.z, self.c = self.s // 2, lax.rem(self.s, 2)
        self.rx = self.y * 2 + (1 - self.x)
        self.ry = (1 - self.y) * 2 + self.x
        self.rd = 3 - self.r
        self.x_side = (self.rx, self.s)
        self.y_side = (self.ry, self.s)
        self.core_side = (self.r, self.z * 2 + (1 - self.c))

    def z_to(self, k):
        return lax.rem(self.z + k, 4)

    def z_from(self, k):
        return lax.rem(self.z + 4 - k, 4)

    def z_side(self, k):
        return (self.r, self.z_to(k) * 2 + self.c)


def greet(devices):
    barrier = pltpu.get_barrier_semaphore()
    for device in devices:
        pl.semaphore_signal(barrier, inc=1, device_id=device, device_id_type=MESH)
    pl.semaphore_wait(barrier, len(devices))


def remote(src, dst, send, recv, device):
    return pltpu.make_async_remote_copy(
        src_ref=src, dst_ref=dst, send_sem=send, recv_sem=recv, device_id=device, device_id_type=MESH
    )


def gather_kernel(own_ref, full_ref, local_sem, send, recv):
    rows = own_ref.shape[0]
    quarter, half = rows // 4, rows // 8
    at = Place()
    greet([at.x_side, at.y_side, at.core_side] + [at.z_side(k) for k in (1, 2, 3)])

    def piece(plane, owner, part=None):
        start = owner * quarter + (0 if part is None else part * half)
        size = quarter if part is None else half
        return full_ref.at[plane, pl.ds(pl.multiple_of(start, half), size), :]

    sent = []

    def push(index, src, dst, device):
        copy = remote(src, dst, send.at[index], recv.at[index], device)
        copy.start()
        sent.append(copy)

    def arrive(index, ref):
        remote(ref, ref, send.at[index], recv.at[index], at.core_side).wait_recv()

    local = pltpu.make_async_copy(own_ref, full_ref.at[at.s], local_sem)
    local.start()
    mine = own_ref.at[pl.ds(pl.multiple_of(at.r * quarter, quarter), quarter), :]
    for k in (1, 2, 3):
        push(k - 1, mine, piece(at.s, at.r), at.z_side(k))
    push(3, own_ref, full_ref.at[at.s], at.core_side)
    planes = [at.z_from(k) * 2 + at.c for k in (1, 2, 3)]
    twins = [at.z_from(k) * 2 + (1 - at.c) for k in (1, 2, 3)]
    for k, plane in enumerate(planes):
        got = piece(plane, at.r)
        arrive(k, got)
        push(4 + k, got, got, at.x_side)
        push(7 + k, got, got, at.y_side)
        push(10 + k, got, got, at.core_side)
    for k, plane in enumerate(planes):
        got = piece(plane, at.rx)
        arrive(4 + k, got)
        push(13 + k, piece(plane, at.rx, 0), piece(plane, at.rx, 0), at.y_side)
        push(16 + k, got, got, at.core_side)
        got = piece(plane, at.ry)
        arrive(7 + k, got)
        push(19 + k, piece(plane, at.ry, 1), piece(plane, at.ry, 1), at.x_side)
        push(22 + k, got, got, at.core_side)
    for k, plane in enumerate(planes):
        arrive(13 + k, piece(plane, at.rd, 0))
        arrive(19 + k, piece(plane, at.rd, 1))
        got = piece(plane, at.rd)
        push(25 + k, got, got, at.core_side)
    arrive(3, full_ref.at[at.core_side[1]])
    for k, plane in enumerate(twins):
        arrive(10 + k, piece(plane, at.r))
        arrive(16 + k, piece(plane, at.rx))
        arrive(22 + k, piece(plane, at.ry))
        arrive(25 + k, piece(plane, at.rd))
    for copy in sent:
        copy.wait_send()
    local.wait()


def gather_rows(own, shards, direct, number):
    if not direct:
        return lax.all_gather(own, "shard", axis=0)
    return pl.pallas_call(
        gather_kernel,
        out_shape=jax.ShapeDtypeStruct((shards,) + own.shape, own.dtype),
        in_specs=[pl.BlockSpec(memory_space=ANY)],
        out_specs=pl.BlockSpec(memory_space=ANY),
        scratch_shapes=[DMA, DMA((28,)), DMA((28,))],
        compiler_params=pltpu.CompilerParams(collective_id=number, has_side_effects=True),
        name=f"gather_{number}",
    )(own)


def reduce_kernel(parts_ref, out_ref, own, r0, r1a, r1b, r2a, r2b, r3, local_sem, send, recv):
    rows = out_ref.shape[0]
    quarter, half = rows // 4, rows // 8
    at = Place()
    greet([at.x_side, at.y_side, at.core_side] + [at.z_side(k) for k in (1, 2, 3)])
    sent = []

    def push(index, src, dst, device):
        copy = remote(src, dst, send.at[index], recv.at[index], device)
        copy.start()
        sent.append(copy)

    def arrive(index, ref):
        remote(ref, ref, send.at[index], recv.at[index], at.core_side).wait_recv()

    def spot(owner, part):
        return pl.ds(pl.multiple_of(owner * quarter + part * half, half), half)

    def add_into(k, where, ref):
        own[k, where, :] = (own[k, where, :].astype(F32) + ref[...].astype(F32)).astype(BF)

    order = [at.z_to(k) for k in (1, 2, 3, 0)]
    local = []
    for k, z in enumerate(order):
        copy = pltpu.make_async_copy(parts_ref.at[z * 2 + at.c], own.at[k], local_sem.at[k])
        copy.start()
        local.append(copy)
        push(k, parts_ref.at[z * 2 + (1 - at.c)], r0.at[k], at.core_side)
    for k in range(4):
        local[k].wait()
        arrive(k, r0.at[k])

        def add_rows(i, _, k=k):
            where = pl.ds(pl.multiple_of(i * half, half), half)
            add_into(k, where, r0.at[k, where, :])
            return 0

        lax.fori_loop(0, rows // half, add_rows, 0)
        for i in range(2):
            push(4 + 4 * k + i, own.at[k, spot(i * 2 + 1 - at.x, 0), :], r1a.at[k, i], at.x_side)
            push(
                6 + 4 * k + i, own.at[k, spot((1 - at.y) * 2 + i, 1), :], r1b.at[k, i], at.y_side
            )
    for k in range(4):
        for i in range(2):
            arrive(4 + 4 * k + i, r1a.at[k, i])
            arrive(6 + 4 * k + i, r1b.at[k, i])
            add_into(k, spot(i * 2 + at.x, 0), r1a.at[k, i])
            add_into(k, spot(at.y * 2 + i, 1), r1b.at[k, i])
        push(20 + 2 * k, own.at[k, spot(at.ry, 0), :], r2a.at[k], at.y_side)
        push(21 + 2 * k, own.at[k, spot(at.rx, 1), :], r2b.at[k], at.x_side)
    mine = pl.ds(pl.multiple_of(at.r * quarter, quarter), quarter)
    for k in range(4):
        arrive(20 + 2 * k, r2a.at[k])
        arrive(21 + 2 * k, r2b.at[k])
        add_into(k, spot(at.r, 0), r2a.at[k])
        add_into(k, spot(at.r, 1), r2b.at[k])
        if k < 3:
            push(28 + k, own.at[k, mine, :], r3.at[k], at.z_side(k + 1))
    for k in range(3):
        arrive(28 + k, r3.at[k])
    for i in range(2):
        where = pl.ds(i * half, half)
        total = own[3, spot(at.r, i), :].astype(F32)
        for k in range(3):
            total += r3[k, where, :].astype(F32)
        out_ref[spot(at.r, i), :] = total.astype(BF)

    def piece(owner):
        return out_ref.at[pl.ds(pl.multiple_of(owner * quarter, quarter), quarter), :]

    push(31, piece(at.r), piece(at.r), at.x_side)
    push(32, piece(at.r), piece(at.r), at.y_side)
    arrive(31, piece(at.rx))
    push(33, out_ref.at[spot(at.rx, 0), :], out_ref.at[spot(at.rx, 0), :], at.y_side)
    arrive(32, piece(at.ry))
    push(34, out_ref.at[spot(at.ry, 1), :], out_ref.at[spot(at.ry, 1), :], at.x_side)
    arrive(33, out_ref.at[spot(at.rd, 0), :])
    arrive(34, out_ref.at[spot(at.rd, 1), :])
    for copy in sent:
        copy.wait_send()


def reduce_rows(parts, direct, number):
    shards, rows, columns = parts.shape
    if not direct:
        own = lax.psum_scatter(parts, "shard", scatter_dimension=0)
        return lax.psum(own, "rep").astype(F32)
    half = rows // 8
    return pl.pallas_call(
        reduce_kernel,
        out_shape=jax.ShapeDtypeStruct((rows, columns), BF),
        in_specs=[pl.BlockSpec(memory_space=ANY)],
        out_specs=pl.BlockSpec(memory_space=VMEM),
        scratch_shapes=[
            VMEM((4, rows, columns), BF),
            VMEM((4, rows, columns), BF),
            VMEM((4, 2, half, columns), BF),
            VMEM((4, 2, half, columns), BF),
            VMEM((4, half, columns), BF),
            VMEM((4, half, columns), BF),
            VMEM((3, 2 * half, columns), BF),
            DMA((4,)),
            DMA((35,)),
            DMA((35,)),
        ],
        compiler_params=pltpu.CompilerParams(
            collective_id=number, has_side_effects=True, vmem_limit_bytes=BIG_VMEM
        ),
        name=f"reduce_{number}",
    )(parts).astype(F32)


def greet_line(at):
    barrier = pltpu.get_barrier_semaphore()
    pl.semaphore_signal(barrier, inc=1, device_id=at.core_side, device_id_type=MESH)

    @pl.when(at.z < 3)
    def _():
        pl.semaphore_signal(barrier, inc=1, device_id=(at.r, at.s + 2), device_id_type=MESH)

    @pl.when(at.z > 0)
    def _():
        pl.semaphore_signal(barrier, inc=1, device_id=(at.r, at.s - 2), device_id_type=MESH)

    count = 1 + jnp.where(at.z < 3, 1, 0) + jnp.where(at.z > 0, 1, 0)
    pl.semaphore_wait(barrier, count)


def spread_kernel(kv_ref, win_ref, send, recv):
    kv_heads = kv_ref.shape[0]
    last = win_ref.shape[0] - 1
    at = Place()
    greet_line(at)
    later = (at.r, lax.min(at.s + 2, 7))

    for block in range(last):
        @pl.when(at.s < last - block)
        def _(block=block):
            win_ref[block] = jnp.zeros(win_ref.shape[1:], win_ref.dtype)

    win_ref[last] = kv_ref[...]
    near, far = jnp.where(at.c == 0, 1, 3), jnp.where(at.c == 0, 3, 1)

    def first(j):
        return remote(kv_ref.at[j], win_ref.at[2, j], send.at[0, j], recv.at[0, j], later)

    def twin_own(j):
        return remote(kv_ref.at[j], win_ref.at[3, j], send.at[1, j], recv.at[1, j], at.core_side)

    def second(j):
        return remote(win_ref.at[2, j], win_ref.at[0, j], send.at[2, j], recv.at[2, j], later)

    def twin_near(j, place):
        return remote(
            win_ref.at[2, j], win_ref.at[place, j], send.at[3, j], recv.at[3, j], at.core_side
        )

    def twin_far(j):
        return remote(win_ref.at[0, j], win_ref.at[1, j], send.at[4, j], recv.at[4, j], at.core_side)

    for j in range(kv_heads):
        @pl.when(at.z < 3)
        def _(j=j):
            first(j).start()

        @pl.when(at.c == 0)
        def _(j=j):
            twin_own(j).start()

    for j in range(kv_heads):
        @pl.when(at.z > 0)
        def _(j=j):
            first(j).wait_recv()
            twin_near(j, near).start()

            @pl.when(at.z < 3)
            def _():
                second(j).start()

    for j in range(kv_heads):
        @pl.when(at.z > 1)
        def _(j=j):
            second(j).wait_recv()

            @pl.when(at.c == 1)
            def _():
                twin_far(j).start()

    for j in range(kv_heads):
        @pl.when(at.c == 1)
        def _(j=j):
            twin_own(j).wait_recv()

        @pl.when(at.z > 0)
        def _(j=j):
            twin_near(j, far).wait_recv()
            twin_near(j, near).wait_send()

        @pl.when((at.c == 0) & (at.z > 1))
        def _(j=j):
            twin_far(j).wait_recv()

        @pl.when((at.c == 1) & (at.z > 1))
        def _(j=j):
            twin_far(j).wait_send()

        @pl.when(at.z < 3)
        def _(j=j):
            first(j).wait_send()

        @pl.when((at.z < 3) & (at.z > 0))
        def _(j=j):
            second(j).wait_send()

        @pl.when(at.c == 0)
        def _(j=j):
            twin_own(j).wait_send()


def spread_pairs(pairs, reach, direct, number):
    if not direct or reach != 4:
        devices = range(lax.axis_size("shard"))
        blocks = []
        for distance in range(reach, 0, -1):
            route = [(i - distance, i) for i in devices if i - distance in devices]
            blocks.append(lax.ppermute(pairs, "shard", route))
        return jnp.stack(blocks + [pairs])
    return pl.pallas_call(
        spread_kernel,
        out_shape=jax.ShapeDtypeStruct((reach + 1,) + pairs.shape, pairs.dtype),
        in_specs=[pl.BlockSpec(memory_space=VMEM)],
        out_specs=pl.BlockSpec(memory_space=VMEM),
        scratch_shapes=[DMA((5, pairs.shape[0])), DMA((5, pairs.shape[0]))],
        compiler_params=pltpu.CompilerParams(
            collective_id=number, has_side_effects=True, vmem_limit_bytes=BIG_VMEM
        ),
        name=f"spread_{number}",
    )(pairs)


def collect_kernel(grad_ref, out_ref, ra, rb, r2, r1, t2, t1, send, recv):
    kv_heads = out_ref.shape[0]
    at = Place()
    greet_line(at)
    earlier = (at.r, lax.max(at.s - 2, 0))

    def twin_a(j):
        return remote(grad_ref.at[3, j], ra.at[j], send.at[0, j], recv.at[0, j], at.core_side)

    def twin_b(j):
        return remote(grad_ref.at[1, j], rb.at[j], send.at[1, j], recv.at[1, j], at.core_side)

    def far(j):
        return remote(t2.at[j], r2.at[j], send.at[2, j], recv.at[2, j], earlier)

    def near(j):
        return remote(t1.at[j], r1.at[j], send.at[3, j], recv.at[3, j], earlier)

    for j in range(kv_heads):
        twin_b(j).start()
        twin_a(j).start()
    even = at.c == 0
    for j in range(kv_heads):
        twin_b(j).wait_recv()
        twin_a(j).wait_recv()
        from_a, from_b = ra[j].astype(F32), rb[j].astype(F32)
        none = jnp.zeros_like(from_a)
        t2[j] = (grad_ref[0, j].astype(F32) + jnp.where(even, none, from_b)).astype(BF)

        @pl.when(at.z > 1)
        def _(j=j):
            far(j).start()

        t1[j] = (grad_ref[2, j].astype(F32) + jnp.where(even, from_b, from_a)).astype(BF)
        out_ref[j] = grad_ref[4, j].astype(F32) + jnp.where(even, from_a, none)
    for j in range(kv_heads):
        @pl.when((at.z > 0) & (at.z < 3))
        def _(j=j):
            far(j).wait_recv()
            t1[j] = (t1[j].astype(F32) + r2[j].astype(F32)).astype(BF)

        @pl.when(at.z > 0)
        def _(j=j):
            near(j).start()

    for j in range(kv_heads):
        @pl.when(at.z < 3)
        def _(j=j):
            near(j).wait_recv()
            out_ref[j] += r1[j].astype(F32)

        @pl.when(at.z > 1)
        def _(j=j):
            far(j).wait_send()

        @pl.when(at.z > 0)
        def _(j=j):
            near(j).wait_send()

        twin_a(j).wait_send()
        twin_b(j).wait_send()


def collect_pairs(grads, reach, direct, number):
    if not direct or reach != 4:
        devices = range(lax.axis_size("shard"))
        own = grads[reach].astype(F32)
        for distance in range(1, reach + 1):
            route = [(i, i - distance) for i in devices if i - distance in devices]
            own = own + lax.ppermute(grads[reach - distance], "shard", route).astype(F32)
        return own
    shape = grads.shape[1:]
    return pl.pallas_call(
        collect_kernel,
        out_shape=jax.ShapeDtypeStruct(shape, F32),
        in_specs=[pl.BlockSpec(memory_space=VMEM)],
        out_specs=pl.BlockSpec(memory_space=VMEM),
        scratch_shapes=[VMEM(shape, BF)] * 6 + [DMA((4, shape[0])), DMA((4, shape[0]))],
        compiler_params=pltpu.CompilerParams(
            collective_id=number, has_side_effects=True, vmem_limit_bytes=BIG_VMEM
        ),
        name=f"collect_{number}",
    )(grads)


def angles(positions):
    half_dim = HEAD_DIM // 2
    inverse = rope_base ** (-(2.0 * jnp.arange(half_dim, dtype=F32) / HEAD_DIM))
    phases = positions.astype(F32)[:, None] * inverse[None, :]
    return (jnp.cos(phases)[:, None, :], jnp.sin(phases)[:, None, :])


def rotate(tensor, cosine_table, sine_table):
    half_dim = HEAD_DIM // 2
    front, back = tensor[..., :half_dim], tensor[..., half_dim:]
    return jnp.concatenate(
        [front * cosine_table - back * sine_table, back * cosine_table + front * sine_table],
        axis=-1,
    )


def norm_back(upstream, normed, scale_rows):
    mean = jnp.sum(upstream * normed, axis=-1, keepdims=True) * (1.0 / D)
    return scale_rows * (upstream - normed * mean)


def adam_step(weight_now, gradient, first, second, decay_factor):
    old_weight = weight_now.astype(F32)
    moment = beta_one * first + (1.0 - beta_one) * gradient
    square = beta_two * second + (1.0 - beta_two) * gradient * gradient
    corrected = moment / (1.0 - beta_one**STEP)
    divisor = jnp.sqrt(square / (1.0 - beta_two**STEP)) + adam_eps
    update = -learn_rate * (corrected / divisor + decay_factor * old_weight)
    return (gradient, moment, square, old_weight + update, update)


def shards(
    direct,
    block_input,
    block_cotangent,
    lengths,
    attend_gain,
    attend_weight,
    output_weight,
    expand_gain,
    expand_weight,
    shrink_weight,
    attend_gain_first,
    attend_weight_first,
    output_weight_first,
    expand_gain_first,
    expand_weight_first,
    shrink_weight_first,
    attend_gain_second,
    attend_weight_second,
    output_weight_second,
    expand_gain_second,
    expand_weight_second,
    shrink_weight_second,
):
    tokens = block_input.shape[0]
    shard_count = lax.axis_size("shard")
    token_count = tokens * shard_count * lax.axis_size("rep")
    reach = (MAXLEN - 2) // tokens + 1
    own_rows = attend_weight.shape[0]
    rows = -(-(own_rows + 2) // 16) * 16
    width = shard_count * rows

    def padded(tensor):
        blocks = tensor.reshape(tokens, shard_count, own_rows)
        return jnp.pad(blocks, ((0, 0), (0, 0), (0, rows - own_rows))).reshape(tokens, width)

    def unpadded(tensor):
        return tensor.reshape(tokens, shard_count, rows)[:, :, :own_rows].reshape(tokens, D)

    def with_gain(weight, gain):
        tail = jnp.pad(gain[None, :], ((0, rows - own_rows - 1), (0, weight.shape[1] - own_rows)))
        return jnp.concatenate([weight, tail], axis=0)

    def gain_of(planes):
        return jnp.pad(
            planes[:, own_rows, :own_rows], ((0, 0), (0, rows - own_rows))
        ).reshape(1, width).astype(F32)

    def add_gain(planes, term):
        row = term.reshape(shard_count, 1, rows).astype(planes.dtype)
        return lax.dynamic_update_slice(planes, row, (0, own_rows, 0))

    first_row = lax.axis_index("shard") * tokens
    local_index = first_row + jnp.arange(tokens, dtype=jnp.int32)
    key_index = first_row - reach * tokens + jnp.arange((reach + 1) * tokens, dtype=jnp.int32)
    ends = jnp.cumsum(lengths[0], dtype=jnp.int32)
    starts = ends - lengths[0]
    seq_count = lengths.shape[1]
    in_key = (key_index[:, None] >= starts[None, :]) & (key_index[:, None] < ends[None, :])
    in_query = (local_index[None, :] >= starts[:, None]) & (local_index[None, :] < ends[:, None])
    lanes = 2 * HEAD_DIM
    feat = jnp.concatenate(
        [
            in_key.astype(BF),
            (key_index < 0).astype(BF)[:, None],
            jnp.zeros((key_index.shape[0], ONES - seq_count - 1), BF),
            jnp.ones((key_index.shape[0], lanes - ONES), BF),
        ],
        axis=1,
    )
    qfeat = jnp.concatenate(
        [
            jnp.where(in_query, 0.0, NEG).astype(BF),
            jnp.full((1, tokens), NEG, BF),
            jnp.zeros((lanes - seq_count - 1, tokens), BF),
        ],
        axis=0,
    )
    start_index = jnp.sum(in_query * starts[:, None], axis=0, dtype=jnp.int32)
    cosine_table, sine_table = angles(local_index - start_index)

    attend_own = with_gain(attend_weight, attend_gain)
    rest_own = with_gain(
        jnp.concatenate([expand_weight, shrink_weight.T, output_weight.T], axis=1), expand_gain
    )
    attend_planes = gather_rows(attend_own, shard_count, direct, 0)
    rest_planes = gather_rows(rest_own, shard_count, direct, 1)
    gain_one, gain_two = gain_of(attend_planes), gain_of(rest_planes)
    joint_weight = attend_planes.reshape(width, JW)
    rest = rest_planes.reshape(width, rest_own.shape[1])
    expand_full, shrink_full, out_full = rest[:, : 2 * FF], rest[:, 2 * FF : 3 * FF], rest[:, 3 * FF :]
    real = (jnp.arange(width, dtype=jnp.int32) % rows < own_rows)[None, :]

    inputs = padded(block_input).astype(F32)
    scale_one = lax.rsqrt(jnp.sum(inputs * inputs, axis=-1, keepdims=True) * (1.0 / D) + eps_norm)
    normed_one = inputs * scale_one
    hidden_one = (normed_one * gain_one).astype(BF)
    joint = dot(hidden_one, joint_weight)
    queries = rotate(joint[:, :QW].reshape(tokens, HEADS, HEAD_DIM), cosine_table, sine_table)
    key_rows = rotate(
        joint[:, QW : QW + KW].reshape(tokens, KV_HEADS, HEAD_DIM), cosine_table, sine_table
    )
    values = joint[:, QW + KW :].reshape(tokens, KV_HEADS, HEAD_DIM)
    pairs = jnp.concatenate([key_rows, values], axis=-1).astype(BF).transpose(1, 0, 2)
    qt = queries.astype(BF).reshape(tokens, QW).T
    window = spread_pairs(pairs, reach, direct, 2)
    mixedt, lse = attend_forward(window, feat, qt, qfeat)
    middle = inputs + dot(mixedt, out_full, 0, 1)
    scale_two = lax.rsqrt(jnp.sum(middle * middle, axis=-1, keepdims=True) * (1.0 / D) + eps_norm)
    normed_two = middle * scale_two
    hidden_two = (normed_two * gain_two).astype(BF)
    gate_up = dot(hidden_two, expand_full)
    gate_value, upper_value = gate_up[:, :FF], gate_up[:, FF:]
    sigmoid_gate = jax.nn.sigmoid(gate_value)
    inner_rows = (gate_value * sigmoid_gate * upper_value).astype(BF)
    block_output = middle + dot(inner_rows, shrink_full, 1, 1)

    cotangent = padded(block_cotangent)
    shrink_term = dot(cotangent, inner_rows, 0, 0)
    inner_grad = dot(cotangent, shrink_full)
    gate_grad = (
        inner_grad * upper_value * sigmoid_gate * (1.0 + gate_value * (1.0 - sigmoid_gate))
    ).astype(BF)
    upper_grad = (inner_grad * gate_value * sigmoid_gate).astype(BF)
    gate_up_grad = jnp.concatenate([gate_grad, upper_grad], axis=1)
    expand_term = dot(hidden_two, gate_up_grad, 0, 0)
    hidden_two_grad = jnp.where(real, dot(gate_up_grad, expand_full, 1, 1), 0.0)
    gain_two_term = jnp.sum(hidden_two_grad * normed_two, axis=0)
    middle_grad = cotangent.astype(F32) + norm_back(
        hidden_two_grad * gain_two, normed_two, scale_two
    )
    branch_grad = middle_grad.astype(BF)
    output_term = dot(branch_grad, mixedt, 0, 1)
    gradt = dot(out_full, branch_grad, 0, 1).astype(BF)
    rest_term = jnp.concatenate(
        [expand_term.astype(BF), shrink_term.astype(BF), output_term.astype(BF)], axis=1
    ).reshape(shard_count, rows, rest_own.shape[1])
    rest_sum = reduce_rows(add_gain(rest_term, gain_two_term), direct, 3)

    dqt, dwindow = attend_backward(window, feat, qt, qfeat, gradt, mixedt, lse)
    own_pairs = collect_pairs(dwindow, reach, direct, 4).transpose(1, 0, 2)
    dq = dqt.T.reshape(tokens, HEADS, HEAD_DIM)
    query_raw = rotate(dq, cosine_table, -sine_table).reshape(tokens, QW)
    key_raw = rotate(own_pairs[..., :HEAD_DIM], cosine_table, -sine_table).reshape(tokens, KW)
    value_raw = own_pairs[..., HEAD_DIM:].reshape(tokens, KW)
    joint_grad = jnp.concatenate([query_raw, key_raw, value_raw], axis=1).astype(BF)
    joint_term = dot(hidden_one, joint_grad, 0, 0).astype(BF)
    hidden_one_grad = jnp.where(real, dot(joint_grad, joint_weight, 1, 1), 0.0)
    gain_one_term = jnp.sum(hidden_one_grad * normed_one, axis=0)
    input_gradient = middle_grad + norm_back(hidden_one_grad * gain_one, normed_one, scale_one)
    attend_sum = reduce_rows(
        add_gain(joint_term.reshape(shard_count, rows, JW), gain_one_term), direct, 5
    )

    grad_scale = grad_factor * token_count ** (-0.5)
    rest_grad, attend_grad = rest_sum * grad_scale, attend_sum * grad_scale
    first_gain = adam_step(
        attend_gain, attend_grad[own_rows, :own_rows], attend_gain_first, attend_gain_second, 0.0
    )
    first_joint = adam_step(
        attend_weight,
        attend_grad[:own_rows],
        attend_weight_first,
        attend_weight_second,
        decay_rate,
    )
    first_output = adam_step(
        output_weight,
        rest_grad[:own_rows, 3 * FF :].T,
        output_weight_first,
        output_weight_second,
        decay_rate,
    )
    second_gain = adam_step(
        expand_gain, rest_grad[own_rows, :own_rows], expand_gain_first, expand_gain_second, 0.0
    )
    second_expand = adam_step(
        expand_weight,
        rest_grad[:own_rows, : 2 * FF],
        expand_weight_first,
        expand_weight_second,
        decay_rate,
    )
    second_shrink = adam_step(
        shrink_weight,
        rest_grad[:own_rows, 2 * FF : 3 * FF].T,
        shrink_weight_first,
        shrink_weight_second,
        decay_rate,
    )
    steps = (first_gain, first_joint, first_output, second_gain, second_expand, second_shrink)
    changed = [step[4] if step[0].ndim == 1 else step[3] for step in steps]
    return (
        unpadded(block_output),
        unpadded(input_gradient),
        *[step[0] for step in steps],
        *[step[1] for step in steps],
        *[step[2] for step in steps],
        *changed,
    )


def solution(mesh):
    whole_rows = P(("rep", "shard"), None)
    state = (P("shard"), P("shard", None), P(None, "shard")) * 2
    state = (state[0], state[1], state[2], state[3], state[4], state[5])
    direct = mesh.shape["rep"] == 4 and mesh.shape["shard"] == 8
    return jax.shard_map(
        functools.partial(shards, direct),
        mesh=mesh,
        in_specs=(whole_rows, whole_rows, P("rep", None), *state, *state, *state),
        out_specs=(whole_rows, whole_rows, *state, *state, *state, *state),
        check_vma=False,
    )
```

```python
import functools
import math

import jax
import jax.numpy as jnp
from jax import lax
from jax.experimental import pallas as pl
from jax.experimental.pallas import tpu as pltpu
from jax.sharding import PartitionSpec as P

HEADS = 15
KV_HEADS = 5
HEAD_DIM = 64
GROUP = HEADS // KV_HEADS
FF = 2560
MAXLEN = 2048
STEP = 10
QW = 960
KW = 320
JW = QW + 2 * KW
D = 960

eps_norm = 1e-05
rope_base = 100000.0
beta_one = 0.9
beta_two = 0.95
adam_eps = 1e-08
learn_rate = 0.05
decay_rate = 0.1
grad_factor = 4.0

F32 = jnp.float32
BF = jnp.bfloat16
MESH = pl.DeviceIdType.MESH
ANY = pl.ANY
VMEM = pltpu.VMEM
DMA = pltpu.SemaphoreType.DMA

QC = 256
KB = 768
HALF = 64
ONES = 112
NEG = -1e30
EXP_SCALE = HEAD_DIM**-0.5 * math.log2(math.e)
BIG_VMEM = 60 * 2**20


def dot(a, b, ca=1, cb=0):
    return lax.dot_general(a, b, (((ca,), (cb,)), ((), ())), preferred_element_type=F32)


def causal_tile():
    key = lax.broadcasted_iota(jnp.int32, (QC, QC), 0)
    query = lax.broadcasted_iota(jnp.int32, (QC, QC), 1)
    return key <= query


def mask_last(scores, causal):
    last = jnp.where(causal, scores[KB - QC :], NEG)
    return jnp.concatenate([scores[: KB - QC], last], axis=0)


def attend_forward_setup(feat_ref, qfeat_ref, kvf, vt, qa):
    lanes = feat_ref.shape[1]
    kvf[:, lanes:] = feat_ref[...]
    qa[HALF:lanes, :] = jnp.zeros((lanes - HALF, qa.shape[1]), BF)
    qa[lanes:, :] = qfeat_ref[...]
    vt[HALF:, :] = jnp.ones((vt.shape[0] - HALF, vt.shape[1]), BF)


def attend_forward_keys(j, kv_ref, kvf, vt):
    blocks, _, rows, lanes = kv_ref.shape
    for block in range(blocks):
        part = kv_ref[block, j]
        kvf[block * rows : (block + 1) * rows, :lanes] = part
        vt[:HALF, block * rows : (block + 1) * rows] = part.T[HALF:, :]


def attend_forward_head(h, qt_ref, mixed_ref, lse_ref, kvf, vt, qa, sb):
    tokens = qt_ref.shape[1]
    steps = (kvf.shape[0] - (tokens - QC)) // KB
    causal = causal_tile()
    row = pl.multiple_of(h * HEAD_DIM, HEAD_DIM)
    qa[:HALF, :] = qt_ref[pl.ds(row, HEAD_DIM), :]
    tops = []
    for chunk in range(tokens // QC):
        low = chunk * QC
        highest = None
        for b in range(steps):
            first = low + b * KB
            s = dot(kvf[first : first + KB, :], qa[:, low : low + QC])
            if b == steps - 1:
                s = mask_last(s, causal)
            sb[chunk, b * KB : (b + 1) * KB, :] = s
            peak = jnp.max(s.reshape(KB // 8, 8, QC), axis=0)
            highest = peak if highest is None else jnp.maximum(highest, peak)
        tops.append(jnp.max(highest, axis=0, keepdims=True))
    for chunk in range(tokens // QC):
        low = chunk * QC
        shift = tops[chunk] * EXP_SCALE
        total = None
        for b in range(steps):
            first = low + b * KB
            s = sb[chunk, b * KB : (b + 1) * KB, :]
            p = jnp.exp2(s * EXP_SCALE - shift).astype(BF)
            term = dot(vt[:, first : first + KB], p)
            total = term if total is None else total + term
        weight = total[HALF : HALF + 1, :]
        mixed_ref[pl.ds(row, HEAD_DIM), low : low + QC] = (
            total[:HALF, :] * (1.0 / weight)
        ).astype(BF)
        lse_ref[pl.ds(h, 1), :, low : low + QC] = (
            tops[chunk] * HEAD_DIM**-0.5 + jnp.log(weight)
        )[None]


def attend_forward_scratch(keys, lanes, tokens):
    return [
        VMEM((keys, 2 * lanes), BF),
        VMEM((HALF + 16, keys), BF),
        VMEM((2 * lanes, tokens), BF),
        VMEM((tokens // QC, keys - (tokens - QC), QC), F32),
    ]


def attend_forward_kernel(
    kv_ref, feat_ref, qt_ref, qfeat_ref, mixed_ref, lse_ref, kvf, vt, qa, sb
):
    attend_forward_setup(feat_ref, qfeat_ref, kvf, vt, qa)

    def key_head(j, _):
        attend_forward_keys(j, kv_ref, kvf, vt)

        def head(g, _):
            attend_forward_head(j * GROUP + g, qt_ref, mixed_ref, lse_ref, kvf, vt, qa, sb)
            return 0

        lax.fori_loop(0, GROUP, head, 0)
        return 0

    lax.fori_loop(0, kv_ref.shape[1], key_head, 0)


def attend_forward(window, feat, qt, qfeat):
    blocks, kv_heads, rows, lanes = window.shape
    tokens = qt.shape[1]
    return pl.pallas_call(
        attend_forward_kernel,
        out_shape=(
            jax.ShapeDtypeStruct(qt.shape, BF),
            jax.ShapeDtypeStruct((HEADS, 1, tokens), F32),
        ),
        scratch_shapes=attend_forward_scratch(blocks * rows, lanes, tokens),
        compiler_params=pltpu.CompilerParams(vmem_limit_bytes=BIG_VMEM),
        name="attend_forward",
    )(window, feat, qt, qfeat)


def three_parts(value, rows):
    one = value.astype(BF).astype(F32)
    two = (value - one).astype(BF).astype(F32)
    three = value - one - two
    shape = (rows, value.shape[1])
    place = lax.broadcasted_iota(jnp.int32, shape, 0)
    parts = [jnp.broadcast_to(part, shape) for part in (one, two, three)]
    chosen = jnp.where(
        place == 0, parts[0], jnp.where(place == 1, parts[1], jnp.where(place == 2, parts[2], 0.0))
    )
    return chosen.astype(BF)


def attend_backward_setup(feat_ref, kvf, qa, da, rhs):
    lanes = feat_ref.shape[1]
    kvf[:, lanes:] = feat_ref[...]
    qa[HALF:lanes, :] = jnp.zeros((lanes - HALF, qa.shape[1]), BF)
    da[...] = jnp.zeros_like(da)
    rhs[...] = jnp.zeros_like(rhs)


def attend_backward_keys(j, kv_ref, kvf, kt, acc):
    blocks, _, rows, lanes = kv_ref.shape
    for block in range(blocks):
        part = kv_ref[block, j]
        kvf[block * rows : (block + 1) * rows, :lanes] = part
        kt[:, block * rows : (block + 1) * rows] = part.T[:HALF, :]
    acc[...] = jnp.zeros_like(acc)


def attend_backward_head(
    h, qt_ref, qfeat_ref, gradt_ref, mixed_ref, lse_ref, dq_ref, kvf, kt, qa, da, acc, rhs
):
    tokens = qt_ref.shape[1]
    lanes = qfeat_ref.shape[0]
    steps = (kvf.shape[0] - (tokens - QC)) // KB
    causal = causal_tile()
    extra = lanes - ONES
    row = pl.multiple_of(h * HEAD_DIM, HEAD_DIM)
    q = qt_ref[pl.ds(row, HEAD_DIM), :]
    grad = gradt_ref[pl.ds(row, HEAD_DIM), :]
    qa[:HALF, :] = q
    da[HALF:lanes, :] = grad
    mixed = mixed_ref[pl.ds(row, HEAD_DIM), :].astype(F32)
    row_total = jnp.sum(grad.astype(F32) * mixed, axis=0, keepdims=True)
    lse = lse_ref[pl.ds(h, 1), :, :][0]
    qa[lanes : lanes + ONES, :] = qfeat_ref[:ONES, :]
    qa[lanes + ONES :, :] = three_parts(-(HEAD_DIM**0.5) * lse, extra)
    da[lanes + ONES :, :] = three_parts(-row_total, extra)
    query_grads = [None] * (tokens // QC)
    for chunk in range(tokens // QC):
        low = chunk * QC
        rhs[chunk, :HALF, :QC] = q[:, low : low + QC]
        rhs[chunk, HALF:, QC:] = grad[:, low : low + QC]
    for b in range(steps):
        for chunk in range(tokens // QC):
            low = chunk * QC
            first = low + b * KB
            keys = kvf[first : first + KB, :]
            s = dot(keys, qa[:, low : low + QC])
            if b == steps - 1:
                s = mask_last(s, causal)
            p = jnp.exp2(s * EXP_SCALE)
            dp = dot(keys, da[:, low : low + QC])
            ds = (p * dp).astype(BF)
            both = jnp.concatenate([ds, p.astype(BF)], axis=1)
            acc[first : first + KB, :] += dot(both, rhs[chunk], 1, 1)
            term = dot(kt[:, first : first + KB], ds)
            old = query_grads[chunk]
            query_grads[chunk] = term if old is None else old + term
    for chunk in range(tokens // QC):
        low = chunk * QC
        dq_ref[pl.ds(row, HEAD_DIM), low : low + QC] = query_grads[chunk] * HEAD_DIM**-0.5


def attend_backward_done(j, acc, dkv_ref):
    blocks, _, rows, lanes = dkv_ref.shape
    lane = lax.broadcasted_iota(jnp.int32, (1, lanes), 1)
    factor = jnp.where(lane < HALF, HEAD_DIM**-0.5, 1.0)
    for block in range(blocks):
        part = acc[block * rows : (block + 1) * rows, :]
        dkv_ref[block, j] = (part * factor).astype(dkv_ref.dtype)


def attend_backward_scratch(keys, lanes, tokens):
    return [
        VMEM((keys, 2 * lanes), BF),
        VMEM((HALF, keys), BF),
        VMEM((2 * lanes, tokens), BF),
        VMEM((2 * lanes, tokens), BF),
        VMEM((keys, lanes), F32),
        VMEM((tokens // QC, lanes, 2 * QC), BF),
    ]


def attend_backward_kernel(
    kv_ref, feat_ref, qt_ref, qfeat_ref, gradt_ref, mixed_ref, lse_ref, dq_ref, dkv_ref, *scratch
):
    kvf, kt, qa, da, acc, rhs = scratch
    attend_backward_setup(feat_ref, kvf, qa, da, rhs)

    def key_head(j, _):
        attend_backward_keys(j, kv_ref, kvf, kt, acc)

        def head(g, _):
            attend_backward_head(
                j * GROUP + g, qt_ref, qfeat_ref, gradt_ref, mixed_ref, lse_ref, dq_ref, *scratch
            )
            return 0

        lax.fori_loop(0, GROUP, head, 0)
        attend_backward_done(j, acc, dkv_ref)
        return 0

    lax.fori_loop(0, kv_ref.shape[1], key_head, 0)


def attend_backward(window, feat, qt, qfeat, gradt, mixed, lse):
    blocks, kv_heads, rows, lanes = window.shape
    tokens = qt.shape[1]
    return pl.pallas_call(
        attend_backward_kernel,
        out_shape=(
            jax.ShapeDtypeStruct(qt.shape, F32),
            jax.ShapeDtypeStruct(window.shape, BF),
        ),
        scratch_shapes=attend_backward_scratch(blocks * rows, lanes, tokens),
        compiler_params=pltpu.CompilerParams(vmem_limit_bytes=BIG_VMEM),
        name="attend_backward",
    )(window, feat, qt, qfeat, gradt, mixed, lse)


class Place:
    def __init__(self):
        self.r = lax.axis_index("rep")
        self.s = lax.axis_index("shard")
        self.x, self.y = lax.rem(self.r, 2), self.r // 2
        self.z, self.c = self.s // 2, lax.rem(self.s, 2)
        self.rx = self.y * 2 + (1 - self.x)
        self.ry = (1 - self.y) * 2 + self.x
        self.rd = 3 - self.r
        self.x_side = (self.rx, self.s)
        self.y_side = (self.ry, self.s)
        self.core_side = (self.r, self.z * 2 + (1 - self.c))
        self.has_later, self.has_earlier = self.z < 3, self.z > 0
        self.later = (self.r, lax.min(self.s + 2, 7))
        self.earlier = (self.r, lax.max(self.s - 2, 0))

    def z_to(self, k):
        return lax.rem(self.z + k, 4)

    def z_side(self, k):
        return (self.r, self.z_to(k) * 2 + self.c)

    def arrival(self, i):
        low = self.z < 2
        first = jnp.where(self.z == 0, 1, jnp.where(self.z == 1, 0, jnp.where(self.z == 2, 3, 2)))
        if i == 0:
            return first
        if i == 1:
            return jnp.where(low, 2, 1)
        return jnp.where(low, 3, 0)


def greet(at, whole_line):
    barrier = pltpu.get_barrier_semaphore()

    def signal(device):
        pl.semaphore_signal(barrier, inc=1, device_id=device, device_id_type=MESH)

    for device in (at.x_side, at.y_side, at.core_side):
        signal(device)
    if whole_line:
        for k in (1, 2, 3):
            signal(at.z_side(k))
        pl.semaphore_wait(barrier, 6)
        return

    @pl.when(at.has_later)
    def _():
        signal(at.later)

    @pl.when(at.has_earlier)
    def _():
        signal(at.earlier)

    count = 3 + jnp.where(at.has_later, 1, 0) + jnp.where(at.has_earlier, 1, 0)
    pl.semaphore_wait(barrier, count)


def remote(src, dst, send, recv, device):
    return pltpu.make_async_remote_copy(
        src_ref=src, dst_ref=dst, send_sem=send, recv_sem=recv, device_id=device, device_id_type=MESH
    )


class Gather:
    COUNT = 31

    def __init__(self, at, own, full, columns, local_sem, send, recv):
        self.at, self.own, self.full, self.columns = at, own, full, columns
        self.local_sem, self.send, self.recv = local_sem, send, recv
        self.rows = own.shape[0]
        self.quarter, self.half = self.rows // 4, self.rows // 8

    def piece(self, plane, owner, part=None):
        start = owner * self.quarter + (0 if part is None else part * self.half)
        size = self.quarter if part is None else self.half
        return self.full.at[
            plane, pl.ds(pl.multiple_of(start, self.half), size), pl.ds(*self.columns)
        ]

    def copy(self, index, src, dst, device, landed=None):
        return remote(
            src, dst, self.send.at[index], self.recv.at[index if landed is None else landed], device
        )

    def core_copy(self):
        src = self.own.at[:, pl.ds(*self.columns)]
        return self.copy(
            28, src, self.full.at[self.at.s, :, pl.ds(*self.columns)], self.at.core_side
        )

    def local_copy(self):
        return pltpu.make_async_copy(
            self.own.at[:, pl.ds(*self.columns)],
            self.full.at[self.at.s, :, pl.ds(*self.columns)],
            self.local_sem,
        )

    def z_copy(self, up):
        at = self.at
        src = self.own.at[
            pl.ds(pl.multiple_of(at.r * self.quarter, self.quarter), self.quarter),
            pl.ds(*self.columns),
        ]
        device = at.later if up else at.earlier
        return self.copy(29 if up else 30, src, self.piece(at.s, at.r), device, at.z)

    def start_core(self):
        self.local_copy().start()
        self.core_copy().start()

    def start_z(self):
        @pl.when(self.at.has_later)
        def _():
            self.z_copy(True).start()

        @pl.when(self.at.has_earlier)
        def _():
            self.z_copy(False).start()

    def plane(self, i, other=False):
        c = 1 - self.at.c if other else self.at.c
        return self.at.arrival(i) * 2 + c

    def forwards(self, i):
        at = self.at
        chip = at.arrival(i)
        got = self.piece(self.plane(i), at.r)
        return [
            ((chip < at.z) & at.has_later, self.copy(i, got, got, at.later, chip)),
            ((chip > at.z) & at.has_earlier, self.copy(i, got, got, at.earlier, chip)),
        ]

    def out_copies(self, i):
        at, plane = self.at, self.plane(i)
        got = self.piece(plane, at.r)
        return [
            self.copy(4 + i, got, got, at.x_side),
            self.copy(7 + i, got, got, at.y_side),
            self.copy(10 + i, got, got, at.core_side),
        ]

    def cross_copies(self, i):
        at, plane = self.at, self.plane(i)
        one, two = self.piece(plane, at.rx, 0), self.piece(plane, at.ry, 1)
        from_x, from_y = self.piece(plane, at.rx), self.piece(plane, at.ry)
        return [
            self.copy(13 + i, one, one, at.y_side),
            self.copy(16 + i, from_x, from_x, at.core_side),
            self.copy(19 + i, two, two, at.x_side),
            self.copy(22 + i, from_y, from_y, at.core_side),
        ]

    def last_copy(self, i):
        got = self.piece(self.plane(i), self.at.rd)
        return self.copy(25 + i, got, got, self.at.core_side)

    def arrive(self, landed, ref):
        remote(
            ref, ref, self.send.at[landed], self.recv.at[landed], self.at.core_side
        ).wait_recv()

    def z(self, i):
        at = self.at
        self.arrive(at.arrival(i), self.piece(self.plane(i), at.r))
        for condition, copy in self.forwards(i):
            pl.when(condition)(copy.start)
        for copy in self.out_copies(i):
            copy.start()

    def cross(self, i):
        at, plane = self.at, self.plane(i)
        copies = self.cross_copies(i)
        self.arrive(4 + i, self.piece(plane, at.rx))
        copies[0].start()
        copies[1].start()
        self.arrive(7 + i, self.piece(plane, at.ry))
        copies[2].start()
        copies[3].start()

    def last(self, i):
        at, plane = self.at, self.plane(i)
        self.arrive(13 + i, self.piece(plane, at.rd, 0))
        self.arrive(19 + i, self.piece(plane, at.rd, 1))
        self.last_copy(i).start()

    def landed(self):
        at = self.at
        self.arrive(28, self.full.at[at.core_side[1], :, pl.ds(*self.columns)])
        for i in range(3):
            plane = self.plane(i, True)
            self.arrive(10 + i, self.piece(plane, at.r))
            self.arrive(16 + i, self.piece(plane, at.rx))
            self.arrive(22 + i, self.piece(plane, at.ry))
            self.arrive(25 + i, self.piece(plane, at.rd))
        self.local_copy().wait()

    def sent(self):
        at = self.at
        self.core_copy().wait_send()
        pl.when(at.has_later)(self.z_copy(True).wait_send)
        pl.when(at.has_earlier)(self.z_copy(False).wait_send)
        for i in range(3):
            for condition, copy in self.forwards(i):
                pl.when(condition)(copy.wait_send)
            for copy in self.out_copies(i) + self.cross_copies(i) + [self.last_copy(i)]:
                copy.wait_send()


class Spread:
    def __init__(self, at, win, send, recv):
        self.at, self.win, self.sems = at, win, (send, recv)
        even = at.c == 0
        self.near, self.far = jnp.where(even, 1, 3), jnp.where(even, 3, 1)

    def copy(self, n, j, src, dst, device):
        send, recv = self.sems
        return remote(
            self.win.at[src, j], self.win.at[dst, j], send.at[n, j], recv.at[n, j], device
        )

    def first(self, j):
        return self.copy(0, j, 4, 2, self.at.later)

    def twin_own(self, j):
        return self.copy(1, j, 4, 3, self.at.core_side)

    def second(self, j):
        return self.copy(2, j, 2, 0, self.at.later)

    def twin_near(self, j, place):
        return self.copy(3, j, 2, place, self.at.core_side)

    def twin_far(self, j):
        return self.copy(4, j, 0, 1, self.at.core_side)

    def clear(self):
        for block in range(4):
            @pl.when(self.at.s < 4 - block)
            def _(block=block):
                self.win[block] = jnp.zeros(self.win.shape[1:], self.win.dtype)

    def start(self, j):
        pl.when(self.at.has_later)(self.first(j).start)
        pl.when(self.at.c == 0)(self.twin_own(j).start)

    def one(self, j):
        at = self.at

        @pl.when(at.has_earlier)
        def _():
            self.first(j).wait_recv()
            self.twin_near(j, self.near).start()
            pl.when(at.has_later)(self.second(j).start)

    def two(self, j):
        at = self.at

        @pl.when(at.z > 1)
        def _():
            self.second(j).wait_recv()
            pl.when(at.c == 1)(self.twin_far(j).start)

    def landed(self, j):
        at = self.at
        pl.when(at.c == 1)(self.twin_own(j).wait_recv)
        pl.when(at.has_earlier)(self.twin_near(j, self.far).wait_recv)
        pl.when((at.c == 0) & (at.z > 1))(self.twin_far(j).wait_recv)

    def sent(self, j):
        at = self.at
        pl.when(at.has_later)(self.first(j).wait_send)
        pl.when(at.c == 0)(self.twin_own(j).wait_send)
        pl.when(at.has_earlier)(self.twin_near(j, self.near).wait_send)
        pl.when(at.has_earlier & at.has_later)(self.second(j).wait_send)
        pl.when((at.c == 1) & (at.z > 1))(self.twin_far(j).wait_send)


class Collect:
    def __init__(self, at, grads, out, ra, rb, r2, r1, t2, t1, send, recv):
        self.at, self.grads, self.out = at, grads, out
        self.ra, self.rb, self.r2, self.r1, self.t2, self.t1 = ra, rb, r2, r1, t2, t1
        self.sems = (send, recv)

    def copy(self, n, j, src, dst, device):
        send, recv = self.sems
        return remote(src, dst, send.at[n, j], recv.at[n, j], device)

    def twin_a(self, j):
        return self.copy(0, j, self.grads.at[3, j], self.ra.at[j], self.at.core_side)

    def twin_b(self, j):
        return self.copy(1, j, self.grads.at[1, j], self.rb.at[j], self.at.core_side)

    def far(self, j):
        return self.copy(2, j, self.t2.at[j], self.r2.at[j], self.at.earlier)

    def near(self, j):
        return self.copy(3, j, self.t1.at[j], self.r1.at[j], self.at.earlier)

    def start(self, j):
        self.twin_b(j).start()
        self.twin_a(j).start()

    def one(self, j):
        self.twin_b(j).wait_recv()
        self.twin_a(j).wait_recv()
        even = self.at.c == 0
        from_a, from_b = self.ra[j].astype(F32), self.rb[j].astype(F32)
        none = jnp.zeros_like(from_a)
        self.t2[j] = (self.grads[0, j].astype(F32) + jnp.where(even, none, from_b)).astype(BF)
        pl.when(self.at.z > 1)(self.far(j).start)
        self.t1[j] = (self.grads[2, j].astype(F32) + jnp.where(even, from_b, from_a)).astype(BF)
        self.out[j] = self.grads[4, j].astype(F32) + jnp.where(even, from_a, none)

    def two(self, j):
        at = self.at

        @pl.when(at.has_earlier & at.has_later)
        def _():
            self.far(j).wait_recv()
            self.t1[j] = (self.t1[j].astype(F32) + self.r2[j].astype(F32)).astype(BF)

        pl.when(at.has_earlier)(self.near(j).start)

    def three(self, j):
        at = self.at

        @pl.when(at.has_later)
        def _():
            self.near(j).wait_recv()
            self.out[j] = self.out[j] + self.r1[j].astype(F32)

    def sent(self, j):
        at = self.at
        self.twin_a(j).wait_send()
        self.twin_b(j).wait_send()
        pl.when(at.z > 1)(self.far(j).wait_send)
        pl.when(at.has_earlier)(self.near(j).wait_send)


class Reduce:
    COUNT = 35

    def __init__(self, at, parts, out, own, r0, r1a, r1b, r2a, r2b, r3, local_sem, send, recv):
        self.at, self.parts, self.out, self.own = at, parts, out, own
        self.r0, self.r1a, self.r1b, self.r2a, self.r2b, self.r3 = r0, r1a, r1b, r2a, r2b, r3
        self.local_sem, self.send, self.recv = local_sem, send, recv
        self.rows = out.shape[0]
        self.quarter, self.half = self.rows // 4, self.rows // 8

    @staticmethod
    def scratch(rows, columns):
        half = rows // 8
        return [
            VMEM((4, rows, columns), BF),
            VMEM((4, rows, columns), BF),
            VMEM((4, 2, half, columns), BF),
            VMEM((4, 2, half, columns), BF),
            VMEM((4, half, columns), BF),
            VMEM((4, half, columns), BF),
            VMEM((3, 2 * half, columns), BF),
            DMA((4,)),
            DMA((Reduce.COUNT,)),
            DMA((Reduce.COUNT,)),
        ]

    def copy(self, index, src, dst, device):
        return remote(src, dst, self.send.at[index], self.recv.at[index], device)

    def arrive(self, index, ref):
        self.copy(index, ref, ref, self.at.core_side).wait_recv()

    def spot(self, owner, part):
        start = owner * self.quarter + part * self.half
        return pl.ds(pl.multiple_of(start, self.half), self.half)

    def piece(self, owner):
        start = pl.multiple_of(owner * self.quarter, self.quarter)
        return self.out.at[pl.ds(start, self.quarter), :]

    def add_into(self, k, where, ref):
        old = self.own[k, where, :].astype(F32)
        self.own[k, where, :] = (old + ref[...].astype(F32)).astype(BF)

    def local_copy(self, k):
        z = self.at.z_to(k + 1 if k < 3 else 0)
        return pltpu.make_async_copy(
            self.parts.at[z * 2 + self.at.c], self.own.at[k], self.local_sem.at[k]
        )

    def core_copy(self, k):
        z = self.at.z_to(k + 1 if k < 3 else 0)
        return self.copy(k, self.parts.at[z * 2 + 1 - self.at.c], self.r0.at[k], self.at.core_side)

    def one_copies(self, k):
        at, copies = self.at, []
        for i in range(2):
            a = self.own.at[k, self.spot(i * 2 + 1 - at.x, 0), :]
            b = self.own.at[k, self.spot((1 - at.y) * 2 + i, 1), :]
            copies.append(self.copy(4 + 4 * k + i, a, self.r1a.at[k, i], at.x_side))
            copies.append(self.copy(6 + 4 * k + i, b, self.r1b.at[k, i], at.y_side))
        return copies

    def two_copies(self, k):
        at = self.at
        a, b = self.own.at[k, self.spot(at.ry, 0), :], self.own.at[k, self.spot(at.rx, 1), :]
        return [
            self.copy(20 + 2 * k, a, self.r2a.at[k], at.y_side),
            self.copy(21 + 2 * k, b, self.r2b.at[k], at.x_side),
        ]

    def z_copy(self, k):
        at = self.at
        mine = pl.ds(pl.multiple_of(at.r * self.quarter, self.quarter), self.quarter)
        return self.copy(28 + k, self.own.at[k, mine, :], self.r3.at[k], at.z_side(k + 1))

    def back_copies(self):
        at, piece = self.at, self.piece
        a, b = self.out.at[self.spot(at.rx, 0), :], self.out.at[self.spot(at.ry, 1), :]
        return [
            self.copy(31, piece(at.r), piece(at.r), at.x_side),
            self.copy(32, piece(at.r), piece(at.r), at.y_side),
            self.copy(33, a, a, at.y_side),
            self.copy(34, b, b, at.x_side),
        ]

    def start(self, k):
        self.local_copy(k).start()
        self.core_copy(k).start()

    def zero(self, k):
        self.local_copy(k).wait()
        self.arrive(k, self.r0.at[k])

        def add_rows(i, _):
            where = pl.ds(pl.multiple_of(i * self.half, self.half), self.half)
            self.add_into(k, where, self.r0.at[k, where, :])
            return 0

        lax.fori_loop(0, self.rows // self.half, add_rows, 0)
        for copy in self.one_copies(k):
            copy.start()

    def one(self, k):
        at = self.at
        for i in range(2):
            self.arrive(4 + 4 * k + i, self.r1a.at[k, i])
            self.arrive(6 + 4 * k + i, self.r1b.at[k, i])
            self.add_into(k, self.spot(i * 2 + at.x, 0), self.r1a.at[k, i])
            self.add_into(k, self.spot(at.y * 2 + i, 1), self.r1b.at[k, i])
        for copy in self.two_copies(k):
            copy.start()

    def two(self, k):
        at = self.at
        self.arrive(20 + 2 * k, self.r2a.at[k])
        self.arrive(21 + 2 * k, self.r2b.at[k])
        self.add_into(k, self.spot(at.r, 0), self.r2a.at[k])
        self.add_into(k, self.spot(at.r, 1), self.r2b.at[k])
        if k < 3:
            self.z_copy(k).start()

    def three(self):
        at = self.at
        for k in range(3):
            self.arrive(28 + k, self.r3.at[k])
        for i in range(2):
            where = pl.ds(i * self.half, self.half)
            total = self.own[3, self.spot(at.r, i), :].astype(F32)
            for k in range(3):
                total += self.r3[k, where, :].astype(F32)
            self.out[self.spot(at.r, i), :] = total.astype(BF)
        copies = self.back_copies()
        copies[0].start()
        copies[1].start()

    def four(self):
        at = self.at
        copies = self.back_copies()
        self.arrive(31, self.piece(at.rx))
        copies[2].start()
        self.arrive(32, self.piece(at.ry))
        copies[3].start()

    def five(self):
        at = self.at
        self.arrive(33, self.out.at[self.spot(at.rd, 0), :])
        self.arrive(34, self.out.at[self.spot(at.rd, 1), :])
        for k in range(4):
            for copy in [self.core_copy(k)] + self.one_copies(k) + self.two_copies(k):
                copy.wait_send()
        for k in range(3):
            self.z_copy(k).wait_send()
        for copy in self.back_copies():
            copy.wait_send()


def at_steps(i, events):
    for n, event in events:
        pl.when(i == n)(event)


def front_kernel(
    x_ref,
    cos_ref,
    sin_ref,
    feat_ref,
    qfeat_ref,
    attend_own,
    rest_own,
    attend_ref,
    rest_ref,
    win_ref,
    qt_ref,
    mixed_ref,
    lse_ref,
    kvf,
    vt,
    qa,
    sb,
    hidden,
    kvt,
    local_sems,
    gather_send,
    gather_recv,
    spread_send,
    spread_recv,
):
    at = Place()
    shard_count, rows, columns = attend_ref.shape
    width = shard_count * rows
    tokens = x_ref.shape[0]
    kv_heads = win_ref.shape[1]
    own_rows = D // shard_count
    cut = 2 * FF
    greet(at, False)

    def gather(n, own, full, cols):
        return Gather(
            at, own, full, cols, local_sems.at[n], gather_send.at[n], gather_recv.at[n]
        )

    first = gather(0, attend_own, attend_ref, (0, columns))
    second = gather(1, rest_own, rest_ref, (0, cut))
    third = gather(2, rest_own, rest_ref, (cut, rest_own.shape[1] - cut))
    spread = Spread(at, win_ref, spread_send, spread_recv)

    first.start_z()
    first.start_core()
    second.start_core()
    third.start_core()
    spread.clear()
    attend_forward_setup(feat_ref, qfeat_ref, kvf, vt, qa)
    for i in range(3):
        first.z(i)
    second.start_z()
    for i in range(3):
        first.cross(i)
    second.z(0)
    for i in range(3):
        first.last(i)
    first.landed()

    inputs = x_ref[...].astype(F32)
    scale = lax.rsqrt(jnp.sum(inputs * inputs, axis=-1, keepdims=True) * (1.0 / D) + eps_norm)
    for s in range(shard_count):
        lane = slice(s * rows, (s + 1) * rows)
        gain = attend_ref[s, own_rows : own_rows + 1, :rows].astype(F32)
        hidden[:, lane] = (x_ref[:, lane].astype(F32) * scale * gain).astype(BF)

    def project(start):
        stop = min(start + 256, columns)
        weight = attend_ref[:, :, start:stop].reshape(width, stop - start)
        flipped = dot(hidden[...], weight).T
        for low in range(0, stop - start, HEAD_DIM):
            column = start + low
            head = flipped[low : low + HEAD_DIM, :]
            if column < QW + KW:
                half = HEAD_DIM // 2
                front, back = head[:half], head[half:]
                head = jnp.concatenate(
                    [
                        front * cos_ref[...] - back * sin_ref[...],
                        back * cos_ref[...] + front * sin_ref[...],
                    ],
                    axis=0,
                )
            if column < QW:
                qt_ref[column : column + HEAD_DIM, :] = head.astype(BF)
            elif column < QW + KW:
                kvt[(column - QW) // HEAD_DIM, :HALF, :] = head.astype(BF)
            else:
                kvt[(column - QW - KW) // HEAD_DIM, HALF:, :] = head.astype(BF)

    split = QW // 128 * 128
    for start in range(split, columns, 256):
        project(start)
    for j in range(kv_heads):
        win_ref[4, j] = kvt[j].T
        spread.start(j)
    second.z(1)
    third.start_z()
    for start in range(0, split, 256):
        project(start)
    spread.one(0)
    second.z(2)
    spread.one(1)
    spread.two(0)
    events = [
        (0, lambda: third.z(0)),
        (1, lambda: second.cross(0)),
        (2, lambda: third.z(1)),
        (3, lambda: second.cross(1)),
        (4, lambda: third.z(2)),
        (5, lambda: second.cross(2)),
        (6, lambda: third.cross(0)),
        (7, lambda: second.last(0)),
        (8, lambda: third.cross(1)),
        (9, lambda: second.last(1)),
        (10, lambda: third.cross(2)),
        (11, lambda: second.last(2)),
        (12, lambda: third.last(0)),
        (13, lambda: third.last(1)),
        (14, lambda: third.last(2)),
    ]

    def key_head(j, _):
        pl.when(j + 2 < kv_heads)(lambda: spread.one(j + 2))
        pl.when(j + 1 < kv_heads)(lambda: spread.two(j + 1))
        spread.landed(j)
        attend_forward_keys(j, win_ref, kvf, vt)

        def head(g, _):
            h = j * GROUP + g
            attend_forward_head(h, qt_ref, mixed_ref, lse_ref, kvf, vt, qa, sb)
            at_steps(h, events)
            return 0

        lax.fori_loop(0, GROUP, head, 0)
        spread.sent(j)
        return 0

    lax.fori_loop(0, kv_heads, key_head, 0)
    second.landed()
    third.landed()
    for part in (first, second, third):
        part.sent()


def front(x, cosine, sine, feat, qfeat, attend_own, rest_own, shard_count, number):
    tokens, width = x.shape
    keys, lanes = feat.shape
    rows = attend_own.shape[0]
    window = (keys // tokens, KV_HEADS, tokens, lanes)
    return pl.pallas_call(
        front_kernel,
        out_shape=(
            jax.ShapeDtypeStruct((shard_count,) + attend_own.shape, BF),
            jax.ShapeDtypeStruct((shard_count,) + rest_own.shape, BF),
            jax.ShapeDtypeStruct(window, BF),
            jax.ShapeDtypeStruct((QW, tokens), BF),
            jax.ShapeDtypeStruct((QW, tokens), BF),
            jax.ShapeDtypeStruct((HEADS, 1, tokens), F32),
        ),
        in_specs=[pl.BlockSpec(memory_space=VMEM)] * 6 + [pl.BlockSpec(memory_space=ANY)],
        out_specs=(
            pl.BlockSpec(memory_space=VMEM),
            pl.BlockSpec(memory_space=ANY),
        )
        + (pl.BlockSpec(memory_space=VMEM),) * 4,
        scratch_shapes=attend_forward_scratch(keys, lanes, tokens)
        + [
            VMEM((tokens, width), BF),
            VMEM((KV_HEADS, lanes, tokens), BF),
            DMA((3,)),
            DMA((3, Gather.COUNT)),
            DMA((3, Gather.COUNT)),
            DMA((5, KV_HEADS)),
            DMA((5, KV_HEADS)),
        ],
        compiler_params=pltpu.CompilerParams(
            collective_id=number, has_side_effects=True, vmem_limit_bytes=BIG_VMEM
        ),
        name="front",
    )(x, cosine, sine, feat, qfeat, attend_own, rest_own)


def back_kernel(
    parts_ref,
    win_ref,
    feat_ref,
    qt_ref,
    qfeat_ref,
    gradt_ref,
    mixed_ref,
    lse_ref,
    dq_ref,
    pairs_ref,
    sum_ref,
    kvf,
    kt,
    qa,
    da,
    acc,
    rhs,
    grads,
    ra,
    rb,
    r2,
    r1,
    t2,
    t1,
    collect_send,
    collect_recv,
    *reduce_scratch,
):
    at = Place()
    kv_heads = win_ref.shape[1]
    greet(at, True)
    total = Reduce(at, parts_ref, sum_ref, *reduce_scratch)
    collect = Collect(
        at, grads, pairs_ref, ra, rb, r2, r1, t2, t1, collect_send, collect_recv
    )
    for k in range(4):
        total.start(k)
    attend_backward_setup(feat_ref, kvf, qa, da, rhs)
    total.zero(0)
    events = [
        (0, lambda: total.zero(1)),
        (1, lambda: total.zero(2)),
        (2, lambda: total.zero(3)),
        (4, lambda: total.one(0)),
        (6, lambda: total.one(1)),
        (7, lambda: total.two(0)),
        (8, lambda: total.one(2)),
        (9, lambda: total.two(1)),
        (11, lambda: total.one(3)),
        (12, lambda: total.two(2)),
        (14, lambda: total.two(3)),
    ]

    def key_head(j, _):
        attend_backward_keys(j, win_ref, kvf, kt, acc)

        def head(g, _):
            h = j * GROUP + g
            attend_backward_head(
                h,
                qt_ref,
                qfeat_ref,
                gradt_ref,
                mixed_ref,
                lse_ref,
                dq_ref,
                kvf,
                kt,
                qa,
                da,
                acc,
                rhs,
            )
            at_steps(h, events)
            return 0

        lax.fori_loop(0, GROUP, head, 0)
        attend_backward_done(j, acc, grads)
        collect.start(j)
        pl.when(j > 0)(lambda: collect.one(j - 1))
        pl.when(j > 1)(lambda: collect.two(j - 2))
        pl.when(j > 2)(lambda: collect.three(j - 3))
        return 0

    lax.fori_loop(0, kv_heads, key_head, 0)
    collect.one(kv_heads - 1)
    collect.two(kv_heads - 2)
    total.three()
    collect.two(kv_heads - 1)
    for j in range(kv_heads - 3, kv_heads):
        collect.three(j)
    total.four()
    for j in range(kv_heads):
        collect.sent(j)
    total.five()


def back(parts, window, feat, qt, qfeat, gradt, mixed, lse, number):
    blocks, kv_heads, tokens, lanes = window.shape
    _, rows, columns = parts.shape
    pairs = (kv_heads, tokens, lanes)
    return pl.pallas_call(
        back_kernel,
        out_shape=(
            jax.ShapeDtypeStruct(qt.shape, F32),
            jax.ShapeDtypeStruct(pairs, F32),
            jax.ShapeDtypeStruct((rows, columns), BF),
        ),
        in_specs=[pl.BlockSpec(memory_space=ANY)] + [pl.BlockSpec(memory_space=VMEM)] * 7,
        out_specs=(pl.BlockSpec(memory_space=VMEM),) * 3,
        scratch_shapes=attend_backward_scratch(blocks * tokens, lanes, tokens)
        + [VMEM(window.shape, BF)]
        + [VMEM(pairs, BF)] * 6
        + [DMA((4, kv_heads)), DMA((4, kv_heads))]
        + Reduce.scratch(rows, columns),
        compiler_params=pltpu.CompilerParams(
            collective_id=number, has_side_effects=True, vmem_limit_bytes=BIG_VMEM
        ),
        name="back",
    )(parts, window, feat, qt, qfeat, gradt, mixed, lse)


def reduce_kernel(parts_ref, out_ref, *scratch):
    at = Place()
    greet(at, True)
    total = Reduce(at, parts_ref, out_ref, *scratch)
    for k in range(4):
        total.start(k)
    for k in range(4):
        total.zero(k)
    for k in range(4):
        total.one(k)
    for k in range(4):
        total.two(k)
    total.three()
    total.four()
    total.five()


def reduce_rows(parts, direct, number):
    _, rows, columns = parts.shape
    if not direct:
        own = lax.psum_scatter(parts, "shard", scatter_dimension=0)
        return lax.psum(own, "rep")
    return pl.pallas_call(
        reduce_kernel,
        out_shape=jax.ShapeDtypeStruct((rows, columns), BF),
        in_specs=[pl.BlockSpec(memory_space=ANY)],
        out_specs=pl.BlockSpec(memory_space=VMEM),
        scratch_shapes=Reduce.scratch(rows, columns),
        compiler_params=pltpu.CompilerParams(
            collective_id=number, has_side_effects=True, vmem_limit_bytes=BIG_VMEM
        ),
        name="reduce",
    )(parts)


def spread_pairs(pairs, reach):
    devices = range(lax.axis_size("shard"))
    blocks = []
    for distance in range(reach, 0, -1):
        route = [(i - distance, i) for i in devices if i - distance in devices]
        blocks.append(lax.ppermute(pairs, "shard", route))
    return jnp.stack(blocks + [pairs])


def collect_pairs(grads, reach):
    devices = range(lax.axis_size("shard"))
    own = grads[reach].astype(F32)
    for distance in range(1, reach + 1):
        route = [(i, i - distance) for i in devices if i - distance in devices]
        own = own + lax.ppermute(grads[reach - distance], "shard", route).astype(F32)
    return own


def angles(positions):
    half_dim = HEAD_DIM // 2
    inverse = rope_base ** (-(2.0 * jnp.arange(half_dim, dtype=F32) / HEAD_DIM))
    phases = positions.astype(F32)[:, None] * inverse[None, :]
    return (jnp.cos(phases)[:, None, :], jnp.sin(phases)[:, None, :])


def rotate(tensor, cosine_table, sine_table):
    half_dim = HEAD_DIM // 2
    front, back = tensor[..., :half_dim], tensor[..., half_dim:]
    return jnp.concatenate(
        [front * cosine_table - back * sine_table, back * cosine_table + front * sine_table],
        axis=-1,
    )


def norm_back(upstream, normed, scale_rows):
    mean = jnp.sum(upstream * normed, axis=-1, keepdims=True) * (1.0 / D)
    return scale_rows * (upstream - normed * mean)


def adam_step(weight_now, gradient, first, second, decay_factor):
    old_weight = weight_now.astype(F32)
    moment = beta_one * first + (1.0 - beta_one) * gradient
    square = beta_two * second + (1.0 - beta_two) * gradient * gradient
    corrected = moment / (1.0 - beta_one**STEP)
    divisor = jnp.sqrt(square / (1.0 - beta_two**STEP)) + adam_eps
    update = -learn_rate * (corrected / divisor + decay_factor * old_weight)
    return (gradient, moment, square, old_weight + update, update)


def shards(
    direct,
    block_input,
    block_cotangent,
    lengths,
    attend_gain,
    attend_weight,
    output_weight,
    expand_gain,
    expand_weight,
    shrink_weight,
    attend_gain_first,
    attend_weight_first,
    output_weight_first,
    expand_gain_first,
    expand_weight_first,
    shrink_weight_first,
    attend_gain_second,
    attend_weight_second,
    output_weight_second,
    expand_gain_second,
    expand_weight_second,
    shrink_weight_second,
):
    tokens = block_input.shape[0]
    shard_count = lax.axis_size("shard")
    token_count = tokens * shard_count * lax.axis_size("rep")
    reach = (MAXLEN - 2) // tokens + 1
    own_rows = attend_weight.shape[0]
    rows = -(-(own_rows + 2) // 16) * 16
    width = shard_count * rows

    def padded(tensor):
        blocks = tensor.reshape(tokens, shard_count, own_rows)
        return jnp.pad(blocks, ((0, 0), (0, 0), (0, rows - own_rows))).reshape(tokens, width)

    def unpadded(tensor):
        return tensor.reshape(tokens, shard_count, rows)[:, :, :own_rows].reshape(tokens, D)

    def with_gain(weight, gain):
        tail = jnp.pad(gain[None, :], ((0, rows - own_rows - 1), (0, weight.shape[1] - own_rows)))
        return jnp.concatenate([weight, tail], axis=0)

    def gain_of(planes):
        return jnp.pad(
            planes[:, own_rows, :own_rows], ((0, 0), (0, rows - own_rows))
        ).reshape(1, width).astype(F32)

    def add_gain(planes, term):
        row = term.reshape(shard_count, 1, rows).astype(planes.dtype)
        return lax.dynamic_update_slice(planes, row, (0, own_rows, 0))

    first_row = lax.axis_index("shard") * tokens
    local_index = first_row + jnp.arange(tokens, dtype=jnp.int32)
    key_index = first_row - reach * tokens + jnp.arange((reach + 1) * tokens, dtype=jnp.int32)
    ends = jnp.cumsum(lengths[0], dtype=jnp.int32)
    starts = ends - lengths[0]
    seq_count = lengths.shape[1]
    in_key = (key_index[:, None] >= starts[None, :]) & (key_index[:, None] < ends[None, :])
    in_query = (local_index[None, :] >= starts[:, None]) & (local_index[None, :] < ends[:, None])
    lanes = 2 * HEAD_DIM
    feat = jnp.concatenate(
        [
            in_key.astype(BF),
            (key_index < 0).astype(BF)[:, None],
            jnp.zeros((key_index.shape[0], ONES - seq_count - 1), BF),
            jnp.ones((key_index.shape[0], lanes - ONES), BF),
        ],
        axis=1,
    )
    qfeat = jnp.concatenate(
        [
            jnp.where(in_query, 0.0, NEG).astype(BF),
            jnp.full((1, tokens), NEG, BF),
            jnp.zeros((lanes - seq_count - 1, tokens), BF),
        ],
        axis=0,
    )
    start_index = jnp.sum(in_query * starts[:, None], axis=0, dtype=jnp.int32)
    cosine_table, sine_table = angles(local_index - start_index)

    attend_own = with_gain(attend_weight, attend_gain)
    rest_own = with_gain(
        jnp.concatenate([expand_weight, shrink_weight.T, output_weight.T], axis=1), expand_gain
    )
    inputs = padded(block_input)
    if direct:
        attend_planes, rest_planes, window, qt, mixedt, lse = front(
            inputs,
            cosine_table[:, 0].T,
            sine_table[:, 0].T,
            feat,
            qfeat,
            attend_own,
            rest_own,
            shard_count,
            0,
        )
    else:
        attend_planes = lax.all_gather(attend_own, "shard", axis=0)
        rest_planes = lax.all_gather(rest_own, "shard", axis=0)
    gain_one, gain_two = gain_of(attend_planes), gain_of(rest_planes)
    joint_weight = attend_planes.reshape(width, JW)
    rest = rest_planes.reshape(width, rest_own.shape[1])
    expand_full, shrink_full, out_full = rest[:, : 2 * FF], rest[:, 2 * FF : 3 * FF], rest[:, 3 * FF :]
    real = (jnp.arange(width, dtype=jnp.int32) % rows < own_rows)[None, :]

    inputs = inputs.astype(F32)
    scale_one = lax.rsqrt(jnp.sum(inputs * inputs, axis=-1, keepdims=True) * (1.0 / D) + eps_norm)
    normed_one = inputs * scale_one
    hidden_one = (normed_one * gain_one).astype(BF)
    if not direct:
        joint = dot(hidden_one, joint_weight)
        queries = rotate(joint[:, :QW].reshape(tokens, HEADS, HEAD_DIM), cosine_table, sine_table)
        key_rows = rotate(
            joint[:, QW : QW + KW].reshape(tokens, KV_HEADS, HEAD_DIM), cosine_table, sine_table
        )
        values = joint[:, QW + KW :].reshape(tokens, KV_HEADS, HEAD_DIM)
        pairs = jnp.concatenate([key_rows, values], axis=-1).astype(BF).transpose(1, 0, 2)
        qt = queries.astype(BF).reshape(tokens, QW).T
        window = spread_pairs(pairs, reach)
        mixedt, lse = attend_forward(window, feat, qt, qfeat)
    middle = inputs + dot(mixedt, out_full, 0, 1)
    scale_two = lax.rsqrt(jnp.sum(middle * middle, axis=-1, keepdims=True) * (1.0 / D) + eps_norm)
    normed_two = middle * scale_two
    hidden_two = (normed_two * gain_two).astype(BF)
    gate_up = dot(hidden_two, expand_full)
    gate_value, upper_value = gate_up[:, :FF], gate_up[:, FF:]
    sigmoid_gate = jax.nn.sigmoid(gate_value)
    inner_rows = (gate_value * sigmoid_gate * upper_value).astype(BF)
    block_output = middle + dot(inner_rows, shrink_full, 1, 1)

    cotangent = padded(block_cotangent)
    shrink_term = dot(cotangent, inner_rows, 0, 0)
    inner_grad = dot(cotangent, shrink_full)
    gate_grad = (
        inner_grad * upper_value * sigmoid_gate * (1.0 + gate_value * (1.0 - sigmoid_gate))
    ).astype(BF)
    upper_grad = (inner_grad * gate_value * sigmoid_gate).astype(BF)
    gate_up_grad = jnp.concatenate([gate_grad, upper_grad], axis=1)
    expand_term = dot(hidden_two, gate_up_grad, 0, 0)
    hidden_two_grad = jnp.where(real, dot(gate_up_grad, expand_full, 1, 1), 0.0)
    gain_two_term = jnp.sum(hidden_two_grad * normed_two, axis=0)
    middle_grad = cotangent.astype(F32) + norm_back(
        hidden_two_grad * gain_two, normed_two, scale_two
    )
    branch_grad = middle_grad.astype(BF)
    output_term = dot(branch_grad, mixedt, 0, 1)
    gradt = dot(out_full, branch_grad, 0, 1).astype(BF)
    rest_term = jnp.concatenate(
        [expand_term.astype(BF), shrink_term.astype(BF), output_term.astype(BF)], axis=1
    ).reshape(shard_count, rows, rest_own.shape[1])
    rest_term = add_gain(rest_term, gain_two_term)
    if direct:
        dqt, own_pairs, rest_sum = back(
            rest_term, window, feat, qt, qfeat, gradt, mixedt, lse, 1
        )
    else:
        rest_sum = reduce_rows(rest_term, direct, 3)
        dqt, dwindow = attend_backward(window, feat, qt, qfeat, gradt, mixedt, lse)
        own_pairs = collect_pairs(dwindow, reach)
    own_pairs = own_pairs.transpose(1, 0, 2)
    dq = dqt.T.reshape(tokens, HEADS, HEAD_DIM)
    query_raw = rotate(dq, cosine_table, -sine_table).reshape(tokens, QW)
    key_raw = rotate(own_pairs[..., :HEAD_DIM], cosine_table, -sine_table).reshape(tokens, KW)
    value_raw = own_pairs[..., HEAD_DIM:].reshape(tokens, KW)
    joint_grad = jnp.concatenate([query_raw, key_raw, value_raw], axis=1).astype(BF)
    joint_term = dot(hidden_one, joint_grad, 0, 0).astype(BF)
    hidden_one_grad = jnp.where(real, dot(joint_grad, joint_weight, 1, 1), 0.0)
    gain_one_term = jnp.sum(hidden_one_grad * normed_one, axis=0)
    input_gradient = middle_grad + norm_back(hidden_one_grad * gain_one, normed_one, scale_one)
    attend_sum = reduce_rows(
        add_gain(joint_term.reshape(shard_count, rows, JW), gain_one_term), direct, 2
    )

    grad_scale = grad_factor * token_count ** (-0.5)
    rest_grad, attend_grad = (total.astype(F32) * grad_scale for total in (rest_sum, attend_sum))
    first_gain = adam_step(
        attend_gain, attend_grad[own_rows, :own_rows], attend_gain_first, attend_gain_second, 0.0
    )
    first_joint = adam_step(
        attend_weight,
        attend_grad[:own_rows],
        attend_weight_first,
        attend_weight_second,
        decay_rate,
    )
    first_output = adam_step(
        output_weight,
        rest_grad[:own_rows, 3 * FF :].T,
        output_weight_first,
        output_weight_second,
        decay_rate,
    )
    second_gain = adam_step(
        expand_gain, rest_grad[own_rows, :own_rows], expand_gain_first, expand_gain_second, 0.0
    )
    second_expand = adam_step(
        expand_weight,
        rest_grad[:own_rows, : 2 * FF],
        expand_weight_first,
        expand_weight_second,
        decay_rate,
    )
    second_shrink = adam_step(
        shrink_weight,
        rest_grad[:own_rows, 2 * FF : 3 * FF].T,
        shrink_weight_first,
        shrink_weight_second,
        decay_rate,
    )
    steps = (first_gain, first_joint, first_output, second_gain, second_expand, second_shrink)
    changed = [step[4] if step[0].ndim == 1 else step[3] for step in steps]
    return (
        unpadded(block_output),
        unpadded(input_gradient),
        *[step[0] for step in steps],
        *[step[1] for step in steps],
        *[step[2] for step in steps],
        *changed,
    )


def solution(mesh):
    whole_rows = P(("rep", "shard"), None)
    state = (P("shard"), P("shard", None), P(None, "shard")) * 2
    state = (state[0], state[1], state[2], state[3], state[4], state[5])
    direct = mesh.shape["rep"] == 4 and mesh.shape["shard"] == 8
    return jax.shard_map(
        functools.partial(shards, direct),
        mesh=mesh,
        in_specs=(whole_rows, whole_rows, P("rep", None), *state, *state, *state),
        out_specs=(whole_rows, whole_rows, *state, *state, *state, *state),
        check_vma=False,
    )
```

```python
import functools
import math

import jax
import jax.numpy as jnp
from jax import lax
from jax.experimental import pallas as pl
from jax.experimental.pallas import tpu as pltpu
from jax.sharding import PartitionSpec as P

HEADS = 15
KV_HEADS = 5
HEAD_DIM = 64
GROUP = HEADS // KV_HEADS
FF = 2560
MAXLEN = 2048
STEP = 10
QW = 960
KW = 320
JW = QW + 2 * KW
D = 960

eps_norm = 1e-05
rope_base = 100000.0
beta_one = 0.9
beta_two = 0.95
adam_eps = 1e-08
learn_rate = 0.05
decay_rate = 0.1
grad_factor = 4.0

F32 = jnp.float32
BF = jnp.bfloat16
MESH = pl.DeviceIdType.MESH
ANY = pl.ANY
VMEM = pltpu.VMEM
DMA = pltpu.SemaphoreType.DMA

QC = 256
KB = 768
HALF = 64
ONES = 112
NEG = -1e30
EXP_SCALE = HEAD_DIM**-0.5 * math.log2(math.e)
BIG_VMEM = 60 * 2**20


def dot(a, b, ca=1, cb=0):
    return lax.dot_general(a, b, (((ca,), (cb,)), ((), ())), preferred_element_type=F32)


def causal_tile():
    key = lax.broadcasted_iota(jnp.int32, (QC, QC), 0)
    query = lax.broadcasted_iota(jnp.int32, (QC, QC), 1)
    return key <= query


def mask_last(scores, causal):
    last = jnp.where(causal, scores[KB - QC :], NEG)
    return jnp.concatenate([scores[: KB - QC], last], axis=0)


def attend_forward_setup(feat_ref, qfeat_ref, kvf, vt, qa):
    lanes = feat_ref.shape[1]
    kvf[:, lanes:] = feat_ref[...]
    qa[HALF:lanes, :] = jnp.zeros((lanes - HALF, qa.shape[1]), BF)
    qa[lanes:, :] = qfeat_ref[...]
    vt[HALF:, :] = jnp.ones((vt.shape[0] - HALF, vt.shape[1]), BF)


def attend_forward_keys(j, kv_ref, kvf, vt):
    blocks, _, rows, lanes = kv_ref.shape
    for block in range(blocks):
        part = kv_ref[block, j]
        kvf[block * rows : (block + 1) * rows, :lanes] = part
        vt[:HALF, block * rows : (block + 1) * rows] = part.T[HALF:, :]


def attend_forward_head(h, qt_ref, mixed_ref, lse_ref, kvf, vt, qa, sb):
    tokens = qt_ref.shape[1]
    steps = (kvf.shape[0] - (tokens - QC)) // KB
    causal = causal_tile()
    row = pl.multiple_of(h * HEAD_DIM, HEAD_DIM)
    qa[:HALF, :] = qt_ref[pl.ds(row, HEAD_DIM), :]
    tops = []
    for chunk in range(tokens // QC):
        low = chunk * QC
        highest = None
        for b in range(steps):
            first = low + b * KB
            s = dot(kvf[first : first + KB, :], qa[:, low : low + QC])
            if b == steps - 1:
                s = mask_last(s, causal)
            sb[chunk, b * KB : (b + 1) * KB, :] = s
            peak = jnp.max(s.reshape(KB // 8, 8, QC), axis=0)
            highest = peak if highest is None else jnp.maximum(highest, peak)
        tops.append(jnp.max(highest, axis=0, keepdims=True))
    for chunk in range(tokens // QC):
        low = chunk * QC
        shift = tops[chunk] * EXP_SCALE
        total = None
        for b in range(steps):
            first = low + b * KB
            s = sb[chunk, b * KB : (b + 1) * KB, :]
            p = jnp.exp2(s * EXP_SCALE - shift).astype(BF)
            term = dot(vt[:, first : first + KB], p)
            total = term if total is None else total + term
        weight = total[HALF : HALF + 1, :]
        mixed_ref[pl.ds(row, HEAD_DIM), low : low + QC] = (
            total[:HALF, :] * (1.0 / weight)
        ).astype(BF)
        lse_ref[pl.ds(h, 1), :, low : low + QC] = (
            tops[chunk] * HEAD_DIM**-0.5 + jnp.log(weight)
        )[None]


def attend_forward_scratch(keys, lanes, tokens):
    return [
        VMEM((keys, 2 * lanes), BF),
        VMEM((HALF + 16, keys), BF),
        VMEM((2 * lanes, tokens), BF),
        VMEM((tokens // QC, keys - (tokens - QC), QC), F32),
    ]


def attend_forward_kernel(
    kv_ref, feat_ref, qt_ref, qfeat_ref, mixed_ref, lse_ref, kvf, vt, qa, sb
):
    attend_forward_setup(feat_ref, qfeat_ref, kvf, vt, qa)

    def key_head(j, _):
        attend_forward_keys(j, kv_ref, kvf, vt)

        def head(g, _):
            attend_forward_head(j * GROUP + g, qt_ref, mixed_ref, lse_ref, kvf, vt, qa, sb)
            return 0

        lax.fori_loop(0, GROUP, head, 0)
        return 0

    lax.fori_loop(0, kv_ref.shape[1], key_head, 0)


def attend_forward(window, feat, qt, qfeat):
    blocks, kv_heads, rows, lanes = window.shape
    tokens = qt.shape[1]
    return pl.pallas_call(
        attend_forward_kernel,
        out_shape=(
            jax.ShapeDtypeStruct(qt.shape, BF),
            jax.ShapeDtypeStruct((HEADS, 1, tokens), F32),
        ),
        scratch_shapes=attend_forward_scratch(blocks * rows, lanes, tokens),
        compiler_params=pltpu.CompilerParams(vmem_limit_bytes=BIG_VMEM),
        name="attend_forward",
    )(window, feat, qt, qfeat)


def three_parts(value, rows):
    one = value.astype(BF).astype(F32)
    two = (value - one).astype(BF).astype(F32)
    three = value - one - two
    shape = (rows, value.shape[1])
    place = lax.broadcasted_iota(jnp.int32, shape, 0)
    parts = [jnp.broadcast_to(part, shape) for part in (one, two, three)]
    chosen = jnp.where(
        place == 0, parts[0], jnp.where(place == 1, parts[1], jnp.where(place == 2, parts[2], 0.0))
    )
    return chosen.astype(BF)


def attend_backward_setup(feat_ref, kvf, qa, da, rhs):
    lanes = feat_ref.shape[1]
    kvf[:, lanes:] = feat_ref[...]
    qa[HALF:lanes, :] = jnp.zeros((lanes - HALF, qa.shape[1]), BF)
    da[...] = jnp.zeros_like(da)
    rhs[...] = jnp.zeros_like(rhs)


def attend_backward_keys(j, kv_ref, kvf, kt, acc):
    blocks, _, rows, lanes = kv_ref.shape
    for block in range(blocks):
        part = kv_ref[block, j]
        kvf[block * rows : (block + 1) * rows, :lanes] = part
        kt[:, block * rows : (block + 1) * rows] = part.T[:HALF, :]
    acc[...] = jnp.zeros_like(acc)


def attend_backward_head(
    h, qt_ref, qfeat_ref, gradt_ref, mixed_ref, lse_ref, dq_ref, kvf, kt, qa, da, acc, rhs
):
    tokens = qt_ref.shape[1]
    lanes = qfeat_ref.shape[0]
    steps = (kvf.shape[0] - (tokens - QC)) // KB
    causal = causal_tile()
    extra = lanes - ONES
    row = pl.multiple_of(h * HEAD_DIM, HEAD_DIM)
    q = qt_ref[pl.ds(row, HEAD_DIM), :]
    grad = gradt_ref[pl.ds(row, HEAD_DIM), :]
    qa[:HALF, :] = q
    da[HALF:lanes, :] = grad
    mixed = mixed_ref[pl.ds(row, HEAD_DIM), :].astype(F32)
    row_total = jnp.sum(grad.astype(F32) * mixed, axis=0, keepdims=True)
    lse = lse_ref[pl.ds(h, 1), :, :][0]
    qa[lanes : lanes + ONES, :] = qfeat_ref[:ONES, :]
    qa[lanes + ONES :, :] = three_parts(-(HEAD_DIM**0.5) * lse, extra)
    da[lanes + ONES :, :] = three_parts(-row_total, extra)
    query_grads = [None] * (tokens // QC)
    for chunk in range(tokens // QC):
        low = chunk * QC
        rhs[chunk, :HALF, :QC] = q[:, low : low + QC]
        rhs[chunk, HALF:, QC:] = grad[:, low : low + QC]
    for b in range(steps):
        for chunk in range(tokens // QC):
            low = chunk * QC
            first = low + b * KB
            keys = kvf[first : first + KB, :]
            s = dot(keys, qa[:, low : low + QC])
            if b == steps - 1:
                s = mask_last(s, causal)
            p = jnp.exp2(s * EXP_SCALE)
            dp = dot(keys, da[:, low : low + QC])
            ds = (p * dp).astype(BF)
            both = jnp.concatenate([ds, p.astype(BF)], axis=1)
            acc[first : first + KB, :] += dot(both, rhs[chunk], 1, 1)
            term = dot(kt[:, first : first + KB], ds)
            old = query_grads[chunk]
            query_grads[chunk] = term if old is None else old + term
    for chunk in range(tokens // QC):
        low = chunk * QC
        dq_ref[pl.ds(row, HEAD_DIM), low : low + QC] = query_grads[chunk] * HEAD_DIM**-0.5


def attend_backward_done(j, acc, dkv_ref):
    blocks, _, rows, lanes = dkv_ref.shape
    lane = lax.broadcasted_iota(jnp.int32, (1, lanes), 1)
    factor = jnp.where(lane < HALF, HEAD_DIM**-0.5, 1.0)
    for block in range(blocks):
        part = acc[block * rows : (block + 1) * rows, :]
        dkv_ref[block, j] = (part * factor).astype(dkv_ref.dtype)


def attend_backward_scratch(keys, lanes, tokens):
    return [
        VMEM((keys, 2 * lanes), BF),
        VMEM((HALF, keys), BF),
        VMEM((2 * lanes, tokens), BF),
        VMEM((2 * lanes, tokens), BF),
        VMEM((keys, lanes), F32),
        VMEM((tokens // QC, lanes, 2 * QC), BF),
    ]


def attend_backward_kernel(
    kv_ref, feat_ref, qt_ref, qfeat_ref, gradt_ref, mixed_ref, lse_ref, dq_ref, dkv_ref, *scratch
):
    kvf, kt, qa, da, acc, rhs = scratch
    attend_backward_setup(feat_ref, kvf, qa, da, rhs)

    def key_head(j, _):
        attend_backward_keys(j, kv_ref, kvf, kt, acc)

        def head(g, _):
            attend_backward_head(
                j * GROUP + g, qt_ref, qfeat_ref, gradt_ref, mixed_ref, lse_ref, dq_ref, *scratch
            )
            return 0

        lax.fori_loop(0, GROUP, head, 0)
        attend_backward_done(j, acc, dkv_ref)
        return 0

    lax.fori_loop(0, kv_ref.shape[1], key_head, 0)


def attend_backward(window, feat, qt, qfeat, gradt, mixed, lse):
    blocks, kv_heads, rows, lanes = window.shape
    tokens = qt.shape[1]
    return pl.pallas_call(
        attend_backward_kernel,
        out_shape=(
            jax.ShapeDtypeStruct(qt.shape, F32),
            jax.ShapeDtypeStruct(window.shape, BF),
        ),
        scratch_shapes=attend_backward_scratch(blocks * rows, lanes, tokens),
        compiler_params=pltpu.CompilerParams(vmem_limit_bytes=BIG_VMEM),
        name="attend_backward",
    )(window, feat, qt, qfeat, gradt, mixed, lse)


class Place:
    def __init__(self):
        self.r = lax.axis_index("rep")
        self.s = lax.axis_index("shard")
        self.x, self.y = lax.rem(self.r, 2), self.r // 2
        self.z, self.c = self.s // 2, lax.rem(self.s, 2)
        self.rx = self.y * 2 + (1 - self.x)
        self.ry = (1 - self.y) * 2 + self.x
        self.rd = 3 - self.r
        self.x_side = (self.rx, self.s)
        self.y_side = (self.ry, self.s)
        self.core_side = (self.r, self.z * 2 + (1 - self.c))
        self.has_later, self.has_earlier = self.z < 3, self.z > 0
        self.later = (self.r, lax.min(self.s + 2, 7))
        self.earlier = (self.r, lax.max(self.s - 2, 0))

    def z_to(self, k):
        return lax.rem(self.z + k, 4)

    def z_side(self, k):
        return (self.r, self.z_to(k) * 2 + self.c)

    def arrival(self, i):
        low = self.z < 2
        first = jnp.where(self.z == 0, 1, jnp.where(self.z == 1, 0, jnp.where(self.z == 2, 3, 2)))
        if i == 0:
            return first
        if i == 1:
            return jnp.where(low, 2, 1)
        return jnp.where(low, 3, 0)


def greet(at, whole_line):
    barrier = pltpu.get_barrier_semaphore()

    def signal(device):
        pl.semaphore_signal(barrier, inc=1, device_id=device, device_id_type=MESH)

    for device in (at.x_side, at.y_side, at.core_side):
        signal(device)
    if whole_line:
        for k in (1, 2, 3):
            signal(at.z_side(k))
        pl.semaphore_wait(barrier, 6)
        return

    @pl.when(at.has_later)
    def _():
        signal(at.later)

    @pl.when(at.has_earlier)
    def _():
        signal(at.earlier)

    count = 3 + jnp.where(at.has_later, 1, 0) + jnp.where(at.has_earlier, 1, 0)
    pl.semaphore_wait(barrier, count)


def remote(src, dst, send, recv, device):
    return pltpu.make_async_remote_copy(
        src_ref=src, dst_ref=dst, send_sem=send, recv_sem=recv, device_id=device, device_id_type=MESH
    )


class Gather:
    COUNT = 31

    def __init__(self, at, own, full, columns, local_sem, send, recv):
        self.at, self.own, self.full, self.columns = at, own, full, columns
        self.local_sem, self.send, self.recv = local_sem, send, recv
        self.rows = own.shape[0]
        self.quarter, self.half = self.rows // 4, self.rows // 8

    def piece(self, plane, owner, part=None):
        start = owner * self.quarter + (0 if part is None else part * self.half)
        size = self.quarter if part is None else self.half
        return self.full.at[
            plane, pl.ds(pl.multiple_of(start, self.half), size), pl.ds(*self.columns)
        ]

    def copy(self, index, src, dst, device, landed=None):
        return remote(
            src, dst, self.send.at[index], self.recv.at[index if landed is None else landed], device
        )

    def core_copy(self):
        src = self.own.at[:, pl.ds(*self.columns)]
        return self.copy(
            28, src, self.full.at[self.at.s, :, pl.ds(*self.columns)], self.at.core_side
        )

    def local_copy(self):
        return pltpu.make_async_copy(
            self.own.at[:, pl.ds(*self.columns)],
            self.full.at[self.at.s, :, pl.ds(*self.columns)],
            self.local_sem,
        )

    def z_copy(self, up):
        at = self.at
        src = self.own.at[
            pl.ds(pl.multiple_of(at.r * self.quarter, self.quarter), self.quarter),
            pl.ds(*self.columns),
        ]
        device = at.later if up else at.earlier
        return self.copy(29 if up else 30, src, self.piece(at.s, at.r), device, at.z)

    def start_core(self):
        self.local_copy().start()
        self.core_copy().start()

    def start_z(self):
        @pl.when(self.at.has_later)
        def _():
            self.z_copy(True).start()

        @pl.when(self.at.has_earlier)
        def _():
            self.z_copy(False).start()

    def plane(self, i, other=False):
        c = 1 - self.at.c if other else self.at.c
        return self.at.arrival(i) * 2 + c

    def forwards(self, i):
        at = self.at
        chip = at.arrival(i)
        got = self.piece(self.plane(i), at.r)
        return [
            ((chip < at.z) & at.has_later, self.copy(i, got, got, at.later, chip)),
            ((chip > at.z) & at.has_earlier, self.copy(i, got, got, at.earlier, chip)),
        ]

    def out_copies(self, i):
        at, plane = self.at, self.plane(i)
        got = self.piece(plane, at.r)
        return [
            self.copy(4 + i, got, got, at.x_side),
            self.copy(7 + i, got, got, at.y_side),
            self.copy(10 + i, got, got, at.core_side),
        ]

    def cross_copies(self, i):
        at, plane = self.at, self.plane(i)
        one, two = self.piece(plane, at.rx, 0), self.piece(plane, at.ry, 1)
        from_x, from_y = self.piece(plane, at.rx), self.piece(plane, at.ry)
        return [
            self.copy(13 + i, one, one, at.y_side),
            self.copy(16 + i, from_x, from_x, at.core_side),
            self.copy(19 + i, two, two, at.x_side),
            self.copy(22 + i, from_y, from_y, at.core_side),
        ]

    def last_copy(self, i):
        got = self.piece(self.plane(i), self.at.rd)
        return self.copy(25 + i, got, got, self.at.core_side)

    def arrive(self, landed, ref):
        remote(
            ref, ref, self.send.at[landed], self.recv.at[landed], self.at.core_side
        ).wait_recv()

    def z(self, i):
        at = self.at
        self.arrive(at.arrival(i), self.piece(self.plane(i), at.r))
        for condition, copy in self.forwards(i):
            pl.when(condition)(copy.start)
        for copy in self.out_copies(i):
            copy.start()

    def cross(self, i):
        at, plane = self.at, self.plane(i)
        copies = self.cross_copies(i)
        self.arrive(4 + i, self.piece(plane, at.rx))
        copies[0].start()
        copies[1].start()
        self.arrive(7 + i, self.piece(plane, at.ry))
        copies[2].start()
        copies[3].start()

    def last(self, i):
        at, plane = self.at, self.plane(i)
        self.arrive(13 + i, self.piece(plane, at.rd, 0))
        self.arrive(19 + i, self.piece(plane, at.rd, 1))
        self.last_copy(i).start()

    def landed(self):
        at = self.at
        self.arrive(28, self.full.at[at.core_side[1], :, pl.ds(*self.columns)])
        for i in range(3):
            plane = self.plane(i, True)
            self.arrive(10 + i, self.piece(plane, at.r))
            self.arrive(16 + i, self.piece(plane, at.rx))
            self.arrive(22 + i, self.piece(plane, at.ry))
            self.arrive(25 + i, self.piece(plane, at.rd))
        self.local_copy().wait()

    def sent(self):
        at = self.at
        self.core_copy().wait_send()
        pl.when(at.has_later)(self.z_copy(True).wait_send)
        pl.when(at.has_earlier)(self.z_copy(False).wait_send)
        for i in range(3):
            for condition, copy in self.forwards(i):
                pl.when(condition)(copy.wait_send)
            for copy in self.out_copies(i) + self.cross_copies(i) + [self.last_copy(i)]:
                copy.wait_send()


class Spread:
    def __init__(self, at, win, send, recv):
        self.at, self.win, self.sems = at, win, (send, recv)
        even = at.c == 0
        self.near, self.far = jnp.where(even, 1, 3), jnp.where(even, 3, 1)

    def copy(self, n, j, src, dst, device):
        send, recv = self.sems
        return remote(
            self.win.at[src, j], self.win.at[dst, j], send.at[n, j], recv.at[n, j], device
        )

    def first(self, j):
        return self.copy(0, j, 4, 2, self.at.later)

    def twin_own(self, j):
        return self.copy(1, j, 4, 3, self.at.core_side)

    def second(self, j):
        return self.copy(2, j, 2, 0, self.at.later)

    def twin_near(self, j, place):
        return self.copy(3, j, 2, place, self.at.core_side)

    def twin_far(self, j):
        return self.copy(4, j, 0, 1, self.at.core_side)

    def clear(self):
        for block in range(4):
            @pl.when(self.at.s < 4 - block)
            def _(block=block):
                self.win[block] = jnp.zeros(self.win.shape[1:], self.win.dtype)

    def start(self, j):
        pl.when(self.at.has_later)(self.first(j).start)
        pl.when(self.at.c == 0)(self.twin_own(j).start)

    def one(self, j):
        at = self.at

        @pl.when(at.has_earlier)
        def _():
            self.first(j).wait_recv()
            self.twin_near(j, self.near).start()
            pl.when(at.has_later)(self.second(j).start)

    def two(self, j):
        at = self.at

        @pl.when(at.z > 1)
        def _():
            self.second(j).wait_recv()
            pl.when(at.c == 1)(self.twin_far(j).start)

    def landed(self, j):
        at = self.at
        pl.when(at.c == 1)(self.twin_own(j).wait_recv)
        pl.when(at.has_earlier)(self.twin_near(j, self.far).wait_recv)
        pl.when((at.c == 0) & (at.z > 1))(self.twin_far(j).wait_recv)

    def sent(self, j):
        at = self.at
        pl.when(at.has_later)(self.first(j).wait_send)
        pl.when(at.c == 0)(self.twin_own(j).wait_send)
        pl.when(at.has_earlier)(self.twin_near(j, self.near).wait_send)
        pl.when(at.has_earlier & at.has_later)(self.second(j).wait_send)
        pl.when((at.c == 1) & (at.z > 1))(self.twin_far(j).wait_send)


class Collect:
    def __init__(self, at, grads, out, ra, rb, r2, r1, t2, t1, send, recv):
        self.at, self.grads, self.out = at, grads, out
        self.ra, self.rb, self.r2, self.r1, self.t2, self.t1 = ra, rb, r2, r1, t2, t1
        self.sems = (send, recv)

    def copy(self, n, j, src, dst, device):
        send, recv = self.sems
        return remote(src, dst, send.at[n, j], recv.at[n, j], device)

    def twin_a(self, j):
        return self.copy(0, j, self.grads.at[3, j], self.ra.at[j], self.at.core_side)

    def twin_b(self, j):
        return self.copy(1, j, self.grads.at[1, j], self.rb.at[j], self.at.core_side)

    def far(self, j):
        return self.copy(2, j, self.t2.at[j], self.r2.at[j], self.at.earlier)

    def near(self, j):
        return self.copy(3, j, self.t1.at[j], self.r1.at[j], self.at.earlier)

    def start(self, j):
        self.twin_b(j).start()
        self.twin_a(j).start()

    def one(self, j):
        self.twin_b(j).wait_recv()
        self.twin_a(j).wait_recv()
        even = self.at.c == 0
        from_a, from_b = self.ra[j].astype(F32), self.rb[j].astype(F32)
        none = jnp.zeros_like(from_a)
        self.t2[j] = (self.grads[0, j].astype(F32) + jnp.where(even, none, from_b)).astype(BF)
        pl.when(self.at.z > 1)(self.far(j).start)
        self.t1[j] = (self.grads[2, j].astype(F32) + jnp.where(even, from_b, from_a)).astype(BF)
        self.out[j] = self.grads[4, j].astype(F32) + jnp.where(even, from_a, none)

    def two(self, j):
        at = self.at

        @pl.when(at.has_earlier & at.has_later)
        def _():
            self.far(j).wait_recv()
            self.t1[j] = (self.t1[j].astype(F32) + self.r2[j].astype(F32)).astype(BF)

        pl.when(at.has_earlier)(self.near(j).start)

    def three(self, j):
        at = self.at

        @pl.when(at.has_later)
        def _():
            self.near(j).wait_recv()
            self.out[j] = self.out[j] + self.r1[j].astype(F32)

    def sent(self, j):
        at = self.at
        self.twin_a(j).wait_send()
        self.twin_b(j).wait_send()
        pl.when(at.z > 1)(self.far(j).wait_send)
        pl.when(at.has_earlier)(self.near(j).wait_send)


class Reduce:
    COUNT = 14

    def __init__(self, at, chunks, out, own, give, r0, r1a, r1b, r2a, r2b, r3, send, recv, free):
        self.at, self.chunks, self.out, self.own, self.give = at, chunks, out, own, give
        self.r0, self.r1a, self.r1b, self.r2a, self.r2b, self.r3 = r0, r1a, r1b, r2a, r2b, r3
        self.send, self.recv, self.free = send, recv, free
        self.rows = out.shape[0]
        self.quarter, self.half = self.rows // 4, self.rows // 8
        self.slots = give.shape[0]

    @staticmethod
    def scratch(rows, chunks, slots):
        half = rows // 8
        columns = sum(width for _, width in chunks)
        widest = max(width for _, width in chunks)
        return [
            VMEM((4, rows, columns), BF),
            VMEM((slots, 4, rows, widest), BF),
            VMEM((slots, 4, rows, widest), BF),
            VMEM((2, 4, half, columns), BF),
            VMEM((2, 4, half, columns), BF),
            VMEM((4, half, columns), BF),
            VMEM((4, half, columns), BF),
            VMEM((3, 2 * half, columns), BF),
            DMA((len(chunks), Reduce.COUNT)),
            DMA((len(chunks), Reduce.COUNT)),
            pltpu.SemaphoreType.REGULAR,
        ]

    def columns(self, n):
        return pl.ds(*self.chunks[n])

    def copy(self, n, index, src, dst, device):
        return remote(src, dst, self.send.at[n, index], self.recv.at[n, index], device)

    def arrive(self, n, index, ref):
        self.copy(n, index, ref, ref, self.at.core_side).wait_recv()

    def spot(self, owner, part):
        start = owner * self.quarter + part * self.half
        return pl.ds(pl.multiple_of(start, self.half), self.half)

    def piece(self, n, owner):
        start = pl.multiple_of(owner * self.quarter, self.quarter)
        return self.out.at[pl.ds(start, self.quarter), self.columns(n)]

    def core_copy(self, n):
        slot, width = n % self.slots, self.chunks[n][1]
        return self.copy(
            n,
            0,
            self.give.at[slot, :, :, pl.ds(0, width)],
            self.r0.at[slot, :, :, pl.ds(0, width)],
            self.at.core_side,
        )

    def one_copies(self, n):
        at, copies, cols = self.at, [], self.columns(n)
        for i in range(2):
            a = self.own.at[:, self.spot(i * 2 + 1 - at.x, 0), cols]
            b = self.own.at[:, self.spot((1 - at.y) * 2 + i, 1), cols]
            copies.append(self.copy(n, 1 + i, a, self.r1a.at[i, :, :, cols], at.x_side))
            copies.append(self.copy(n, 3 + i, b, self.r1b.at[i, :, :, cols], at.y_side))
        return copies

    def two_copies(self, n):
        at, cols = self.at, self.columns(n)
        a = self.own.at[:, self.spot(at.ry, 0), cols]
        b = self.own.at[:, self.spot(at.rx, 1), cols]
        return [
            self.copy(n, 5, a, self.r2a.at[:, :, cols], at.y_side),
            self.copy(n, 6, b, self.r2b.at[:, :, cols], at.x_side),
        ]

    def z_copy(self, n, k):
        at, cols = self.at, self.columns(n)
        mine = pl.ds(pl.multiple_of(at.r * self.quarter, self.quarter), self.quarter)
        src = self.own.at[at.z_to(k), mine, cols]
        return self.copy(n, 6 + k, src, self.r3.at[k - 1, :, cols], at.z_side(k))

    def back_copy(self, n, i):
        at, cols = self.at, self.columns(n)
        if i < 2:
            ref = self.piece(n, at.r)
            return self.copy(n, 10 + i, ref, ref, at.x_side if i == 0 else at.y_side)
        owner, device = (at.rx, at.y_side) if i == 2 else (at.ry, at.x_side)
        ref = self.out.at[self.spot(owner, i - 2), cols]
        return self.copy(n, 10 + i, ref, ref, device)

    def claim(self, n):
        if n >= self.slots:
            self.core_copy(n - self.slots).wait_send()

    def start(self, n):
        if n >= self.slots:
            pl.semaphore_wait(self.free, 1)
        self.core_copy(n).start()

    def zero(self, n):
        slot, (first, width) = n % self.slots, self.chunks[n]
        self.arrive(n, 0, self.r0.at[slot, :, :, pl.ds(0, width)])
        per_plane = self.rows // (2 * self.half)

        def add_rows(i, _):
            z, where = i // per_plane, pl.ds(
                pl.multiple_of(lax.rem(i, per_plane) * 2 * self.half, 2 * self.half), 2 * self.half
            )
            old = self.own[z, where, first : first + width].astype(F32)
            new = self.r0[slot, z, where, :width].astype(F32)
            self.own[z, where, first : first + width] = (old + new).astype(BF)
            return 0

        lax.fori_loop(0, 4 * per_plane, add_rows, 0)
        if n + self.slots < len(self.chunks):
            pl.semaphore_signal(
                self.free, inc=1, device_id=self.at.core_side, device_id_type=MESH
            )

    def push(self, n):
        for copy in self.one_copies(n):
            copy.start()

    def add(self, n, where, ref):
        cols = self.columns(n)
        for z in range(4):
            old = self.own[z, where, cols].astype(F32)
            self.own[z, where, cols] = (old + ref[z, :, cols].astype(F32)).astype(BF)

    def one(self, n):
        at, cols = self.at, self.columns(n)
        for i in range(2):
            self.arrive(n, 1 + i, self.r1a.at[i, :, :, cols])
            self.arrive(n, 3 + i, self.r1b.at[i, :, :, cols])
            self.add(n, self.spot(i * 2 + at.x, 0), self.r1a.at[i])
            self.add(n, self.spot(at.y * 2 + i, 1), self.r1b.at[i])
        for copy in self.two_copies(n):
            copy.start()

    def two(self, n):
        at, cols = self.at, self.columns(n)
        self.arrive(n, 5, self.r2a.at[:, :, cols])
        self.arrive(n, 6, self.r2b.at[:, :, cols])
        self.add(n, self.spot(at.r, 0), self.r2a)
        self.add(n, self.spot(at.r, 1), self.r2b)
        for k in (1, 2, 3):
            self.z_copy(n, k).start()

    def three(self, n):
        at, cols = self.at, self.columns(n)
        for k in (1, 2, 3):
            self.arrive(n, 6 + k, self.r3.at[k - 1, :, cols])
        for i in range(2):
            where = pl.ds(i * self.half, self.half)
            total = self.own[at.z, self.spot(at.r, i), cols].astype(F32)
            for k in range(3):
                total += self.r3[k, where, cols].astype(F32)
            self.out[self.spot(at.r, i), cols] = total.astype(BF)
        self.back_copy(n, 0).start()
        self.back_copy(n, 1).start()

    def four(self, n):
        at = self.at
        self.arrive(n, 10, self.piece(n, at.rx))
        self.back_copy(n, 2).start()
        self.arrive(n, 11, self.piece(n, at.ry))
        self.back_copy(n, 3).start()

    def five(self, n):
        at, cols = self.at, self.columns(n)
        self.arrive(n, 12, self.out.at[self.spot(at.rd, 0), cols])
        self.arrive(n, 13, self.out.at[self.spot(at.rd, 1), cols])

    def sent(self):
        for n in range(len(self.chunks)):
            if n + self.slots >= len(self.chunks):
                self.core_copy(n).wait_send()
            copies = self.one_copies(n) + self.two_copies(n)
            copies += [self.z_copy(n, k) for k in (1, 2, 3)]
            for copy in copies + [self.back_copy(n, i) for i in range(4)]:
                copy.wait_send()


def at_steps(i, events):
    for n, event in events:
        pl.when(i == n)(event)


def front_kernel(
    x_ref,
    cos_ref,
    sin_ref,
    feat_ref,
    qfeat_ref,
    attend_own,
    rest_own,
    attend_ref,
    rest_ref,
    win_ref,
    qt_ref,
    mixed_ref,
    lse_ref,
    kvf,
    vt,
    qa,
    sb,
    hidden,
    kvt,
    local_sems,
    gather_send,
    gather_recv,
    spread_send,
    spread_recv,
):
    at = Place()
    shard_count, rows, columns = attend_ref.shape
    width = shard_count * rows
    tokens = x_ref.shape[0]
    kv_heads = win_ref.shape[1]
    own_rows = D // shard_count
    cut = 2 * FF
    greet(at, False)

    def gather(n, own, full, cols):
        return Gather(
            at, own, full, cols, local_sems.at[n], gather_send.at[n], gather_recv.at[n]
        )

    first = gather(0, attend_own, attend_ref, (0, columns))
    second = gather(1, rest_own, rest_ref, (0, cut))
    third = gather(2, rest_own, rest_ref, (cut, rest_own.shape[1] - cut))
    spread = Spread(at, win_ref, spread_send, spread_recv)

    first.start_z()
    first.start_core()
    second.start_core()
    third.start_core()
    spread.clear()
    attend_forward_setup(feat_ref, qfeat_ref, kvf, vt, qa)
    for i in range(3):
        first.z(i)
    second.start_z()
    for i in range(3):
        first.cross(i)
    second.z(0)
    for i in range(3):
        first.last(i)
    first.landed()

    inputs = x_ref[...].astype(F32)
    scale = lax.rsqrt(jnp.sum(inputs * inputs, axis=-1, keepdims=True) * (1.0 / D) + eps_norm)
    for s in range(shard_count):
        lane = slice(s * rows, (s + 1) * rows)
        gain = attend_ref[s, own_rows : own_rows + 1, :rows].astype(F32)
        hidden[:, lane] = (x_ref[:, lane].astype(F32) * scale * gain).astype(BF)

    def project(start):
        stop = min(start + 256, columns)
        weight = attend_ref[:, :, start:stop].reshape(width, stop - start)
        flipped = dot(hidden[...], weight).T
        for low in range(0, stop - start, HEAD_DIM):
            column = start + low
            head = flipped[low : low + HEAD_DIM, :]
            if column < QW + KW:
                half = HEAD_DIM // 2
                front, back = head[:half], head[half:]
                head = jnp.concatenate(
                    [
                        front * cos_ref[...] - back * sin_ref[...],
                        back * cos_ref[...] + front * sin_ref[...],
                    ],
                    axis=0,
                )
            if column < QW:
                qt_ref[column : column + HEAD_DIM, :] = head.astype(BF)
            elif column < QW + KW:
                kvt[(column - QW) // HEAD_DIM, :HALF, :] = head.astype(BF)
            else:
                kvt[(column - QW - KW) // HEAD_DIM, HALF:, :] = head.astype(BF)

    split = QW // 128 * 128
    for start in range(split, columns, 256):
        project(start)
    for j in range(kv_heads):
        win_ref[4, j] = kvt[j].T
        spread.start(j)
    second.z(1)
    third.start_z()
    for start in range(0, split, 256):
        project(start)
    spread.one(0)
    second.z(2)
    spread.one(1)
    spread.two(0)
    events = [
        (0, lambda: third.z(0)),
        (1, lambda: second.cross(0)),
        (2, lambda: third.z(1)),
        (3, lambda: second.cross(1)),
        (4, lambda: third.z(2)),
        (5, lambda: second.cross(2)),
        (6, lambda: third.cross(0)),
        (7, lambda: second.last(0)),
        (8, lambda: third.cross(1)),
        (9, lambda: second.last(1)),
        (10, lambda: third.cross(2)),
        (11, lambda: second.last(2)),
        (12, lambda: third.last(0)),
        (13, lambda: third.last(1)),
        (14, lambda: third.last(2)),
    ]

    def key_head(j, _):
        pl.when(j + 2 < kv_heads)(lambda: spread.one(j + 2))
        pl.when(j + 1 < kv_heads)(lambda: spread.two(j + 1))
        spread.landed(j)
        attend_forward_keys(j, win_ref, kvf, vt)

        def head(g, _):
            h = j * GROUP + g
            attend_forward_head(h, qt_ref, mixed_ref, lse_ref, kvf, vt, qa, sb)
            at_steps(h, events)
            return 0

        lax.fori_loop(0, GROUP, head, 0)
        spread.sent(j)
        return 0

    lax.fori_loop(0, kv_heads, key_head, 0)
    second.landed()
    third.landed()
    for part in (first, second, third):
        part.sent()


def front(x, cosine, sine, feat, qfeat, attend_own, rest_own, shard_count, number):
    tokens, width = x.shape
    keys, lanes = feat.shape
    rows = attend_own.shape[0]
    window = (keys // tokens, KV_HEADS, tokens, lanes)
    return pl.pallas_call(
        front_kernel,
        out_shape=(
            jax.ShapeDtypeStruct((shard_count,) + attend_own.shape, BF),
            jax.ShapeDtypeStruct((shard_count,) + rest_own.shape, BF),
            jax.ShapeDtypeStruct(window, BF),
            jax.ShapeDtypeStruct((QW, tokens), BF),
            jax.ShapeDtypeStruct((QW, tokens), BF),
            jax.ShapeDtypeStruct((HEADS, 1, tokens), F32),
        ),
        in_specs=[pl.BlockSpec(memory_space=VMEM)] * 6 + [pl.BlockSpec(memory_space=ANY)],
        out_specs=(
            pl.BlockSpec(memory_space=VMEM),
            pl.BlockSpec(memory_space=ANY),
        )
        + (pl.BlockSpec(memory_space=VMEM),) * 4,
        scratch_shapes=attend_forward_scratch(keys, lanes, tokens)
        + [
            VMEM((tokens, width), BF),
            VMEM((KV_HEADS, lanes, tokens), BF),
            DMA((3,)),
            DMA((3, Gather.COUNT)),
            DMA((3, Gather.COUNT)),
            DMA((5, KV_HEADS)),
            DMA((5, KV_HEADS)),
        ],
        compiler_params=pltpu.CompilerParams(
            collective_id=number, has_side_effects=True, vmem_limit_bytes=BIG_VMEM
        ),
        name="front",
    )(x, cosine, sine, feat, qfeat, attend_own, rest_own)


def pad_features(src, dst, own_rows, rows):
    for s in range(D // own_rows):
        dst[:, s * rows : s * rows + own_rows] = src[:, s * own_rows : (s + 1) * own_rows].astype(
            dst.dtype
        )
        dst[:, s * rows + own_rows : (s + 1) * rows] = jnp.zeros(
            (dst.shape[0], rows - own_rows), dst.dtype
        )


def flip_blocks(value, dst):
    blocks, rows, _ = dst.shape
    for s in range(blocks):
        dst[s] = value[:, s * rows : (s + 1) * rows].T


def split_cores(at, flipped, own, give):
    for z in range(own.shape[0]):
        own[z] = flipped[2 * z + at.c]
        give[z] = flipped[2 * z + 1 - at.c]


PART = 128
SUB = 256
CHUNK = 2 * SUB


def rear_chunks():
    chunks = [(3 * CHUNK * n, 3 * CHUNK) for n in range(FF // CHUNK)]
    return chunks + [(3 * FF, -(-QW // 128) * 128)]


def feed_forward(
    at,
    total,
    x_ref,
    cot_ref,
    mixed_ref,
    rest_ref,
    out_ref,
    middle_grad_ref,
    gradt_ref,
    events,
    cot,
    hidden,
    middle,
    acc_out,
    acc_grad,
    flipped,
    hidden_own,
    hidden_give,
    cot_own,
    cot_give,
    out_weight,
    gain_rows,
    gain_term,
    weights,
    sems,
):
    shard_count, rows, _ = rest_ref.shape
    width = shard_count * rows
    tokens = x_ref.shape[0]
    own_rows = D // shard_count
    planes = shard_count // 2
    block = own_rows // 16 * 16

    def weight_copies(n, slot):
        return [
            pltpu.make_async_copy(
                rest_ref.at[:, :, pl.ds(pl.multiple_of(i * FF + n * SUB, 128), SUB)],
                weights.at[slot, i],
                sems.at[slot, i],
            )
            for i in range(3)
        ]

    out_copy = pltpu.make_async_copy(
        rest_ref.at[:, :, pl.ds(3 * FF, QW)], out_weight, sems.at[2, 0]
    )
    gain_copy = pltpu.make_async_copy(
        rest_ref.at[:, pl.ds(block, rows - block), pl.ds(0, 128)], gain_rows, sems.at[2, 1]
    )
    out_copy.start()
    gain_copy.start()
    for copy in weight_copies(0, 0):
        copy.start()
    pad_features(x_ref, middle, own_rows, rows)
    pad_features(cot_ref, cot, own_rows, rows)
    flip_blocks(cot, flipped)
    split_cores(at, flipped, cot_own, cot_give)

    gain_copy.wait()
    gain = jnp.concatenate(
        [
            gain_rows[s, own_rows - block : own_rows - block + 1, :rows].astype(F32)
            for s in range(shard_count)
        ],
        axis=1,
    )
    lane = lax.broadcasted_iota(jnp.int32, (1, width), 1)
    real = lax.rem(lane, rows) < own_rows
    gain = jnp.where(real, gain, 0.0)
    out_copy.wait()
    out_full = out_weight.reshape(width, QW)

    def scale_of(value):
        return lax.rsqrt(jnp.sum(value * value, axis=-1, keepdims=True) * (1.0 / D) + eps_norm)

    for low in range(0, tokens, PART):
        where = slice(low, low + PART)
        value = middle[where, :] + dot(mixed_ref[:, where].T, out_full[...], 1, 1)
        middle[where, :] = value
        hidden[where, :] = (value * scale_of(value) * gain).astype(BF)
    flip_blocks(hidden, flipped)
    split_cores(at, flipped, hidden_own, hidden_give)
    acc_out[...] = jnp.zeros_like(acc_out)
    acc_grad[...] = jnp.zeros_like(acc_grad)

    def put(ref, column, value):
        where = pl.ds(pl.multiple_of(column, 128), value.shape[1])
        ref[:, :, where] = value.reshape(planes, rows, value.shape[1]).astype(BF)

    def step(n, _):
        slot = lax.rem(n, 2)
        for copy in weight_copies(n, slot):
            copy.wait()

        @pl.when(n + 1 < FF // SUB)
        def _():
            for copy in weight_copies(n + 1, 1 - slot):
                copy.start()

        gate_weight = weights[slot, 0].reshape(width, SUB)
        upper_weight = weights[slot, 1].reshape(width, SUB)
        shrink_weight = weights[slot, 2].reshape(width, SUB)
        gate = dot(hidden[...], gate_weight)
        upper = dot(hidden[...], upper_weight)
        inner_grad = dot(cot[...], shrink_weight)
        sigmoid = jax.nn.sigmoid(gate)
        active = gate * sigmoid
        inner = (active * upper).astype(BF)
        gate_grad = (inner_grad * upper * sigmoid * (1.0 + gate * (1.0 - sigmoid))).astype(BF)
        upper_grad = (inner_grad * active).astype(BF)
        for low in range(0, width, width // 2):
            cols = slice(low, low + width // 2)
            acc_out[:, cols] += dot(inner, shrink_weight[cols], 1, 1)
            acc_grad[:, cols] += dot(gate_grad, gate_weight[cols], 1, 1) + dot(
                upper_grad, upper_weight[cols], 1, 1
            )
        chunk, part = n // 2, lax.rem(n, 2) * SUB
        first = chunk * 3 * CHUNK + part
        put(total.own, first, dot(hidden_own[...].reshape(width // 2, tokens), gate_grad))
        put(total.own, first + CHUNK, dot(hidden_own[...].reshape(width // 2, tokens), upper_grad))
        put(total.own, first + 2 * CHUNK, dot(cot_own[...].reshape(width // 2, tokens), inner))
        for n_start in range(2 * total.slots, FF // SUB, 2):
            pl.when(n == n_start)(lambda: total.claim(n_start // 2))
        give = total.give.at[lax.rem(chunk, total.slots)]
        put(give, part, dot(hidden_give[...].reshape(width // 2, tokens), gate_grad))
        put(give, part + CHUNK, dot(hidden_give[...].reshape(width // 2, tokens), upper_grad))
        put(give, part + 2 * CHUNK, dot(cot_give[...].reshape(width // 2, tokens), inner))
        for n_end in range(1, FF // SUB, 2):
            pl.when(n == n_end)(lambda: total.start(n_end // 2))
        at_steps(n, events)
        return 0

    lax.fori_loop(0, FF // SUB, step, 0)

    term = jnp.zeros((1, width), F32)
    for low in range(0, tokens, PART):
        where = slice(low, low + PART)
        value = middle[where, :]
        result = value + acc_out[where, :]
        for s in range(shard_count):
            out_ref[where, s * own_rows : (s + 1) * own_rows] = result[
                :, s * rows : s * rows + own_rows
            ]
        scale = scale_of(value)
        normed = value * scale
        hidden_grad = jnp.where(real, acc_grad[where, :], 0.0)
        term = term + jnp.sum(hidden_grad * normed, axis=0, keepdims=True)
        upstream = hidden_grad * gain
        mean = jnp.sum(upstream * normed, axis=-1, keepdims=True) * (1.0 / D)
        value = cot[where, :].astype(F32) + scale * (upstream - normed * mean)
        middle_grad_ref[where, :] = value
        branch = value.astype(BF)
        hidden[where, :] = branch
        gradt_ref[:, where] = dot(branch, out_full[...]).T.astype(BF)
    for s in range(shard_count):
        gain_term[s] = jnp.broadcast_to(term[:, s * rows : (s + 1) * rows], (8, rows))
    flip_blocks(hidden, flipped)
    split_cores(at, flipped, hidden_own, hidden_give)
    place = lax.broadcasted_iota(jnp.int32, (rows, rows), 0)
    last = len(total.chunks) - 1
    total.claim(last)
    for lhs, core, ref, column in (
        (hidden_own, at.c, total.own, total.chunks[last][0]),
        (hidden_give, 1 - at.c, total.give.at[last % total.slots], 0),
    ):
        for z in range(planes):
            product = dot(lhs[z], mixed_ref[...], 1, 1)
            row = gain_term[2 * z + core][:1]
            ref[z, :, column : column + rows] = jnp.where(
                place == own_rows, row, product[:, :rows]
            ).astype(BF)
            ref[z, :, column + rows : column + QW] = product[:, rows:].astype(BF)
            end = column + total.chunks[last][1]
            ref[z, :, column + QW : end] = jnp.zeros((rows, end - column - QW), BF)
    total.start(last)


def rear_kernel(
    x_ref,
    cot_ref,
    mixed_ref,
    rest_ref,
    win_hbm,
    feat_hbm,
    qt_hbm,
    qfeat_ref,
    lse_ref,
    out_ref,
    middle_grad_ref,
    dq_ref,
    pairs_ref,
    sum_ref,
    gradt_ref,
    ra,
    rb,
    r2,
    r1,
    collect_send,
    collect_recv,
    *reduce_scratch,
):
    at = Place()
    tokens = x_ref.shape[0]
    shard_count, rows, _ = rest_ref.shape
    width = shard_count * rows
    kv_heads, _, lanes = pairs_ref.shape
    keys = feat_hbm.shape[0]
    greet(at, True)
    total = Reduce(at, rear_chunks(), sum_ref, *reduce_scratch)

    def run(*names):
        def event():
            for name, n in names:
                getattr(total, name)(n)

        return event

    forward_events = [
        (2, run(("zero", 0), ("push", 0))),
        (4, run(("zero", 1))),
        (5, run(("one", 0), ("push", 1))),
        (6, run(("zero", 2), ("two", 0))),
        (8, run(("zero", 3))),
        (9, run(("one", 1), ("push", 2), ("three", 0))),
    ]
    backward_events = [
        (0, run(("zero", 4), ("two", 1), ("four", 0))),
        (2, run(("one", 2), ("push", 3), ("five", 0))),
        (3, run(("zero", 5), ("two", 2), ("three", 1))),
        (4, run(("four", 1))),
        (5, run(("three", 2))),
        (6, run(("one", 3), ("push", 4), ("five", 1), ("four", 2))),
        (7, run(("two", 3))),
        (9, run(("three", 3), ("five", 2))),
        (10, run(("one", 4), ("push", 5), ("four", 3))),
        (11, run(("two", 4))),
        (12, run(("one", 5), ("three", 4), ("five", 3))),
        (13, run(("two", 5), ("four", 4))),
        (14, run(("three", 5), ("five", 4))),
    ]

    pl.run_scoped(
        functools.partial(
            feed_forward,
            at,
            total,
            x_ref,
            cot_ref,
            mixed_ref,
            rest_ref,
            out_ref,
            middle_grad_ref,
            gradt_ref,
            forward_events,
        ),
        VMEM((tokens, width), BF),
        VMEM((tokens, width), BF),
        VMEM((tokens, width), F32),
        VMEM((tokens, width), F32),
        VMEM((tokens, width), F32),
        VMEM((shard_count, rows, tokens), BF),
        VMEM((shard_count // 2, rows, tokens), BF),
        VMEM((shard_count // 2, rows, tokens), BF),
        VMEM((shard_count // 2, rows, tokens), BF),
        VMEM((shard_count // 2, rows, tokens), BF),
        VMEM((shard_count, rows, QW), BF),
        VMEM((shard_count, rows - D // shard_count // 16 * 16, 128), BF),
        VMEM((shard_count, 8, rows), F32),
        VMEM((2, 3, shard_count, rows, SUB), BF),
        DMA((3, 3)),
    )

    def attention(kvf, kt, qa, da, acc, rhs, grads, t2, t1, win_ref, feat_ref, qt_ref, sems):
        loads = [
            pltpu.make_async_copy(src, dst, sems.at[i])
            for i, (src, dst) in enumerate(
                ((feat_hbm, feat_ref), (win_hbm, win_ref), (qt_hbm, qt_ref))
            )
        ]
        for load in loads:
            load.start()
        for load in loads:
            load.wait()
        collect = Collect(
            at, grads, pairs_ref, ra, rb, r2, r1, t2, t1, collect_send, collect_recv
        )
        attend_backward_setup(feat_ref, kvf, qa, da, rhs)

        def key_head(j, _):
            attend_backward_keys(j, win_ref, kvf, kt, acc)

            def head(g, _):
                h = j * GROUP + g
                attend_backward_head(
                    h,
                    qt_ref,
                    qfeat_ref,
                    gradt_ref,
                    mixed_ref,
                    lse_ref,
                    dq_ref,
                    kvf,
                    kt,
                    qa,
                    da,
                    acc,
                    rhs,
                )
                at_steps(h, backward_events)
                return 0

            lax.fori_loop(0, GROUP, head, 0)
            attend_backward_done(j, acc, grads)
            collect.start(j)
            pl.when(j > 0)(lambda: collect.one(j - 1))
            pl.when(j > 1)(lambda: collect.two(j - 2))
            pl.when(j > 2)(lambda: collect.three(j - 3))
            return 0

        lax.fori_loop(0, kv_heads, key_head, 0)
        collect.one(kv_heads - 1)
        collect.two(kv_heads - 2)
        total.four(5)
        collect.two(kv_heads - 1)
        for j in range(kv_heads - 3, kv_heads):
            collect.three(j)
        total.five(5)
        for j in range(kv_heads):
            collect.sent(j)
        total.sent()

    pl.run_scoped(
        attention,
        *attend_backward_scratch(keys, lanes, tokens),
        VMEM(win_hbm.shape, BF),
        VMEM(pairs_ref.shape, BF),
        VMEM(pairs_ref.shape, BF),
        VMEM(win_hbm.shape, BF),
        VMEM(feat_hbm.shape, BF),
        VMEM(qt_hbm.shape, BF),
        DMA((3,)),
    )


def rear(x, cotangent, mixed, rest, window, feat, qt, qfeat, lse, number):
    blocks, kv_heads, tokens, lanes = window.shape
    shard_count, rows, _ = rest.shape
    columns = sum(width for _, width in rear_chunks())
    pairs = (kv_heads, tokens, lanes)
    return pl.pallas_call(
        rear_kernel,
        out_shape=(
            jax.ShapeDtypeStruct(x.shape, F32),
            jax.ShapeDtypeStruct((tokens, shard_count * rows), F32),
            jax.ShapeDtypeStruct(qt.shape, F32),
            jax.ShapeDtypeStruct(pairs, F32),
            jax.ShapeDtypeStruct((rows, columns), BF),
        ),
        in_specs=[pl.BlockSpec(memory_space=VMEM)] * 3
        + [pl.BlockSpec(memory_space=ANY)] * 4
        + [pl.BlockSpec(memory_space=VMEM)] * 2,
        out_specs=(pl.BlockSpec(memory_space=VMEM),) * 5,
        scratch_shapes=[VMEM(qt.shape, BF)]
        + [VMEM(pairs, BF)] * 4
        + [DMA((4, kv_heads)), DMA((4, kv_heads))]
        + Reduce.scratch(rows, rear_chunks(), 2),
        compiler_params=pltpu.CompilerParams(
            collective_id=number, has_side_effects=True, vmem_limit_bytes=BIG_VMEM
        ),
        name="rear",
    )(x, cotangent, mixed, rest, window, feat, qt, qfeat, lse)


def tail_kernel(
    x_ref,
    middle_grad_ref,
    dq_ref,
    pairs_ref,
    cos_ref,
    sin_ref,
    attend_ref,
    grad_ref,
    sum_ref,
    inputs,
    hidden,
    jointt,
    flipped,
    hidden_own,
    hidden_give,
    gain_term,
    *reduce_scratch,
):
    at = Place()
    shard_count, rows, columns = attend_ref.shape
    width = shard_count * rows
    tokens = x_ref.shape[0]
    own_rows = D // shard_count
    greet(at, True)
    total = Reduce(at, [(0, columns)], sum_ref, *reduce_scratch)
    pad_features(x_ref, inputs, own_rows, rows)
    lane = lax.broadcasted_iota(jnp.int32, (1, width), 1)
    real = lax.rem(lane, rows) < own_rows
    gain = jnp.concatenate(
        [
            attend_ref[s, own_rows : own_rows + 1, :rows].astype(F32)
            for s in range(shard_count)
        ],
        axis=1,
    )
    gain = jnp.where(real, gain, 0.0)

    def unrotate(head):
        half = HEAD_DIM // 2
        front, back = head[:half], head[half:]
        cosine, sine = cos_ref[...], sin_ref[...]
        return jnp.concatenate(
            [front * cosine + back * sine, back * cosine - front * sine], axis=0
        ).astype(BF)

    for h in range(HEADS):
        where = slice(h * HEAD_DIM, (h + 1) * HEAD_DIM)
        jointt[where, :] = unrotate(dq_ref[where, :])
    for j in range(KV_HEADS):
        pair = pairs_ref[j].T
        low = QW + j * HEAD_DIM
        jointt[low : low + HEAD_DIM, :] = unrotate(pair[:HALF])
        jointt[low + KW : low + KW + HEAD_DIM, :] = pair[HALF:].astype(BF)

    weight = attend_ref.reshape(width, columns)
    term = jnp.zeros((1, width), F32)
    for low in range(0, tokens, PART):
        where = slice(low, low + PART)
        value = inputs[where, :]
        scale = lax.rsqrt(jnp.sum(value * value, axis=-1, keepdims=True) * (1.0 / D) + eps_norm)
        normed = value * scale
        hidden[where, :] = (normed * gain).astype(BF)
        hidden_grad = dot(jointt[:, where].T, weight[...], 1, 1)
        hidden_grad = jnp.where(real, hidden_grad, 0.0)
        term = term + jnp.sum(hidden_grad * normed, axis=0, keepdims=True)
        upstream = hidden_grad * gain
        mean = jnp.sum(upstream * normed, axis=-1, keepdims=True) * (1.0 / D)
        result = middle_grad_ref[where, :] + scale * (upstream - normed * mean)
        for s in range(shard_count):
            grad_ref[where, s * own_rows : (s + 1) * own_rows] = result[
                :, s * rows : s * rows + own_rows
            ]
    for s in range(shard_count):
        gain_term[s] = jnp.broadcast_to(term[:, s * rows : (s + 1) * rows], (8, rows))
    flip_blocks(hidden, flipped)
    split_cores(at, flipped, hidden_own, hidden_give)
    place = lax.broadcasted_iota(jnp.int32, (rows, rows), 0)
    for lhs, core, ref in (
        (hidden_give, 1 - at.c, total.give.at[0]),
        (hidden_own, at.c, total.own),
    ):
        for z in range(lhs.shape[0]):
            product = dot(lhs[z], jointt[...], 1, 1)
            row = gain_term[2 * z + core][:1]
            ref[z, :, :rows] = jnp.where(place == own_rows, row, product[:, :rows]).astype(BF)
            ref[z, :, rows:] = product[:, rows:].astype(BF)
        if ref is not total.own:
            total.start(0)
    for step in (total.zero, total.push, total.one, total.two, total.three):
        step(0)
    total.four(0)
    total.five(0)
    total.sent()


def tail(x, middle_grad, dq, pairs, cosine, sine, attend_planes, number):
    tokens, width = middle_grad.shape
    shard_count, rows, columns = attend_planes.shape
    return pl.pallas_call(
        tail_kernel,
        out_shape=(
            jax.ShapeDtypeStruct(x.shape, F32),
            jax.ShapeDtypeStruct((rows, columns), BF),
        ),
        in_specs=[pl.BlockSpec(memory_space=VMEM)] * 7,
        out_specs=(pl.BlockSpec(memory_space=VMEM),) * 2,
        scratch_shapes=[
            VMEM((tokens, width), F32),
            VMEM((tokens, width), BF),
            VMEM((columns, tokens), BF),
            VMEM((shard_count, rows, tokens), BF),
            VMEM((shard_count // 2, rows, tokens), BF),
            VMEM((shard_count // 2, rows, tokens), BF),
            VMEM((shard_count, 8, rows), F32),
        ]
        + Reduce.scratch(rows, [(0, columns)], 1),
        compiler_params=pltpu.CompilerParams(
            collective_id=number, has_side_effects=True, vmem_limit_bytes=BIG_VMEM
        ),
        name="tail",
    )(x, middle_grad, dq, pairs, cosine, sine, attend_planes)


def adam_parts(old_weight, gradient, first, second, decay_factor):
    moment = beta_one * first + (1.0 - beta_one) * gradient
    square = beta_two * second + (1.0 - beta_two) * gradient * gradient
    corrected = moment * (1.0 / (1.0 - beta_one**STEP))
    divisor = jnp.sqrt(square * (1.0 / (1.0 - beta_two**STEP))) + adam_eps
    update = -learn_rate * (corrected / divisor + decay_factor * old_weight)
    return moment, square, update


def adam_kernel(grad_scale, own_rows, *refs):
    attend_sum, rest_sum, attend_planes, rest_planes = refs[:4]
    states, results = refs[4:12], refs[12:28]
    buffers, weights, in_sems, out_sems = refs[28:44], refs[44:46], refs[46], refs[47]
    shard = lax.axis_index("shard")
    loads = [
        pltpu.make_async_copy(attend_planes.at[shard], weights[0], in_sems.at[8]),
        pltpu.make_async_copy(rest_planes.at[shard], weights[1], in_sems.at[9]),
    ]
    order = (0, 1, 3, 2)
    for n in order:
        for i in range(2):
            loads.append(
                pltpu.make_async_copy(
                    states[2 * n + i], buffers[4 * n + 1 + i], in_sems.at[2 * n + i]
                )
            )
    for load in loads:
        load.start()
    loads[0].wait()
    loads[1].wait()
    stores = []

    def update(n, where, total, weight, flip):
        gradient, moment, square, changed = buffers[4 * n : 4 * n + 4]
        total = total.astype(F32)
        weight = weight.astype(F32)
        if flip:
            total, weight = total.T[:, :own_rows], weight.T[:, :own_rows]
        total = total * grad_scale
        new_moment, new_square, step = adam_parts(
            weight, total, moment[where], square[where], decay_rate
        )
        gradient[where] = total
        moment[where] = new_moment
        square[where] = new_square
        changed[where] = weight + step

    everything = slice(None)
    for place, n in enumerate(order):
        loads[2 + 2 * place].wait()
        loads[3 + 2 * place].wait()
        if n == 0:
            columns = weights[0].shape[1]
            for low in range(0, columns, CHUNK):
                cols = slice(low, min(low + CHUNK, columns))
                update(
                    0,
                    (everything, cols),
                    attend_sum[:own_rows, cols],
                    weights[0][:own_rows, cols],
                    False,
                )
        elif n == 1:
            cols = slice(3 * FF, 3 * FF + QW)
            update(1, (everything, everything), rest_sum[:, cols], weights[1][:, cols], True)
        else:
            for c in range(FF // CHUNK):
                for part in (0, 1) if n == 2 else (2,):
                    low = 3 * CHUNK * c + CHUNK * part
                    first = part * FF + CHUNK * c
                    rows = slice(None) if n == 3 else slice(0, own_rows)
                    total = rest_sum[rows, low : low + CHUNK]
                    weight = weights[1][rows, first : first + CHUNK]
                    if n == 3:
                        where = (slice(c * CHUNK, (c + 1) * CHUNK), everything)
                    else:
                        where = (everything, slice(first, first + CHUNK))
                    update(n, where, total, weight, n == 3)
        for i in range(4):
            store = pltpu.make_async_copy(
                buffers[4 * n + i], results[4 * n + i], out_sems.at[4 * n + i]
            )
            store.start()
            stores.append(store)
    for store in stores:
        store.wait()


def adam(grad_scale, own_rows, attend_sum, rest_sum, attend_planes, rest_planes, states):
    flat = [array for pair in states for array in pair]
    shapes = [pair[0].shape for pair in states]
    return pl.pallas_call(
        functools.partial(adam_kernel, grad_scale, own_rows),
        out_shape=tuple(jax.ShapeDtypeStruct(shape, F32) for shape in shapes for _ in range(4)),
        in_specs=[pl.BlockSpec(memory_space=VMEM)] * 2 + [pl.BlockSpec(memory_space=ANY)] * 10,
        out_specs=(pl.BlockSpec(memory_space=ANY),) * 16,
        scratch_shapes=[VMEM(shape, F32) for shape in shapes for _ in range(4)]
        + [VMEM(attend_planes.shape[1:], BF), VMEM(rest_planes.shape[1:], BF)]
        + [DMA((10,)), DMA((16,))],
        compiler_params=pltpu.CompilerParams(vmem_limit_bytes=BIG_VMEM),
        name="adam",
    )(attend_sum, rest_sum, attend_planes, rest_planes, *flat)


def reduce_rows(parts):
    own = lax.psum_scatter(parts, "shard", scatter_dimension=0)
    return lax.psum(own, "rep")


def spread_pairs(pairs, reach):
    devices = range(lax.axis_size("shard"))
    blocks = []
    for distance in range(reach, 0, -1):
        route = [(i - distance, i) for i in devices if i - distance in devices]
        blocks.append(lax.ppermute(pairs, "shard", route))
    return jnp.stack(blocks + [pairs])


def collect_pairs(grads, reach):
    devices = range(lax.axis_size("shard"))
    own = grads[reach].astype(F32)
    for distance in range(1, reach + 1):
        route = [(i, i - distance) for i in devices if i - distance in devices]
        own = own + lax.ppermute(grads[reach - distance], "shard", route).astype(F32)
    return own


def angles(positions):
    half_dim = HEAD_DIM // 2
    inverse = rope_base ** (-(2.0 * jnp.arange(half_dim, dtype=F32) / HEAD_DIM))
    phases = positions.astype(F32)[:, None] * inverse[None, :]
    return (jnp.cos(phases)[:, None, :], jnp.sin(phases)[:, None, :])


def rotate(tensor, cosine_table, sine_table):
    half_dim = HEAD_DIM // 2
    front, back = tensor[..., :half_dim], tensor[..., half_dim:]
    return jnp.concatenate(
        [front * cosine_table - back * sine_table, back * cosine_table + front * sine_table],
        axis=-1,
    )


def norm_back(upstream, normed, scale_rows):
    mean = jnp.sum(upstream * normed, axis=-1, keepdims=True) * (1.0 / D)
    return scale_rows * (upstream - normed * mean)


def adam_step(weight_now, gradient, first, second, decay_factor):
    moment, square, update = adam_parts(
        weight_now.astype(F32), gradient, first, second, decay_factor
    )
    return (gradient, moment, square, update)


def shards(
    direct,
    block_input,
    block_cotangent,
    lengths,
    attend_gain,
    attend_weight,
    output_weight,
    expand_gain,
    expand_weight,
    shrink_weight,
    attend_gain_first,
    attend_weight_first,
    output_weight_first,
    expand_gain_first,
    expand_weight_first,
    shrink_weight_first,
    attend_gain_second,
    attend_weight_second,
    output_weight_second,
    expand_gain_second,
    expand_weight_second,
    shrink_weight_second,
):
    tokens = block_input.shape[0]
    shard_count = lax.axis_size("shard")
    token_count = tokens * shard_count * lax.axis_size("rep")
    reach = (MAXLEN - 2) // tokens + 1
    own_rows = attend_weight.shape[0]
    rows = -(-(own_rows + 2) // 16) * 16
    width = shard_count * rows

    def padded(tensor):
        blocks = tensor.reshape(tokens, shard_count, own_rows)
        return jnp.pad(blocks, ((0, 0), (0, 0), (0, rows - own_rows))).reshape(tokens, width)

    def unpadded(tensor):
        return tensor.reshape(tokens, shard_count, rows)[:, :, :own_rows].reshape(tokens, D)

    def with_gain(weight, gain):
        tail = jnp.pad(gain[None, :], ((0, rows - own_rows - 1), (0, weight.shape[1] - own_rows)))
        return jnp.concatenate([weight, tail], axis=0)

    def gain_of(planes):
        return jnp.pad(
            planes[:, own_rows, :own_rows], ((0, 0), (0, rows - own_rows))
        ).reshape(1, width).astype(F32)

    def add_gain(planes, term, column):
        row = term.reshape(shard_count, 1, rows).astype(planes.dtype)
        return lax.dynamic_update_slice(planes, row, (0, own_rows, column))

    def in_chunks(expand, shrink):
        parts = jnp.concatenate([expand, shrink], axis=1).reshape(-1, 3, FF // CHUNK, CHUNK)
        return parts.transpose(0, 2, 1, 3).reshape(-1, 3 * FF)

    first_row = lax.axis_index("shard") * tokens
    local_index = first_row + jnp.arange(tokens, dtype=jnp.int32)
    key_index = first_row - reach * tokens + jnp.arange((reach + 1) * tokens, dtype=jnp.int32)
    ends = jnp.cumsum(lengths[0], dtype=jnp.int32)
    starts = ends - lengths[0]
    seq_count = lengths.shape[1]
    in_key = (key_index[:, None] >= starts[None, :]) & (key_index[:, None] < ends[None, :])
    in_query = (local_index[None, :] >= starts[:, None]) & (local_index[None, :] < ends[:, None])
    lanes = 2 * HEAD_DIM
    feat = jnp.concatenate(
        [
            in_key.astype(BF),
            (key_index < 0).astype(BF)[:, None],
            jnp.zeros((key_index.shape[0], ONES - seq_count - 1), BF),
            jnp.ones((key_index.shape[0], lanes - ONES), BF),
        ],
        axis=1,
    )
    qfeat = jnp.concatenate(
        [
            jnp.where(in_query, 0.0, NEG).astype(BF),
            jnp.full((1, tokens), NEG, BF),
            jnp.zeros((lanes - seq_count - 1, tokens), BF),
        ],
        axis=0,
    )
    start_index = jnp.sum(in_query * starts[:, None], axis=0, dtype=jnp.int32)
    cosine_table, sine_table = angles(local_index - start_index)

    attend_own = with_gain(attend_weight, attend_gain)
    rest_own = with_gain(
        jnp.concatenate([expand_weight, shrink_weight.T, output_weight.T], axis=1), expand_gain
    )
    if direct:
        tables = (cosine_table[:, 0].T, sine_table[:, 0].T)
        attend_planes, rest_planes, window, qt, mixedt, lse = front(
            padded(block_input), *tables, feat, qfeat, attend_own, rest_own, shard_count, 0
        )
        block_output, middle_grad, dqt, own_pairs, rest_sum = rear(
            block_input, block_cotangent, mixedt, rest_planes, window, feat, qt, qfeat, lse, 1
        )
        input_gradient, attend_sum = tail(
            block_input, middle_grad, dqt, own_pairs, *tables, attend_planes, 2
        )
    else:
        attend_planes = lax.all_gather(attend_own, "shard", axis=0)
        rest_planes = lax.all_gather(rest_own, "shard", axis=0)
        gain_one, gain_two = gain_of(attend_planes), gain_of(rest_planes)
        joint_weight = attend_planes.reshape(width, JW)
        rest = rest_planes.reshape(width, rest_own.shape[1])
        expand_full, shrink_full, out_full = rest[:, : 2 * FF], rest[:, 2 * FF : 3 * FF], rest[:, 3 * FF :]
        real = (jnp.arange(width, dtype=jnp.int32) % rows < own_rows)[None, :]

        inputs = padded(block_input).astype(F32)
        scale_one = lax.rsqrt(jnp.sum(inputs * inputs, axis=-1, keepdims=True) * (1.0 / D) + eps_norm)
        normed_one = inputs * scale_one
        hidden_one = (normed_one * gain_one).astype(BF)
        joint = dot(hidden_one, joint_weight)
        queries = rotate(joint[:, :QW].reshape(tokens, HEADS, HEAD_DIM), cosine_table, sine_table)
        key_rows = rotate(
            joint[:, QW : QW + KW].reshape(tokens, KV_HEADS, HEAD_DIM), cosine_table, sine_table
        )
        values = joint[:, QW + KW :].reshape(tokens, KV_HEADS, HEAD_DIM)
        pairs = jnp.concatenate([key_rows, values], axis=-1).astype(BF).transpose(1, 0, 2)
        qt = queries.astype(BF).reshape(tokens, QW).T
        window = spread_pairs(pairs, reach)
        mixedt, lse = attend_forward(window, feat, qt, qfeat)
        middle = inputs + dot(mixedt, out_full, 0, 1)
        scale_two = lax.rsqrt(jnp.sum(middle * middle, axis=-1, keepdims=True) * (1.0 / D) + eps_norm)
        normed_two = middle * scale_two
        hidden_two = (normed_two * gain_two).astype(BF)
        gate_up = dot(hidden_two, expand_full)
        gate_value, upper_value = gate_up[:, :FF], gate_up[:, FF:]
        sigmoid_gate = jax.nn.sigmoid(gate_value)
        inner_rows = (gate_value * sigmoid_gate * upper_value).astype(BF)
        block_output = middle + dot(inner_rows, shrink_full, 1, 1)

        cotangent = padded(block_cotangent)
        shrink_term = dot(cotangent, inner_rows, 0, 0)
        inner_grad = dot(cotangent, shrink_full)
        gate_grad = (
            inner_grad * upper_value * sigmoid_gate * (1.0 + gate_value * (1.0 - sigmoid_gate))
        ).astype(BF)
        upper_grad = (inner_grad * gate_value * sigmoid_gate).astype(BF)
        gate_up_grad = jnp.concatenate([gate_grad, upper_grad], axis=1)
        expand_term = dot(hidden_two, gate_up_grad, 0, 0)
        hidden_two_grad = jnp.where(real, dot(gate_up_grad, expand_full, 1, 1), 0.0)
        gain_two_term = jnp.sum(hidden_two_grad * normed_two, axis=0)
        middle_grad = cotangent.astype(F32) + norm_back(
            hidden_two_grad * gain_two, normed_two, scale_two
        )
        branch_grad = middle_grad.astype(BF)
        output_term = dot(branch_grad, mixedt, 0, 1)
        gradt = dot(out_full, branch_grad, 0, 1).astype(BF)
        rest_term = jnp.concatenate(
            [in_chunks(expand_term, shrink_term), output_term], axis=1
        ).astype(BF).reshape(shard_count, rows, rest_own.shape[1])
        rest_sum = reduce_rows(add_gain(rest_term, gain_two_term, 3 * FF))
        dqt, dwindow = attend_backward(window, feat, qt, qfeat, gradt, mixedt, lse)
        own_pairs = collect_pairs(dwindow, reach)
        block_output = unpadded(block_output)
        own_pairs = own_pairs.transpose(1, 0, 2)
        dq = dqt.T.reshape(tokens, HEADS, HEAD_DIM)
        query_raw = rotate(dq, cosine_table, -sine_table).reshape(tokens, QW)
        key_raw = rotate(own_pairs[..., :HEAD_DIM], cosine_table, -sine_table).reshape(tokens, KW)
        value_raw = own_pairs[..., HEAD_DIM:].reshape(tokens, KW)
        joint_grad = jnp.concatenate([query_raw, key_raw, value_raw], axis=1).astype(BF)
        joint_term = dot(hidden_one, joint_grad, 0, 0).astype(BF)
        hidden_one_grad = jnp.where(real, dot(joint_grad, joint_weight, 1, 1), 0.0)
        gain_one_term = jnp.sum(hidden_one_grad * normed_one, axis=0)
        input_gradient = middle_grad + norm_back(hidden_one_grad * gain_one, normed_one, scale_one)
        attend_sum = reduce_rows(
            add_gain(joint_term.reshape(shard_count, rows, JW), gain_one_term, 0)
        )
        input_gradient = unpadded(input_gradient)

    grad_scale = grad_factor * token_count ** (-0.5)
    first_gain, second_gain = (
        adam_step(weight, total.astype(F32) * grad_scale, first, second, 0.0)
        for weight, total, first, second in (
            (
                attend_gain,
                attend_sum[own_rows, :own_rows],
                attend_gain_first,
                attend_gain_second,
            ),
            (
                expand_gain,
                rest_sum[own_rows, 3 * FF : 3 * FF + own_rows],
                expand_gain_first,
                expand_gain_second,
            ),
        )
    )
    matrices = adam(
        grad_scale,
        own_rows,
        attend_sum,
        rest_sum,
        attend_planes,
        rest_planes,
        (
            (attend_weight_first, attend_weight_second),
            (output_weight_first, output_weight_second),
            (expand_weight_first, expand_weight_second),
            (shrink_weight_first, shrink_weight_second),
        ),
    )
    first_joint, first_output, second_expand, second_shrink = (
        matrices[4 * n : 4 * n + 4] for n in range(4)
    )
    steps = (first_gain, first_joint, first_output, second_gain, second_expand, second_shrink)
    return (block_output, input_gradient, *[step[i] for i in range(4) for step in steps])


def solution(mesh):
    whole_rows = P(("rep", "shard"), None)
    state = (P("shard"), P("shard", None), P(None, "shard")) * 2
    direct = mesh.shape["rep"] == 4 and mesh.shape["shard"] == 8
    return jax.shard_map(
        functools.partial(shards, direct),
        mesh=mesh,
        in_specs=(whole_rows, whole_rows, P("rep", None), *state, *state, *state),
        out_specs=(whole_rows, whole_rows, *state, *state, *state, *state),
        check_vma=False,
    )
```

```python
import functools
import math

import jax
import jax.numpy as jnp
import numpy as np
from jax import lax
from jax.experimental import pallas as pl
from jax.experimental.pallas import tpu as pltpu
from jax.sharding import PartitionSpec as P

HEADS = 15
KV_HEADS = 5
HEAD_DIM = 64
GROUP = HEADS // KV_HEADS
FF = 2560
MAXLEN = 2048
STEP = 10
QW = 960
KW = 320
JW = QW + 2 * KW
D = 960

eps_norm = 1e-05
rope_base = 100000.0
beta_one = 0.9
beta_two = 0.95
adam_eps = 1e-08
learn_rate = 0.05
decay_rate = 0.1
grad_factor = 4.0

F32 = jnp.float32
BF = jnp.bfloat16
MESH = pl.DeviceIdType.MESH
ANY = pl.ANY
VMEM = pltpu.VMEM
DMA = pltpu.SemaphoreType.DMA

QC = 256
KB = 768
HALF = 64
ONES = 112
NEG = -1e30
EXP_SCALE = HEAD_DIM**-0.5 * math.log2(math.e)
BIG_VMEM = 60 * 2**20
PART = 128


def dot(a, b, ca=1, cb=0):
    return lax.dot_general(a, b, (((ca,), (cb,)), ((), ())), preferred_element_type=F32)


def causal_tile():
    key = lax.broadcasted_iota(jnp.int32, (QC, QC), 0)
    query = lax.broadcasted_iota(jnp.int32, (QC, QC), 1)
    return key <= query


def mask_last(scores, causal):
    last = jnp.where(causal, scores[KB - QC :], NEG)
    return jnp.concatenate([scores[: KB - QC], last], axis=0)


def attend_forward_setup(feat_ref, qfeat_ref, kvf, vt, qa):
    lanes = feat_ref.shape[1]
    kvf[:, lanes:] = feat_ref[...]
    qa[HALF:lanes, :] = jnp.zeros((lanes - HALF, qa.shape[1]), BF)
    qa[lanes:, :] = qfeat_ref[...]
    vt[HALF:, :] = jnp.ones((vt.shape[0] - HALF, vt.shape[1]), BF)


def attend_forward_keys(j, kv_ref, kvf, vt):
    blocks, _, rows, lanes = kv_ref.shape
    for block in range(blocks):
        part = kv_ref[block, j]
        kvf[block * rows : (block + 1) * rows, :lanes] = part
        vt[:HALF, block * rows : (block + 1) * rows] = part.T[HALF:, :]


def attend_forward_head(h, qt_ref, mixed_ref, lse_ref, kvf, vt, qa, sb):
    tokens = qt_ref.shape[1]
    steps = (kvf.shape[0] - (tokens - QC)) // KB
    causal = causal_tile()
    row = pl.multiple_of(h * HEAD_DIM, HEAD_DIM)
    qa[:HALF, :] = qt_ref[pl.ds(row, HEAD_DIM), :]
    tops = []
    for chunk in range(tokens // QC):
        low = chunk * QC
        highest = None
        for b in range(steps):
            first = low + b * KB
            s = dot(kvf[first : first + KB, :], qa[:, low : low + QC])
            if b == steps - 1:
                s = mask_last(s, causal)
            sb[chunk, b * KB : (b + 1) * KB, :] = s
            peak = jnp.max(s.reshape(KB // 8, 8, QC), axis=0)
            highest = peak if highest is None else jnp.maximum(highest, peak)
        tops.append(jnp.max(highest, axis=0, keepdims=True))
    for chunk in range(tokens // QC):
        low = chunk * QC
        shift = tops[chunk] * EXP_SCALE
        total = None
        for b in range(steps):
            first = low + b * KB
            s = sb[chunk, b * KB : (b + 1) * KB, :]
            p = jnp.exp2(s * EXP_SCALE - shift).astype(BF)
            term = dot(vt[:, first : first + KB], p)
            total = term if total is None else total + term
        weight = total[HALF : HALF + 1, :]
        mixed_ref[pl.ds(row, HEAD_DIM), low : low + QC] = (
            total[:HALF, :] * (1.0 / weight)
        ).astype(BF)
        lse_ref[pl.ds(h, 1), :, low : low + QC] = (
            tops[chunk] * HEAD_DIM**-0.5 + jnp.log(weight)
        )[None]


def attend_forward_scratch(keys, lanes, tokens):
    return [
        VMEM((keys, 2 * lanes), BF),
        VMEM((HALF + 16, keys), BF),
        VMEM((2 * lanes, tokens), BF),
        VMEM((tokens // QC, keys - (tokens - QC), QC), F32),
    ]


def attend_forward_kernel(
    kv_ref, feat_ref, qt_ref, qfeat_ref, mixed_ref, lse_ref, kvf, vt, qa, sb
):
    attend_forward_setup(feat_ref, qfeat_ref, kvf, vt, qa)

    def key_head(j, _):
        attend_forward_keys(j, kv_ref, kvf, vt)

        def head(g, _):
            attend_forward_head(j * GROUP + g, qt_ref, mixed_ref, lse_ref, kvf, vt, qa, sb)
            return 0

        lax.fori_loop(0, GROUP, head, 0)
        return 0

    lax.fori_loop(0, kv_ref.shape[1], key_head, 0)


def attend_forward(window, feat, qt, qfeat):
    blocks, kv_heads, rows, lanes = window.shape
    tokens = qt.shape[1]
    return pl.pallas_call(
        attend_forward_kernel,
        out_shape=(
            jax.ShapeDtypeStruct(qt.shape, BF),
            jax.ShapeDtypeStruct((HEADS, 1, tokens), F32),
        ),
        scratch_shapes=attend_forward_scratch(blocks * rows, lanes, tokens),
        compiler_params=pltpu.CompilerParams(vmem_limit_bytes=BIG_VMEM),
        name="attend_forward",
    )(window, feat, qt, qfeat)


def three_parts(value, rows):
    one = value.astype(BF).astype(F32)
    two = (value - one).astype(BF).astype(F32)
    three = value - one - two
    shape = (rows, value.shape[1])
    place = lax.broadcasted_iota(jnp.int32, shape, 0)
    parts = [jnp.broadcast_to(part, shape) for part in (one, two, three)]
    chosen = jnp.where(
        place == 0, parts[0], jnp.where(place == 1, parts[1], jnp.where(place == 2, parts[2], 0.0))
    )
    return chosen.astype(BF)


def attend_backward_setup(feat_ref, kvf, qa, da, rhs):
    lanes = feat_ref.shape[1]
    kvf[:, lanes:] = feat_ref[...]
    qa[HALF:lanes, :] = jnp.zeros((lanes - HALF, qa.shape[1]), BF)
    da[...] = jnp.zeros_like(da)
    rhs[...] = jnp.zeros_like(rhs)


def attend_backward_keys(j, kv_ref, kvf, kt, acc):
    blocks, _, rows, lanes = kv_ref.shape
    for block in range(blocks):
        part = kv_ref[block, j]
        kvf[block * rows : (block + 1) * rows, :lanes] = part
        kt[:, block * rows : (block + 1) * rows] = part.T[:HALF, :]
    acc[...] = jnp.zeros_like(acc)


def attend_backward_head(
    h, put_query, qt_ref, qfeat_ref, gradt_ref, mixed_ref, lse_ref, kvf, kt, qa, da, acc, rhs
):
    tokens = qt_ref.shape[1]
    lanes = qfeat_ref.shape[0]
    steps = (kvf.shape[0] - (tokens - QC)) // KB
    causal = causal_tile()
    extra = lanes - ONES
    row = pl.multiple_of(h * HEAD_DIM, HEAD_DIM)
    q = qt_ref[pl.ds(row, HEAD_DIM), :]
    grad = gradt_ref[pl.ds(row, HEAD_DIM), :]
    qa[:HALF, :] = q
    da[HALF:lanes, :] = grad
    mixed = mixed_ref[pl.ds(row, HEAD_DIM), :].astype(F32)
    row_total = jnp.sum(grad.astype(F32) * mixed, axis=0, keepdims=True)
    lse = lse_ref[pl.ds(h, 1), :, :][0]
    qa[lanes : lanes + ONES, :] = qfeat_ref[:ONES, :]
    qa[lanes + ONES :, :] = three_parts(-(HEAD_DIM**0.5) * lse, extra)
    da[lanes + ONES :, :] = three_parts(-row_total, extra)
    query_grads = [None] * (tokens // QC)
    for chunk in range(tokens // QC):
        low = chunk * QC
        rhs[chunk, :HALF, :QC] = q[:, low : low + QC]
        rhs[chunk, HALF:, QC:] = grad[:, low : low + QC]
    for b in range(steps):
        for chunk in range(tokens // QC):
            low = chunk * QC
            first = low + b * KB
            keys = kvf[first : first + KB, :]
            s = dot(keys, qa[:, low : low + QC])
            if b == steps - 1:
                s = mask_last(s, causal)
            p = jnp.exp2(s * EXP_SCALE)
            dp = dot(keys, da[:, low : low + QC])
            ds = (p * dp).astype(BF)
            both = jnp.concatenate([ds, p.astype(BF)], axis=1)
            acc[first : first + KB, :] += dot(both, rhs[chunk], 1, 1)
            term = dot(kt[:, first : first + KB], ds)
            old = query_grads[chunk]
            query_grads[chunk] = term if old is None else old + term
    for chunk in range(tokens // QC):
        low = chunk * QC
        put_query(row, low, query_grads[chunk] * HEAD_DIM**-0.5)


def attend_backward_done(j, acc, dkv_ref):
    blocks, _, rows, lanes = dkv_ref.shape
    lane = lax.broadcasted_iota(jnp.int32, (1, lanes), 1)
    factor = jnp.where(lane < HALF, HEAD_DIM**-0.5, 1.0)
    for block in range(blocks):
        part = acc[block * rows : (block + 1) * rows, :]
        dkv_ref[block, j] = (part * factor).astype(dkv_ref.dtype)


def attend_backward_scratch(keys, lanes, tokens):
    return [
        VMEM((keys, 2 * lanes), BF),
        VMEM((HALF, keys), BF),
        VMEM((2 * lanes, tokens), BF),
        VMEM((2 * lanes, tokens), BF),
        VMEM((keys, lanes), F32),
        VMEM((tokens // QC, lanes, 2 * QC), BF),
    ]


def attend_backward_kernel(
    kv_ref, feat_ref, qt_ref, qfeat_ref, gradt_ref, mixed_ref, lse_ref, dq_ref, dkv_ref, *scratch
):
    kvf, kt, qa, da, acc, rhs = scratch
    attend_backward_setup(feat_ref, kvf, qa, da, rhs)

    def put_query(row, low, value):
        dq_ref[pl.ds(row, HEAD_DIM), low : low + QC] = value

    def key_head(j, _):
        attend_backward_keys(j, kv_ref, kvf, kt, acc)

        def head(g, _):
            attend_backward_head(
                j * GROUP + g,
                put_query,
                qt_ref,
                qfeat_ref,
                gradt_ref,
                mixed_ref,
                lse_ref,
                *scratch,
            )
            return 0

        lax.fori_loop(0, GROUP, head, 0)
        attend_backward_done(j, acc, dkv_ref)
        return 0

    lax.fori_loop(0, kv_ref.shape[1], key_head, 0)


def attend_backward(window, feat, qt, qfeat, gradt, mixed, lse):
    blocks, kv_heads, rows, lanes = window.shape
    tokens = qt.shape[1]
    return pl.pallas_call(
        attend_backward_kernel,
        out_shape=(
            jax.ShapeDtypeStruct(qt.shape, F32),
            jax.ShapeDtypeStruct(window.shape, BF),
        ),
        scratch_shapes=attend_backward_scratch(blocks * rows, lanes, tokens),
        compiler_params=pltpu.CompilerParams(vmem_limit_bytes=BIG_VMEM),
        name="attend_backward",
    )(window, feat, qt, qfeat, gradt, mixed, lse)


class Place:
    def __init__(self):
        self.r = lax.axis_index("rep")
        self.s = lax.axis_index("shard")
        self.x, self.y = lax.rem(self.r, 2), self.r // 2
        self.z, self.c = self.s // 2, lax.rem(self.s, 2)
        self.rx = self.y * 2 + (1 - self.x)
        self.ry = (1 - self.y) * 2 + self.x
        self.rd = 3 - self.r
        self.x_side = (self.rx, self.s)
        self.y_side = (self.ry, self.s)
        self.core_side = (self.r, self.z * 2 + (1 - self.c))
        self.has_later, self.has_earlier = self.z < 3, self.z > 0
        self.later = (self.r, lax.min(self.s + 2, 7))
        self.earlier = (self.r, lax.max(self.s - 2, 0))
        self.two_earlier = (self.r, lax.max(self.s - 4, 0))

    def z_to(self, k):
        return lax.rem(self.z + k, 4)

    def z_side(self, k):
        return (self.r, self.z_to(k) * 2 + self.c)

    def arrival(self, i):
        low = self.z < 2
        first = jnp.where(self.z == 0, 1, jnp.where(self.z == 1, 0, jnp.where(self.z == 2, 3, 2)))
        if i == 0:
            return first
        if i == 1:
            return jnp.where(low, 2, 1)
        return jnp.where(low, 3, 0)


def greet(at, whole_line):
    barrier = pltpu.get_barrier_semaphore()

    def signal(device):
        pl.semaphore_signal(barrier, inc=1, device_id=device, device_id_type=MESH)

    for device in (at.x_side, at.y_side, at.core_side):
        signal(device)
    if whole_line:
        for k in (1, 2, 3):
            signal(at.z_side(k))
        pl.semaphore_wait(barrier, 6)
        return

    @pl.when(at.has_later)
    def _():
        signal(at.later)

    @pl.when(at.has_earlier)
    def _():
        signal(at.earlier)

    count = 3 + jnp.where(at.has_later, 1, 0) + jnp.where(at.has_earlier, 1, 0)
    pl.semaphore_wait(barrier, count)


def remote(src, dst, send, recv, device):
    return pltpu.make_async_remote_copy(
        src_ref=src, dst_ref=dst, send_sem=send, recv_sem=recv, device_id=device, device_id_type=MESH
    )


class Gather:
    COUNT = 31

    def __init__(self, at, own, full, columns, local_sem, send, recv):
        self.at, self.own, self.full, self.columns = at, own, full, columns
        self.local_sem, self.send, self.recv = local_sem, send, recv
        self.rows = own.shape[0]
        self.quarter, self.half = self.rows // 4, self.rows // 8

    def piece(self, plane, owner, part=None):
        start = owner * self.quarter + (0 if part is None else part * self.half)
        size = self.quarter if part is None else self.half
        return self.full.at[
            plane, pl.ds(pl.multiple_of(start, self.half), size), pl.ds(*self.columns)
        ]

    def copy(self, index, src, dst, device, landed=None):
        return remote(
            src, dst, self.send.at[index], self.recv.at[index if landed is None else landed], device
        )

    def core_copy(self):
        src = self.own.at[:, pl.ds(*self.columns)]
        return self.copy(
            28, src, self.full.at[self.at.s, :, pl.ds(*self.columns)], self.at.core_side
        )

    def local_copy(self):
        return pltpu.make_async_copy(
            self.own.at[:, pl.ds(*self.columns)],
            self.full.at[self.at.s, :, pl.ds(*self.columns)],
            self.local_sem,
        )

    def z_copy(self, up):
        at = self.at
        src = self.own.at[
            pl.ds(pl.multiple_of(at.r * self.quarter, self.quarter), self.quarter),
            pl.ds(*self.columns),
        ]
        device = at.later if up else at.earlier
        return self.copy(29 if up else 30, src, self.piece(at.s, at.r), device, at.z)

    def start_core(self):
        self.local_copy().start()
        self.core_copy().start()

    def start_z(self):
        @pl.when(self.at.has_later)
        def _():
            self.z_copy(True).start()

        @pl.when(self.at.has_earlier)
        def _():
            self.z_copy(False).start()

    def plane(self, i, other=False):
        c = 1 - self.at.c if other else self.at.c
        return self.at.arrival(i) * 2 + c

    def forwards(self, i):
        at = self.at
        chip = at.arrival(i)
        got = self.piece(self.plane(i), at.r)
        return [
            ((chip < at.z) & at.has_later, self.copy(i, got, got, at.later, chip)),
            ((chip > at.z) & at.has_earlier, self.copy(i, got, got, at.earlier, chip)),
        ]

    def out_copies(self, i):
        at, plane = self.at, self.plane(i)
        got = self.piece(plane, at.r)
        return [
            self.copy(4 + i, got, got, at.x_side),
            self.copy(7 + i, got, got, at.y_side),
            self.copy(10 + i, got, got, at.core_side),
        ]

    def cross_copies(self, i):
        at, plane = self.at, self.plane(i)
        one, two = self.piece(plane, at.rx, 0), self.piece(plane, at.ry, 1)
        from_x, from_y = self.piece(plane, at.rx), self.piece(plane, at.ry)
        return [
            self.copy(13 + i, one, one, at.y_side),
            self.copy(16 + i, from_x, from_x, at.core_side),
            self.copy(19 + i, two, two, at.x_side),
            self.copy(22 + i, from_y, from_y, at.core_side),
        ]

    def last_copy(self, i):
        got = self.piece(self.plane(i), self.at.rd)
        return self.copy(25 + i, got, got, self.at.core_side)

    def arrive(self, landed, ref):
        remote(
            ref, ref, self.send.at[landed], self.recv.at[landed], self.at.core_side
        ).wait_recv()

    def z(self, i):
        at = self.at
        self.arrive(at.arrival(i), self.piece(self.plane(i), at.r))
        for condition, copy in self.forwards(i):
            pl.when(condition)(copy.start)
        for copy in self.out_copies(i):
            copy.start()

    def cross(self, i):
        at, plane = self.at, self.plane(i)
        copies = self.cross_copies(i)
        self.arrive(4 + i, self.piece(plane, at.rx))
        copies[0].start()
        copies[1].start()
        self.arrive(7 + i, self.piece(plane, at.ry))
        copies[2].start()
        copies[3].start()

    def last(self, i):
        at, plane = self.at, self.plane(i)
        self.arrive(13 + i, self.piece(plane, at.rd, 0))
        self.arrive(19 + i, self.piece(plane, at.rd, 1))
        self.last_copy(i).start()

    def landed(self):
        at = self.at
        self.arrive(28, self.full.at[at.core_side[1], :, pl.ds(*self.columns)])
        for i in range(3):
            plane = self.plane(i, True)
            self.arrive(10 + i, self.piece(plane, at.r))
            self.arrive(16 + i, self.piece(plane, at.rx))
            self.arrive(22 + i, self.piece(plane, at.ry))
            self.arrive(25 + i, self.piece(plane, at.rd))
        self.local_copy().wait()

    def sent(self):
        at = self.at
        self.core_copy().wait_send()
        pl.when(at.has_later)(self.z_copy(True).wait_send)
        pl.when(at.has_earlier)(self.z_copy(False).wait_send)
        for i in range(3):
            for condition, copy in self.forwards(i):
                pl.when(condition)(copy.wait_send)
            for copy in self.out_copies(i) + self.cross_copies(i) + [self.last_copy(i)]:
                copy.wait_send()


class Spread:
    def __init__(self, at, win, send, recv):
        self.at, self.win, self.sems = at, win, (send, recv)
        even = at.c == 0
        self.near, self.far = jnp.where(even, 1, 3), jnp.where(even, 3, 1)

    def copy(self, n, j, src, dst, device):
        send, recv = self.sems
        return remote(
            self.win.at[src, j], self.win.at[dst, j], send.at[n, j], recv.at[n, j], device
        )

    def first(self, j):
        return self.copy(0, j, 4, 2, self.at.later)

    def twin_own(self, j):
        return self.copy(1, j, 4, 3, self.at.core_side)

    def second(self, j):
        return self.copy(2, j, 2, 0, self.at.later)

    def twin_near(self, j, place):
        return self.copy(3, j, 2, place, self.at.core_side)

    def twin_far(self, j):
        return self.copy(4, j, 0, 1, self.at.core_side)

    def clear(self):
        for block in range(4):
            @pl.when(self.at.s < 4 - block)
            def _(block=block):
                self.win[block] = jnp.zeros(self.win.shape[1:], self.win.dtype)

    def start(self, j):
        pl.when(self.at.has_later)(self.first(j).start)
        pl.when(self.at.c == 0)(self.twin_own(j).start)

    def one(self, j):
        at = self.at

        @pl.when(at.has_earlier)
        def _():
            self.first(j).wait_recv()
            self.twin_near(j, self.near).start()
            pl.when(at.has_later)(self.second(j).start)

    def two(self, j):
        at = self.at

        @pl.when(at.z > 1)
        def _():
            self.second(j).wait_recv()
            pl.when(at.c == 1)(self.twin_far(j).start)

    def landed(self, j):
        at = self.at
        pl.when(at.c == 1)(self.twin_own(j).wait_recv)
        pl.when(at.has_earlier)(self.twin_near(j, self.far).wait_recv)
        pl.when((at.c == 0) & (at.z > 1))(self.twin_far(j).wait_recv)

    def sent(self, j):
        at = self.at
        pl.when(at.has_later)(self.first(j).wait_send)
        pl.when(at.c == 0)(self.twin_own(j).wait_send)
        pl.when(at.has_earlier)(self.twin_near(j, self.near).wait_send)
        pl.when(at.has_earlier & at.has_later)(self.second(j).wait_send)
        pl.when((at.c == 1) & (at.z > 1))(self.twin_far(j).wait_send)


class Collect:
    def __init__(self, at, grads, out, ra, rb, r2, r1, t2, t1, send, recv):
        self.at, self.grads, self.out = at, grads, out
        self.ra, self.rb, self.r2, self.r1, self.t2, self.t1 = ra, rb, r2, r1, t2, t1
        self.sems = (send, recv)

    def copy(self, n, j, src, dst, device):
        send, recv = self.sems
        return remote(src, dst, send.at[n, j], recv.at[n, j], device)

    def twin_a(self, j):
        return self.copy(0, j, self.grads.at[3, j], self.ra.at[j], self.at.core_side)

    def twin_b(self, j):
        return self.copy(1, j, self.grads.at[1, j], self.rb.at[j], self.at.core_side)

    def far(self, j):
        return self.copy(2, j, self.t2.at[j], self.r2.at[j], self.at.two_earlier)

    def near(self, j):
        return self.copy(3, j, self.t1.at[j], self.r1.at[j], self.at.earlier)

    def start(self, j):
        self.twin_b(j).start()
        self.twin_a(j).start()

    def one(self, j):
        self.twin_b(j).wait_recv()
        self.twin_a(j).wait_recv()
        even = self.at.c == 0
        from_a, from_b = self.ra[j].astype(F32), self.rb[j].astype(F32)
        none = jnp.zeros_like(from_a)
        self.t2[j] = (self.grads[0, j].astype(F32) + jnp.where(even, none, from_b)).astype(BF)
        pl.when(self.at.z > 1)(self.far(j).start)
        self.t1[j] = (self.grads[2, j].astype(F32) + jnp.where(even, from_b, from_a)).astype(BF)
        pl.when(self.at.has_earlier)(self.near(j).start)
        self.out[j] = self.grads[4, j].astype(F32) + jnp.where(even, from_a, none)

    def two(self, j):
        at = self.at

        @pl.when(at.has_later)
        def _():
            self.near(j).wait_recv()
            self.out[j] = self.out[j] + self.r1[j].astype(F32)

        @pl.when(at.z < 2)
        def _():
            self.far(j).wait_recv()
            self.out[j] = self.out[j] + self.r2[j].astype(F32)

    def sent(self, j):
        at = self.at
        self.twin_a(j).wait_send()
        self.twin_b(j).wait_send()
        pl.when(at.z > 1)(self.far(j).wait_send)
        pl.when(at.has_earlier)(self.near(j).wait_send)


class Reduce:
    COUNT = 14

    def __init__(self, at, chunks, out, own, give, r0, r1a, r1b, r2a, r2b, r3, send, recv, free):
        self.at, self.chunks, self.out, self.own, self.give = at, chunks, out, own, give
        self.r0, self.r1a, self.r1b, self.r2a, self.r2b, self.r3 = r0, r1a, r1b, r2a, r2b, r3
        self.send, self.recv, self.free = send, recv, free
        self.rows = out.shape[0]
        self.quarter, self.half = self.rows // 4, self.rows // 8
        self.slots = give.shape[0]

    @staticmethod
    def scratch(rows, chunks, slots):
        half = rows // 8
        columns = sum(width for _, width in chunks)
        widest = max(width for _, width in chunks)
        return [
            VMEM((4, rows, columns), BF),
            VMEM((slots, 4, rows, widest), BF),
            VMEM((slots, 4, rows, widest), BF),
            VMEM((2, 4, half, columns), BF),
            VMEM((2, 4, half, columns), BF),
            VMEM((4, half, columns), BF),
            VMEM((4, half, columns), BF),
            VMEM((3, 2 * half, columns), BF),
            DMA((len(chunks), Reduce.COUNT)),
            DMA((len(chunks), Reduce.COUNT)),
            pltpu.SemaphoreType.REGULAR,
        ]

    def columns(self, n):
        return pl.ds(*self.chunks[n])

    def copy(self, n, index, src, dst, device):
        return remote(src, dst, self.send.at[n, index], self.recv.at[n, index], device)

    def arrive(self, n, index, ref):
        self.copy(n, index, ref, ref, self.at.core_side).wait_recv()

    def spot(self, owner, part):
        start = owner * self.quarter + part * self.half
        return pl.ds(pl.multiple_of(start, self.half), self.half)

    def piece(self, n, owner):
        start = pl.multiple_of(owner * self.quarter, self.quarter)
        return self.out.at[pl.ds(start, self.quarter), self.columns(n)]

    def core_copy(self, n):
        slot, width = n % self.slots, self.chunks[n][1]
        return self.copy(
            n,
            0,
            self.give.at[slot, :, :, pl.ds(0, width)],
            self.r0.at[slot, :, :, pl.ds(0, width)],
            self.at.core_side,
        )

    def one_copies(self, n):
        at, copies, cols = self.at, [], self.columns(n)
        for i in range(2):
            a = self.own.at[:, self.spot(i * 2 + 1 - at.x, 0), cols]
            b = self.own.at[:, self.spot((1 - at.y) * 2 + i, 1), cols]
            copies.append(self.copy(n, 1 + i, a, self.r1a.at[i, :, :, cols], at.x_side))
            copies.append(self.copy(n, 3 + i, b, self.r1b.at[i, :, :, cols], at.y_side))
        return copies

    def two_copies(self, n):
        at, cols = self.at, self.columns(n)
        a = self.own.at[:, self.spot(at.ry, 0), cols]
        b = self.own.at[:, self.spot(at.rx, 1), cols]
        return [
            self.copy(n, 5, a, self.r2a.at[:, :, cols], at.y_side),
            self.copy(n, 6, b, self.r2b.at[:, :, cols], at.x_side),
        ]

    def z_copy(self, n, k):
        at, cols = self.at, self.columns(n)
        mine = pl.ds(pl.multiple_of(at.r * self.quarter, self.quarter), self.quarter)
        src = self.own.at[at.z_to(k), mine, cols]
        return self.copy(n, 6 + k, src, self.r3.at[k - 1, :, cols], at.z_side(k))

    def back_copy(self, n, i):
        at, cols = self.at, self.columns(n)
        if i < 2:
            ref = self.piece(n, at.r)
            return self.copy(n, 10 + i, ref, ref, at.x_side if i == 0 else at.y_side)
        owner, device = (at.rx, at.y_side) if i == 2 else (at.ry, at.x_side)
        ref = self.out.at[self.spot(owner, i - 2), cols]
        return self.copy(n, 10 + i, ref, ref, device)

    def claim(self, n):
        if n >= self.slots:
            self.core_copy(n - self.slots).wait_send()

    def start(self, n):
        if n >= self.slots:
            pl.semaphore_wait(self.free, 1)
        self.core_copy(n).start()

    def zero(self, n):
        slot, (first, width) = n % self.slots, self.chunks[n]
        self.arrive(n, 0, self.r0.at[slot, :, :, pl.ds(0, width)])
        per_plane = self.rows // (2 * self.half)

        def add_rows(i, _):
            z, where = i // per_plane, pl.ds(
                pl.multiple_of(lax.rem(i, per_plane) * 2 * self.half, 2 * self.half), 2 * self.half
            )
            old = self.own[z, where, first : first + width].astype(F32)
            new = self.r0[slot, z, where, :width].astype(F32)
            self.own[z, where, first : first + width] = (old + new).astype(BF)
            return 0

        lax.fori_loop(0, 4 * per_plane, add_rows, 0)
        if n + self.slots < len(self.chunks):
            pl.semaphore_signal(
                self.free, inc=1, device_id=self.at.core_side, device_id_type=MESH
            )

    def push(self, n):
        for copy in self.one_copies(n):
            copy.start()

    def add(self, n, where, ref):
        cols = self.columns(n)
        for z in range(4):
            old = self.own[z, where, cols].astype(F32)
            self.own[z, where, cols] = (old + ref[z, :, cols].astype(F32)).astype(BF)

    def one(self, n):
        at, cols = self.at, self.columns(n)
        for i in range(2):
            self.arrive(n, 1 + i, self.r1a.at[i, :, :, cols])
            self.arrive(n, 3 + i, self.r1b.at[i, :, :, cols])
            self.add(n, self.spot(i * 2 + at.x, 0), self.r1a.at[i])
            self.add(n, self.spot(at.y * 2 + i, 1), self.r1b.at[i])
        for copy in self.two_copies(n):
            copy.start()

    def two(self, n):
        at, cols = self.at, self.columns(n)
        self.arrive(n, 5, self.r2a.at[:, :, cols])
        self.arrive(n, 6, self.r2b.at[:, :, cols])
        self.add(n, self.spot(at.r, 0), self.r2a)
        self.add(n, self.spot(at.r, 1), self.r2b)
        for k in (1, 2, 3):
            self.z_copy(n, k).start()

    def three(self, n):
        at, cols = self.at, self.columns(n)
        for k in (1, 2, 3):
            self.arrive(n, 6 + k, self.r3.at[k - 1, :, cols])
        for i in range(2):
            where = pl.ds(i * self.half, self.half)
            total = self.own[at.z, self.spot(at.r, i), cols].astype(F32)
            for k in range(3):
                total += self.r3[k, where, cols].astype(F32)
            self.out[self.spot(at.r, i), cols] = total.astype(BF)
        self.back_copy(n, 0).start()
        self.back_copy(n, 1).start()

    def four(self, n):
        at = self.at
        self.arrive(n, 10, self.piece(n, at.rx))
        self.back_copy(n, 2).start()
        self.arrive(n, 11, self.piece(n, at.ry))
        self.back_copy(n, 3).start()

    def five(self, n):
        at, cols = self.at, self.columns(n)
        self.arrive(n, 12, self.out.at[self.spot(at.rd, 0), cols])
        self.arrive(n, 13, self.out.at[self.spot(at.rd, 1), cols])

    def sent(self):
        for n in range(len(self.chunks)):
            if n + self.slots >= len(self.chunks):
                self.core_copy(n).wait_send()
            copies = self.one_copies(n) + self.two_copies(n)
            copies += [self.z_copy(n, k) for k in (1, 2, 3)]
            for copy in copies + [self.back_copy(n, i) for i in range(4)]:
                copy.wait_send()


def at_steps(i, events):
    for n, event in events:
        if n >= 0:
            pl.when(i == n)(event)


def flip_blocks(value, dst):
    blocks, rows, _ = dst.shape
    for s in range(blocks):
        dst[s] = value[:, s * rows : (s + 1) * rows].T


def sequence_features(lengths_ref, first_row, feat_ref, qfeat_ref):
    keys, lanes = feat_ref.shape
    tokens = qfeat_ref.shape[1]
    count = lengths_ref.shape[1]
    starts, ends = [], []
    for i in range(count):
        starts.append(ends[-1] if ends else 0)
        ends.append(starts[-1] + lengths_ref[0, i])
    for low in range(0, keys, tokens):
        place = lax.broadcasted_iota(jnp.int32, (tokens, lanes), 0)
        key = first_row - (keys - tokens) + low + place
        column = lax.broadcasted_iota(jnp.int32, (tokens, lanes), 1)
        value = jnp.where(column >= ONES, 1.0, 0.0)
        value = jnp.where((column == count) & (key < 0), 1.0, value)
        for i in range(count):
            inside = (column == i) & (key >= starts[i]) & (key < ends[i])
            value = jnp.where(inside, 1.0, value)
        feat_ref[low : low + tokens, :] = value.astype(BF)
    row = lax.broadcasted_iota(jnp.int32, (lanes, tokens), 0)
    query = first_row + lax.broadcasted_iota(jnp.int32, (lanes, tokens), 1)
    value = jnp.where(row == count, NEG, 0.0)
    start = jnp.zeros((1, tokens), jnp.int32)
    for i in range(count):
        inside = (query >= starts[i]) & (query < ends[i])
        value = jnp.where((row == i) & jnp.logical_not(inside), NEG, value)
        start = jnp.where(inside[:1], starts[i], start)
    qfeat_ref[...] = value.astype(BF)
    return query[:1] - start


def front_kernel(
    lengths_ref,
    inverse_ref,
    xt_ref,
    cott_ref,
    attend_gain,
    attend_weight,
    expand_gain,
    expand_weight,
    shrinkt,
    output_weight,
    rest_ref,
    attend_hbm,
    win_hbm,
    feat_hbm,
    qt_hbm,
    flipped_hbm,
    x_hbm,
    cot_hbm,
    cott_hbm,
    middle_hbm,
    hidden_hbm,
    hiddent_hbm,
    mixed_ref,
    lse_ref,
    qfeat_ref,
    cos_ref,
    sin_ref,
    kvf,
    vt,
    qa,
    sb,
    attend_own,
    rest_own,
    attend_ref,
    win_ref,
    feat_ref,
    qt_ref,
    flipped,
    inputs,
    cot,
    cott,
    middle,
    hidden,
    hiddent,
    kvt,
    out_weight,
    local_sems,
    store_sems,
    gather_send,
    gather_recv,
    spread_send,
    spread_recv,
):
    at = Place()
    shard_count, rows, columns = attend_ref.shape
    width = shard_count * rows
    tokens = xt_ref.shape[1]
    kv_heads = win_ref.shape[1]
    own_rows = D // shard_count
    cut = 2 * FF
    greet(at, False)

    def gather(n, own, full, cols):
        return Gather(
            at, own, full, cols, local_sems.at[n], gather_send.at[n], gather_recv.at[n]
        )

    first = gather(0, attend_own, attend_ref, (0, columns))
    second = gather(1, rest_own, rest_ref, (3 * FF, QW))
    third = gather(2, rest_own, rest_ref, (0, cut))
    fourth = gather(3, rest_own, rest_ref, (cut, FF))
    spread = Spread(at, win_ref, spread_send, spread_recv)
    stores = []

    def store(src, dst):
        copy = pltpu.make_async_copy(src, dst, store_sems.at[len(stores)])
        copy.start()
        stores.append(copy)

    def place(ref, low, weight, gain):
        count = weight.shape[1]
        block = own_rows // 16 * 16
        ref[:block, low : low + count] = weight[:block]
        tail = jnp.concatenate(
            [weight[block:].astype(F32), jnp.zeros((rows - own_rows, count), F32)], axis=0
        )
        if gain is not None:
            row = jnp.concatenate(
                [gain[...].astype(F32), jnp.zeros((1, count - own_rows), F32)], axis=1
            )
            where = lax.broadcasted_iota(jnp.int32, tail.shape, 0) == own_rows - block
            tail = jnp.where(where, row, tail)
        ref[block:, low : low + count] = tail.astype(BF)

    place(attend_own, 0, attend_weight, attend_gain)
    first.start_z()
    first.start_core()
    place(rest_own, 3 * FF, output_weight[...].T, expand_gain)
    second.start_core()
    place(rest_own, 0, expand_weight, None)
    third.start_core()
    place(rest_own, cut, shrinkt, None)
    fourth.start_core()
    spread.clear()
    position = sequence_features(lengths_ref, at.s * tokens, feat_ref, qfeat_ref)
    store(feat_ref, feat_hbm)
    attend_forward_setup(feat_ref, qfeat_ref, kvf, vt, qa)
    phases = inverse_ref[...] * position.astype(F32)
    cos_ref[...] = jnp.cos(phases)
    sin_ref[...] = jnp.sin(phases)
    first.z(0)
    for s in range(shard_count):
        block = slice(s * rows, (s + 1) * rows)
        source = slice(s * own_rows, (s + 1) * own_rows)
        blank = jnp.zeros((rows - own_rows, tokens), F32)
        value = jnp.concatenate([xt_ref[source, :].astype(F32), blank], axis=0)
        inputs[:, block] = value.T.astype(BF)
    first.z(1)
    for s in range(shard_count):
        block = slice(s * rows, (s + 1) * rows)
        source = slice(s * own_rows, (s + 1) * own_rows)
        value = jnp.concatenate([cott_ref[source, :].astype(F32), blank], axis=0)
        cott[s] = value.astype(BF)
        cot[:, block] = value.T.astype(BF)
    store(inputs, x_hbm)
    store(cot, cot_hbm)
    store(cott, cott_hbm)
    first.z(2)
    second.start_z()
    for i in range(3):
        first.cross(i)
    second.z(0)
    third.start_z()
    for i in range(3):
        first.last(i)
    first.landed()
    store(attend_ref, attend_hbm)

    value = inputs[...].astype(F32)
    scale = scale_of(value)
    for s in range(shard_count):
        lane = slice(s * rows, (s + 1) * rows)
        gain = attend_ref[s, own_rows : own_rows + 1, :rows].astype(F32)
        hidden[:, lane] = (inputs[:, lane].astype(F32) * scale * gain).astype(BF)

    def project(start):
        stop = min(start + 256, columns)
        weight = attend_ref[:, :, start:stop].reshape(width, stop - start)
        turned = dot(hidden[...], weight).T
        for low in range(0, stop - start, HEAD_DIM):
            column = start + low
            head = turned[low : low + HEAD_DIM, :]
            if column < QW + KW:
                half = HEAD_DIM // 2
                front, back = head[:half], head[half:]
                head = jnp.concatenate(
                    [
                        front * cos_ref[...] - back * sin_ref[...],
                        back * cos_ref[...] + front * sin_ref[...],
                    ],
                    axis=0,
                )
            if column < QW:
                qt_ref[column : column + HEAD_DIM, :] = head.astype(BF)
            elif column < QW + KW:
                kvt[(column - QW) // HEAD_DIM, :HALF, :] = head.astype(BF)
            else:
                kvt[(column - QW - KW) // HEAD_DIM, HALF:, :] = head.astype(BF)

    split = QW // 128 * 128
    for start in range(split, columns, 256):
        project(start)
    for j in range(kv_heads):
        win_ref[4, j] = kvt[j].T
        spread.start(j)
    second.z(1)
    second.z(2)
    for start in range(0, split, 256):
        project(start)
    store(qt_ref, qt_hbm)
    flip_blocks(hidden, flipped)
    store(flipped, flipped_hbm)
    spread.one(0)
    third.z(0)
    spread.one(1)
    spread.two(0)
    events = [
        (0, lambda: second.cross(0)),
        (1, lambda: second.cross(1)),
        (2, lambda: third.z(1)),
        (2, lambda: second.cross(2)),
        (3, lambda: second.last(0)),
        (4, lambda: second.last(1)),
        (4, lambda: third.z(2)),
        (4, fourth.start_z),
        (5, lambda: second.last(2)),
        (6, lambda: third.cross(0)),
        (7, lambda: fourth.z(0)),
        (8, lambda: third.cross(1)),
        (9, lambda: fourth.z(1)),
        (10, lambda: third.cross(2)),
        (11, lambda: third.last(0)),
        (12, lambda: fourth.z(2)),
        (13, lambda: third.last(1)),
        (14, lambda: third.last(2)),
    ]

    def key_head(j, _):
        pl.when(j + 2 < kv_heads)(lambda: spread.one(j + 2))
        pl.when(j + 1 < kv_heads)(lambda: spread.two(j + 1))
        spread.landed(j)
        attend_forward_keys(j, win_ref, kvf, vt)

        def head(g, _):
            h = j * GROUP + g
            attend_forward_head(h, qt_ref, mixed_ref, lse_ref, kvf, vt, qa, sb)
            at_steps(h, events)
            return 0

        lax.fori_loop(0, GROUP, head, 0)
        spread.sent(j)
        return 0

    lax.fori_loop(0, kv_heads, key_head, 0)
    store(win_ref, win_hbm)
    second.landed()
    load = pltpu.make_async_copy(
        rest_ref.at[:, :, pl.ds(3 * FF, QW)], out_weight, local_sems.at[4]
    )
    load.start()
    for i in range(3):
        fourth.cross(i)
    load.wait()
    real = real_lanes(width, rows, own_rows)
    gain = jnp.concatenate(
        [out_weight[s, own_rows : own_rows + 1, :rows].astype(F32) for s in range(shard_count)],
        axis=1,
    )
    gain = jnp.where(real, gain, 0.0)
    out_full = out_weight.reshape(width, QW)
    for low in range(0, tokens, PART):
        where = slice(low, low + PART)
        value = jnp.where(real, dot(mixed_ref[:, where].T, out_full[...], 1, 1), 0.0)
        value = inputs[where, :].astype(F32) + value
        middle[where, :] = value
        hidden[where, :] = (value * scale_of(value) * gain).astype(BF)
    store(middle, middle_hbm)
    store(hidden, hidden_hbm)
    flip_blocks(hidden, hiddent)
    store(hiddent, hiddent_hbm)
    for i in range(3):
        fourth.last(i)
    third.landed()
    fourth.landed()
    for part in (first, second, third, fourth):
        part.sent()
    for copy in stores:
        copy.wait()


def front(lengths, xt, cott, weights, shard_count, number):
    _, tokens = xt.shape
    attend_weight, expand_weight, output_weight = weights[1], weights[3], weights[5]
    own_rows, columns = attend_weight.shape
    rows = -(-(own_rows + 2) // 16) * 16
    width = shard_count * rows
    lanes = 2 * HEAD_DIM
    blocks = (MAXLEN - 2) // tokens + 2
    keys = blocks * tokens
    half = HEAD_DIM // 2
    inverse = rope_base ** (-(2.0 * np.arange(half, dtype=np.float32) / HEAD_DIM))
    rest_columns = 3 * FF + QW

    def shape(*sizes, dtype=BF):
        return jax.ShapeDtypeStruct(sizes, dtype)

    attend, rest = shape(shard_count, rows, columns), shape(shard_count, rows, rest_columns)
    window = shape(blocks, KV_HEADS, tokens, lanes)
    feat, heads = shape(keys, lanes), shape(QW, tokens)
    natural, turned = shape(tokens, width), shape(shard_count, rows, tokens)
    middle = shape(tokens, width, dtype=F32)
    in_hbm = (
        rest, attend, window, feat, heads, turned, natural, natural, turned, middle, natural, turned
    )
    table = shape(half, tokens, dtype=F32)
    in_vmem = (heads, shape(HEADS, 1, tokens, dtype=F32), shape(lanes, tokens), table, table)

    def scratch(struct):
        return VMEM(struct.shape, struct.dtype)

    return pl.pallas_call(
        front_kernel,
        out_shape=in_hbm + in_vmem,
        in_specs=[pl.BlockSpec(memory_space=pltpu.SMEM)] + [pl.BlockSpec(memory_space=VMEM)] * 9,
        out_specs=(pl.BlockSpec(memory_space=ANY),) * len(in_hbm)
        + (pl.BlockSpec(memory_space=VMEM),) * len(in_vmem),
        scratch_shapes=attend_forward_scratch(keys, lanes, tokens)
        + [VMEM((rows, columns), BF), VMEM((rows, rest_columns), BF)]
        + [
            scratch(struct)
            for struct in (
                attend, window, feat, heads, turned, natural, natural, turned, middle, natural, turned
            )
        ]
        + [
            VMEM((KV_HEADS, lanes, tokens), BF),
            VMEM((shard_count, rows, QW), BF),
            DMA((5,)),
            DMA((len(in_hbm),)),
            DMA((4, Gather.COUNT)),
            DMA((4, Gather.COUNT)),
            DMA((5, KV_HEADS)),
            DMA((5, KV_HEADS)),
        ],
        compiler_params=pltpu.CompilerParams(
            collective_id=number, has_side_effects=True, vmem_limit_bytes=BIG_VMEM
        ),
        name="front",
    )(lengths, jnp.asarray(inverse, F32)[:, None], xt, cott, *weights)


SUB = 256
CHUNK = 2 * SUB


def up_to_lanes(columns):
    return -(-columns // 128) * 128


def sum_chunks():
    widths = [3 * CHUNK] * (FF // CHUNK) + [up_to_lanes(QW)] * 2 + [2 * KW]
    return [(sum(widths[:n]), width) for n, width in enumerate(widths)]


OUT_CHUNK = FF // CHUNK
QUERY_CHUNK, PAIR_CHUNK = OUT_CHUNK + 1, OUT_CHUNK + 2


def unrotate(head, cosine, sine):
    half = HEAD_DIM // 2
    front, back = head[:half], head[half:]
    return jnp.concatenate(
        [front * cosine + back * sine, back * cosine - front * sine], axis=0
    ).astype(BF)


def real_lanes(width, rows, own_rows):
    return lax.rem(lax.broadcasted_iota(jnp.int32, (1, width), 1), rows) < own_rows


def scale_of(value):
    return lax.rsqrt(jnp.sum(value * value, axis=-1, keepdims=True) * (1.0 / D) + eps_norm)


def put_turned(value, dst, rows, own_rows):
    turned = value.T
    for s in range(turned.shape[0] // rows):
        dst[s * own_rows : (s + 1) * own_rows, :] = turned[s * rows : s * rows + own_rows]


def put_gradient(total, n, column, ref, z, product, row=None):
    rows, columns = product.shape
    first = product[:, :rows]
    if row is not None:
        own_rows, gain_row = row
        place = lax.broadcasted_iota(jnp.int32, (rows, rows), 0)
        first = jnp.where(place == own_rows, gain_row, first)
    ref[z, :, column : column + rows] = first.astype(BF)
    ref[z, :, column + rows : column + columns] = product[:, rows:].astype(BF)
    width = total.chunks[n][1]
    if columns < width:
        ref[z, :, column + columns : column + width] = jnp.zeros((rows, width - columns), BF)


def feed_forward(
    at,
    total,
    mixed_ref,
    gradt_ref,
    middle_hbm,
    hidden_hbm,
    hiddent_hbm,
    cot_hbm,
    cott_hbm,
    rest_ref,
    out_hbm,
    middle_grad_hbm,
    events,
    cot,
    hidden,
    middle,
    acc_out,
    acc_grad,
    hidden_own,
    hidden_give,
    cot_own,
    cot_give,
    flipped,
    out_weight,
    gain_term,
    weights,
    results,
    sems,
    load_sems,
):
    shard_count, rows, _ = rest_ref.shape
    width = shard_count * rows
    tokens = middle.shape[0]
    own_rows = D // shard_count
    planes = shard_count // 2

    def weight_copies(n, slot):
        return [
            pltpu.make_async_copy(
                rest_ref.at[:, :, pl.ds(pl.multiple_of(i * FF + n * SUB, 128), SUB)],
                weights.at[slot, i],
                sems.at[slot, i],
            )
            for i in range(3)
        ]

    pairs = [(hidden_hbm, hidden), (cot_hbm, cot)]
    for z in range(planes):
        mine, other = 2 * z + at.c, 2 * z + 1 - at.c
        pairs += [(hiddent_hbm.at[mine], hidden_own.at[z]), (cott_hbm.at[mine], cot_own.at[z])]
        pairs += [(hiddent_hbm.at[other], hidden_give.at[z])]
        pairs += [(cott_hbm.at[other], cot_give.at[z])]
    pairs += [(middle_hbm, middle), (rest_ref.at[:, :, pl.ds(3 * FF, QW)], out_weight)]
    loads = [
        pltpu.make_async_copy(src, dst, load_sems.at[i]) for i, (src, dst) in enumerate(pairs)
    ]
    for copy in weight_copies(0, 0) + loads:
        copy.start()
    acc_out[...] = jnp.zeros_like(acc_out)
    acc_grad[...] = jnp.zeros_like(acc_grad)
    for load in loads:
        load.wait()
    out_full = out_weight.reshape(width, QW)

    def put(ref, column, value):
        where = pl.ds(pl.multiple_of(column, 128), value.shape[1])
        ref[:, :, where] = value.reshape(planes, rows, value.shape[1]).astype(BF)

    def step(n, _):
        slot = lax.rem(n, 2)
        for copy in weight_copies(n, slot):
            copy.wait()

        @pl.when(n + 1 < FF // SUB)
        def _():
            for copy in weight_copies(n + 1, 1 - slot):
                copy.start()

        gate_weight = weights[slot, 0].reshape(width, SUB)
        upper_weight = weights[slot, 1].reshape(width, SUB)
        shrink_weight = weights[slot, 2].reshape(width, SUB)
        gate = dot(hidden[...], gate_weight)
        upper = dot(hidden[...], upper_weight)
        inner_grad = dot(cot[...], shrink_weight)
        sigmoid = jax.nn.sigmoid(gate)
        active = gate * sigmoid
        inner = (active * upper).astype(BF)
        gate_grad = (inner_grad * upper * sigmoid * (1.0 + gate * (1.0 - sigmoid))).astype(BF)
        upper_grad = (inner_grad * active).astype(BF)
        for low in range(0, width, width // 2):
            cols = slice(low, low + width // 2)
            acc_out[:, cols] += dot(inner, shrink_weight[cols], 1, 1)
            acc_grad[:, cols] += dot(gate_grad, gate_weight[cols], 1, 1) + dot(
                upper_grad, upper_weight[cols], 1, 1
            )
        chunk, part = n // 2, lax.rem(n, 2) * SUB
        first = chunk * 3 * CHUNK + part
        put(total.own, first, dot(hidden_own[...].reshape(width // 2, tokens), gate_grad))
        put(total.own, first + CHUNK, dot(hidden_own[...].reshape(width // 2, tokens), upper_grad))
        put(total.own, first + 2 * CHUNK, dot(cot_own[...].reshape(width // 2, tokens), inner))
        for n_start in range(2 * total.slots, FF // SUB, 2):
            pl.when(n == n_start)(functools.partial(total.claim, n_start // 2))
        give = total.give.at[lax.rem(chunk, total.slots)]
        put(give, part, dot(hidden_give[...].reshape(width // 2, tokens), gate_grad))
        put(give, part + CHUNK, dot(hidden_give[...].reshape(width // 2, tokens), upper_grad))
        put(give, part + 2 * CHUNK, dot(cot_give[...].reshape(width // 2, tokens), inner))
        for n_end in range(1, FF // SUB, 2):
            pl.when(n == n_end)(functools.partial(total.start, n_end // 2))
        at_steps(n, events)
        return 0

    lax.fori_loop(0, FF // SUB, step, 0)

    real = real_lanes(width, rows, own_rows)
    gain = jnp.concatenate(
        [out_weight[s, own_rows : own_rows + 1, :rows].astype(F32) for s in range(shard_count)],
        axis=1,
    )
    gain = jnp.where(real, gain, 0.0)
    term = jnp.zeros((1, width), F32)
    stores = []
    for n, low in enumerate(range(0, tokens, PART)):
        where = slice(low, low + PART)
        value = middle[where, :]
        if n >= 2:
            stores[n - 2].wait()
        put_turned(value + acc_out[where, :], results.at[n % 2], rows, own_rows)
        stores.append(
            pltpu.make_async_copy(
                results.at[n % 2], out_hbm.at[:, pl.ds(low, PART)], sems.at[2, n % 2]
            )
        )
        stores[n].start()
        scale = scale_of(value)
        normed = value * scale
        hidden_grad = jnp.where(real, acc_grad[where, :], 0.0)
        term = term + jnp.sum(hidden_grad * normed, axis=0, keepdims=True)
        upstream = hidden_grad * gain
        mean = jnp.sum(upstream * normed, axis=-1, keepdims=True) * (1.0 / D)
        value = cot[where, :].astype(F32) + scale * (upstream - normed * mean)
        acc_grad[where, :] = value
        branch = value.astype(BF)
        hidden[where, :] = branch
        gradt_ref[:, where] = dot(branch, out_full[...]).T.astype(BF)
    store = pltpu.make_async_copy(acc_grad, middle_grad_hbm, sems.at[2, 2])
    store.start()
    stores[-2:] += [store]
    for s in range(shard_count):
        gain_term[s] = jnp.broadcast_to(term[:, s * rows : (s + 1) * rows], (8, rows))
    flip_blocks(hidden, flipped)
    for z in range(planes):
        hidden_own[z] = flipped[2 * z + at.c]
        hidden_give[z] = flipped[2 * z + 1 - at.c]
    total.claim(OUT_CHUNK)
    for lhs, core, ref, column in (
        (hidden_give, 1 - at.c, total.give.at[OUT_CHUNK % total.slots], 0),
        (hidden_own, at.c, total.own, total.chunks[OUT_CHUNK][0]),
    ):
        product = dot(lhs[...].reshape(width // 2, tokens), mixed_ref[...], 1, 1)
        for z in range(planes):
            row = (own_rows, gain_term[2 * z + core][:1])
            plane = product[z * rows : (z + 1) * rows]
            put_gradient(total, OUT_CHUNK, column, ref, z, plane, row)
        if lhs is hidden_give:
            total.start(OUT_CHUNK)
    for store in stores[-3:]:
        store.wait()


def attention_backward(
    at,
    total,
    collect,
    events,
    cos_ref,
    sin_ref,
    qfeat_ref,
    lse_ref,
    mixed_ref,
    gradt_ref,
    jointt,
    win_hbm,
    feat_hbm,
    qt_hbm,
    kvf,
    kt,
    qa,
    da,
    acc,
    rhs,
    win_ref,
    feat_ref,
    qt_ref,
    sems,
):
    loads = [
        pltpu.make_async_copy(src, dst, sems.at[i])
        for i, (src, dst) in enumerate(
            ((feat_hbm, feat_ref), (win_hbm, win_ref), (qt_hbm, qt_ref))
        )
    ]
    for load in loads:
        load.start()
    for load in loads:
        load.wait()
    attend_backward_setup(feat_ref, kvf, qa, da, rhs)
    for n, event in events:
        if n < 0:
            event()

    def put_query(row, low, value):
        cols = slice(low, low + QC)
        jointt[pl.ds(row, HEAD_DIM), cols] = unrotate(value, cos_ref[:, cols], sin_ref[:, cols])

    def key_head(j, _):
        attend_backward_keys(j, win_ref, kvf, kt, acc)

        def head(g, _):
            h = j * GROUP + g
            attend_backward_head(
                h,
                put_query,
                qt_ref,
                qfeat_ref,
                gradt_ref,
                mixed_ref,
                lse_ref,
                kvf,
                kt,
                qa,
                da,
                acc,
                rhs,
            )
            at_steps(h, events)
            return 0

        lax.fori_loop(0, GROUP, head, 0)
        attend_backward_done(j, acc, collect.grads)
        collect.start(j)
        pl.when(j > 0)(lambda: collect.one(j - 1))
        pl.when(j > 1)(lambda: collect.two(j - 2))
        return 0

    lax.fori_loop(0, KV_HEADS, key_head, 0)


def projection_backward(
    at,
    total,
    collect,
    events,
    cos_ref,
    sin_ref,
    jointt,
    flipped,
    x_hbm,
    middle_grad_hbm,
    attend_hbm,
    grad_hbm,
    attend_ref,
    inputs,
    middle_grad,
    hidden_grad,
    gain_term,
    results,
    sems,
):
    shard_count, rows, columns = attend_ref.shape
    width = shard_count * rows
    tokens = inputs.shape[0]
    own_rows = D // shard_count
    planes = shard_count // 2
    loads = [
        pltpu.make_async_copy(src, dst, sems.at[i])
        for i, (src, dst) in enumerate(
            ((attend_hbm, attend_ref), (x_hbm, inputs), (middle_grad_hbm, middle_grad))
        )
    ]
    for load in loads:
        load.start()
    last = KV_HEADS - 1
    sides = (
        (1 - at.c, lambda n: (total.give.at[n % total.slots], 0)),
        (at.c, lambda n: (total.own, total.chunks[n][0])),
    )

    def gradients(n, rows_of_joint, gain):
        total.claim(n)
        for side, (core, target) in enumerate(sides):
            ref, column = target(n)
            for z in range(planes):
                plane = 2 * z + core
                product = dot(flipped[plane], jointt[rows_of_joint, :], 1, 1)
                row = (own_rows, gain_term[plane][:1]) if gain else None
                put_gradient(total, n, column, ref, z, product, row)
            if side == 0:
                total.start(n)

    gradients(QUERY_CHUNK, slice(0, QW), False)
    collect.one(last)
    total.zero(QUERY_CHUNK)
    total.push(QUERY_CHUNK)
    events[0]()
    for load in loads:
        load.wait()
    weight = attend_ref.reshape(width, columns)
    for low in range(0, tokens, PART):
        where = slice(low, low + PART)
        hidden_grad[where, :] = dot(jointt[:QW, where].T, weight[:, :QW], 1, 1)
    events[1]()
    collect.two(last - 1)
    collect.two(last)
    for j in range(KV_HEADS):
        pair = collect.out[j].T
        low = QW + j * HEAD_DIM
        jointt[low : low + HEAD_DIM, :] = unrotate(pair[:HALF], cos_ref[...], sin_ref[...])
        jointt[low + KW : low + KW + HEAD_DIM, :] = pair[HALF:].astype(BF)
    real = real_lanes(width, rows, own_rows)
    term = jnp.zeros((1, width), F32)
    for low in range(0, tokens, PART):
        where = slice(low, low + PART)
        value = inputs[where, :].astype(F32)
        normed = value * scale_of(value)
        value = hidden_grad[where, :] + dot(jointt[QW:, where].T, weight[:, QW:], 1, 1)
        value = jnp.where(real, value, 0.0)
        hidden_grad[where, :] = value
        term = term + jnp.sum(value * normed, axis=0, keepdims=True)
    for s in range(shard_count):
        gain_term[s] = jnp.broadcast_to(term[:, s * rows : (s + 1) * rows], (8, rows))
    gradients(PAIR_CHUNK, slice(QW, columns), True)
    total.one(QUERY_CHUNK)
    total.zero(PAIR_CHUNK)
    total.push(PAIR_CHUNK)
    events[2]()
    total.two(QUERY_CHUNK)
    gain = jnp.concatenate(
        [
            attend_ref[s, own_rows : own_rows + 1, :rows].astype(F32)
            for s in range(shard_count)
        ],
        axis=1,
    )
    gain = jnp.where(real, gain, 0.0)
    stores = []
    for n, low in enumerate(range(0, tokens, PART)):
        where = slice(low, low + PART)
        value = inputs[where, :].astype(F32)
        scale = scale_of(value)
        normed = value * scale
        upstream = hidden_grad[where, :] * gain
        mean = jnp.sum(upstream * normed, axis=-1, keepdims=True) * (1.0 / D)
        result = middle_grad[where, :] + scale * (upstream - normed * mean)
        if n >= 2:
            stores[n - 2].wait()
        put_turned(result, results.at[n % 2], rows, own_rows)
        stores.append(
            pltpu.make_async_copy(
                results.at[n % 2], grad_hbm.at[:, pl.ds(low, PART)], sems.at[3 + n % 2]
            )
        )
        stores[n].start()
    total.one(PAIR_CHUNK)
    total.three(QUERY_CHUNK)
    total.two(PAIR_CHUNK)
    total.four(QUERY_CHUNK)
    total.three(PAIR_CHUNK)
    total.five(QUERY_CHUNK)
    total.four(PAIR_CHUNK)
    total.five(PAIR_CHUNK)
    for j in range(KV_HEADS):
        collect.sent(j)
    total.sent()
    for store in stores[-2:]:
        store.wait()


def rear_kernel(
    mixed_ref,
    lse_ref,
    qfeat_ref,
    cos_ref,
    sin_ref,
    rest_ref,
    attend_hbm,
    win_hbm,
    feat_hbm,
    qt_hbm,
    flipped_hbm,
    x_hbm,
    cot_hbm,
    cott_hbm,
    middle_hbm,
    hidden_hbm,
    hiddent_hbm,
    sum_ref,
    out_hbm,
    grad_hbm,
    middle_grad_hbm,
    gradt_ref,
    jointt,
    pairs,
    ra,
    rb,
    r2,
    r1,
    collect_send,
    collect_recv,
    *reduce_scratch,
):
    at = Place()
    tokens = x_hbm.shape[0]
    shard_count, rows, _ = rest_ref.shape
    width = shard_count * rows
    lanes = pairs.shape[2]
    keys = feat_hbm.shape[0]
    greet(at, True)
    total = Reduce(at, sum_chunks(), sum_ref, *reduce_scratch)

    def run(*names):
        def event():
            for name, n in names:
                getattr(total, name)(n)

        return event

    def round_of(t):
        due = [("one", t), ("push", t + 1), ("two", t - 1), ("three", t - 2), ("four", t - 3)]
        return [(name, n) for name, n in due + [("five", t - 4)] if 0 <= n <= OUT_CHUNK]

    forward_events = [
        (2, run(("zero", 0), ("push", 0))),
        (4, run(("zero", 1))),
        (6, run(("zero", 2), *round_of(0))),
        (8, run(("zero", 3))),
    ]
    backward_events = [
        (-1, run(("zero", 4), *round_of(1))),
        (3, run(("zero", 5), *round_of(2))),
        (6, run(*round_of(3))),
        (9, run(*round_of(4))),
        (12, run(*round_of(5))),
    ]
    last_events = [run(*round_of(6)), run(*round_of(7), *round_of(8)), run(*round_of(9))]

    pl.run_scoped(
        functools.partial(
            feed_forward,
            at,
            total,
            mixed_ref,
            gradt_ref,
            middle_hbm,
            hidden_hbm,
            hiddent_hbm,
            cot_hbm,
            cott_hbm,
            rest_ref,
            out_hbm,
            middle_grad_hbm,
            forward_events,
        ),
        VMEM((tokens, width), BF),
        VMEM((tokens, width), BF),
        VMEM((tokens, width), F32),
        VMEM((tokens, width), F32),
        VMEM((tokens, width), F32),
        VMEM((shard_count // 2, rows, tokens), BF),
        VMEM((shard_count // 2, rows, tokens), BF),
        VMEM((shard_count // 2, rows, tokens), BF),
        VMEM((shard_count // 2, rows, tokens), BF),
        VMEM((shard_count, rows, tokens), BF),
        VMEM((shard_count, rows, QW), BF),
        VMEM((shard_count, 8, rows), F32),
        VMEM((2, 3, shard_count, rows, SUB), BF),
        VMEM((2, D, PART), F32),
        DMA((3, 3)),
        DMA((4 + 2 * shard_count,)),
    )

    def attention(grads, t2, t1, flipped, flipped_sem):
        collect = Collect(at, grads, pairs, ra, rb, r2, r1, t2, t1, collect_send, collect_recv)
        load = pltpu.make_async_copy(flipped_hbm, flipped, flipped_sem)
        load.start()
        pl.run_scoped(
            functools.partial(
                attention_backward,
                at,
                total,
                collect,
                backward_events,
                cos_ref,
                sin_ref,
                qfeat_ref,
                lse_ref,
                mixed_ref,
                gradt_ref,
                jointt,
                win_hbm,
                feat_hbm,
                qt_hbm,
            ),
            *attend_backward_scratch(keys, lanes, tokens),
            VMEM(win_hbm.shape, BF),
            VMEM(feat_hbm.shape, BF),
            VMEM(qt_hbm.shape, BF),
            DMA((3,)),
        )
        load.wait()
        pl.run_scoped(
            functools.partial(
                projection_backward,
                at,
                total,
                collect,
                last_events,
                cos_ref,
                sin_ref,
                jointt,
                flipped,
                x_hbm,
                middle_grad_hbm,
                attend_hbm,
                grad_hbm,
            ),
            VMEM(attend_hbm.shape, BF),
            VMEM((tokens, width), BF),
            VMEM((tokens, width), F32),
            VMEM((tokens, width), F32),
            VMEM((shard_count, 8, rows), F32),
            VMEM((2, D, PART), F32),
            DMA((5,)),
        )

    pl.run_scoped(
        attention,
        VMEM(win_hbm.shape, BF),
        VMEM(pairs.shape, BF),
        VMEM(pairs.shape, BF),
        VMEM(flipped_hbm.shape, BF),
        DMA,
    )


def rear(in_hbm, in_vmem, number):
    rest, attend, window, _, qt, _, x = in_hbm[:7]
    _, kv_heads, tokens, lanes = window.shape
    shard_count, rows, _ = rest.shape
    columns = sum(width for _, width in sum_chunks())
    pairs = (kv_heads, tokens, lanes)
    return pl.pallas_call(
        rear_kernel,
        out_shape=(
            jax.ShapeDtypeStruct((rows, columns), BF),
            jax.ShapeDtypeStruct((D, tokens), F32),
            jax.ShapeDtypeStruct((D, tokens), F32),
            jax.ShapeDtypeStruct((tokens, shard_count * rows), F32),
        ),
        in_specs=[pl.BlockSpec(memory_space=VMEM)] * len(in_vmem)
        + [pl.BlockSpec(memory_space=ANY)] * len(in_hbm),
        out_specs=(pl.BlockSpec(memory_space=VMEM),) + (pl.BlockSpec(memory_space=ANY),) * 3,
        scratch_shapes=[VMEM(qt.shape, BF), VMEM((JW, tokens), BF), VMEM(pairs, F32)]
        + [VMEM(pairs, BF)] * 4
        + [DMA((4, kv_heads)), DMA((4, kv_heads))]
        + Reduce.scratch(rows, sum_chunks(), 2),
        compiler_params=pltpu.CompilerParams(
            collective_id=number, has_side_effects=True, vmem_limit_bytes=BIG_VMEM
        ),
        name="rear",
    )(*in_vmem, *in_hbm)


def adam_parts(old_weight, gradient, first, second, decay_factor):
    moment = beta_one * first + (1.0 - beta_one) * gradient
    square = beta_two * second + (1.0 - beta_two) * gradient * gradient
    corrected = moment * (1.0 / (1.0 - beta_one**STEP))
    divisor = jnp.sqrt(square * (1.0 / (1.0 - beta_two**STEP))) + adam_eps
    update = -learn_rate * (corrected / divisor + decay_factor * old_weight)
    return moment, square, update


def adam_kernel(grad_scale, own_rows, *refs):
    sums, attend_planes, rest_planes = refs[:3]
    states, passed_in, results, passed_out = refs[3:11], refs[11:13], refs[13:29], refs[29:31]
    buffers, weights, staged = refs[31:47], refs[47:49], refs[49:51]
    in_sems, out_sems = refs[51], refs[52]
    chunks = sum_chunks()
    shard = lax.axis_index("shard")
    loads = [
        pltpu.make_async_copy(attend_planes.at[shard], weights[0], in_sems.at[8]),
        pltpu.make_async_copy(rest_planes.at[shard], weights[1], in_sems.at[9]),
    ]
    order = (0, 1, 3, 2)
    for n in order:
        for i in range(2):
            loads.append(
                pltpu.make_async_copy(
                    states[2 * n + i], buffers[4 * n + 1 + i], in_sems.at[2 * n + i]
                )
            )
    for i in range(2):
        loads.append(pltpu.make_async_copy(passed_in[i], staged[i], in_sems.at[10 + i]))
    for load in loads:
        load.start()
    loads[0].wait()
    loads[1].wait()
    stores = []

    def update(n, where, total, weight, flip):
        gradient, moment, square, changed = buffers[4 * n : 4 * n + 4]
        total = total.astype(F32)
        weight = weight.astype(F32)
        if flip:
            total, weight = total.T[:, :own_rows], weight.T[:, :own_rows]
        total = total * grad_scale
        new_moment, new_square, step = adam_parts(
            weight, total, moment[where], square[where], decay_rate
        )
        gradient[where] = total
        moment[where] = new_moment
        square[where] = new_square
        changed[where] = weight + step

    everything = slice(None)
    for place, n in enumerate(order):
        loads[2 + 2 * place].wait()
        loads[3 + 2 * place].wait()
        if n == 0:
            for chunk, first, count in ((QUERY_CHUNK, 0, QW), (PAIR_CHUNK, QW, 2 * KW)):
                low, cols = chunks[chunk][0], slice(first, first + count)
                update(
                    0,
                    (everything, cols),
                    sums[:own_rows, low : low + count],
                    weights[0][:own_rows, cols],
                    False,
                )
        elif n == 1:
            low = chunks[OUT_CHUNK][0]
            cols = slice(3 * FF, 3 * FF + QW)
            update(
                1, (everything, everything), sums[:, low : low + QW], weights[1][:, cols], True
            )
        else:
            for c in range(FF // CHUNK):
                for part in (0, 1) if n == 2 else (2,):
                    low = 3 * CHUNK * c + CHUNK * part
                    first = part * FF + CHUNK * c
                    total = sums[:own_rows, low : low + CHUNK]
                    weight = weights[1][:own_rows, first : first + CHUNK]
                    column = first if n == 2 else first - 2 * FF
                    cols = slice(column, column + CHUNK)
                    update(n, (everything, cols), total, weight, False)
        for i in range(4):
            store = pltpu.make_async_copy(
                buffers[4 * n + i], results[4 * n + i], out_sems.at[4 * n + i]
            )
            store.start()
            stores.append(store)
        if place < 2:
            loads[10 + place].wait()
            store = pltpu.make_async_copy(
                staged[place], passed_out[place], out_sems.at[16 + place]
            )
            store.start()
            stores.append(store)
    for store in stores:
        store.wait()


def adam(grad_scale, own_rows, sums, attend_planes, rest_planes, states, passed):
    flat = [array for pair in states for array in pair]
    shapes = [pair[0].shape for pair in states]
    return pl.pallas_call(
        functools.partial(adam_kernel, grad_scale, own_rows),
        out_shape=tuple(jax.ShapeDtypeStruct(shape, F32) for shape in shapes for _ in range(4))
        + tuple(jax.ShapeDtypeStruct(array.shape, array.dtype) for array in passed),
        in_specs=[pl.BlockSpec(memory_space=VMEM)] + [pl.BlockSpec(memory_space=ANY)] * 12,
        out_specs=(pl.BlockSpec(memory_space=ANY),) * 18,
        scratch_shapes=[VMEM(shape, F32) for shape in shapes for _ in range(4)]
        + [VMEM(attend_planes.shape[1:], BF), VMEM(rest_planes.shape[1:], BF)]
        + [VMEM(array.shape, F32) for array in passed]
        + [DMA((12,)), DMA((18,))],
        compiler_params=pltpu.CompilerParams(vmem_limit_bytes=BIG_VMEM),
        name="adam",
    )(sums, attend_planes, rest_planes, *flat, *passed)


def spread_pairs(pairs, reach):
    devices = range(lax.axis_size("shard"))
    blocks = []
    for distance in range(reach, 0, -1):
        route = [(i - distance, i) for i in devices if i - distance in devices]
        blocks.append(lax.ppermute(pairs, "shard", route))
    return jnp.stack(blocks + [pairs])


def collect_pairs(grads, reach):
    devices = range(lax.axis_size("shard"))
    own = grads[reach].astype(F32)
    for distance in range(1, reach + 1):
        route = [(i, i - distance) for i in devices if i - distance in devices]
        own = own + lax.ppermute(grads[reach - distance], "shard", route).astype(F32)
    return own


def angles(positions):
    half_dim = HEAD_DIM // 2
    inverse = rope_base ** (-(2.0 * jnp.arange(half_dim, dtype=F32) / HEAD_DIM))
    phases = positions.astype(F32)[:, None] * inverse[None, :]
    return (jnp.cos(phases)[:, None, :], jnp.sin(phases)[:, None, :])


def rotate(tensor, cosine_table, sine_table):
    half_dim = HEAD_DIM // 2
    front, back = tensor[..., :half_dim], tensor[..., half_dim:]
    return jnp.concatenate(
        [front * cosine_table - back * sine_table, back * cosine_table + front * sine_table],
        axis=-1,
    )


def norm_back(upstream, normed, scale_rows):
    mean = jnp.sum(upstream * normed, axis=-1, keepdims=True) * (1.0 / D)
    return scale_rows * (upstream - normed * mean)


def adam_step(weight_now, gradient, first, second, decay_factor):
    moment, square, update = adam_parts(
        weight_now.astype(F32), gradient, first, second, decay_factor
    )
    return (gradient, moment, square, update)


def shards(
    direct,
    block_input,
    block_cotangent,
    lengths,
    attend_gain,
    attend_weight,
    output_weight,
    expand_gain,
    expand_weight,
    shrink_weight,
    attend_gain_first,
    attend_weight_first,
    output_weight_first,
    expand_gain_first,
    expand_weight_first,
    shrink_weight_first,
    attend_gain_second,
    attend_weight_second,
    output_weight_second,
    expand_gain_second,
    expand_weight_second,
    shrink_weight_second,
):
    tokens = block_input.shape[0]
    shard_count = lax.axis_size("shard")
    token_count = tokens * shard_count * lax.axis_size("rep")
    reach = (MAXLEN - 2) // tokens + 1
    own_rows = attend_weight.shape[0]
    rows = -(-(own_rows + 2) // 16) * 16
    width = shard_count * rows

    def padded(tensor):
        blocks = tensor.reshape(tokens, shard_count, own_rows)
        return jnp.pad(blocks, ((0, 0), (0, 0), (0, rows - own_rows))).reshape(tokens, width)

    def unpadded(tensor):
        return tensor.reshape(tokens, shard_count, rows)[:, :, :own_rows].reshape(tokens, D)

    def with_gain(weight, gain):
        if gain is None:
            return jnp.pad(weight, ((0, rows - own_rows), (0, 0)))
        tail = jnp.pad(gain[None, :], ((0, rows - own_rows - 1), (0, weight.shape[1] - own_rows)))
        return jnp.concatenate([weight, tail], axis=0)

    def gain_of(planes, column):
        return jnp.pad(
            planes[:, own_rows, column : column + own_rows], ((0, 0), (0, rows - own_rows))
        ).reshape(1, width).astype(F32)

    def add_gain(planes, term, column):
        row = term.reshape(shard_count, 1, rows).astype(planes.dtype)
        return lax.dynamic_update_slice(planes, row, (0, own_rows, column))

    def in_chunks(expand, shrink):
        parts = jnp.concatenate([expand, shrink], axis=1).reshape(-1, 3, FF // CHUNK, CHUNK)
        return parts.transpose(0, 2, 1, 3).reshape(-1, 3 * FF)

    if direct:
        weights = (
            attend_gain[None, :],
            attend_weight,
            expand_gain[None, :],
            expand_weight,
            shrink_weight.T,
            output_weight,
        )
        made = front(lengths, block_input.T, block_cotangent.T, weights, shard_count, 0)
        rest_planes, attend_planes = made[:2]
        sums, block_output, input_gradient, _ = rear(made[:12], made[12:], 1)
    else:
        first_row = lax.axis_index("shard") * tokens
        local_index = first_row + jnp.arange(tokens, dtype=jnp.int32)
        key_index = first_row - reach * tokens + jnp.arange((reach + 1) * tokens, dtype=jnp.int32)
        ends = jnp.cumsum(lengths[0], dtype=jnp.int32)
        starts = ends - lengths[0]
        seq_count = lengths.shape[1]
        in_key = (key_index[:, None] >= starts[None, :]) & (key_index[:, None] < ends[None, :])
        in_query = (local_index[None, :] >= starts[:, None]) & (local_index[None, :] < ends[:, None])
        lanes = 2 * HEAD_DIM
        feat = jnp.concatenate(
            [
                in_key.astype(BF),
                (key_index < 0).astype(BF)[:, None],
                jnp.zeros((key_index.shape[0], ONES - seq_count - 1), BF),
                jnp.ones((key_index.shape[0], lanes - ONES), BF),
            ],
            axis=1,
        )
        qfeat = jnp.concatenate(
            [
                jnp.where(in_query, 0.0, NEG).astype(BF),
                jnp.full((1, tokens), NEG, BF),
                jnp.zeros((lanes - seq_count - 1, tokens), BF),
            ],
            axis=0,
        )
        start_index = jnp.sum(in_query * starts[:, None], axis=0, dtype=jnp.int32)
        cosine_table, sine_table = angles(local_index - start_index)
        attend_own = with_gain(attend_weight, attend_gain)
        rest_own = jnp.concatenate(
            [
                with_gain(jnp.concatenate([expand_weight, shrink_weight.T], axis=1), None),
                with_gain(output_weight.T, expand_gain),
            ],
            axis=1,
        )
        attend_planes = lax.all_gather(attend_own, "shard", axis=0)
        rest_planes = lax.all_gather(rest_own, "shard", axis=0)
        gain_one, gain_two = gain_of(attend_planes, 0), gain_of(rest_planes, 3 * FF)
        joint_weight = attend_planes.reshape(width, JW)
        rest = rest_planes.reshape(width, rest_own.shape[1])
        expand_full, shrink_full, out_full = rest[:, : 2 * FF], rest[:, 2 * FF : 3 * FF], rest[:, 3 * FF :]
        real = (jnp.arange(width, dtype=jnp.int32) % rows < own_rows)[None, :]

        inputs = padded(block_input).astype(F32)
        scale_one = lax.rsqrt(jnp.sum(inputs * inputs, axis=-1, keepdims=True) * (1.0 / D) + eps_norm)
        normed_one = inputs * scale_one
        hidden_one = (normed_one * gain_one).astype(BF)
        joint = dot(hidden_one, joint_weight)
        queries = rotate(joint[:, :QW].reshape(tokens, HEADS, HEAD_DIM), cosine_table, sine_table)
        key_rows = rotate(
            joint[:, QW : QW + KW].reshape(tokens, KV_HEADS, HEAD_DIM), cosine_table, sine_table
        )
        values = joint[:, QW + KW :].reshape(tokens, KV_HEADS, HEAD_DIM)
        pairs = jnp.concatenate([key_rows, values], axis=-1).astype(BF).transpose(1, 0, 2)
        qt = queries.astype(BF).reshape(tokens, QW).T
        window = spread_pairs(pairs, reach)
        mixedt, lse = attend_forward(window, feat, qt, qfeat)
        middle = inputs + jnp.where(real, dot(mixedt, out_full, 0, 1), 0.0)
        scale_two = lax.rsqrt(jnp.sum(middle * middle, axis=-1, keepdims=True) * (1.0 / D) + eps_norm)
        normed_two = middle * scale_two
        hidden_two = (normed_two * gain_two).astype(BF)
        gate_up = dot(hidden_two, expand_full)
        gate_value, upper_value = gate_up[:, :FF], gate_up[:, FF:]
        sigmoid_gate = jax.nn.sigmoid(gate_value)
        inner_rows = (gate_value * sigmoid_gate * upper_value).astype(BF)
        block_output = middle + dot(inner_rows, shrink_full, 1, 1)

        cotangent = padded(block_cotangent)
        shrink_term = dot(cotangent, inner_rows, 0, 0)
        inner_grad = dot(cotangent, shrink_full)
        gate_grad = (
            inner_grad * upper_value * sigmoid_gate * (1.0 + gate_value * (1.0 - sigmoid_gate))
        ).astype(BF)
        upper_grad = (inner_grad * gate_value * sigmoid_gate).astype(BF)
        gate_up_grad = jnp.concatenate([gate_grad, upper_grad], axis=1)
        expand_term = dot(hidden_two, gate_up_grad, 0, 0)
        hidden_two_grad = jnp.where(real, dot(gate_up_grad, expand_full, 1, 1), 0.0)
        gain_two_term = jnp.sum(hidden_two_grad * normed_two, axis=0)
        middle_grad = cotangent.astype(F32) + norm_back(
            hidden_two_grad * gain_two, normed_two, scale_two
        )
        branch_grad = middle_grad.astype(BF)
        output_term = dot(branch_grad, mixedt, 0, 1)
        gradt = dot(out_full, branch_grad, 0, 1).astype(BF)
        dqt, dwindow = attend_backward(window, feat, qt, qfeat, gradt, mixedt, lse)
        own_pairs = collect_pairs(dwindow, reach)
        block_output = unpadded(block_output).T
        own_pairs = own_pairs.transpose(1, 0, 2)
        dq = dqt.T.reshape(tokens, HEADS, HEAD_DIM)
        query_raw = rotate(dq, cosine_table, -sine_table).reshape(tokens, QW)
        key_raw = rotate(own_pairs[..., :HEAD_DIM], cosine_table, -sine_table).reshape(tokens, KW)
        value_raw = own_pairs[..., HEAD_DIM:].reshape(tokens, KW)
        joint_grad = jnp.concatenate([query_raw, key_raw, value_raw], axis=1).astype(BF)
        joint_term = dot(hidden_one, joint_grad, 0, 0).astype(BF)
        hidden_one_grad = jnp.where(real, dot(joint_grad, joint_weight, 1, 1), 0.0)
        gain_one_term = jnp.sum(hidden_one_grad * normed_one, axis=0)
        input_gradient = middle_grad + norm_back(hidden_one_grad * gain_one, normed_one, scale_one)
        to_lanes = ((0, 0), (0, up_to_lanes(QW) - QW))
        terms = jnp.concatenate(
            [
                in_chunks(expand_term, shrink_term).astype(BF),
                jnp.pad(output_term.astype(BF), to_lanes),
                jnp.pad(joint_term[:, :QW], to_lanes),
                joint_term[:, QW:],
            ],
            axis=1,
        ).reshape(shard_count, rows, -1)
        terms = add_gain(terms, gain_two_term, sum_chunks()[OUT_CHUNK][0])
        terms = add_gain(terms, gain_one_term, sum_chunks()[PAIR_CHUNK][0])
        sums = lax.psum(lax.psum_scatter(terms, "shard", scatter_dimension=0), "rep")
        input_gradient = unpadded(input_gradient).T

    grad_scale = grad_factor * token_count ** (-0.5)
    def gain_sum(chunk):
        first = sum_chunks()[chunk][0]
        return sums[own_rows, first : first + own_rows]

    first_gain, second_gain = (
        adam_step(weight, total.astype(F32) * grad_scale, first, second, 0.0)
        for weight, total, first, second in (
            (
                attend_gain,
                gain_sum(PAIR_CHUNK),
                attend_gain_first,
                attend_gain_second,
            ),
            (
                expand_gain,
                gain_sum(OUT_CHUNK),
                expand_gain_first,
                expand_gain_second,
            ),
        )
    )
    matrices = adam(
        grad_scale,
        own_rows,
        sums,
        attend_planes,
        rest_planes,
        (
            (attend_weight_first, attend_weight_second),
            (output_weight_first, output_weight_second),
            (expand_weight_first, expand_weight_second),
            (shrink_weight_first.T, shrink_weight_second.T),
        ),
        (block_output, input_gradient),
    )
    first_joint, first_output, second_expand, second_shrink = (
        matrices[4 * n : 4 * n + 4] for n in range(4)
    )
    second_shrink = [result.T for result in second_shrink]
    block_output, input_gradient = (result.T for result in matrices[16:])
    steps = (first_gain, first_joint, first_output, second_gain, second_expand, second_shrink)
    return (block_output, input_gradient, *[step[i] for i in range(4) for step in steps])


def solution(mesh):
    whole_rows = P(("rep", "shard"), None)
    state = (P("shard"), P("shard", None), P(None, "shard")) * 2
    direct = mesh.shape["rep"] == 4 and mesh.shape["shard"] == 8
    return jax.shard_map(
        functools.partial(shards, direct),
        mesh=mesh,
        in_specs=(whole_rows, whole_rows, P("rep", None), *state, *state, *state),
        out_specs=(whole_rows, whole_rows, *state, *state, *state, *state),
        check_vma=False,
    )
```

```python
import functools
import math

import jax
import jax.numpy as jnp
import numpy as np
from jax import lax
from jax.experimental import pallas as pl
from jax.experimental.pallas import tpu as pltpu
from jax.sharding import PartitionSpec as P

HEADS = 15
KV_HEADS = 5
HEAD_DIM = 64
GROUP = HEADS // KV_HEADS
FF = 2560
MAXLEN = 2048
STEP = 10
QW = 960
KW = 320
JW = QW + 2 * KW
D = 960

eps_norm = 1e-05
rope_base = 100000.0
beta_one = 0.9
beta_two = 0.95
adam_eps = 1e-08
learn_rate = 0.05
decay_rate = 0.1
grad_factor = 4.0

F32 = jnp.float32
BF = jnp.bfloat16
MESH = pl.DeviceIdType.MESH
ANY = pl.ANY
VMEM = pltpu.VMEM
DMA = pltpu.SemaphoreType.DMA

QC = 256
KB = 768
HALF = 64
ONES = 112
NEG = -1e30
EXP_SCALE = HEAD_DIM**-0.5 * math.log2(math.e)
BIG_VMEM = 60 * 2**20
PART = 128


def dot(a, b, ca=1, cb=0):
    return lax.dot_general(a, b, (((ca,), (cb,)), ((), ())), preferred_element_type=F32)


def causal_tile():
    key = lax.broadcasted_iota(jnp.int32, (QC, QC), 0)
    query = lax.broadcasted_iota(jnp.int32, (QC, QC), 1)
    return key <= query


def mask_last(scores, causal):
    last = jnp.where(causal, scores[KB - QC :], NEG)
    return jnp.concatenate([scores[: KB - QC], last], axis=0)


def attend_forward_setup(feat_ref, qfeat_ref, kvf, vt, qa):
    lanes = feat_ref.shape[1]
    kvf[:, lanes:] = feat_ref[...]
    qa[HALF:lanes, :] = jnp.zeros((lanes - HALF, qa.shape[1]), BF)
    qa[lanes:, :] = qfeat_ref[...]
    vt[HALF:, :] = jnp.ones((vt.shape[0] - HALF, vt.shape[1]), BF)


def attend_forward_keys(j, kv_ref, kvf, vt):
    blocks, _, rows, lanes = kv_ref.shape
    for block in range(blocks):
        part = kv_ref[block, j]
        kvf[block * rows : (block + 1) * rows, :lanes] = part
        vt[:HALF, block * rows : (block + 1) * rows] = part.T[HALF:, :]


def attend_forward_head(h, qt_ref, mixed_ref, lse_ref, kvf, vt, qa, sb):
    tokens = qt_ref.shape[1]
    steps = (kvf.shape[0] - (tokens - QC)) // KB
    causal = causal_tile()
    row = pl.multiple_of(h * HEAD_DIM, HEAD_DIM)
    qa[:HALF, :] = qt_ref[pl.ds(row, HEAD_DIM), :]
    tops = []
    for chunk in range(tokens // QC):
        low = chunk * QC
        highest = None
        for b in range(steps):
            first = low + b * KB
            s = dot(kvf[first : first + KB, :], qa[:, low : low + QC])
            if b == steps - 1:
                s = mask_last(s, causal)
            sb[chunk, b * KB : (b + 1) * KB, :] = s
            peak = jnp.max(s.reshape(KB // 8, 8, QC), axis=0)
            highest = peak if highest is None else jnp.maximum(highest, peak)
        tops.append(jnp.max(highest, axis=0, keepdims=True))
    for chunk in range(tokens // QC):
        low = chunk * QC
        shift = tops[chunk] * EXP_SCALE
        total = None
        for b in range(steps):
            first = low + b * KB
            s = sb[chunk, b * KB : (b + 1) * KB, :]
            p = jnp.exp2(s * EXP_SCALE - shift).astype(BF)
            term = dot(vt[:, first : first + KB], p)
            total = term if total is None else total + term
        weight = total[HALF : HALF + 1, :]
        mixed_ref[pl.ds(row, HEAD_DIM), low : low + QC] = (
            total[:HALF, :] * (1.0 / weight)
        ).astype(BF)
        lse_ref[pl.ds(h, 1), :, low : low + QC] = (
            tops[chunk] * HEAD_DIM**-0.5 + jnp.log(weight)
        )[None]


def attend_forward_scratch(keys, lanes, tokens):
    return [
        VMEM((keys, 2 * lanes), BF),
        VMEM((HALF + 16, keys), BF),
        VMEM((2 * lanes, tokens), BF),
        VMEM((tokens // QC, keys - (tokens - QC), QC), F32),
    ]


def attend_forward_kernel(
    kv_ref, feat_ref, qt_ref, qfeat_ref, mixed_ref, lse_ref, kvf, vt, qa, sb
):
    attend_forward_setup(feat_ref, qfeat_ref, kvf, vt, qa)

    def key_head(j, _):
        attend_forward_keys(j, kv_ref, kvf, vt)

        def head(g, _):
            attend_forward_head(j * GROUP + g, qt_ref, mixed_ref, lse_ref, kvf, vt, qa, sb)
            return 0

        lax.fori_loop(0, GROUP, head, 0)
        return 0

    lax.fori_loop(0, kv_ref.shape[1], key_head, 0)


def attend_forward(window, feat, qt, qfeat):
    blocks, kv_heads, rows, lanes = window.shape
    tokens = qt.shape[1]
    return pl.pallas_call(
        attend_forward_kernel,
        out_shape=(
            jax.ShapeDtypeStruct(qt.shape, BF),
            jax.ShapeDtypeStruct((HEADS, 1, tokens), F32),
        ),
        scratch_shapes=attend_forward_scratch(blocks * rows, lanes, tokens),
        compiler_params=pltpu.CompilerParams(vmem_limit_bytes=BIG_VMEM),
        name="attend_forward",
    )(window, feat, qt, qfeat)


def three_parts(value, rows):
    one = value.astype(BF).astype(F32)
    two = (value - one).astype(BF).astype(F32)
    three = value - one - two
    shape = (rows, value.shape[1])
    place = lax.broadcasted_iota(jnp.int32, shape, 0)
    parts = [jnp.broadcast_to(part, shape) for part in (one, two, three)]
    chosen = jnp.where(
        place == 0, parts[0], jnp.where(place == 1, parts[1], jnp.where(place == 2, parts[2], 0.0))
    )
    return chosen.astype(BF)


def attend_backward_setup(feat_ref, kvf, qa, da, rhs):
    lanes = feat_ref.shape[1]
    kvf[:, lanes:] = feat_ref[...]
    qa[HALF:lanes, :] = jnp.zeros((lanes - HALF, qa.shape[1]), BF)
    da[...] = jnp.zeros_like(da)
    rhs[...] = jnp.zeros_like(rhs)


def attend_backward_keys(j, kv_ref, kvf, kt, acc):
    blocks, _, rows, lanes = kv_ref.shape
    for block in range(blocks):
        part = kv_ref[block, j]
        kvf[block * rows : (block + 1) * rows, :lanes] = part
        kt[:, block * rows : (block + 1) * rows] = part.T[:HALF, :]
    acc[...] = jnp.zeros_like(acc)


def attend_backward_head(
    h, put_query, qt_ref, qfeat_ref, gradt_ref, mixed_ref, lse_ref, kvf, kt, qa, da, acc, rhs
):
    tokens = qt_ref.shape[1]
    lanes = qfeat_ref.shape[0]
    steps = (kvf.shape[0] - (tokens - QC)) // KB
    causal = causal_tile()
    extra = lanes - ONES
    row = pl.multiple_of(h * HEAD_DIM, HEAD_DIM)
    q = qt_ref[pl.ds(row, HEAD_DIM), :]
    grad = gradt_ref[pl.ds(row, HEAD_DIM), :]
    qa[:HALF, :] = q
    da[HALF:lanes, :] = grad
    mixed = mixed_ref[pl.ds(row, HEAD_DIM), :].astype(F32)
    row_total = jnp.sum(grad.astype(F32) * mixed, axis=0, keepdims=True)
    lse = lse_ref[pl.ds(h, 1), :, :][0]
    qa[lanes : lanes + ONES, :] = qfeat_ref[:ONES, :]
    qa[lanes + ONES :, :] = three_parts(-(HEAD_DIM**0.5) * lse, extra)
    da[lanes + ONES :, :] = three_parts(-row_total, extra)
    query_grads = [None] * (tokens // QC)
    for chunk in range(tokens // QC):
        low = chunk * QC
        rhs[chunk, :HALF, :QC] = q[:, low : low + QC]
        rhs[chunk, HALF:, QC:] = grad[:, low : low + QC]
    for b in range(steps):
        for chunk in range(tokens // QC):
            low = chunk * QC
            first = low + b * KB
            keys = kvf[first : first + KB, :]
            s = dot(keys, qa[:, low : low + QC])
            if b == steps - 1:
                s = mask_last(s, causal)
            p = jnp.exp2(s * EXP_SCALE)
            dp = dot(keys, da[:, low : low + QC])
            ds = (p * dp).astype(BF)
            both = jnp.concatenate([ds, p.astype(BF)], axis=1)
            acc[first : first + KB, :] += dot(both, rhs[chunk], 1, 1)
            term = dot(kt[:, first : first + KB], ds)
            old = query_grads[chunk]
            query_grads[chunk] = term if old is None else old + term
    for chunk in range(tokens // QC):
        low = chunk * QC
        put_query(row, low, query_grads[chunk] * HEAD_DIM**-0.5)


def attend_backward_done(j, acc, dkv_ref):
    blocks, _, rows, lanes = dkv_ref.shape
    lane = lax.broadcasted_iota(jnp.int32, (1, lanes), 1)
    factor = jnp.where(lane < HALF, HEAD_DIM**-0.5, 1.0)
    for block in range(blocks):
        part = acc[block * rows : (block + 1) * rows, :]
        dkv_ref[block, j] = (part * factor).astype(dkv_ref.dtype)


def attend_backward_scratch(keys, lanes, tokens):
    return [
        VMEM((keys, 2 * lanes), BF),
        VMEM((HALF, keys), BF),
        VMEM((2 * lanes, tokens), BF),
        VMEM((2 * lanes, tokens), BF),
        VMEM((keys, lanes), F32),
        VMEM((tokens // QC, lanes, 2 * QC), BF),
    ]


def attend_backward_kernel(
    kv_ref, feat_ref, qt_ref, qfeat_ref, gradt_ref, mixed_ref, lse_ref, dq_ref, dkv_ref, *scratch
):
    kvf, kt, qa, da, acc, rhs = scratch
    attend_backward_setup(feat_ref, kvf, qa, da, rhs)

    def put_query(row, low, value):
        dq_ref[pl.ds(row, HEAD_DIM), low : low + QC] = value

    def key_head(j, _):
        attend_backward_keys(j, kv_ref, kvf, kt, acc)

        def head(g, _):
            attend_backward_head(
                j * GROUP + g,
                put_query,
                qt_ref,
                qfeat_ref,
                gradt_ref,
                mixed_ref,
                lse_ref,
                *scratch,
            )
            return 0

        lax.fori_loop(0, GROUP, head, 0)
        attend_backward_done(j, acc, dkv_ref)
        return 0

    lax.fori_loop(0, kv_ref.shape[1], key_head, 0)


def attend_backward(window, feat, qt, qfeat, gradt, mixed, lse):
    blocks, kv_heads, rows, lanes = window.shape
    tokens = qt.shape[1]
    return pl.pallas_call(
        attend_backward_kernel,
        out_shape=(
            jax.ShapeDtypeStruct(qt.shape, F32),
            jax.ShapeDtypeStruct(window.shape, BF),
        ),
        scratch_shapes=attend_backward_scratch(blocks * rows, lanes, tokens),
        compiler_params=pltpu.CompilerParams(vmem_limit_bytes=BIG_VMEM),
        name="attend_backward",
    )(window, feat, qt, qfeat, gradt, mixed, lse)


class Place:
    def __init__(self):
        self.r = lax.axis_index("rep")
        self.s = lax.axis_index("shard")
        self.x, self.y = lax.rem(self.r, 2), self.r // 2
        self.z, self.c = self.s // 2, lax.rem(self.s, 2)
        self.rx = self.y * 2 + (1 - self.x)
        self.ry = (1 - self.y) * 2 + self.x
        self.rd = 3 - self.r
        self.x_side = (self.rx, self.s)
        self.y_side = (self.ry, self.s)
        self.core_side = (self.r, self.z * 2 + (1 - self.c))
        self.has_later, self.has_earlier = self.z < 3, self.z > 0
        self.later = (self.r, lax.min(self.s + 2, 7))
        self.earlier = (self.r, lax.max(self.s - 2, 0))
        self.two_earlier = (self.r, lax.max(self.s - 4, 0))

    def z_to(self, k):
        return lax.rem(self.z + k, 4)

    def z_side(self, k):
        return (self.r, self.z_to(k) * 2 + self.c)

    def arrival(self, i):
        low = self.z < 2
        first = jnp.where(self.z == 0, 1, jnp.where(self.z == 1, 0, jnp.where(self.z == 2, 3, 2)))
        if i == 0:
            return first
        if i == 1:
            return jnp.where(low, 2, 1)
        return jnp.where(low, 3, 0)


def greet(at, whole_line):
    barrier = pltpu.get_barrier_semaphore()

    def signal(device):
        pl.semaphore_signal(barrier, inc=1, device_id=device, device_id_type=MESH)

    for device in (at.x_side, at.y_side, at.core_side):
        signal(device)
    if whole_line:
        for k in (1, 2, 3):
            signal(at.z_side(k))
        pl.semaphore_wait(barrier, 6)
        return

    @pl.when(at.has_later)
    def _():
        signal(at.later)

    @pl.when(at.has_earlier)
    def _():
        signal(at.earlier)

    count = 3 + jnp.where(at.has_later, 1, 0) + jnp.where(at.has_earlier, 1, 0)
    pl.semaphore_wait(barrier, count)


def remote(src, dst, send, recv, device):
    return pltpu.make_async_remote_copy(
        src_ref=src, dst_ref=dst, send_sem=send, recv_sem=recv, device_id=device, device_id_type=MESH
    )


class Gather:
    COUNT = 31

    def __init__(self, at, own, full, columns, local_sem, send, recv):
        self.at, self.own, self.full, self.columns = at, own, full, columns
        self.local_sem, self.send, self.recv = local_sem, send, recv
        self.rows = own.shape[0]
        self.quarter, self.half = self.rows // 4, self.rows // 8

    def piece(self, plane, owner, part=None):
        start = owner * self.quarter + (0 if part is None else part * self.half)
        size = self.quarter if part is None else self.half
        return self.full.at[
            plane, pl.ds(pl.multiple_of(start, self.half), size), pl.ds(*self.columns)
        ]

    def copy(self, index, src, dst, device, landed=None):
        return remote(
            src, dst, self.send.at[index], self.recv.at[index if landed is None else landed], device
        )

    def core_copy(self):
        src = self.own.at[:, pl.ds(*self.columns)]
        return self.copy(
            28, src, self.full.at[self.at.s, :, pl.ds(*self.columns)], self.at.core_side
        )

    def local_copy(self):
        return pltpu.make_async_copy(
            self.own.at[:, pl.ds(*self.columns)],
            self.full.at[self.at.s, :, pl.ds(*self.columns)],
            self.local_sem,
        )

    def z_copy(self, up):
        at = self.at
        src = self.own.at[
            pl.ds(pl.multiple_of(at.r * self.quarter, self.quarter), self.quarter),
            pl.ds(*self.columns),
        ]
        device = at.later if up else at.earlier
        return self.copy(29 if up else 30, src, self.piece(at.s, at.r), device, at.z)

    def start_core(self):
        self.local_copy().start()
        self.core_copy().start()

    def start_z(self):
        @pl.when(self.at.has_later)
        def _():
            self.z_copy(True).start()

        @pl.when(self.at.has_earlier)
        def _():
            self.z_copy(False).start()

    def plane(self, i, other=False):
        c = 1 - self.at.c if other else self.at.c
        return self.at.arrival(i) * 2 + c

    def forwards(self, i):
        at = self.at
        chip = at.arrival(i)
        got = self.piece(self.plane(i), at.r)
        return [
            ((chip < at.z) & at.has_later, self.copy(i, got, got, at.later, chip)),
            ((chip > at.z) & at.has_earlier, self.copy(i, got, got, at.earlier, chip)),
        ]

    def out_copies(self, i):
        at, plane = self.at, self.plane(i)
        got = self.piece(plane, at.r)
        return [
            self.copy(4 + i, got, got, at.x_side),
            self.copy(7 + i, got, got, at.y_side),
            self.copy(10 + i, got, got, at.core_side),
        ]

    def cross_copies(self, i):
        at, plane = self.at, self.plane(i)
        one, two = self.piece(plane, at.rx, 0), self.piece(plane, at.ry, 1)
        from_x, from_y = self.piece(plane, at.rx), self.piece(plane, at.ry)
        return [
            self.copy(13 + i, one, one, at.y_side),
            self.copy(16 + i, from_x, from_x, at.core_side),
            self.copy(19 + i, two, two, at.x_side),
            self.copy(22 + i, from_y, from_y, at.core_side),
        ]

    def last_copy(self, i):
        got = self.piece(self.plane(i), self.at.rd)
        return self.copy(25 + i, got, got, self.at.core_side)

    def arrive(self, landed, ref):
        remote(
            ref, ref, self.send.at[landed], self.recv.at[landed], self.at.core_side
        ).wait_recv()

    def z(self, i):
        at = self.at
        self.arrive(at.arrival(i), self.piece(self.plane(i), at.r))
        for condition, copy in self.forwards(i):
            pl.when(condition)(copy.start)
        for copy in self.out_copies(i):
            copy.start()

    def cross(self, i):
        at, plane = self.at, self.plane(i)
        copies = self.cross_copies(i)
        self.arrive(4 + i, self.piece(plane, at.rx))
        copies[0].start()
        copies[1].start()
        self.arrive(7 + i, self.piece(plane, at.ry))
        copies[2].start()
        copies[3].start()

    def last(self, i):
        at, plane = self.at, self.plane(i)
        self.arrive(13 + i, self.piece(plane, at.rd, 0))
        self.arrive(19 + i, self.piece(plane, at.rd, 1))
        self.last_copy(i).start()

    def landed(self):
        at = self.at
        self.arrive(28, self.full.at[at.core_side[1], :, pl.ds(*self.columns)])
        for i in range(3):
            plane = self.plane(i, True)
            self.arrive(10 + i, self.piece(plane, at.r))
            self.arrive(16 + i, self.piece(plane, at.rx))
            self.arrive(22 + i, self.piece(plane, at.ry))
            self.arrive(25 + i, self.piece(plane, at.rd))
        self.local_copy().wait()

    def sent(self):
        at = self.at
        self.core_copy().wait_send()
        pl.when(at.has_later)(self.z_copy(True).wait_send)
        pl.when(at.has_earlier)(self.z_copy(False).wait_send)
        for i in range(3):
            for condition, copy in self.forwards(i):
                pl.when(condition)(copy.wait_send)
            for copy in self.out_copies(i) + self.cross_copies(i) + [self.last_copy(i)]:
                copy.wait_send()


class Spread:
    def __init__(self, at, win, send, recv):
        self.at, self.win, self.sems = at, win, (send, recv)
        even = at.c == 0
        self.near, self.far = jnp.where(even, 1, 3), jnp.where(even, 3, 1)

    def copy(self, n, j, src, dst, device):
        send, recv = self.sems
        return remote(
            self.win.at[src, j], self.win.at[dst, j], send.at[n, j], recv.at[n, j], device
        )

    def first(self, j):
        return self.copy(0, j, 4, 2, self.at.later)

    def twin_own(self, j):
        return self.copy(1, j, 4, 3, self.at.core_side)

    def second(self, j):
        return self.copy(2, j, 2, 0, self.at.later)

    def twin_near(self, j, place):
        return self.copy(3, j, 2, place, self.at.core_side)

    def twin_far(self, j):
        return self.copy(4, j, 0, 1, self.at.core_side)

    def clear(self):
        for block in range(4):
            @pl.when(self.at.s < 4 - block)
            def _(block=block):
                self.win[block] = jnp.zeros(self.win.shape[1:], self.win.dtype)

    def start(self, j):
        pl.when(self.at.has_later)(self.first(j).start)
        pl.when(self.at.c == 0)(self.twin_own(j).start)

    def one(self, j):
        at = self.at

        @pl.when(at.has_earlier)
        def _():
            self.first(j).wait_recv()
            self.twin_near(j, self.near).start()
            pl.when(at.has_later)(self.second(j).start)

    def two(self, j):
        at = self.at

        @pl.when(at.z > 1)
        def _():
            self.second(j).wait_recv()
            pl.when(at.c == 1)(self.twin_far(j).start)

    def landed(self, j):
        at = self.at
        pl.when(at.c == 1)(self.twin_own(j).wait_recv)
        pl.when(at.has_earlier)(self.twin_near(j, self.far).wait_recv)
        pl.when((at.c == 0) & (at.z > 1))(self.twin_far(j).wait_recv)

    def sent(self, j):
        at = self.at
        pl.when(at.has_later)(self.first(j).wait_send)
        pl.when(at.c == 0)(self.twin_own(j).wait_send)
        pl.when(at.has_earlier)(self.twin_near(j, self.near).wait_send)
        pl.when(at.has_earlier & at.has_later)(self.second(j).wait_send)
        pl.when((at.c == 1) & (at.z > 1))(self.twin_far(j).wait_send)


class Collect:
    def __init__(self, at, grads, out, ra, rb, r2, r1, t2, t1, send, recv):
        self.at, self.grads, self.out = at, grads, out
        self.ra, self.rb, self.r2, self.r1, self.t2, self.t1 = ra, rb, r2, r1, t2, t1
        self.sems = (send, recv)

    def copy(self, n, j, src, dst, device):
        send, recv = self.sems
        return remote(src, dst, send.at[n, j], recv.at[n, j], device)

    def twin_a(self, j):
        return self.copy(0, j, self.grads.at[3, j], self.ra.at[j], self.at.core_side)

    def twin_b(self, j):
        return self.copy(1, j, self.grads.at[1, j], self.rb.at[j], self.at.core_side)

    def far(self, j, relayed=True):
        device = self.at.earlier if relayed else self.at.two_earlier
        return self.copy(2, j, self.t2.at[j], self.r2.at[j], device)

    def near(self, j):
        return self.copy(3, j, self.t1.at[j], self.r1.at[j], self.at.earlier)

    def start(self, j):
        self.twin_b(j).start()
        self.twin_a(j).start()

    def one(self, j, relayed=True):
        self.twin_b(j).wait_recv()
        self.twin_a(j).wait_recv()
        even = self.at.c == 0
        from_a, from_b = self.ra[j].astype(F32), self.rb[j].astype(F32)
        none = jnp.zeros_like(from_a)
        self.t2[j] = (self.grads[0, j].astype(F32) + jnp.where(even, none, from_b)).astype(BF)
        pl.when(self.at.z > 1)(self.far(j, relayed).start)
        self.t1[j] = (self.grads[2, j].astype(F32) + jnp.where(even, from_b, from_a)).astype(BF)
        if not relayed:
            pl.when(self.at.has_earlier)(self.near(j).start)
        self.out[j] = self.grads[4, j].astype(F32) + jnp.where(even, from_a, none)

    def two(self, j):
        at = self.at

        @pl.when(at.has_earlier & at.has_later)
        def _():
            self.far(j).wait_recv()
            self.t1[j] = (self.t1[j].astype(F32) + self.r2[j].astype(F32)).astype(BF)

        pl.when(at.has_earlier)(self.near(j).start)

    def three(self, j, relayed=True):
        at = self.at

        @pl.when(at.has_later)
        def _():
            self.near(j).wait_recv()
            self.out[j] = self.out[j] + self.r1[j].astype(F32)

        if not relayed:
            @pl.when(at.z < 2)
            def _():
                self.far(j).wait_recv()
                self.out[j] = self.out[j] + self.r2[j].astype(F32)

    def sent(self, j):
        at = self.at
        self.twin_a(j).wait_send()
        self.twin_b(j).wait_send()
        pl.when(at.z > 1)(self.far(j).wait_send)
        pl.when(at.has_earlier)(self.near(j).wait_send)


class Reduce:
    COUNT = 14

    def __init__(self, at, chunks, out, own, give, r0, r1a, r1b, r2a, r2b, r3, send, recv, free):
        self.at, self.chunks, self.out, self.own, self.give = at, chunks, out, own, give
        self.r0, self.r1a, self.r1b, self.r2a, self.r2b, self.r3 = r0, r1a, r1b, r2a, r2b, r3
        self.send, self.recv, self.free = send, recv, free
        self.rows = out.shape[0]
        self.quarter, self.half = self.rows // 4, self.rows // 8
        self.slots = give.shape[0]

    @staticmethod
    def scratch(rows, chunks, slots):
        half = rows // 8
        columns = sum(width for _, width in chunks)
        widest = max(width for _, width in chunks)
        return [
            VMEM((4, rows, columns), BF),
            VMEM((slots, 4, rows, widest), BF),
            VMEM((slots, 4, rows, widest), BF),
            VMEM((2, 4, half, columns), BF),
            VMEM((2, 4, half, columns), BF),
            VMEM((4, half, columns), BF),
            VMEM((4, half, columns), BF),
            VMEM((3, 2 * half, columns), BF),
            DMA((len(chunks), Reduce.COUNT)),
            DMA((len(chunks), Reduce.COUNT)),
            pltpu.SemaphoreType.REGULAR,
        ]

    def columns(self, n):
        return pl.ds(*self.chunks[n])

    def copy(self, n, index, src, dst, device):
        return remote(src, dst, self.send.at[n, index], self.recv.at[n, index], device)

    def arrive(self, n, index, ref):
        self.copy(n, index, ref, ref, self.at.core_side).wait_recv()

    def spot(self, owner, part):
        start = owner * self.quarter + part * self.half
        return pl.ds(pl.multiple_of(start, self.half), self.half)

    def piece(self, n, owner):
        start = pl.multiple_of(owner * self.quarter, self.quarter)
        return self.out.at[pl.ds(start, self.quarter), self.columns(n)]

    def core_copy(self, n):
        slot, width = n % self.slots, self.chunks[n][1]
        return self.copy(
            n,
            0,
            self.give.at[slot, :, :, pl.ds(0, width)],
            self.r0.at[slot, :, :, pl.ds(0, width)],
            self.at.core_side,
        )

    def one_copies(self, n):
        at, copies, cols = self.at, [], self.columns(n)
        for i in range(2):
            a = self.own.at[:, self.spot(i * 2 + 1 - at.x, 0), cols]
            b = self.own.at[:, self.spot((1 - at.y) * 2 + i, 1), cols]
            copies.append(self.copy(n, 1 + i, a, self.r1a.at[i, :, :, cols], at.x_side))
            copies.append(self.copy(n, 3 + i, b, self.r1b.at[i, :, :, cols], at.y_side))
        return copies

    def two_copies(self, n):
        at, cols = self.at, self.columns(n)
        a = self.own.at[:, self.spot(at.ry, 0), cols]
        b = self.own.at[:, self.spot(at.rx, 1), cols]
        return [
            self.copy(n, 5, a, self.r2a.at[:, :, cols], at.y_side),
            self.copy(n, 6, b, self.r2b.at[:, :, cols], at.x_side),
        ]

    def z_copy(self, n, k):
        at, cols = self.at, self.columns(n)
        mine = pl.ds(pl.multiple_of(at.r * self.quarter, self.quarter), self.quarter)
        src = self.own.at[at.z_to(k), mine, cols]
        return self.copy(n, 6 + k, src, self.r3.at[k - 1, :, cols], at.z_side(k))

    def back_copy(self, n, i):
        at, cols = self.at, self.columns(n)
        if i < 2:
            ref = self.piece(n, at.r)
            return self.copy(n, 10 + i, ref, ref, at.x_side if i == 0 else at.y_side)
        owner, device = (at.rx, at.y_side) if i == 2 else (at.ry, at.x_side)
        ref = self.out.at[self.spot(owner, i - 2), cols]
        return self.copy(n, 10 + i, ref, ref, device)

    def claim(self, n):
        if n >= self.slots:
            self.core_copy(n - self.slots).wait_send()

    def start(self, n):
        if n >= self.slots:
            pl.semaphore_wait(self.free, 1)
        self.core_copy(n).start()

    def zero(self, n):
        slot, (first, width) = n % self.slots, self.chunks[n]
        self.arrive(n, 0, self.r0.at[slot, :, :, pl.ds(0, width)])
        for z in range(4):
            self.own[z, :, first : first + width] += self.r0[slot, z, :, :width]
        if n + self.slots < len(self.chunks):
            pl.semaphore_signal(
                self.free, inc=1, device_id=self.at.core_side, device_id_type=MESH
            )

    def push(self, n):
        for copy in self.one_copies(n):
            copy.start()

    def add(self, n, where, ref):
        cols = self.columns(n)
        for z in range(4):
            self.own[z, where, cols] += ref[z, :, cols]

    def one(self, n):
        at, cols = self.at, self.columns(n)
        for i in range(2):
            self.arrive(n, 1 + i, self.r1a.at[i, :, :, cols])
            self.arrive(n, 3 + i, self.r1b.at[i, :, :, cols])
            self.add(n, self.spot(i * 2 + at.x, 0), self.r1a.at[i])
            self.add(n, self.spot(at.y * 2 + i, 1), self.r1b.at[i])
        for copy in self.two_copies(n):
            copy.start()

    def two(self, n):
        at, cols = self.at, self.columns(n)
        self.arrive(n, 5, self.r2a.at[:, :, cols])
        self.arrive(n, 6, self.r2b.at[:, :, cols])
        self.add(n, self.spot(at.r, 0), self.r2a)
        self.add(n, self.spot(at.r, 1), self.r2b)
        for k in (1, 2, 3):
            self.z_copy(n, k).start()

    def three(self, n):
        at, cols = self.at, self.columns(n)
        for k in (1, 2, 3):
            self.arrive(n, 6 + k, self.r3.at[k - 1, :, cols])
        for i in range(2):
            where = pl.ds(i * self.half, self.half)
            total = self.own[at.z, self.spot(at.r, i), cols].astype(F32)
            for k in range(3):
                total += self.r3[k, where, cols].astype(F32)
            self.out[self.spot(at.r, i), cols] = total.astype(BF)
        self.back_copy(n, 0).start()
        self.back_copy(n, 1).start()

    def four(self, n):
        at = self.at
        self.arrive(n, 10, self.piece(n, at.rx))
        self.back_copy(n, 2).start()
        self.arrive(n, 11, self.piece(n, at.ry))
        self.back_copy(n, 3).start()

    def five(self, n):
        at, cols = self.at, self.columns(n)
        self.arrive(n, 12, self.out.at[self.spot(at.rd, 0), cols])
        self.arrive(n, 13, self.out.at[self.spot(at.rd, 1), cols])

    def sent(self):
        for n in range(len(self.chunks)):
            if n + self.slots >= len(self.chunks):
                self.core_copy(n).wait_send()
            copies = self.one_copies(n) + self.two_copies(n)
            copies += [self.z_copy(n, k) for k in (1, 2, 3)]
            for copy in copies + [self.back_copy(n, i) for i in range(4)]:
                copy.wait_send()


def at_steps(i, events):
    for n, event in events:
        if n >= 0:
            pl.when(i == n)(event)


def flip_blocks(value, dst):
    blocks, rows, _ = dst.shape
    for s in range(blocks):
        dst[s] = value[:, s * rows : (s + 1) * rows].T


def sequence_features(lengths_ref, first_row, feat_ref, qfeat_ref):
    keys, lanes = feat_ref.shape
    tokens = qfeat_ref.shape[1]
    count = lengths_ref.shape[1]
    starts, ends = [], []
    for i in range(count):
        starts.append(ends[-1] if ends else 0)
        ends.append(starts[-1] + lengths_ref[0, i])
    for low in range(0, keys, tokens):
        place = lax.broadcasted_iota(jnp.int32, (tokens, lanes), 0)
        key = first_row - (keys - tokens) + low + place
        column = lax.broadcasted_iota(jnp.int32, (tokens, lanes), 1)
        value = jnp.where(column >= ONES, 1.0, 0.0)
        value = jnp.where((column == count) & (key < 0), 1.0, value)
        for i in range(count):
            inside = (column == i) & (key >= starts[i]) & (key < ends[i])
            value = jnp.where(inside, 1.0, value)
        feat_ref[low : low + tokens, :] = value.astype(BF)
    row = lax.broadcasted_iota(jnp.int32, (lanes, tokens), 0)
    query = first_row + lax.broadcasted_iota(jnp.int32, (lanes, tokens), 1)
    value = jnp.where(row == count, NEG, 0.0)
    start = jnp.zeros((1, tokens), jnp.int32)
    for i in range(count):
        inside = (query >= starts[i]) & (query < ends[i])
        value = jnp.where((row == i) & jnp.logical_not(inside), NEG, value)
        start = jnp.where(inside[:1], starts[i], start)
    qfeat_ref[...] = value.astype(BF)
    return query[:1] - start


def front_kernel(
    lengths_ref,
    inverse_ref,
    xt_ref,
    cott_ref,
    attend_gain,
    attend_weight,
    expand_gain,
    expand_weight,
    shrinkt,
    output_weight,
    rest_ref,
    attend_hbm,
    win_hbm,
    feat_hbm,
    qt_hbm,
    flipped_hbm,
    x_hbm,
    cot_hbm,
    cott_hbm,
    middle_hbm,
    hidden_hbm,
    hiddent_hbm,
    mixed_ref,
    lse_ref,
    qfeat_ref,
    cos_ref,
    sin_ref,
    kvf,
    vt,
    qa,
    sb,
    attend_own,
    rest_own,
    attend_ref,
    win_ref,
    feat_ref,
    qt_ref,
    flipped,
    inputs,
    cot,
    cott,
    middle,
    hidden,
    hiddent,
    kvt,
    out_weight,
    local_sems,
    store_sems,
    gather_send,
    gather_recv,
    spread_send,
    spread_recv,
):
    at = Place()
    shard_count, rows, columns = attend_ref.shape
    width = shard_count * rows
    tokens = xt_ref.shape[1]
    kv_heads = win_ref.shape[1]
    own_rows = D // shard_count
    cut = 2 * FF
    greet(at, False)

    def gather(n, own, full, cols):
        return Gather(
            at, own, full, cols, local_sems.at[n], gather_send.at[n], gather_recv.at[n]
        )

    first = gather(0, attend_own, attend_ref, (0, columns))
    second = gather(1, rest_own, rest_ref, (3 * FF, QW))
    third = gather(2, rest_own, rest_ref, (0, cut))
    fourth = gather(3, rest_own, rest_ref, (cut, FF))
    spread = Spread(at, win_ref, spread_send, spread_recv)
    stores = []

    def store(src, dst):
        copy = pltpu.make_async_copy(src, dst, store_sems.at[len(stores)])
        copy.start()
        stores.append(copy)

    def place(ref, low, weight, gain):
        count = weight.shape[1]
        block = own_rows // 16 * 16
        ref[:block, low : low + count] = weight[:block]
        tail = jnp.concatenate(
            [weight[block:].astype(F32), jnp.zeros((rows - own_rows, count), F32)], axis=0
        )
        if gain is not None:
            row = jnp.concatenate(
                [gain[...].astype(F32), jnp.zeros((1, count - own_rows), F32)], axis=1
            )
            where = lax.broadcasted_iota(jnp.int32, tail.shape, 0) == own_rows - block
            tail = jnp.where(where, row, tail)
        ref[block:, low : low + count] = tail.astype(BF)

    place(attend_own, 0, attend_weight, attend_gain)
    first.start_z()
    first.start_core()
    place(rest_own, 3 * FF, output_weight[...].T, expand_gain)
    second.start_core()
    place(rest_own, 0, expand_weight, None)
    third.start_core()
    place(rest_own, cut, shrinkt, None)
    fourth.start_core()
    spread.clear()
    position = sequence_features(lengths_ref, at.s * tokens, feat_ref, qfeat_ref)
    store(feat_ref, feat_hbm)
    attend_forward_setup(feat_ref, qfeat_ref, kvf, vt, qa)
    phases = inverse_ref[...] * position.astype(F32)
    cos_ref[...] = jnp.cos(phases)
    sin_ref[...] = jnp.sin(phases)
    first.z(0)
    for s in range(shard_count):
        block = slice(s * rows, (s + 1) * rows)
        source = slice(s * own_rows, (s + 1) * own_rows)
        blank = jnp.zeros((rows - own_rows, tokens), F32)
        value = jnp.concatenate([xt_ref[source, :].astype(F32), blank], axis=0)
        inputs[:, block] = value.T.astype(BF)
    first.z(1)
    for s in range(shard_count):
        block = slice(s * rows, (s + 1) * rows)
        source = slice(s * own_rows, (s + 1) * own_rows)
        value = jnp.concatenate([cott_ref[source, :].astype(F32), blank], axis=0)
        cott[s] = value.astype(BF)
        cot[:, block] = value.T.astype(BF)
    store(inputs, x_hbm)
    store(cot, cot_hbm)
    store(cott, cott_hbm)
    first.z(2)
    second.start_z()
    third.start_z()
    for i in range(3):
        first.cross(i)
    second.z(0)
    for i in range(3):
        first.last(i)
    second.z(1)
    first.landed()
    store(attend_ref, attend_hbm)

    value = inputs[...].astype(F32)
    scale = scale_of(value)
    for s in range(shard_count):
        lane = slice(s * rows, (s + 1) * rows)
        gain = attend_ref[s, own_rows : own_rows + 1, :rows].astype(F32)
        hidden[:, lane] = (inputs[:, lane].astype(F32) * scale * gain).astype(BF)

    def project(start):
        stop = min(start + 256, columns)
        weight = attend_ref[:, :, start:stop].reshape(width, stop - start)
        turned = dot(hidden[...], weight).T
        for low in range(0, stop - start, HEAD_DIM):
            column = start + low
            head = turned[low : low + HEAD_DIM, :]
            if column < QW + KW:
                half = HEAD_DIM // 2
                front, back = head[:half], head[half:]
                head = jnp.concatenate(
                    [
                        front * cos_ref[...] - back * sin_ref[...],
                        back * cos_ref[...] + front * sin_ref[...],
                    ],
                    axis=0,
                )
            if column < QW:
                qt_ref[column : column + HEAD_DIM, :] = head.astype(BF)
            elif column < QW + KW:
                kvt[(column - QW) // HEAD_DIM, :HALF, :] = head.astype(BF)
            else:
                kvt[(column - QW - KW) // HEAD_DIM, HALF:, :] = head.astype(BF)

    split = QW // 128 * 128
    for start in range(split, columns, 256):
        project(start)
    for j in range(kv_heads):
        win_ref[4, j] = kvt[j].T
        spread.start(j)
    third.z(0)
    second.z(2)
    for start in range(0, split, 256):
        project(start)
    third.z(1)
    fourth.start_z()
    second.cross(0)
    store(qt_ref, qt_hbm)
    flip_blocks(hidden, flipped)
    store(flipped, flipped_hbm)
    spread.one(0)
    third.cross(0)
    spread.one(1)
    second.cross(1)
    spread.two(0)
    events = [
        (0, lambda: third.z(2)),
        (1, lambda: second.cross(2)),
        (2, lambda: second.last(0)),
        (2, lambda: fourth.z(0)),
        (3, lambda: third.cross(1)),
        (4, lambda: second.last(1)),
        (5, lambda: fourth.z(1)),
        (5, lambda: second.last(2)),
        (6, lambda: third.cross(2)),
        (7, lambda: third.last(0)),
        (8, lambda: fourth.cross(0)),
        (9, lambda: fourth.z(2)),
        (10, lambda: third.last(1)),
        (11, lambda: fourth.cross(1)),
        (12, lambda: third.last(2)),
        (13, lambda: fourth.last(0)),
    ]

    def key_head(j, _):
        pl.when(j + 2 < kv_heads)(lambda: spread.one(j + 2))
        pl.when(j + 1 < kv_heads)(lambda: spread.two(j + 1))
        spread.landed(j)
        attend_forward_keys(j, win_ref, kvf, vt)

        def head(g, _):
            h = j * GROUP + g
            attend_forward_head(h, qt_ref, mixed_ref, lse_ref, kvf, vt, qa, sb)
            at_steps(h, events)
            return 0

        lax.fori_loop(0, GROUP, head, 0)
        spread.sent(j)
        return 0

    lax.fori_loop(0, kv_heads, key_head, 0)
    store(win_ref, win_hbm)
    second.landed()
    load = pltpu.make_async_copy(
        rest_ref.at[:, :, pl.ds(3 * FF, QW)], out_weight, local_sems.at[4]
    )
    load.start()
    fourth.cross(2)
    fourth.last(1)
    load.wait()
    real = real_lanes(width, rows, own_rows)
    gain = jnp.concatenate(
        [out_weight[s, own_rows : own_rows + 1, :rows].astype(F32) for s in range(shard_count)],
        axis=1,
    )
    gain = jnp.where(real, gain, 0.0)
    out_full = out_weight.reshape(width, QW)
    for low in range(0, tokens, PART):
        where = slice(low, low + PART)
        value = jnp.where(real, dot(mixed_ref[:, where].T, out_full[...], 1, 1), 0.0)
        value = inputs[where, :].astype(F32) + value
        middle[where, :] = value
        hidden[where, :] = (value * scale_of(value) * gain).astype(BF)
    store(middle, middle_hbm)
    store(hidden, hidden_hbm)
    flip_blocks(hidden, hiddent)
    store(hiddent, hiddent_hbm)
    fourth.last(2)
    third.landed()
    fourth.landed()
    for part in (first, second, third, fourth):
        part.sent()
    for copy in stores:
        copy.wait()


def front(lengths, xt, cott, weights, shard_count, number):
    _, tokens = xt.shape
    attend_weight, expand_weight, output_weight = weights[1], weights[3], weights[5]
    own_rows, columns = attend_weight.shape
    rows = -(-(own_rows + 2) // 16) * 16
    width = shard_count * rows
    lanes = 2 * HEAD_DIM
    blocks = (MAXLEN - 2) // tokens + 2
    keys = blocks * tokens
    half = HEAD_DIM // 2
    inverse = rope_base ** (-(2.0 * np.arange(half, dtype=np.float32) / HEAD_DIM))
    rest_columns = 3 * FF + QW

    def shape(*sizes, dtype=BF):
        return jax.ShapeDtypeStruct(sizes, dtype)

    attend, rest = shape(shard_count, rows, columns), shape(shard_count, rows, rest_columns)
    window = shape(blocks, KV_HEADS, tokens, lanes)
    feat, heads = shape(keys, lanes), shape(QW, tokens)
    natural, turned = shape(tokens, width), shape(shard_count, rows, tokens)
    middle = shape(tokens, width, dtype=F32)
    in_hbm = (
        rest, attend, window, feat, heads, turned, natural, natural, turned, middle, natural, turned
    )
    table = shape(half, tokens, dtype=F32)
    in_vmem = (heads, shape(HEADS, 1, tokens, dtype=F32), shape(lanes, tokens), table, table)

    def scratch(struct):
        return VMEM(struct.shape, struct.dtype)

    return pl.pallas_call(
        front_kernel,
        out_shape=in_hbm + in_vmem,
        in_specs=[pl.BlockSpec(memory_space=pltpu.SMEM)] + [pl.BlockSpec(memory_space=VMEM)] * 9,
        out_specs=(pl.BlockSpec(memory_space=ANY),) * len(in_hbm)
        + (pl.BlockSpec(memory_space=VMEM),) * len(in_vmem),
        scratch_shapes=attend_forward_scratch(keys, lanes, tokens)
        + [VMEM((rows, columns), BF), VMEM((rows, rest_columns), BF)]
        + [
            scratch(struct)
            for struct in (
                attend, window, feat, heads, turned, natural, natural, turned, middle, natural, turned
            )
        ]
        + [
            VMEM((KV_HEADS, lanes, tokens), BF),
            VMEM((shard_count, rows, QW), BF),
            DMA((5,)),
            DMA((len(in_hbm),)),
            DMA((4, Gather.COUNT)),
            DMA((4, Gather.COUNT)),
            DMA((5, KV_HEADS)),
            DMA((5, KV_HEADS)),
        ],
        compiler_params=pltpu.CompilerParams(
            collective_id=number, has_side_effects=True, vmem_limit_bytes=BIG_VMEM
        ),
        name="front",
    )(lengths, jnp.asarray(inverse, F32)[:, None], xt, cott, *weights)


SUB = 256
CHUNK = 2 * SUB


def up_to_lanes(columns):
    return -(-columns // 128) * 128


def sum_chunks():
    widths = [3 * CHUNK] * (FF // CHUNK) + [up_to_lanes(QW)] * 2 + [2 * KW]
    return [(sum(widths[:n]), width) for n, width in enumerate(widths)]


OUT_CHUNK = FF // CHUNK
QUERY_CHUNK, PAIR_CHUNK = OUT_CHUNK + 1, OUT_CHUNK + 2


def unrotate(head, cosine, sine):
    half = HEAD_DIM // 2
    front, back = head[:half], head[half:]
    return jnp.concatenate(
        [front * cosine + back * sine, back * cosine - front * sine], axis=0
    ).astype(BF)


def real_lanes(width, rows, own_rows):
    return lax.rem(lax.broadcasted_iota(jnp.int32, (1, width), 1), rows) < own_rows


def scale_of(value):
    return lax.rsqrt(jnp.sum(value * value, axis=-1, keepdims=True) * (1.0 / D) + eps_norm)


def put_turned(value, dst, rows, own_rows):
    turned = value.T
    for s in range(turned.shape[0] // rows):
        dst[s * own_rows : (s + 1) * own_rows, :] = turned[s * rows : s * rows + own_rows]


def put_gradient(total, n, column, ref, z, product, row=None):
    rows, columns = product.shape
    first = product[:, :rows]
    if row is not None:
        own_rows, gain_row = row
        place = lax.broadcasted_iota(jnp.int32, (rows, rows), 0)
        first = jnp.where(place == own_rows, gain_row, first)
    ref[z, :, column : column + rows] = first.astype(BF)
    ref[z, :, column + rows : column + columns] = product[:, rows:].astype(BF)
    width = total.chunks[n][1]
    if columns < width:
        ref[z, :, column + columns : column + width] = jnp.zeros((rows, width - columns), BF)


def feed_forward(
    at,
    total,
    mixed_ref,
    gradt_ref,
    middle_hbm,
    hidden_hbm,
    hiddent_hbm,
    cot_hbm,
    cott_hbm,
    rest_ref,
    out_hbm,
    middle_grad_hbm,
    events,
    cot,
    hidden,
    middle,
    acc_out,
    acc_grad,
    hidden_own,
    hidden_give,
    cot_own,
    cot_give,
    flipped,
    out_weight,
    gain_term,
    weights,
    results,
    sems,
    load_sems,
):
    shard_count, rows, _ = rest_ref.shape
    width = shard_count * rows
    tokens = middle.shape[0]
    own_rows = D // shard_count
    planes = shard_count // 2

    def weight_copies(n, slot):
        return [
            pltpu.make_async_copy(
                rest_ref.at[:, :, pl.ds(pl.multiple_of(i * FF + n * SUB, 128), SUB)],
                weights.at[slot, i],
                sems.at[slot, i],
            )
            for i in range(3)
        ]

    pairs = [(hidden_hbm, hidden), (cot_hbm, cot)]
    for z in range(planes):
        mine, other = 2 * z + at.c, 2 * z + 1 - at.c
        pairs += [(hiddent_hbm.at[mine], hidden_own.at[z]), (cott_hbm.at[mine], cot_own.at[z])]
        pairs += [(hiddent_hbm.at[other], hidden_give.at[z])]
        pairs += [(cott_hbm.at[other], cot_give.at[z])]
    pairs += [(middle_hbm, middle), (rest_ref.at[:, :, pl.ds(3 * FF, QW)], out_weight)]
    loads = [
        pltpu.make_async_copy(src, dst, load_sems.at[i]) for i, (src, dst) in enumerate(pairs)
    ]
    for copy in weight_copies(0, 0) + loads:
        copy.start()
    acc_out[...] = jnp.zeros_like(acc_out)
    acc_grad[...] = jnp.zeros_like(acc_grad)
    for load in loads[:-2]:
        load.wait()

    def put(ref, column, value):
        where = pl.ds(pl.multiple_of(column, 128), value.shape[1])
        ref[:, :, where] = value.reshape(planes, rows, value.shape[1]).astype(BF)

    def step(n, _):
        slot = lax.rem(n, 2)
        for copy in weight_copies(n, slot):
            copy.wait()

        @pl.when(n + 1 < FF // SUB)
        def _():
            for copy in weight_copies(n + 1, 1 - slot):
                copy.start()

        gate_weight = weights[slot, 0].reshape(width, SUB)
        upper_weight = weights[slot, 1].reshape(width, SUB)
        shrink_weight = weights[slot, 2].reshape(width, SUB)
        gate = dot(hidden[...], gate_weight)
        upper = dot(hidden[...], upper_weight)
        inner_grad = dot(cot[...], shrink_weight)
        sigmoid = jax.nn.sigmoid(gate)
        active = gate * sigmoid
        inner = (active * upper).astype(BF)
        gate_grad = (inner_grad * upper * sigmoid * (1.0 + gate * (1.0 - sigmoid))).astype(BF)
        upper_grad = (inner_grad * active).astype(BF)
        for low in range(0, width, width // 2):
            cols = slice(low, low + width // 2)
            acc_out[:, cols] += dot(inner, shrink_weight[cols], 1, 1)
            acc_grad[:, cols] += dot(gate_grad, gate_weight[cols], 1, 1) + dot(
                upper_grad, upper_weight[cols], 1, 1
            )
        chunk, part = n // 2, lax.rem(n, 2) * SUB
        first = chunk * 3 * CHUNK + part
        put(total.own, first, dot(hidden_own[...].reshape(width // 2, tokens), gate_grad))
        put(total.own, first + CHUNK, dot(hidden_own[...].reshape(width // 2, tokens), upper_grad))
        put(total.own, first + 2 * CHUNK, dot(cot_own[...].reshape(width // 2, tokens), inner))
        for n_start in range(2 * total.slots, FF // SUB, 2):
            pl.when(n == n_start)(functools.partial(total.claim, n_start // 2))
        give = total.give.at[lax.rem(chunk, total.slots)]
        put(give, part, dot(hidden_give[...].reshape(width // 2, tokens), gate_grad))
        put(give, part + CHUNK, dot(hidden_give[...].reshape(width // 2, tokens), upper_grad))
        put(give, part + 2 * CHUNK, dot(cot_give[...].reshape(width // 2, tokens), inner))
        for n_end in range(1, FF // SUB, 2):
            pl.when(n == n_end)(functools.partial(total.start, n_end // 2))
        at_steps(n, events)
        return 0

    lax.fori_loop(0, FF // SUB, step, 0)

    for load in loads[-2:]:
        load.wait()
    out_full = out_weight.reshape(width, QW)
    real = real_lanes(width, rows, own_rows)
    gain = jnp.concatenate(
        [out_weight[s, own_rows : own_rows + 1, :rows].astype(F32) for s in range(shard_count)],
        axis=1,
    )
    gain = jnp.where(real, gain, 0.0)
    term = jnp.zeros((1, width), F32)
    stores = []
    for n, low in enumerate(range(0, tokens, PART)):
        where = slice(low, low + PART)
        value = middle[where, :]
        if n >= 2:
            stores[n - 2].wait()
        put_turned(value + acc_out[where, :], results.at[n % 2], rows, own_rows)
        stores.append(
            pltpu.make_async_copy(
                results.at[n % 2], out_hbm.at[:, pl.ds(low, PART)], sems.at[2, n % 2]
            )
        )
        stores[n].start()
        scale = scale_of(value)
        normed = value * scale
        hidden_grad = jnp.where(real, acc_grad[where, :], 0.0)
        term = term + jnp.sum(hidden_grad * normed, axis=0, keepdims=True)
        upstream = hidden_grad * gain
        mean = jnp.sum(upstream * normed, axis=-1, keepdims=True) * (1.0 / D)
        value = cot[where, :].astype(F32) + scale * (upstream - normed * mean)
        acc_grad[where, :] = value
        branch = value.astype(BF)
        hidden[where, :] = branch
        gradt_ref[:, where] = dot(branch, out_full[...]).T.astype(BF)
        for step_number, event in events:
            if step_number == FF // SUB + n:
                event()
    store = pltpu.make_async_copy(acc_grad, middle_grad_hbm, sems.at[2, 2])
    store.start()
    stores[-2:] += [store]
    for s in range(shard_count):
        gain_term[s] = jnp.broadcast_to(term[:, s * rows : (s + 1) * rows], (8, rows))
    flip_blocks(hidden, flipped)
    for z in range(planes):
        hidden_own[z] = flipped[2 * z + at.c]
        hidden_give[z] = flipped[2 * z + 1 - at.c]
    total.claim(OUT_CHUNK)
    for lhs, core, ref, column in (
        (hidden_give, 1 - at.c, total.give.at[OUT_CHUNK % total.slots], 0),
        (hidden_own, at.c, total.own, total.chunks[OUT_CHUNK][0]),
    ):
        product = dot(lhs[...].reshape(width // 2, tokens), mixed_ref[...], 1, 1)
        for z in range(planes):
            row = (own_rows, gain_term[2 * z + core][:1])
            plane = product[z * rows : (z + 1) * rows]
            put_gradient(total, OUT_CHUNK, column, ref, z, plane, row)
        if lhs is hidden_give:
            total.start(OUT_CHUNK)
    for store in stores[-3:]:
        store.wait()


def attention_backward(
    at,
    total,
    collect,
    events,
    cos_ref,
    sin_ref,
    qfeat_ref,
    lse_ref,
    mixed_ref,
    gradt_ref,
    jointt,
    win_hbm,
    feat_hbm,
    qt_hbm,
    kvf,
    kt,
    qa,
    da,
    acc,
    rhs,
    win_ref,
    feat_ref,
    qt_ref,
    sems,
):
    loads = [
        pltpu.make_async_copy(src, dst, sems.at[i])
        for i, (src, dst) in enumerate(
            ((feat_hbm, feat_ref), (win_hbm, win_ref), (qt_hbm, qt_ref))
        )
    ]
    for load in loads:
        load.start()
    for load in loads:
        load.wait()
    attend_backward_setup(feat_ref, kvf, qa, da, rhs)
    for n, event in events:
        if n < 0:
            event()

    def put_query(row, low, value):
        cols = slice(low, low + QC)
        jointt[pl.ds(row, HEAD_DIM), cols] = unrotate(value, cos_ref[:, cols], sin_ref[:, cols])

    def key_head(j, _):
        attend_backward_keys(j, win_ref, kvf, kt, acc)

        def head(g, _):
            h = j * GROUP + g
            attend_backward_head(
                h,
                put_query,
                qt_ref,
                qfeat_ref,
                gradt_ref,
                mixed_ref,
                lse_ref,
                kvf,
                kt,
                qa,
                da,
                acc,
                rhs,
            )
            at_steps(h, events)
            return 0

        lax.fori_loop(0, GROUP, head, 0)
        attend_backward_done(j, acc, collect.grads)
        collect.start(j)
        pl.when(j > 0)(lambda: collect.one(j - 1))
        pl.when(j > 1)(lambda: collect.two(j - 2))
        pl.when(j > 2)(lambda: collect.three(j - 3))
        return 0

    lax.fori_loop(0, KV_HEADS, key_head, 0)


def projection_backward(
    at,
    total,
    collect,
    events,
    cos_ref,
    sin_ref,
    jointt,
    hidden_own,
    hidden_give,
    x_hbm,
    middle_grad_hbm,
    attend_hbm,
    grad_hbm,
    attend_ref,
    inputs,
    middle_grad,
    hidden_grad,
    gain_term,
    results,
    sems,
):
    shard_count, rows, columns = attend_ref.shape
    width = shard_count * rows
    tokens = inputs.shape[0]
    own_rows = D // shard_count
    planes = shard_count // 2
    loads = [
        pltpu.make_async_copy(src, dst, sems.at[i])
        for i, (src, dst) in enumerate(
            ((attend_hbm, attend_ref), (x_hbm, inputs), (middle_grad_hbm, middle_grad))
        )
    ]
    for load in loads:
        load.start()
    last = KV_HEADS - 1
    sides = (
        (1 - at.c, hidden_give, lambda n: (total.give.at[n % total.slots], 0)),
        (at.c, hidden_own, lambda n: (total.own, total.chunks[n][0])),
    )

    def gradients(n, rows_of_joint, gain):
        total.claim(n)
        for side, (core, lhs, target) in enumerate(sides):
            ref, column = target(n)
            product = dot(
                lhs[...].reshape(planes * rows, tokens), jointt[rows_of_joint, :], 1, 1
            )
            for z in range(planes):
                row = (own_rows, gain_term[2 * z + core][:1]) if gain else None
                plane = product[z * rows : (z + 1) * rows]
                put_gradient(total, n, column, ref, z, plane, row)
            if side == 0:
                total.start(n)

    gradients(QUERY_CHUNK, slice(0, QW), False)
    collect.one(last, False)
    collect.two(last - 1)
    for load in loads:
        load.wait()
    weight = attend_ref.reshape(width, columns)
    for low in range(0, tokens, PART):
        where = slice(low, low + PART)
        hidden_grad[where, :] = dot(jointt[:QW, where].T, weight[:, :QW], 1, 1)
    total.zero(QUERY_CHUNK)
    total.push(QUERY_CHUNK)
    events[0]()
    collect.three(last - 2)
    collect.three(last - 1)
    collect.three(last, False)
    for j in range(KV_HEADS):
        pair = collect.out[j].T
        low = QW + j * HEAD_DIM
        jointt[low : low + HEAD_DIM, :] = unrotate(pair[:HALF], cos_ref[...], sin_ref[...])
        jointt[low + KW : low + KW + HEAD_DIM, :] = pair[HALF:].astype(BF)
    real = real_lanes(width, rows, own_rows)
    term = jnp.zeros((1, width), F32)
    for low in range(0, tokens, PART):
        where = slice(low, low + PART)
        value = inputs[where, :].astype(F32)
        normed = value * scale_of(value)
        value = hidden_grad[where, :] + dot(jointt[QW:, where].T, weight[:, QW:], 1, 1)
        value = jnp.where(real, value, 0.0)
        hidden_grad[where, :] = value
        term = term + jnp.sum(value * normed, axis=0, keepdims=True)
    for s in range(shard_count):
        gain_term[s] = jnp.broadcast_to(term[:, s * rows : (s + 1) * rows], (8, rows))
    gradients(PAIR_CHUNK, slice(QW, columns), True)
    events[1]()
    total.one(QUERY_CHUNK)
    total.zero(PAIR_CHUNK)
    total.push(PAIR_CHUNK)
    events[2]()
    total.two(QUERY_CHUNK)
    gain = jnp.concatenate(
        [
            attend_ref[s, own_rows : own_rows + 1, :rows].astype(F32)
            for s in range(shard_count)
        ],
        axis=1,
    )
    gain = jnp.where(real, gain, 0.0)
    stores = []
    for n, low in enumerate(range(0, tokens, PART)):
        where = slice(low, low + PART)
        value = inputs[where, :].astype(F32)
        scale = scale_of(value)
        normed = value * scale
        upstream = hidden_grad[where, :] * gain
        mean = jnp.sum(upstream * normed, axis=-1, keepdims=True) * (1.0 / D)
        result = middle_grad[where, :] + scale * (upstream - normed * mean)
        if n >= 2:
            stores[n - 2].wait()
        put_turned(result, results.at[n % 2], rows, own_rows)
        stores.append(
            pltpu.make_async_copy(
                results.at[n % 2], grad_hbm.at[:, pl.ds(low, PART)], sems.at[3 + n % 2]
            )
        )
        stores[n].start()
    total.one(PAIR_CHUNK)
    total.three(QUERY_CHUNK)
    total.two(PAIR_CHUNK)
    total.four(QUERY_CHUNK)
    total.three(PAIR_CHUNK)
    total.five(QUERY_CHUNK)
    total.four(PAIR_CHUNK)
    total.five(PAIR_CHUNK)
    for j in range(KV_HEADS):
        collect.sent(j)
    total.sent()
    for store in stores[-2:]:
        store.wait()


def rear_kernel(
    mixed_ref,
    lse_ref,
    qfeat_ref,
    cos_ref,
    sin_ref,
    rest_ref,
    attend_hbm,
    win_hbm,
    feat_hbm,
    qt_hbm,
    flipped_hbm,
    x_hbm,
    cot_hbm,
    cott_hbm,
    middle_hbm,
    hidden_hbm,
    hiddent_hbm,
    sum_ref,
    out_hbm,
    grad_hbm,
    middle_grad_hbm,
    gradt_ref,
    jointt,
    pairs,
    ra,
    rb,
    r2,
    r1,
    collect_send,
    collect_recv,
    *reduce_scratch,
):
    at = Place()
    tokens = x_hbm.shape[0]
    shard_count, rows, _ = rest_ref.shape
    width = shard_count * rows
    lanes = pairs.shape[2]
    keys = feat_hbm.shape[0]
    greet(at, True)
    total = Reduce(at, sum_chunks(), sum_ref, *reduce_scratch)

    def run(*names):
        def event():
            for name, n in names:
                getattr(total, name)(n)

        return event

    def round_of(t):
        due = [("one", t), ("push", t + 1), ("two", t - 1), ("three", t - 3), ("four", t - 4)]
        return [(name, n) for name, n in due + [("five", t - 5)] if 0 <= n <= OUT_CHUNK]

    forward_events = [
        (2, run(("zero", 0), ("push", 0))),
        (4, run(("zero", 1))),
        (6, run(("zero", 2), *round_of(0))),
        (8, run(("zero", 3))),
        (12, run(("zero", 4), *round_of(1))),
    ]
    backward_events = [
        (0, run(("zero", 5))),
        (1, run(*round_of(2))),
        (4, run(*round_of(3))),
        (7, run(*round_of(4))),
        (10, run(*round_of(5))),
        (12, run(*round_of(6))),
        (13, run(*round_of(7))),
        (14, run(*round_of(8))),
    ]
    last_events = [run(), run(*round_of(9)), run(*round_of(10))]

    pl.run_scoped(
        functools.partial(
            feed_forward,
            at,
            total,
            mixed_ref,
            gradt_ref,
            middle_hbm,
            hidden_hbm,
            hiddent_hbm,
            cot_hbm,
            cott_hbm,
            rest_ref,
            out_hbm,
            middle_grad_hbm,
            forward_events,
        ),
        VMEM((tokens, width), BF),
        VMEM((tokens, width), BF),
        VMEM((tokens, width), F32),
        VMEM((tokens, width), F32),
        VMEM((tokens, width), F32),
        VMEM((shard_count // 2, rows, tokens), BF),
        VMEM((shard_count // 2, rows, tokens), BF),
        VMEM((shard_count // 2, rows, tokens), BF),
        VMEM((shard_count // 2, rows, tokens), BF),
        VMEM((shard_count, rows, tokens), BF),
        VMEM((shard_count, rows, QW), BF),
        VMEM((shard_count, 8, rows), F32),
        VMEM((2, 3, shard_count, rows, SUB), BF),
        VMEM((2, D, PART), F32),
        DMA((3, 3)),
        DMA((4 + 2 * shard_count,)),
    )

    def attention(grads, t2, t1, hidden_own, hidden_give, sems):
        collect = Collect(at, grads, pairs, ra, rb, r2, r1, t2, t1, collect_send, collect_recv)
        loads = []
        for z in range(shard_count // 2):
            for i, (dst, core) in enumerate(((hidden_own, at.c), (hidden_give, 1 - at.c))):
                src = flipped_hbm.at[2 * z + core]
                loads.append(pltpu.make_async_copy(src, dst.at[z], sems.at[i, z]))
        for load in loads:
            load.start()
        pl.run_scoped(
            functools.partial(
                attention_backward,
                at,
                total,
                collect,
                backward_events,
                cos_ref,
                sin_ref,
                qfeat_ref,
                lse_ref,
                mixed_ref,
                gradt_ref,
                jointt,
                win_hbm,
                feat_hbm,
                qt_hbm,
            ),
            *attend_backward_scratch(keys, lanes, tokens),
            VMEM(win_hbm.shape, BF),
            VMEM(feat_hbm.shape, BF),
            VMEM(qt_hbm.shape, BF),
            DMA((3,)),
        )
        for load in loads:
            load.wait()
        pl.run_scoped(
            functools.partial(
                projection_backward,
                at,
                total,
                collect,
                last_events,
                cos_ref,
                sin_ref,
                jointt,
                hidden_own,
                hidden_give,
                x_hbm,
                middle_grad_hbm,
                attend_hbm,
                grad_hbm,
            ),
            VMEM(attend_hbm.shape, BF),
            VMEM((tokens, width), BF),
            VMEM((tokens, width), F32),
            VMEM((tokens, width), F32),
            VMEM((shard_count, 8, rows), F32),
            VMEM((2, D, PART), F32),
            DMA((5,)),
        )

    pl.run_scoped(
        attention,
        VMEM(win_hbm.shape, BF),
        VMEM(pairs.shape, BF),
        VMEM(pairs.shape, BF),
        VMEM((shard_count // 2, rows, tokens), BF),
        VMEM((shard_count // 2, rows, tokens), BF),
        DMA((2, shard_count // 2)),
    )


def rear(in_hbm, in_vmem, number):
    rest, attend, window, _, qt, _, x = in_hbm[:7]
    _, kv_heads, tokens, lanes = window.shape
    shard_count, rows, _ = rest.shape
    columns = sum(width for _, width in sum_chunks())
    pairs = (kv_heads, tokens, lanes)
    return pl.pallas_call(
        rear_kernel,
        out_shape=(
            jax.ShapeDtypeStruct((rows, columns), BF),
            jax.ShapeDtypeStruct((D, tokens), F32),
            jax.ShapeDtypeStruct((D, tokens), F32),
            jax.ShapeDtypeStruct((tokens, shard_count * rows), F32),
        ),
        in_specs=[pl.BlockSpec(memory_space=VMEM)] * len(in_vmem)
        + [pl.BlockSpec(memory_space=ANY)] * len(in_hbm),
        out_specs=(pl.BlockSpec(memory_space=VMEM),) + (pl.BlockSpec(memory_space=ANY),) * 3,
        scratch_shapes=[VMEM(qt.shape, BF), VMEM((JW, tokens), BF), VMEM(pairs, F32)]
        + [VMEM(pairs, BF)] * 4
        + [DMA((4, kv_heads)), DMA((4, kv_heads))]
        + Reduce.scratch(rows, sum_chunks(), 2),
        compiler_params=pltpu.CompilerParams(
            collective_id=number, has_side_effects=True, vmem_limit_bytes=BIG_VMEM
        ),
        name="rear",
    )(*in_vmem, *in_hbm)


def adam_parts(old_weight, gradient, first, second, decay_factor):
    moment = beta_one * first + (1.0 - beta_one) * gradient
    square = beta_two * second + (1.0 - beta_two) * gradient * gradient
    corrected = moment * (1.0 / (1.0 - beta_one**STEP))
    divisor = jnp.sqrt(square * (1.0 / (1.0 - beta_two**STEP))) + adam_eps
    update = -learn_rate * (corrected / divisor + decay_factor * old_weight)
    return moment, square, update


def adam_kernel(grad_scale, own_rows, *refs):
    sums, attend_planes, rest_planes = refs[:3]
    states, passed_in, results, passed_out = refs[3:11], refs[11:13], refs[13:29], refs[29:31]
    buffers, weights, staged = refs[31:47], refs[47:49], refs[49:51]
    in_sems, out_sems = refs[51], refs[52]
    chunks = sum_chunks()
    shard = lax.axis_index("shard")
    loads = [
        pltpu.make_async_copy(attend_planes.at[shard], weights[0], in_sems.at[8]),
        pltpu.make_async_copy(rest_planes.at[shard], weights[1], in_sems.at[9]),
    ]
    order = (0, 1, 3, 2)
    for n in order:
        for i in range(2):
            loads.append(
                pltpu.make_async_copy(
                    states[2 * n + i], buffers[4 * n + 1 + i], in_sems.at[2 * n + i]
                )
            )
    for i in range(2):
        loads.append(pltpu.make_async_copy(passed_in[i], staged[i], in_sems.at[10 + i]))
    for load in loads:
        load.start()
    loads[0].wait()
    loads[1].wait()
    stores = []

    def update(n, where, total, weight, flip):
        gradient, moment, square, changed = buffers[4 * n : 4 * n + 4]
        total = total.astype(F32)
        weight = weight.astype(F32)
        if flip:
            total, weight = total.T[:, :own_rows], weight.T[:, :own_rows]
        total = total * grad_scale
        new_moment, new_square, step = adam_parts(
            weight, total, moment[where], square[where], decay_rate
        )
        gradient[where] = total
        moment[where] = new_moment
        square[where] = new_square
        changed[where] = weight + step

    everything = slice(None)
    for place, n in enumerate(order):
        loads[2 + 2 * place].wait()
        loads[3 + 2 * place].wait()
        if n == 0:
            for chunk, first, count in ((QUERY_CHUNK, 0, QW), (PAIR_CHUNK, QW, 2 * KW)):
                low, cols = chunks[chunk][0], slice(first, first + count)
                update(
                    0,
                    (everything, cols),
                    sums[:own_rows, low : low + count],
                    weights[0][:own_rows, cols],
                    False,
                )
        elif n == 1:
            low = chunks[OUT_CHUNK][0]
            cols = slice(3 * FF, 3 * FF + QW)
            update(
                1, (everything, everything), sums[:, low : low + QW], weights[1][:, cols], True
            )
        else:
            for c in range(FF // CHUNK):
                for part in (0, 1) if n == 2 else (2,):
                    low = 3 * CHUNK * c + CHUNK * part
                    first = part * FF + CHUNK * c
                    total = sums[:own_rows, low : low + CHUNK]
                    weight = weights[1][:own_rows, first : first + CHUNK]
                    column = first if n == 2 else first - 2 * FF
                    cols = slice(column, column + CHUNK)
                    update(n, (everything, cols), total, weight, False)
        for i in range(4):
            store = pltpu.make_async_copy(
                buffers[4 * n + i], results[4 * n + i], out_sems.at[4 * n + i]
            )
            store.start()
            stores.append(store)
        if place < 2:
            loads[10 + place].wait()
            store = pltpu.make_async_copy(
                staged[place], passed_out[place], out_sems.at[16 + place]
            )
            store.start()
            stores.append(store)
    for store in stores:
        store.wait()


def adam(grad_scale, own_rows, sums, attend_planes, rest_planes, states, passed):
    flat = [array for pair in states for array in pair]
    shapes = [pair[0].shape for pair in states]
    return pl.pallas_call(
        functools.partial(adam_kernel, grad_scale, own_rows),
        out_shape=tuple(jax.ShapeDtypeStruct(shape, F32) for shape in shapes for _ in range(4))
        + tuple(jax.ShapeDtypeStruct(array.shape, array.dtype) for array in passed),
        in_specs=[pl.BlockSpec(memory_space=VMEM)] + [pl.BlockSpec(memory_space=ANY)] * 12,
        out_specs=(pl.BlockSpec(memory_space=ANY),) * 18,
        scratch_shapes=[VMEM(shape, F32) for shape in shapes for _ in range(4)]
        + [VMEM(attend_planes.shape[1:], BF), VMEM(rest_planes.shape[1:], BF)]
        + [VMEM(array.shape, F32) for array in passed]
        + [DMA((12,)), DMA((18,))],
        compiler_params=pltpu.CompilerParams(vmem_limit_bytes=BIG_VMEM),
        name="adam",
    )(sums, attend_planes, rest_planes, *flat, *passed)


def spread_pairs(pairs, reach):
    devices = range(lax.axis_size("shard"))
    blocks = []
    for distance in range(reach, 0, -1):
        route = [(i - distance, i) for i in devices if i - distance in devices]
        blocks.append(lax.ppermute(pairs, "shard", route))
    return jnp.stack(blocks + [pairs])


def collect_pairs(grads, reach):
    devices = range(lax.axis_size("shard"))
    own = grads[reach].astype(F32)
    for distance in range(1, reach + 1):
        route = [(i, i - distance) for i in devices if i - distance in devices]
        own = own + lax.ppermute(grads[reach - distance], "shard", route).astype(F32)
    return own


def angles(positions):
    half_dim = HEAD_DIM // 2
    inverse = rope_base ** (-(2.0 * jnp.arange(half_dim, dtype=F32) / HEAD_DIM))
    phases = positions.astype(F32)[:, None] * inverse[None, :]
    return (jnp.cos(phases)[:, None, :], jnp.sin(phases)[:, None, :])


def rotate(tensor, cosine_table, sine_table):
    half_dim = HEAD_DIM // 2
    front, back = tensor[..., :half_dim], tensor[..., half_dim:]
    return jnp.concatenate(
        [front * cosine_table - back * sine_table, back * cosine_table + front * sine_table],
        axis=-1,
    )


def norm_back(upstream, normed, scale_rows):
    mean = jnp.sum(upstream * normed, axis=-1, keepdims=True) * (1.0 / D)
    return scale_rows * (upstream - normed * mean)


def adam_step(weight_now, gradient, first, second, decay_factor):
    moment, square, update = adam_parts(
        weight_now.astype(F32), gradient, first, second, decay_factor
    )
    return (gradient, moment, square, update)


def shards(
    direct,
    block_input,
    block_cotangent,
    lengths,
    attend_gain,
    attend_weight,
    output_weight,
    expand_gain,
    expand_weight,
    shrink_weight,
    attend_gain_first,
    attend_weight_first,
    output_weight_first,
    expand_gain_first,
    expand_weight_first,
    shrink_weight_first,
    attend_gain_second,
    attend_weight_second,
    output_weight_second,
    expand_gain_second,
    expand_weight_second,
    shrink_weight_second,
):
    tokens = block_input.shape[0]
    shard_count = lax.axis_size("shard")
    token_count = tokens * shard_count * lax.axis_size("rep")
    reach = (MAXLEN - 2) // tokens + 1
    own_rows = attend_weight.shape[0]
    rows = -(-(own_rows + 2) // 16) * 16
    width = shard_count * rows

    def padded(tensor):
        blocks = tensor.reshape(tokens, shard_count, own_rows)
        return jnp.pad(blocks, ((0, 0), (0, 0), (0, rows - own_rows))).reshape(tokens, width)

    def unpadded(tensor):
        return tensor.reshape(tokens, shard_count, rows)[:, :, :own_rows].reshape(tokens, D)

    def with_gain(weight, gain):
        if gain is None:
            return jnp.pad(weight, ((0, rows - own_rows), (0, 0)))
        tail = jnp.pad(gain[None, :], ((0, rows - own_rows - 1), (0, weight.shape[1] - own_rows)))
        return jnp.concatenate([weight, tail], axis=0)

    def gain_of(planes, column):
        return jnp.pad(
            planes[:, own_rows, column : column + own_rows], ((0, 0), (0, rows - own_rows))
        ).reshape(1, width).astype(F32)

    def add_gain(planes, term, column):
        row = term.reshape(shard_count, 1, rows).astype(planes.dtype)
        return lax.dynamic_update_slice(planes, row, (0, own_rows, column))

    def in_chunks(expand, shrink):
        parts = jnp.concatenate([expand, shrink], axis=1).reshape(-1, 3, FF // CHUNK, CHUNK)
        return parts.transpose(0, 2, 1, 3).reshape(-1, 3 * FF)

    if direct:
        weights = (
            attend_gain[None, :],
            attend_weight,
            expand_gain[None, :],
            expand_weight,
            shrink_weight.T,
            output_weight,
        )
        made = front(lengths, block_input.T, block_cotangent.T, weights, shard_count, 0)
        rest_planes, attend_planes = made[:2]
        sums, block_output, input_gradient, _ = rear(made[:12], made[12:], 1)
    else:
        first_row = lax.axis_index("shard") * tokens
        local_index = first_row + jnp.arange(tokens, dtype=jnp.int32)
        key_index = first_row - reach * tokens + jnp.arange((reach + 1) * tokens, dtype=jnp.int32)
        ends = jnp.cumsum(lengths[0], dtype=jnp.int32)
        starts = ends - lengths[0]
        seq_count = lengths.shape[1]
        in_key = (key_index[:, None] >= starts[None, :]) & (key_index[:, None] < ends[None, :])
        in_query = (local_index[None, :] >= starts[:, None]) & (local_index[None, :] < ends[:, None])
        lanes = 2 * HEAD_DIM
        feat = jnp.concatenate(
            [
                in_key.astype(BF),
                (key_index < 0).astype(BF)[:, None],
                jnp.zeros((key_index.shape[0], ONES - seq_count - 1), BF),
                jnp.ones((key_index.shape[0], lanes - ONES), BF),
            ],
            axis=1,
        )
        qfeat = jnp.concatenate(
            [
                jnp.where(in_query, 0.0, NEG).astype(BF),
                jnp.full((1, tokens), NEG, BF),
                jnp.zeros((lanes - seq_count - 1, tokens), BF),
            ],
            axis=0,
        )
        start_index = jnp.sum(in_query * starts[:, None], axis=0, dtype=jnp.int32)
        cosine_table, sine_table = angles(local_index - start_index)
        attend_own = with_gain(attend_weight, attend_gain)
        rest_own = jnp.concatenate(
            [
                with_gain(jnp.concatenate([expand_weight, shrink_weight.T], axis=1), None),
                with_gain(output_weight.T, expand_gain),
            ],
            axis=1,
        )
        attend_planes = lax.all_gather(attend_own, "shard", axis=0)
        rest_planes = lax.all_gather(rest_own, "shard", axis=0)
        gain_one, gain_two = gain_of(attend_planes, 0), gain_of(rest_planes, 3 * FF)
        joint_weight = attend_planes.reshape(width, JW)
        rest = rest_planes.reshape(width, rest_own.shape[1])
        expand_full, shrink_full, out_full = rest[:, : 2 * FF], rest[:, 2 * FF : 3 * FF], rest[:, 3 * FF :]
        real = (jnp.arange(width, dtype=jnp.int32) % rows < own_rows)[None, :]

        inputs = padded(block_input).astype(F32)
        scale_one = lax.rsqrt(jnp.sum(inputs * inputs, axis=-1, keepdims=True) * (1.0 / D) + eps_norm)
        normed_one = inputs * scale_one
        hidden_one = (normed_one * gain_one).astype(BF)
        joint = dot(hidden_one, joint_weight)
        queries = rotate(joint[:, :QW].reshape(tokens, HEADS, HEAD_DIM), cosine_table, sine_table)
        key_rows = rotate(
            joint[:, QW : QW + KW].reshape(tokens, KV_HEADS, HEAD_DIM), cosine_table, sine_table
        )
        values = joint[:, QW + KW :].reshape(tokens, KV_HEADS, HEAD_DIM)
        pairs = jnp.concatenate([key_rows, values], axis=-1).astype(BF).transpose(1, 0, 2)
        qt = queries.astype(BF).reshape(tokens, QW).T
        window = spread_pairs(pairs, reach)
        mixedt, lse = attend_forward(window, feat, qt, qfeat)
        middle = inputs + jnp.where(real, dot(mixedt, out_full, 0, 1), 0.0)
        scale_two = lax.rsqrt(jnp.sum(middle * middle, axis=-1, keepdims=True) * (1.0 / D) + eps_norm)
        normed_two = middle * scale_two
        hidden_two = (normed_two * gain_two).astype(BF)
        gate_up = dot(hidden_two, expand_full)
        gate_value, upper_value = gate_up[:, :FF], gate_up[:, FF:]
        sigmoid_gate = jax.nn.sigmoid(gate_value)
        inner_rows = (gate_value * sigmoid_gate * upper_value).astype(BF)
        block_output = middle + dot(inner_rows, shrink_full, 1, 1)

        cotangent = padded(block_cotangent)
        shrink_term = dot(cotangent, inner_rows, 0, 0)
        inner_grad = dot(cotangent, shrink_full)
        gate_grad = (
            inner_grad * upper_value * sigmoid_gate * (1.0 + gate_value * (1.0 - sigmoid_gate))
        ).astype(BF)
        upper_grad = (inner_grad * gate_value * sigmoid_gate).astype(BF)
        gate_up_grad = jnp.concatenate([gate_grad, upper_grad], axis=1)
        expand_term = dot(hidden_two, gate_up_grad, 0, 0)
        hidden_two_grad = jnp.where(real, dot(gate_up_grad, expand_full, 1, 1), 0.0)
        gain_two_term = jnp.sum(hidden_two_grad * normed_two, axis=0)
        middle_grad = cotangent.astype(F32) + norm_back(
            hidden_two_grad * gain_two, normed_two, scale_two
        )
        branch_grad = middle_grad.astype(BF)
        output_term = dot(branch_grad, mixedt, 0, 1)
        gradt = dot(out_full, branch_grad, 0, 1).astype(BF)
        dqt, dwindow = attend_backward(window, feat, qt, qfeat, gradt, mixedt, lse)
        own_pairs = collect_pairs(dwindow, reach)
        block_output = unpadded(block_output).T
        own_pairs = own_pairs.transpose(1, 0, 2)
        dq = dqt.T.reshape(tokens, HEADS, HEAD_DIM)
        query_raw = rotate(dq, cosine_table, -sine_table).reshape(tokens, QW)
        key_raw = rotate(own_pairs[..., :HEAD_DIM], cosine_table, -sine_table).reshape(tokens, KW)
        value_raw = own_pairs[..., HEAD_DIM:].reshape(tokens, KW)
        joint_grad = jnp.concatenate([query_raw, key_raw, value_raw], axis=1).astype(BF)
        joint_term = dot(hidden_one, joint_grad, 0, 0).astype(BF)
        hidden_one_grad = jnp.where(real, dot(joint_grad, joint_weight, 1, 1), 0.0)
        gain_one_term = jnp.sum(hidden_one_grad * normed_one, axis=0)
        input_gradient = middle_grad + norm_back(hidden_one_grad * gain_one, normed_one, scale_one)
        to_lanes = ((0, 0), (0, up_to_lanes(QW) - QW))
        terms = jnp.concatenate(
            [
                in_chunks(expand_term, shrink_term).astype(BF),
                jnp.pad(output_term.astype(BF), to_lanes),
                jnp.pad(joint_term[:, :QW], to_lanes),
                joint_term[:, QW:],
            ],
            axis=1,
        ).reshape(shard_count, rows, -1)
        terms = add_gain(terms, gain_two_term, sum_chunks()[OUT_CHUNK][0])
        terms = add_gain(terms, gain_one_term, sum_chunks()[PAIR_CHUNK][0])
        sums = lax.psum(lax.psum_scatter(terms, "shard", scatter_dimension=0), "rep")
        input_gradient = unpadded(input_gradient).T

    grad_scale = grad_factor * token_count ** (-0.5)
    def gain_sum(chunk):
        first = sum_chunks()[chunk][0]
        return sums[own_rows, first : first + own_rows]

    first_gain, second_gain = (
        adam_step(weight, total.astype(F32) * grad_scale, first, second, 0.0)
        for weight, total, first, second in (
            (
                attend_gain,
                gain_sum(PAIR_CHUNK),
                attend_gain_first,
                attend_gain_second,
            ),
            (
                expand_gain,
                gain_sum(OUT_CHUNK),
                expand_gain_first,
                expand_gain_second,
            ),
        )
    )
    matrices = adam(
        grad_scale,
        own_rows,
        sums,
        attend_planes,
        rest_planes,
        (
            (attend_weight_first, attend_weight_second),
            (output_weight_first, output_weight_second),
            (expand_weight_first, expand_weight_second),
            (shrink_weight_first.T, shrink_weight_second.T),
        ),
        (block_output, input_gradient),
    )
    first_joint, first_output, second_expand, second_shrink = (
        matrices[4 * n : 4 * n + 4] for n in range(4)
    )
    second_shrink = [result.T for result in second_shrink]
    block_output, input_gradient = (result.T for result in matrices[16:])
    steps = (first_gain, first_joint, first_output, second_gain, second_expand, second_shrink)
    return (block_output, input_gradient, *[step[i] for i in range(4) for step in steps])


def solution(mesh):
    whole_rows = P(("rep", "shard"), None)
    state = (P("shard"), P("shard", None), P(None, "shard")) * 2
    direct = mesh.shape["rep"] == 4 and mesh.shape["shard"] == 8
    return jax.shard_map(
        functools.partial(shards, direct),
        mesh=mesh,
        in_specs=(whole_rows, whole_rows, P("rep", None), *state, *state, *state),
        out_specs=(whole_rows, whole_rows, *state, *state, *state, *state),
        check_vma=False,
    )
```

```python
import functools
import math

import jax
import jax.numpy as jnp
import numpy as np
from jax import lax
from jax.experimental import pallas as pl
from jax.experimental.pallas import tpu as pltpu
from jax.sharding import PartitionSpec as P

HEADS = 15
KV_HEADS = 5
HEAD_DIM = 64
GROUP = HEADS // KV_HEADS
FF = 2560
MAXLEN = 2048
STEP = 10
QW = 960
KW = 320
JW = QW + 2 * KW
D = 960

eps_norm = 1e-05
rope_base = 100000.0
beta_one = 0.9
beta_two = 0.95
adam_eps = 1e-08
learn_rate = 0.05
decay_rate = 0.1
grad_factor = 4.0

F32 = jnp.float32
BF = jnp.bfloat16
MESH = pl.DeviceIdType.MESH
ANY = pl.ANY
VMEM = pltpu.VMEM
DMA = pltpu.SemaphoreType.DMA

QC = 256
KB = 768
HALF = 64
ONES = 112
NEG = -1e30
EXP_SCALE = HEAD_DIM**-0.5 * math.log2(math.e)
BIG_VMEM = 60 * 2**20
PART = 128


def dot(a, b, ca=1, cb=0):
    return lax.dot_general(a, b, (((ca,), (cb,)), ((), ())), preferred_element_type=F32)


def causal_tile():
    key = lax.broadcasted_iota(jnp.int32, (QC, QC), 0)
    query = lax.broadcasted_iota(jnp.int32, (QC, QC), 1)
    return key <= query


def mask_last(scores, causal):
    last = jnp.where(causal, scores[KB - QC :], NEG)
    return jnp.concatenate([scores[: KB - QC], last], axis=0)


def attend_forward_setup(feat_ref, qfeat_ref, kvf, vt, qa):
    lanes = feat_ref.shape[1]
    kvf[:, lanes:] = feat_ref[...]
    qa[HALF:lanes, :] = jnp.zeros((lanes - HALF, qa.shape[1]), BF)
    qa[lanes:, :] = qfeat_ref[...]
    vt[HALF:, :] = jnp.ones((vt.shape[0] - HALF, vt.shape[1]), BF)


def attend_forward_keys(j, kv_ref, kvf, vt):
    blocks, _, rows, lanes = kv_ref.shape
    for block in range(blocks):
        part = kv_ref[block, j]
        kvf[block * rows : (block + 1) * rows, :lanes] = part
        vt[:HALF, block * rows : (block + 1) * rows] = part.T[HALF:, :]


def attend_forward_head(h, qt_ref, mixed_ref, lse_ref, kvf, vt, qa, sb):
    tokens = qt_ref.shape[1]
    steps = (kvf.shape[0] - (tokens - QC)) // KB
    causal = causal_tile()
    row = pl.multiple_of(h * HEAD_DIM, HEAD_DIM)
    qa[:HALF, :] = qt_ref[pl.ds(row, HEAD_DIM), :]
    tops = []
    for chunk in range(tokens // QC):
        low = chunk * QC
        highest = None
        for b in range(steps):
            first = low + b * KB
            s = dot(kvf[first : first + KB, :], qa[:, low : low + QC])
            if b == steps - 1:
                s = mask_last(s, causal)
            sb[chunk, b * KB : (b + 1) * KB, :] = s
            peak = jnp.max(s.reshape(KB // 8, 8, QC), axis=0)
            highest = peak if highest is None else jnp.maximum(highest, peak)
        tops.append(jnp.max(highest, axis=0, keepdims=True))
    for chunk in range(tokens // QC):
        low = chunk * QC
        shift = tops[chunk] * EXP_SCALE
        total = None
        for b in range(steps):
            first = low + b * KB
            s = sb[chunk, b * KB : (b + 1) * KB, :]
            p = jnp.exp2(s * EXP_SCALE - shift).astype(BF)
            term = dot(vt[:, first : first + KB], p)
            total = term if total is None else total + term
        weight = total[HALF : HALF + 1, :]
        mixed_ref[pl.ds(row, HEAD_DIM), low : low + QC] = (
            total[:HALF, :] * (1.0 / weight)
        ).astype(BF)
        lse_ref[pl.ds(h, 1), :, low : low + QC] = (
            tops[chunk] * HEAD_DIM**-0.5 + jnp.log(weight)
        )[None]


def attend_forward_scratch(keys, lanes, tokens):
    return [
        VMEM((keys, 2 * lanes), BF),
        VMEM((HALF + 16, keys), BF),
        VMEM((2 * lanes, tokens), BF),
        VMEM((tokens // QC, keys - (tokens - QC), QC), F32),
    ]


def attend_forward_kernel(
    kv_ref, feat_ref, qt_ref, qfeat_ref, mixed_ref, lse_ref, kvf, vt, qa, sb
):
    attend_forward_setup(feat_ref, qfeat_ref, kvf, vt, qa)

    def key_head(j, _):
        attend_forward_keys(j, kv_ref, kvf, vt)

        def head(g, _):
            attend_forward_head(j * GROUP + g, qt_ref, mixed_ref, lse_ref, kvf, vt, qa, sb)
            return 0

        lax.fori_loop(0, GROUP, head, 0)
        return 0

    lax.fori_loop(0, kv_ref.shape[1], key_head, 0)


def attend_forward(window, feat, qt, qfeat):
    blocks, kv_heads, rows, lanes = window.shape
    tokens = qt.shape[1]
    return pl.pallas_call(
        attend_forward_kernel,
        out_shape=(
            jax.ShapeDtypeStruct(qt.shape, BF),
            jax.ShapeDtypeStruct((HEADS, 1, tokens), F32),
        ),
        scratch_shapes=attend_forward_scratch(blocks * rows, lanes, tokens),
        compiler_params=pltpu.CompilerParams(vmem_limit_bytes=BIG_VMEM),
        name="attend_forward",
    )(window, feat, qt, qfeat)


def three_parts(value, rows):
    one = value.astype(BF).astype(F32)
    two = (value - one).astype(BF).astype(F32)
    three = value - one - two
    shape = (rows, value.shape[1])
    place = lax.broadcasted_iota(jnp.int32, shape, 0)
    parts = [jnp.broadcast_to(part, shape) for part in (one, two, three)]
    chosen = jnp.where(
        place == 0, parts[0], jnp.where(place == 1, parts[1], jnp.where(place == 2, parts[2], 0.0))
    )
    return chosen.astype(BF)


def attend_backward_setup(feat_ref, kvf, qa, da, rhs):
    lanes = feat_ref.shape[1]
    kvf[:, lanes:] = feat_ref[...]
    qa[HALF:lanes, :] = jnp.zeros((lanes - HALF, qa.shape[1]), BF)
    da[...] = jnp.zeros_like(da)
    rhs[...] = jnp.zeros_like(rhs)


def attend_backward_keys(j, kv_ref, kvf, kt, acc):
    blocks, _, rows, lanes = kv_ref.shape
    for block in range(blocks):
        part = kv_ref[block, j]
        kvf[block * rows : (block + 1) * rows, :lanes] = part
        kt[:, block * rows : (block + 1) * rows] = part.T[:HALF, :]
    acc[...] = jnp.zeros_like(acc)


def attend_backward_head(
    h, put_query, qt_ref, qfeat_ref, gradt_ref, mixed_ref, lse_ref, kvf, kt, qa, da, acc, rhs
):
    tokens = qt_ref.shape[1]
    lanes = qfeat_ref.shape[0]
    steps = (kvf.shape[0] - (tokens - QC)) // KB
    causal = causal_tile()
    extra = lanes - ONES
    row = pl.multiple_of(h * HEAD_DIM, HEAD_DIM)
    q = qt_ref[pl.ds(row, HEAD_DIM), :]
    grad = gradt_ref[pl.ds(row, HEAD_DIM), :]
    qa[:HALF, :] = q
    da[HALF:lanes, :] = grad
    mixed = mixed_ref[pl.ds(row, HEAD_DIM), :].astype(F32)
    row_total = jnp.sum(grad.astype(F32) * mixed, axis=0, keepdims=True)
    lse = lse_ref[pl.ds(h, 1), :, :][0]
    qa[lanes : lanes + ONES, :] = qfeat_ref[:ONES, :]
    qa[lanes + ONES :, :] = three_parts(-(HEAD_DIM**0.5) * lse, extra)
    da[lanes + ONES :, :] = three_parts(-row_total, extra)
    query_grads = [None] * (tokens // QC)
    for chunk in range(tokens // QC):
        low = chunk * QC
        rhs[chunk, :HALF, :QC] = q[:, low : low + QC]
        rhs[chunk, HALF:, QC:] = grad[:, low : low + QC]
    for b in range(steps):
        for chunk in range(tokens // QC):
            low = chunk * QC
            first = low + b * KB
            keys = kvf[first : first + KB, :]
            s = dot(keys, qa[:, low : low + QC])
            if b == steps - 1:
                s = mask_last(s, causal)
            p = jnp.exp2(s * EXP_SCALE)
            dp = dot(keys, da[:, low : low + QC])
            ds = (p * dp).astype(BF)
            both = jnp.concatenate([ds, p.astype(BF)], axis=1)
            acc[first : first + KB, :] += dot(both, rhs[chunk], 1, 1)
            term = dot(kt[:, first : first + KB], ds)
            old = query_grads[chunk]
            query_grads[chunk] = term if old is None else old + term
    for chunk in range(tokens // QC):
        low = chunk * QC
        put_query(row, low, query_grads[chunk] * HEAD_DIM**-0.5)


def attend_backward_done(j, acc, dkv_ref):
    blocks, _, rows, lanes = dkv_ref.shape
    lane = lax.broadcasted_iota(jnp.int32, (1, lanes), 1)
    factor = jnp.where(lane < HALF, HEAD_DIM**-0.5, 1.0)
    for block in range(blocks):
        part = acc[block * rows : (block + 1) * rows, :]
        dkv_ref[block, j] = (part * factor).astype(dkv_ref.dtype)


def attend_backward_scratch(keys, lanes, tokens):
    return [
        VMEM((keys, 2 * lanes), BF),
        VMEM((HALF, keys), BF),
        VMEM((2 * lanes, tokens), BF),
        VMEM((2 * lanes, tokens), BF),
        VMEM((keys, lanes), F32),
        VMEM((tokens // QC, lanes, 2 * QC), BF),
    ]


def attend_backward_kernel(
    kv_ref, feat_ref, qt_ref, qfeat_ref, gradt_ref, mixed_ref, lse_ref, dq_ref, dkv_ref, *scratch
):
    kvf, kt, qa, da, acc, rhs = scratch
    attend_backward_setup(feat_ref, kvf, qa, da, rhs)

    def put_query(row, low, value):
        dq_ref[pl.ds(row, HEAD_DIM), low : low + QC] = value

    def key_head(j, _):
        attend_backward_keys(j, kv_ref, kvf, kt, acc)

        def head(g, _):
            attend_backward_head(
                j * GROUP + g,
                put_query,
                qt_ref,
                qfeat_ref,
                gradt_ref,
                mixed_ref,
                lse_ref,
                *scratch,
            )
            return 0

        lax.fori_loop(0, GROUP, head, 0)
        attend_backward_done(j, acc, dkv_ref)
        return 0

    lax.fori_loop(0, kv_ref.shape[1], key_head, 0)


def attend_backward(window, feat, qt, qfeat, gradt, mixed, lse):
    blocks, kv_heads, rows, lanes = window.shape
    tokens = qt.shape[1]
    return pl.pallas_call(
        attend_backward_kernel,
        out_shape=(
            jax.ShapeDtypeStruct(qt.shape, F32),
            jax.ShapeDtypeStruct(window.shape, BF),
        ),
        scratch_shapes=attend_backward_scratch(blocks * rows, lanes, tokens),
        compiler_params=pltpu.CompilerParams(vmem_limit_bytes=BIG_VMEM),
        name="attend_backward",
    )(window, feat, qt, qfeat, gradt, mixed, lse)


class Place:
    def __init__(self):
        self.r = lax.axis_index("rep")
        self.s = lax.axis_index("shard")
        self.x, self.y = lax.rem(self.r, 2), self.r // 2
        self.z, self.c = self.s // 2, lax.rem(self.s, 2)
        self.rx = self.y * 2 + (1 - self.x)
        self.ry = (1 - self.y) * 2 + self.x
        self.rd = 3 - self.r
        self.x_side = (self.rx, self.s)
        self.y_side = (self.ry, self.s)
        self.core_side = (self.r, self.z * 2 + (1 - self.c))
        self.has_later, self.has_earlier = self.z < 3, self.z > 0
        self.later = (self.r, lax.min(self.s + 2, 7))
        self.earlier = (self.r, lax.max(self.s - 2, 0))
        self.two_earlier = (self.r, lax.max(self.s - 4, 0))

    def z_to(self, k):
        return lax.rem(self.z + k, 4)

    def z_side(self, k):
        return (self.r, self.z_to(k) * 2 + self.c)

    def arrival(self, i):
        low = self.z < 2
        first = jnp.where(self.z == 0, 1, jnp.where(self.z == 1, 0, jnp.where(self.z == 2, 3, 2)))
        if i == 0:
            return first
        if i == 1:
            return jnp.where(low, 2, 1)
        return jnp.where(low, 3, 0)


def greet(at, whole_line):
    barrier = pltpu.get_barrier_semaphore()

    def signal(device):
        pl.semaphore_signal(barrier, inc=1, device_id=device, device_id_type=MESH)

    for device in (at.x_side, at.y_side, at.core_side):
        signal(device)
    if whole_line:
        for k in (1, 2, 3):
            signal(at.z_side(k))
        pl.semaphore_wait(barrier, 6)
        return

    @pl.when(at.has_later)
    def _():
        signal(at.later)

    @pl.when(at.has_earlier)
    def _():
        signal(at.earlier)

    count = 3 + jnp.where(at.has_later, 1, 0) + jnp.where(at.has_earlier, 1, 0)
    pl.semaphore_wait(barrier, count)


def remote(src, dst, send, recv, device):
    return pltpu.make_async_remote_copy(
        src_ref=src, dst_ref=dst, send_sem=send, recv_sem=recv, device_id=device, device_id_type=MESH
    )


class Gather:
    COUNT = 31

    def __init__(self, at, own, full, columns, local_sem, send, recv):
        self.at, self.own, self.full, self.columns = at, own, full, columns
        self.local_sem, self.send, self.recv = local_sem, send, recv
        self.rows = own.shape[0]
        self.quarter, self.half = self.rows // 4, self.rows // 8

    def piece(self, plane, owner, part=None):
        start = owner * self.quarter + (0 if part is None else part * self.half)
        size = self.quarter if part is None else self.half
        return self.full.at[
            plane, pl.ds(pl.multiple_of(start, self.half), size), pl.ds(*self.columns)
        ]

    def copy(self, index, src, dst, device, landed=None):
        return remote(
            src, dst, self.send.at[index], self.recv.at[index if landed is None else landed], device
        )

    def core_copy(self):
        src = self.own.at[:, pl.ds(*self.columns)]
        return self.copy(
            28, src, self.full.at[self.at.s, :, pl.ds(*self.columns)], self.at.core_side
        )

    def local_copy(self):
        return pltpu.make_async_copy(
            self.own.at[:, pl.ds(*self.columns)],
            self.full.at[self.at.s, :, pl.ds(*self.columns)],
            self.local_sem,
        )

    def z_copy(self, up):
        at = self.at
        src = self.own.at[
            pl.ds(pl.multiple_of(at.r * self.quarter, self.quarter), self.quarter),
            pl.ds(*self.columns),
        ]
        device = at.later if up else at.earlier
        return self.copy(29 if up else 30, src, self.piece(at.s, at.r), device, at.z)

    def start_core(self):
        self.local_copy().start()
        self.core_copy().start()

    def start_z(self):
        @pl.when(self.at.has_later)
        def _():
            self.z_copy(True).start()

        @pl.when(self.at.has_earlier)
        def _():
            self.z_copy(False).start()

    def plane(self, i, other=False):
        c = 1 - self.at.c if other else self.at.c
        return self.at.arrival(i) * 2 + c

    def forwards(self, i):
        at = self.at
        chip = at.arrival(i)
        got = self.piece(self.plane(i), at.r)
        return [
            ((chip < at.z) & at.has_later, self.copy(i, got, got, at.later, chip)),
            ((chip > at.z) & at.has_earlier, self.copy(i, got, got, at.earlier, chip)),
        ]

    def out_copies(self, i):
        at, plane = self.at, self.plane(i)
        got = self.piece(plane, at.r)
        return [
            self.copy(4 + i, got, got, at.x_side),
            self.copy(7 + i, got, got, at.y_side),
            self.copy(10 + i, got, got, at.core_side),
        ]

    def cross_copies(self, i):
        at, plane = self.at, self.plane(i)
        one, two = self.piece(plane, at.rx, 0), self.piece(plane, at.ry, 1)
        from_x, from_y = self.piece(plane, at.rx), self.piece(plane, at.ry)
        return [
            self.copy(13 + i, one, one, at.y_side),
            self.copy(16 + i, from_x, from_x, at.core_side),
            self.copy(19 + i, two, two, at.x_side),
            self.copy(22 + i, from_y, from_y, at.core_side),
        ]

    def last_copy(self, i):
        got = self.piece(self.plane(i), self.at.rd)
        return self.copy(25 + i, got, got, self.at.core_side)

    def arrive(self, landed, ref):
        remote(
            ref, ref, self.send.at[landed], self.recv.at[landed], self.at.core_side
        ).wait_recv()

    def z(self, i):
        at = self.at
        self.arrive(at.arrival(i), self.piece(self.plane(i), at.r))
        for condition, copy in self.forwards(i):
            pl.when(condition)(copy.start)
        for copy in self.out_copies(i):
            copy.start()

    def cross(self, i):
        at, plane = self.at, self.plane(i)
        copies = self.cross_copies(i)
        self.arrive(4 + i, self.piece(plane, at.rx))
        copies[0].start()
        copies[1].start()
        self.arrive(7 + i, self.piece(plane, at.ry))
        copies[2].start()
        copies[3].start()

    def last(self, i):
        at, plane = self.at, self.plane(i)
        self.arrive(13 + i, self.piece(plane, at.rd, 0))
        self.arrive(19 + i, self.piece(plane, at.rd, 1))
        self.last_copy(i).start()

    def landed(self):
        at = self.at
        self.arrive(28, self.full.at[at.core_side[1], :, pl.ds(*self.columns)])
        for i in range(3):
            plane = self.plane(i, True)
            self.arrive(10 + i, self.piece(plane, at.r))
            self.arrive(16 + i, self.piece(plane, at.rx))
            self.arrive(22 + i, self.piece(plane, at.ry))
            self.arrive(25 + i, self.piece(plane, at.rd))
        self.local_copy().wait()

    def sent(self):
        at = self.at
        self.core_copy().wait_send()
        pl.when(at.has_later)(self.z_copy(True).wait_send)
        pl.when(at.has_earlier)(self.z_copy(False).wait_send)
        for i in range(3):
            for condition, copy in self.forwards(i):
                pl.when(condition)(copy.wait_send)
            for copy in self.out_copies(i) + self.cross_copies(i) + [self.last_copy(i)]:
                copy.wait_send()


class Spread:
    def __init__(self, at, win, send, recv):
        self.at, self.win, self.sems = at, win, (send, recv)
        even = at.c == 0
        self.near, self.far = jnp.where(even, 1, 3), jnp.where(even, 3, 1)

    def copy(self, n, j, src, dst, device):
        send, recv = self.sems
        return remote(
            self.win.at[src, j], self.win.at[dst, j], send.at[n, j], recv.at[n, j], device
        )

    def first(self, j):
        return self.copy(0, j, 4, 2, self.at.later)

    def twin_own(self, j):
        return self.copy(1, j, 4, 3, self.at.core_side)

    def second(self, j):
        return self.copy(2, j, 2, 0, self.at.later)

    def twin_near(self, j, place):
        return self.copy(3, j, 2, place, self.at.core_side)

    def twin_far(self, j):
        return self.copy(4, j, 0, 1, self.at.core_side)

    def clear(self):
        for block in range(4):
            @pl.when(self.at.s < 4 - block)
            def _(block=block):
                self.win[block] = jnp.zeros(self.win.shape[1:], self.win.dtype)

    def start(self, j):
        pl.when(self.at.has_later)(self.first(j).start)
        pl.when(self.at.c == 0)(self.twin_own(j).start)

    def one(self, j):
        at = self.at

        @pl.when(at.has_earlier)
        def _():
            self.first(j).wait_recv()
            self.twin_near(j, self.near).start()
            pl.when(at.has_later)(self.second(j).start)

    def two(self, j):
        at = self.at

        @pl.when(at.z > 1)
        def _():
            self.second(j).wait_recv()
            pl.when(at.c == 1)(self.twin_far(j).start)

    def landed(self, j):
        at = self.at
        pl.when(at.c == 1)(self.twin_own(j).wait_recv)
        pl.when(at.has_earlier)(self.twin_near(j, self.far).wait_recv)
        pl.when((at.c == 0) & (at.z > 1))(self.twin_far(j).wait_recv)

    def sent(self, j):
        at = self.at
        pl.when(at.has_later)(self.first(j).wait_send)
        pl.when(at.c == 0)(self.twin_own(j).wait_send)
        pl.when(at.has_earlier)(self.twin_near(j, self.near).wait_send)
        pl.when(at.has_earlier & at.has_later)(self.second(j).wait_send)
        pl.when((at.c == 1) & (at.z > 1))(self.twin_far(j).wait_send)


class Collect:
    def __init__(self, at, grads, out, ra, rb, r2, r1, t2, t1, send, recv):
        self.at, self.grads, self.out = at, grads, out
        self.ra, self.rb, self.r2, self.r1, self.t2, self.t1 = ra, rb, r2, r1, t2, t1
        self.sems = (send, recv)

    def copy(self, n, j, src, dst, device):
        send, recv = self.sems
        return remote(src, dst, send.at[n, j], recv.at[n, j], device)

    def twin_a(self, j):
        return self.copy(0, j, self.grads.at[3, j], self.ra.at[j], self.at.core_side)

    def twin_b(self, j):
        return self.copy(1, j, self.grads.at[1, j], self.rb.at[j], self.at.core_side)

    def far(self, j, relayed=True):
        device = self.at.earlier if relayed else self.at.two_earlier
        return self.copy(2, j, self.t2.at[j], self.r2.at[j], device)

    def near(self, j):
        return self.copy(3, j, self.t1.at[j], self.r1.at[j], self.at.earlier)

    def start(self, j):
        self.twin_b(j).start()
        self.twin_a(j).start()

    def one(self, j, relayed=True):
        self.twin_b(j).wait_recv()
        self.twin_a(j).wait_recv()
        even = self.at.c == 0
        from_a, from_b = self.ra[j].astype(F32), self.rb[j].astype(F32)
        none = jnp.zeros_like(from_a)
        self.t2[j] = (self.grads[0, j].astype(F32) + jnp.where(even, none, from_b)).astype(BF)
        pl.when(self.at.z > 1)(self.far(j, relayed).start)
        self.t1[j] = (self.grads[2, j].astype(F32) + jnp.where(even, from_b, from_a)).astype(BF)
        if not relayed:
            pl.when(self.at.has_earlier)(self.near(j).start)
        self.out[j] = self.grads[4, j].astype(F32) + jnp.where(even, from_a, none)

    def two(self, j):
        at = self.at

        @pl.when(at.has_earlier & at.has_later)
        def _():
            self.far(j).wait_recv()
            self.t1[j] = (self.t1[j].astype(F32) + self.r2[j].astype(F32)).astype(BF)

        pl.when(at.has_earlier)(self.near(j).start)

    def three(self, j, relayed=True):
        at = self.at

        @pl.when(at.has_later)
        def _():
            self.near(j).wait_recv()
            self.out[j] = self.out[j] + self.r1[j].astype(F32)

        if not relayed:
            @pl.when(at.z < 2)
            def _():
                self.far(j).wait_recv()
                self.out[j] = self.out[j] + self.r2[j].astype(F32)

    def sent(self, j):
        at = self.at
        self.twin_a(j).wait_send()
        self.twin_b(j).wait_send()
        pl.when(at.z > 1)(self.far(j).wait_send)
        pl.when(at.has_earlier)(self.near(j).wait_send)


class Reduce:
    COUNT = 14

    def __init__(self, at, chunks, out, own, give, r0, r1a, r1b, r2a, r2b, r3, send, recv, free):
        self.at, self.chunks, self.out, self.own, self.give = at, chunks, out, own, give
        self.r0, self.r1a, self.r1b, self.r2a, self.r2b, self.r3 = r0, r1a, r1b, r2a, r2b, r3
        self.send, self.recv, self.free = send, recv, free
        self.rows = out.shape[0]
        self.quarter, self.half = self.rows // 4, self.rows // 8
        self.slots = give.shape[0]

    @staticmethod
    def scratch(rows, chunks, slots):
        half = rows // 8
        columns = sum(width for _, width in chunks)
        widest = max(width for _, width in chunks)
        return [
            VMEM((4, rows, columns), BF),
            VMEM((slots, 4, rows, widest), BF),
            VMEM((slots, 4, rows, widest), BF),
            VMEM((2, 4, half, columns), BF),
            VMEM((2, 4, half, columns), BF),
            VMEM((4, half, columns), BF),
            VMEM((4, half, columns), BF),
            VMEM((3, 2 * half, columns), BF),
            DMA((len(chunks), Reduce.COUNT)),
            DMA((len(chunks), Reduce.COUNT)),
            pltpu.SemaphoreType.REGULAR,
        ]

    def columns(self, n):
        return pl.ds(*self.chunks[n])

    def copy(self, n, index, src, dst, device):
        return remote(src, dst, self.send.at[n, index], self.recv.at[n, index], device)

    def arrive(self, n, index, ref):
        self.copy(n, index, ref, ref, self.at.core_side).wait_recv()

    def spot(self, owner, part):
        start = owner * self.quarter + part * self.half
        return pl.ds(pl.multiple_of(start, self.half), self.half)

    def piece(self, n, owner):
        start = pl.multiple_of(owner * self.quarter, self.quarter)
        return self.out.at[pl.ds(start, self.quarter), self.columns(n)]

    def core_copy(self, n):
        slot, width = n % self.slots, self.chunks[n][1]
        return self.copy(
            n,
            0,
            self.give.at[slot, :, :, pl.ds(0, width)],
            self.r0.at[slot, :, :, pl.ds(0, width)],
            self.at.core_side,
        )

    def one_copies(self, n):
        at, copies, cols = self.at, [], self.columns(n)
        for i in range(2):
            a = self.own.at[:, self.spot(i * 2 + 1 - at.x, 0), cols]
            b = self.own.at[:, self.spot((1 - at.y) * 2 + i, 1), cols]
            copies.append(self.copy(n, 1 + i, a, self.r1a.at[i, :, :, cols], at.x_side))
            copies.append(self.copy(n, 3 + i, b, self.r1b.at[i, :, :, cols], at.y_side))
        return copies

    def two_copies(self, n):
        at, cols = self.at, self.columns(n)
        a = self.own.at[:, self.spot(at.ry, 0), cols]
        b = self.own.at[:, self.spot(at.rx, 1), cols]
        return [
            self.copy(n, 5, a, self.r2a.at[:, :, cols], at.y_side),
            self.copy(n, 6, b, self.r2b.at[:, :, cols], at.x_side),
        ]

    def z_copy(self, n, k):
        at, cols = self.at, self.columns(n)
        mine = pl.ds(pl.multiple_of(at.r * self.quarter, self.quarter), self.quarter)
        src = self.own.at[at.z_to(k), mine, cols]
        return self.copy(n, 6 + k, src, self.r3.at[k - 1, :, cols], at.z_side(k))

    def back_copy(self, n, i):
        at, cols = self.at, self.columns(n)
        if i < 2:
            ref = self.piece(n, at.r)
            return self.copy(n, 10 + i, ref, ref, at.x_side if i == 0 else at.y_side)
        owner, device = (at.rx, at.y_side) if i == 2 else (at.ry, at.x_side)
        ref = self.out.at[self.spot(owner, i - 2), cols]
        return self.copy(n, 10 + i, ref, ref, device)

    def claim(self, n):
        if n >= self.slots:
            self.core_copy(n - self.slots).wait_send()

    def start(self, n):
        if n >= self.slots:
            pl.semaphore_wait(self.free, 1)
        self.core_copy(n).start()

    def zero(self, n):
        slot, (first, width) = n % self.slots, self.chunks[n]
        self.arrive(n, 0, self.r0.at[slot, :, :, pl.ds(0, width)])
        for z in range(4):
            self.own[z, :, first : first + width] += self.r0[slot, z, :, :width]
        if n + self.slots < len(self.chunks):
            pl.semaphore_signal(
                self.free, inc=1, device_id=self.at.core_side, device_id_type=MESH
            )

    def push(self, n):
        for copy in self.one_copies(n):
            copy.start()

    def add(self, n, where, ref):
        cols = self.columns(n)
        for z in range(4):
            self.own[z, where, cols] += ref[z, :, cols]

    def one(self, n):
        at, cols = self.at, self.columns(n)
        for i in range(2):
            self.arrive(n, 1 + i, self.r1a.at[i, :, :, cols])
            self.arrive(n, 3 + i, self.r1b.at[i, :, :, cols])
            self.add(n, self.spot(i * 2 + at.x, 0), self.r1a.at[i])
            self.add(n, self.spot(at.y * 2 + i, 1), self.r1b.at[i])
        for copy in self.two_copies(n):
            copy.start()

    def two(self, n):
        at, cols = self.at, self.columns(n)
        self.arrive(n, 5, self.r2a.at[:, :, cols])
        self.arrive(n, 6, self.r2b.at[:, :, cols])
        self.add(n, self.spot(at.r, 0), self.r2a)
        self.add(n, self.spot(at.r, 1), self.r2b)
        for k in (1, 2, 3):
            self.z_copy(n, k).start()

    def three(self, n):
        at, cols = self.at, self.columns(n)
        for k in (1, 2, 3):
            self.arrive(n, 6 + k, self.r3.at[k - 1, :, cols])
        for i in range(2):
            where = pl.ds(i * self.half, self.half)
            total = self.own[at.z, self.spot(at.r, i), cols].astype(F32)
            for k in range(3):
                total += self.r3[k, where, cols].astype(F32)
            self.out[self.spot(at.r, i), cols] = total.astype(BF)
        self.back_copy(n, 0).start()
        self.back_copy(n, 1).start()

    def four(self, n):
        at = self.at
        self.arrive(n, 10, self.piece(n, at.rx))
        self.back_copy(n, 2).start()
        self.arrive(n, 11, self.piece(n, at.ry))
        self.back_copy(n, 3).start()

    def five(self, n):
        at, cols = self.at, self.columns(n)
        self.arrive(n, 12, self.out.at[self.spot(at.rd, 0), cols])
        self.arrive(n, 13, self.out.at[self.spot(at.rd, 1), cols])

    def sent(self):
        for n in range(len(self.chunks)):
            if n + self.slots >= len(self.chunks):
                self.core_copy(n).wait_send()
            copies = self.one_copies(n) + self.two_copies(n)
            copies += [self.z_copy(n, k) for k in (1, 2, 3)]
            for copy in copies + [self.back_copy(n, i) for i in range(4)]:
                copy.wait_send()


def at_steps(i, events):
    for n, event in events:
        if n >= 0:
            pl.when(i == n)(event)


def flip_blocks(value, dst):
    blocks, rows, _ = dst.shape
    for s in range(blocks):
        dst[s] = value[:, s * rows : (s + 1) * rows].T


def sequence_features(lengths_ref, first_row, feat_ref, qfeat_ref):
    keys, lanes = feat_ref.shape
    tokens = qfeat_ref.shape[1]
    count = lengths_ref.shape[1]
    starts, ends = [], []
    for i in range(count):
        starts.append(ends[-1] if ends else 0)
        ends.append(starts[-1] + lengths_ref[0, i])
    for low in range(0, keys, tokens):
        place = lax.broadcasted_iota(jnp.int32, (tokens, lanes), 0)
        key = first_row - (keys - tokens) + low + place
        column = lax.broadcasted_iota(jnp.int32, (tokens, lanes), 1)
        value = jnp.where(column >= ONES, 1.0, 0.0)
        value = jnp.where((column == count) & (key < 0), 1.0, value)
        for i in range(count):
            inside = (column == i) & (key >= starts[i]) & (key < ends[i])
            value = jnp.where(inside, 1.0, value)
        feat_ref[low : low + tokens, :] = value.astype(BF)
    row = lax.broadcasted_iota(jnp.int32, (lanes, tokens), 0)
    query = first_row + lax.broadcasted_iota(jnp.int32, (lanes, tokens), 1)
    value = jnp.where(row == count, NEG, 0.0)
    start = jnp.zeros((1, tokens), jnp.int32)
    for i in range(count):
        inside = (query >= starts[i]) & (query < ends[i])
        value = jnp.where((row == i) & jnp.logical_not(inside), NEG, value)
        start = jnp.where(inside[:1], starts[i], start)
    qfeat_ref[...] = value.astype(BF)
    return query[:1] - start


def front_kernel(
    lengths_ref,
    inverse_ref,
    xt_ref,
    cott_ref,
    attend_gain,
    attend_weight,
    expand_gain,
    expand_weight,
    shrinkt,
    output_weight,
    rest_ref,
    attend_hbm,
    win_hbm,
    feat_hbm,
    qt_hbm,
    flipped_hbm,
    x_hbm,
    cot_hbm,
    cott_hbm,
    middle_hbm,
    hidden_hbm,
    hiddent_hbm,
    mixed_ref,
    lse_ref,
    qfeat_ref,
    cos_ref,
    sin_ref,
    kvf,
    vt,
    qa,
    sb,
    attend_own,
    rest_own,
    attend_ref,
    win_ref,
    feat_ref,
    qt_ref,
    flipped,
    inputs,
    cot,
    cott,
    middle,
    hidden,
    hiddent,
    kvt,
    out_weight,
    local_sems,
    store_sems,
    gather_send,
    gather_recv,
    spread_send,
    spread_recv,
):
    at = Place()
    shard_count, rows, columns = attend_ref.shape
    width = shard_count * rows
    tokens = xt_ref.shape[1]
    kv_heads = win_ref.shape[1]
    own_rows = D // shard_count
    cut = 2 * FF
    greet(at, False)

    def gather(n, own, full, cols):
        return Gather(
            at, own, full, cols, local_sems.at[n], gather_send.at[n], gather_recv.at[n]
        )

    first = gather(0, attend_own, attend_ref, (0, columns))
    second = gather(1, rest_own, rest_ref, (3 * FF, QW))
    third = gather(2, rest_own, rest_ref, (0, cut))
    fourth = gather(3, rest_own, rest_ref, (cut, FF))
    spread = Spread(at, win_ref, spread_send, spread_recv)
    stores = []

    def store(src, dst):
        copy = pltpu.make_async_copy(src, dst, store_sems.at[len(stores)])
        copy.start()
        stores.append(copy)

    def place(ref, low, weight, gain):
        count = weight.shape[1]
        block = own_rows // 16 * 16
        ref[:block, low : low + count] = weight[:block]
        tail = jnp.concatenate(
            [weight[block:].astype(F32), jnp.zeros((rows - own_rows, count), F32)], axis=0
        )
        if gain is not None:
            row = jnp.concatenate(
                [gain[...].astype(F32), jnp.zeros((1, count - own_rows), F32)], axis=1
            )
            where = lax.broadcasted_iota(jnp.int32, tail.shape, 0) == own_rows - block
            tail = jnp.where(where, row, tail)
        ref[block:, low : low + count] = tail.astype(BF)

    place(attend_own, 0, attend_weight, attend_gain)
    first.start_z()
    first.start_core()
    place(rest_own, 3 * FF, output_weight[...].T, expand_gain)
    second.start_core()
    place(rest_own, 0, expand_weight, None)
    third.start_core()
    place(rest_own, cut, shrinkt, None)
    fourth.start_core()
    spread.clear()
    position = sequence_features(lengths_ref, at.s * tokens, feat_ref, qfeat_ref)
    store(feat_ref, feat_hbm)
    attend_forward_setup(feat_ref, qfeat_ref, kvf, vt, qa)
    phases = inverse_ref[...] * position.astype(F32)
    cos_ref[...] = jnp.cos(phases)
    sin_ref[...] = jnp.sin(phases)
    first.z(0)
    for s in range(shard_count):
        block = slice(s * rows, (s + 1) * rows)
        source = slice(s * own_rows, (s + 1) * own_rows)
        blank = jnp.zeros((rows - own_rows, tokens), F32)
        value = jnp.concatenate([xt_ref[source, :].astype(F32), blank], axis=0)
        inputs[:, block] = value.T.astype(BF)
    first.z(1)
    for s in range(shard_count):
        block = slice(s * rows, (s + 1) * rows)
        source = slice(s * own_rows, (s + 1) * own_rows)
        value = jnp.concatenate([cott_ref[source, :].astype(F32), blank], axis=0)
        cott[s] = value.astype(BF)
        cot[:, block] = value.T.astype(BF)
    store(inputs, x_hbm)
    store(cot, cot_hbm)
    store(cott, cott_hbm)
    first.z(2)
    second.start_z()
    third.start_z()
    for i in range(3):
        first.cross(i)
    second.z(0)
    for i in range(3):
        first.last(i)
    second.z(1)
    first.landed()
    store(attend_ref, attend_hbm)

    value = inputs[...].astype(F32)
    scale = scale_of(value)
    for s in range(shard_count):
        lane = slice(s * rows, (s + 1) * rows)
        gain = attend_ref[s, own_rows : own_rows + 1, :rows].astype(F32)
        hidden[:, lane] = (inputs[:, lane].astype(F32) * scale * gain).astype(BF)

    def project(start):
        stop = min(start + 256, columns)
        weight = attend_ref[:, :, start:stop].reshape(width, stop - start)
        turned = dot(hidden[...], weight).T
        for low in range(0, stop - start, HEAD_DIM):
            column = start + low
            head = turned[low : low + HEAD_DIM, :]
            if column < QW + KW:
                half = HEAD_DIM // 2
                front, back = head[:half], head[half:]
                head = jnp.concatenate(
                    [
                        front * cos_ref[...] - back * sin_ref[...],
                        back * cos_ref[...] + front * sin_ref[...],
                    ],
                    axis=0,
                )
            if column < QW:
                qt_ref[column : column + HEAD_DIM, :] = head.astype(BF)
            elif column < QW + KW:
                kvt[(column - QW) // HEAD_DIM, :HALF, :] = head.astype(BF)
            else:
                kvt[(column - QW - KW) // HEAD_DIM, HALF:, :] = head.astype(BF)

    split = QW // 128 * 128
    for start in range(split, columns, 256):
        project(start)
    for j in range(kv_heads):
        win_ref[4, j] = kvt[j].T
        spread.start(j)
    third.z(0)
    second.z(2)
    for start in range(0, split, 256):
        project(start)
    third.z(1)
    fourth.start_z()
    second.cross(0)
    store(qt_ref, qt_hbm)
    flip_blocks(hidden, flipped)
    store(flipped, flipped_hbm)
    spread.one(0)
    third.cross(0)
    spread.one(1)
    second.cross(1)
    spread.two(0)
    events = [
        (0, lambda: third.z(2)),
        (1, lambda: second.cross(2)),
        (2, lambda: second.last(0)),
        (2, lambda: fourth.z(0)),
        (3, lambda: third.cross(1)),
        (4, lambda: second.last(1)),
        (5, lambda: fourth.z(1)),
        (5, lambda: second.last(2)),
        (6, lambda: third.cross(2)),
        (7, lambda: third.last(0)),
        (8, lambda: fourth.cross(0)),
        (9, lambda: fourth.z(2)),
        (10, lambda: third.last(1)),
        (11, lambda: fourth.cross(1)),
        (12, lambda: third.last(2)),
        (13, lambda: fourth.last(0)),
    ]

    def key_head(j, _):
        pl.when(j + 2 < kv_heads)(lambda: spread.one(j + 2))
        pl.when(j + 1 < kv_heads)(lambda: spread.two(j + 1))
        spread.landed(j)
        attend_forward_keys(j, win_ref, kvf, vt)

        def head(g, _):
            h = j * GROUP + g
            attend_forward_head(h, qt_ref, mixed_ref, lse_ref, kvf, vt, qa, sb)
            at_steps(h, events)
            return 0

        lax.fori_loop(0, GROUP, head, 0)
        spread.sent(j)
        return 0

    lax.fori_loop(0, kv_heads, key_head, 0)
    store(win_ref, win_hbm)
    second.landed()
    load = pltpu.make_async_copy(
        rest_ref.at[:, :, pl.ds(3 * FF, QW)], out_weight, local_sems.at[4]
    )
    load.start()
    fourth.cross(2)
    fourth.last(1)
    load.wait()
    real = real_lanes(width, rows, own_rows)
    gain = jnp.concatenate(
        [out_weight[s, own_rows : own_rows + 1, :rows].astype(F32) for s in range(shard_count)],
        axis=1,
    )
    gain = jnp.where(real, gain, 0.0)
    out_full = out_weight.reshape(width, QW)
    for low in range(0, tokens, PART):
        where = slice(low, low + PART)
        value = jnp.where(real, dot(mixed_ref[:, where].T, out_full[...], 1, 1), 0.0)
        value = inputs[where, :].astype(F32) + value
        middle[where, :] = value
        hidden[where, :] = (value * scale_of(value) * gain).astype(BF)
    store(middle, middle_hbm)
    store(hidden, hidden_hbm)
    flip_blocks(hidden, hiddent)
    store(hiddent, hiddent_hbm)
    fourth.last(2)
    third.landed()
    fourth.landed()
    for part in (first, second, third, fourth):
        part.sent()
    for copy in stores:
        copy.wait()


def front(lengths, xt, cott, weights, shard_count, number):
    _, tokens = xt.shape
    attend_weight, expand_weight, output_weight = weights[1], weights[3], weights[5]
    own_rows, columns = attend_weight.shape
    rows = -(-(own_rows + 2) // 16) * 16
    width = shard_count * rows
    lanes = 2 * HEAD_DIM
    blocks = (MAXLEN - 2) // tokens + 2
    keys = blocks * tokens
    half = HEAD_DIM // 2
    inverse = rope_base ** (-(2.0 * np.arange(half, dtype=np.float32) / HEAD_DIM))
    rest_columns = 3 * FF + QW

    def shape(*sizes, dtype=BF):
        return jax.ShapeDtypeStruct(sizes, dtype)

    attend, rest = shape(shard_count, rows, columns), shape(shard_count, rows, rest_columns)
    window = shape(blocks, KV_HEADS, tokens, lanes)
    feat, heads = shape(keys, lanes), shape(QW, tokens)
    natural, turned = shape(tokens, width), shape(shard_count, rows, tokens)
    middle = shape(tokens, width, dtype=F32)
    in_hbm = (
        rest, attend, window, feat, heads, turned, natural, natural, turned, middle, natural, turned
    )
    table = shape(half, tokens, dtype=F32)
    in_vmem = (heads, shape(HEADS, 1, tokens, dtype=F32), shape(lanes, tokens), table, table)

    def scratch(struct):
        return VMEM(struct.shape, struct.dtype)

    return pl.pallas_call(
        front_kernel,
        out_shape=in_hbm + in_vmem,
        in_specs=[pl.BlockSpec(memory_space=pltpu.SMEM)] + [pl.BlockSpec(memory_space=VMEM)] * 9,
        out_specs=(pl.BlockSpec(memory_space=ANY),) * len(in_hbm)
        + (pl.BlockSpec(memory_space=VMEM),) * len(in_vmem),
        scratch_shapes=attend_forward_scratch(keys, lanes, tokens)
        + [VMEM((rows, columns), BF), VMEM((rows, rest_columns), BF)]
        + [
            scratch(struct)
            for struct in (
                attend, window, feat, heads, turned, natural, natural, turned, middle, natural, turned
            )
        ]
        + [
            VMEM((KV_HEADS, lanes, tokens), BF),
            VMEM((shard_count, rows, QW), BF),
            DMA((5,)),
            DMA((len(in_hbm),)),
            DMA((4, Gather.COUNT)),
            DMA((4, Gather.COUNT)),
            DMA((5, KV_HEADS)),
            DMA((5, KV_HEADS)),
        ],
        compiler_params=pltpu.CompilerParams(
            collective_id=number, has_side_effects=True, vmem_limit_bytes=BIG_VMEM
        ),
        name="front",
    )(lengths, jnp.asarray(inverse, F32)[:, None], xt, cott, *weights)


SUB = 256
CHUNK = 2 * SUB


def up_to_lanes(columns):
    return -(-columns // 128) * 128


def sum_chunks():
    widths = [3 * CHUNK] * (FF // CHUNK) + [up_to_lanes(QW)] * 2 + [2 * KW]
    return [(sum(widths[:n]), width) for n, width in enumerate(widths)]


OUT_CHUNK = FF // CHUNK
QUERY_CHUNK, PAIR_CHUNK = OUT_CHUNK + 1, OUT_CHUNK + 2


def unrotate(head, cosine, sine):
    half = HEAD_DIM // 2
    front, back = head[:half], head[half:]
    return jnp.concatenate(
        [front * cosine + back * sine, back * cosine - front * sine], axis=0
    ).astype(BF)


def real_lanes(width, rows, own_rows):
    return lax.rem(lax.broadcasted_iota(jnp.int32, (1, width), 1), rows) < own_rows


def scale_of(value):
    return lax.rsqrt(jnp.sum(value * value, axis=-1, keepdims=True) * (1.0 / D) + eps_norm)


def put_turned(value, dst, rows, own_rows):
    turned = value.T
    for s in range(turned.shape[0] // rows):
        dst[s * own_rows : (s + 1) * own_rows, :] = turned[s * rows : s * rows + own_rows]


def put_gradient(total, n, column, ref, z, product, row=None):
    rows, columns = product.shape
    first = product[:, :rows]
    if row is not None:
        own_rows, gain_row = row
        place = lax.broadcasted_iota(jnp.int32, (rows, rows), 0)
        first = jnp.where(place == own_rows, gain_row, first)
    ref[z, :, column : column + rows] = first.astype(BF)
    ref[z, :, column + rows : column + columns] = product[:, rows:].astype(BF)
    width = total.chunks[n][1]
    if columns < width:
        ref[z, :, column + columns : column + width] = jnp.zeros((rows, width - columns), BF)


def feed_forward(
    at,
    total,
    mixed_ref,
    gradt_ref,
    middle_hbm,
    hidden_hbm,
    hiddent_hbm,
    cot_hbm,
    cott_hbm,
    rest_ref,
    out_hbm,
    middle_grad_hbm,
    events,
    cot,
    hidden,
    middle,
    acc_out,
    acc_grad,
    hidden_own,
    hidden_give,
    cot_own,
    cot_give,
    flipped,
    out_weight,
    gain_term,
    weights,
    results,
    sems,
    load_sems,
):
    shard_count, rows, _ = rest_ref.shape
    width = shard_count * rows
    tokens = middle.shape[0]
    own_rows = D // shard_count
    planes = shard_count // 2

    def weight_copies(n, slot):
        return [
            pltpu.make_async_copy(
                rest_ref.at[:, :, pl.ds(pl.multiple_of(i * FF + n * SUB, 128), SUB)],
                weights.at[slot, i],
                sems.at[slot, i],
            )
            for i in range(3)
        ]

    pairs = [(hidden_hbm, hidden), (cot_hbm, cot)]
    for z in range(planes):
        mine, other = 2 * z + at.c, 2 * z + 1 - at.c
        pairs += [(hiddent_hbm.at[mine], hidden_own.at[z]), (cott_hbm.at[mine], cot_own.at[z])]
        pairs += [(hiddent_hbm.at[other], hidden_give.at[z])]
        pairs += [(cott_hbm.at[other], cot_give.at[z])]
    pairs += [(middle_hbm, middle), (rest_ref.at[:, :, pl.ds(3 * FF, QW)], out_weight)]
    loads = [
        pltpu.make_async_copy(src, dst, load_sems.at[i]) for i, (src, dst) in enumerate(pairs)
    ]
    for copy in weight_copies(0, 0) + loads:
        copy.start()
    acc_out[...] = jnp.zeros_like(acc_out)
    acc_grad[...] = jnp.zeros_like(acc_grad)
    for load in loads[:-2]:
        load.wait()

    def put(ref, column, value):
        where = pl.ds(pl.multiple_of(column, 128), value.shape[1])
        ref[:, :, where] = value.reshape(planes, rows, value.shape[1]).astype(BF)

    def step(n, _):
        slot = lax.rem(n, 2)
        for copy in weight_copies(n, slot):
            copy.wait()

        @pl.when(n + 1 < FF // SUB)
        def _():
            for copy in weight_copies(n + 1, 1 - slot):
                copy.start()

        gate_weight = weights[slot, 0].reshape(width, SUB)
        upper_weight = weights[slot, 1].reshape(width, SUB)
        shrink_weight = weights[slot, 2].reshape(width, SUB)
        gate = dot(hidden[...], gate_weight)
        upper = dot(hidden[...], upper_weight)
        inner_grad = dot(cot[...], shrink_weight)
        sigmoid = jax.nn.sigmoid(gate)
        active = gate * sigmoid
        inner = (active * upper).astype(BF)
        gate_grad = (inner_grad * upper * sigmoid * (1.0 + gate * (1.0 - sigmoid))).astype(BF)
        upper_grad = (inner_grad * active).astype(BF)
        for low in range(0, width, width // 2):
            cols = slice(low, low + width // 2)
            acc_out[:, cols] += dot(inner, shrink_weight[cols], 1, 1)
            acc_grad[:, cols] += dot(gate_grad, gate_weight[cols], 1, 1) + dot(
                upper_grad, upper_weight[cols], 1, 1
            )
        chunk, part = n // 2, lax.rem(n, 2) * SUB
        first = chunk * 3 * CHUNK + part
        put(total.own, first, dot(hidden_own[...].reshape(width // 2, tokens), gate_grad))
        put(total.own, first + CHUNK, dot(hidden_own[...].reshape(width // 2, tokens), upper_grad))
        put(total.own, first + 2 * CHUNK, dot(cot_own[...].reshape(width // 2, tokens), inner))
        for n_start in range(2 * total.slots, FF // SUB, 2):
            pl.when(n == n_start)(functools.partial(total.claim, n_start // 2))
        give = total.give.at[lax.rem(chunk, total.slots)]
        put(give, part, dot(hidden_give[...].reshape(width // 2, tokens), gate_grad))
        put(give, part + CHUNK, dot(hidden_give[...].reshape(width // 2, tokens), upper_grad))
        put(give, part + 2 * CHUNK, dot(cot_give[...].reshape(width // 2, tokens), inner))
        for n_end in range(1, FF // SUB, 2):
            pl.when(n == n_end)(functools.partial(total.start, n_end // 2))
        at_steps(n, events)
        return 0

    lax.fori_loop(0, FF // SUB, step, 0)

    for load in loads[-2:]:
        load.wait()
    out_full = out_weight.reshape(width, QW)
    real = real_lanes(width, rows, own_rows)
    gain = jnp.concatenate(
        [out_weight[s, own_rows : own_rows + 1, :rows].astype(F32) for s in range(shard_count)],
        axis=1,
    )
    gain = jnp.where(real, gain, 0.0)
    term = jnp.zeros((1, width), F32)
    stores = []
    for n, low in enumerate(range(0, tokens, PART)):
        where = slice(low, low + PART)
        value = middle[where, :]
        if n >= 2:
            stores[n - 2].wait()
        put_turned(value + acc_out[where, :], results.at[n % 2], rows, own_rows)
        stores.append(
            pltpu.make_async_copy(
                results.at[n % 2], out_hbm.at[:, pl.ds(low, PART)], sems.at[2, n % 2]
            )
        )
        stores[n].start()
        scale = scale_of(value)
        normed = value * scale
        hidden_grad = jnp.where(real, acc_grad[where, :], 0.0)
        term = term + jnp.sum(hidden_grad * normed, axis=0, keepdims=True)
        upstream = hidden_grad * gain
        mean = jnp.sum(upstream * normed, axis=-1, keepdims=True) * (1.0 / D)
        value = cot[where, :].astype(F32) + scale * (upstream - normed * mean)
        acc_grad[where, :] = value
        branch = value.astype(BF)
        hidden[where, :] = branch
        gradt_ref[:, where] = dot(branch, out_full[...]).T.astype(BF)
        for step_number, event in events:
            if step_number == FF // SUB + n:
                event()
    store = pltpu.make_async_copy(acc_grad, middle_grad_hbm, sems.at[2, 2])
    store.start()
    stores[-2:] += [store]
    for s in range(shard_count):
        gain_term[s] = jnp.broadcast_to(term[:, s * rows : (s + 1) * rows], (8, rows))
    flip_blocks(hidden, flipped)
    for z in range(planes):
        hidden_own[z] = flipped[2 * z + at.c]
        hidden_give[z] = flipped[2 * z + 1 - at.c]
    total.claim(OUT_CHUNK)
    for lhs, core, ref, column in (
        (hidden_give, 1 - at.c, total.give.at[OUT_CHUNK % total.slots], 0),
        (hidden_own, at.c, total.own, total.chunks[OUT_CHUNK][0]),
    ):
        product = dot(lhs[...].reshape(width // 2, tokens), mixed_ref[...], 1, 1)
        for z in range(planes):
            row = (own_rows, gain_term[2 * z + core][:1])
            plane = product[z * rows : (z + 1) * rows]
            put_gradient(total, OUT_CHUNK, column, ref, z, plane, row)
        if lhs is hidden_give:
            total.start(OUT_CHUNK)
    for store in stores[-3:]:
        store.wait()


def attention_backward(
    at,
    total,
    collect,
    events,
    cos_ref,
    sin_ref,
    qfeat_ref,
    lse_ref,
    mixed_ref,
    gradt_ref,
    jointt,
    win_hbm,
    feat_hbm,
    qt_hbm,
    kvf,
    kt,
    qa,
    da,
    acc,
    rhs,
    win_ref,
    feat_ref,
    qt_ref,
    sems,
):
    loads = [
        pltpu.make_async_copy(src, dst, sems.at[i])
        for i, (src, dst) in enumerate(
            ((feat_hbm, feat_ref), (win_hbm, win_ref), (qt_hbm, qt_ref))
        )
    ]
    for load in loads:
        load.start()
    for load in loads:
        load.wait()
    attend_backward_setup(feat_ref, kvf, qa, da, rhs)
    for n, event in events:
        if n < 0:
            event()

    def put_query(row, low, value):
        cols = slice(low, low + QC)
        jointt[pl.ds(row, HEAD_DIM), cols] = unrotate(value, cos_ref[:, cols], sin_ref[:, cols])

    def key_head(j, _):
        attend_backward_keys(j, win_ref, kvf, kt, acc)

        def head(g, _):
            h = j * GROUP + g
            attend_backward_head(
                h,
                put_query,
                qt_ref,
                qfeat_ref,
                gradt_ref,
                mixed_ref,
                lse_ref,
                kvf,
                kt,
                qa,
                da,
                acc,
                rhs,
            )
            at_steps(h, events)
            return 0

        lax.fori_loop(0, GROUP, head, 0)
        attend_backward_done(j, acc, collect.grads)
        collect.start(j)
        pl.when(j > 0)(lambda: collect.one(j - 1))
        pl.when(j > 1)(lambda: collect.two(j - 2))
        pl.when(j > 2)(lambda: collect.three(j - 3))
        return 0

    lax.fori_loop(0, KV_HEADS, key_head, 0)


def projection_backward(
    at,
    total,
    collect,
    events,
    cos_ref,
    sin_ref,
    jointt,
    hidden_own,
    hidden_give,
    x_hbm,
    middle_grad_hbm,
    attend_hbm,
    grad_hbm,
    attend_ref,
    inputs,
    middle_grad,
    hidden_grad,
    gain_term,
    results,
    sems,
):
    shard_count, rows, columns = attend_ref.shape
    width = shard_count * rows
    tokens = inputs.shape[0]
    own_rows = D // shard_count
    planes = shard_count // 2
    loads = [
        pltpu.make_async_copy(src, dst, sems.at[i])
        for i, (src, dst) in enumerate(
            ((attend_hbm, attend_ref), (x_hbm, inputs), (middle_grad_hbm, middle_grad))
        )
    ]
    for load in loads:
        load.start()
    last = KV_HEADS - 1
    sides = (
        (1 - at.c, hidden_give, lambda n: (total.give.at[n % total.slots], 0)),
        (at.c, hidden_own, lambda n: (total.own, total.chunks[n][0])),
    )

    def gradients(n, rows_of_joint, gain):
        total.claim(n)
        for side, (core, lhs, target) in enumerate(sides):
            ref, column = target(n)
            product = dot(
                lhs[...].reshape(planes * rows, tokens), jointt[rows_of_joint, :], 1, 1
            )
            for z in range(planes):
                row = (own_rows, gain_term[2 * z + core][:1]) if gain else None
                plane = product[z * rows : (z + 1) * rows]
                put_gradient(total, n, column, ref, z, plane, row)
            if side == 0:
                total.start(n)

    gradients(QUERY_CHUNK, slice(0, QW), False)
    collect.one(last, False)
    collect.two(last - 1)
    for load in loads:
        load.wait()
    weight = attend_ref.reshape(width, columns)
    for low in range(0, tokens, PART):
        where = slice(low, low + PART)
        hidden_grad[where, :] = dot(jointt[:QW, where].T, weight[:, :QW], 1, 1)
    total.zero(QUERY_CHUNK)
    total.push(QUERY_CHUNK)
    events[0]()
    collect.three(last - 2)
    collect.three(last - 1)
    collect.three(last, False)
    for j in range(KV_HEADS):
        pair = collect.out[j].T
        low = QW + j * HEAD_DIM
        jointt[low : low + HEAD_DIM, :] = unrotate(pair[:HALF], cos_ref[...], sin_ref[...])
        jointt[low + KW : low + KW + HEAD_DIM, :] = pair[HALF:].astype(BF)
    real = real_lanes(width, rows, own_rows)
    term = jnp.zeros((1, width), F32)
    for low in range(0, tokens, PART):
        where = slice(low, low + PART)
        value = inputs[where, :].astype(F32)
        normed = value * scale_of(value)
        value = hidden_grad[where, :] + dot(jointt[QW:, where].T, weight[:, QW:], 1, 1)
        value = jnp.where(real, value, 0.0)
        hidden_grad[where, :] = value
        term = term + jnp.sum(value * normed, axis=0, keepdims=True)
    for s in range(shard_count):
        gain_term[s] = jnp.broadcast_to(term[:, s * rows : (s + 1) * rows], (8, rows))
    gradients(PAIR_CHUNK, slice(QW, columns), True)
    events[1]()
    total.one(QUERY_CHUNK)
    total.zero(PAIR_CHUNK)
    total.push(PAIR_CHUNK)
    events[2]()
    total.two(QUERY_CHUNK)
    gain = jnp.concatenate(
        [
            attend_ref[s, own_rows : own_rows + 1, :rows].astype(F32)
            for s in range(shard_count)
        ],
        axis=1,
    )
    gain = jnp.where(real, gain, 0.0)
    stores = []
    for n, low in enumerate(range(0, tokens, PART)):
        where = slice(low, low + PART)
        value = inputs[where, :].astype(F32)
        scale = scale_of(value)
        normed = value * scale
        upstream = hidden_grad[where, :] * gain
        mean = jnp.sum(upstream * normed, axis=-1, keepdims=True) * (1.0 / D)
        result = middle_grad[where, :] + scale * (upstream - normed * mean)
        if n >= 2:
            stores[n - 2].wait()
        put_turned(result, results.at[n % 2], rows, own_rows)
        stores.append(
            pltpu.make_async_copy(
                results.at[n % 2], grad_hbm.at[:, pl.ds(low, PART)], sems.at[3 + n % 2]
            )
        )
        stores[n].start()
    total.one(PAIR_CHUNK)
    total.three(QUERY_CHUNK)
    total.two(PAIR_CHUNK)
    total.four(QUERY_CHUNK)
    total.three(PAIR_CHUNK)
    total.five(QUERY_CHUNK)
    total.four(PAIR_CHUNK)
    total.five(PAIR_CHUNK)
    for j in range(KV_HEADS):
        collect.sent(j)
    total.sent()
    for store in stores[-2:]:
        store.wait()


def rear_kernel(
    mixed_ref,
    lse_ref,
    qfeat_ref,
    cos_ref,
    sin_ref,
    rest_ref,
    attend_hbm,
    win_hbm,
    feat_hbm,
    qt_hbm,
    flipped_hbm,
    x_hbm,
    cot_hbm,
    cott_hbm,
    middle_hbm,
    hidden_hbm,
    hiddent_hbm,
    sum_ref,
    out_hbm,
    grad_hbm,
    middle_grad_hbm,
    gradt_ref,
    jointt,
    pairs,
    ra,
    rb,
    r2,
    r1,
    collect_send,
    collect_recv,
    *reduce_scratch,
):
    at = Place()
    tokens = x_hbm.shape[0]
    shard_count, rows, _ = rest_ref.shape
    width = shard_count * rows
    lanes = pairs.shape[2]
    keys = feat_hbm.shape[0]
    greet(at, True)
    total = Reduce(at, sum_chunks(), sum_ref, *reduce_scratch)

    def run(*names):
        def event():
            for name, n in names:
                getattr(total, name)(n)

        return event

    def round_of(t):
        due = [("one", t), ("push", t + 1), ("two", t - 1), ("three", t - 3), ("four", t - 4)]
        return [(name, n) for name, n in due + [("five", t - 5)] if 0 <= n <= OUT_CHUNK]

    forward_events = [
        (2, run(("zero", 0), ("push", 0))),
        (4, run(("zero", 1))),
        (6, run(("zero", 2), *round_of(0))),
        (8, run(("zero", 3))),
        (12, run(("zero", 4), *round_of(1))),
    ]
    backward_events = [
        (0, run(("zero", 5))),
        (1, run(*round_of(2))),
        (4, run(*round_of(3))),
        (7, run(*round_of(4))),
        (10, run(*round_of(5))),
        (12, run(*round_of(6))),
        (13, run(*round_of(7))),
        (14, run(*round_of(8))),
    ]
    last_events = [run(), run(*round_of(9)), run(*round_of(10))]

    pl.run_scoped(
        functools.partial(
            feed_forward,
            at,
            total,
            mixed_ref,
            gradt_ref,
            middle_hbm,
            hidden_hbm,
            hiddent_hbm,
            cot_hbm,
            cott_hbm,
            rest_ref,
            out_hbm,
            middle_grad_hbm,
            forward_events,
        ),
        VMEM((tokens, width), BF),
        VMEM((tokens, width), BF),
        VMEM((tokens, width), F32),
        VMEM((tokens, width), F32),
        VMEM((tokens, width), F32),
        VMEM((shard_count // 2, rows, tokens), BF),
        VMEM((shard_count // 2, rows, tokens), BF),
        VMEM((shard_count // 2, rows, tokens), BF),
        VMEM((shard_count // 2, rows, tokens), BF),
        VMEM((shard_count, rows, tokens), BF),
        VMEM((shard_count, rows, QW), BF),
        VMEM((shard_count, 8, rows), F32),
        VMEM((2, 3, shard_count, rows, SUB), BF),
        VMEM((2, D, PART), F32),
        DMA((3, 3)),
        DMA((4 + 2 * shard_count,)),
    )

    def attention(grads, t2, t1, hidden_own, hidden_give, sems):
        collect = Collect(at, grads, pairs, ra, rb, r2, r1, t2, t1, collect_send, collect_recv)
        loads = []
        for z in range(shard_count // 2):
            for i, (dst, core) in enumerate(((hidden_own, at.c), (hidden_give, 1 - at.c))):
                src = flipped_hbm.at[2 * z + core]
                loads.append(pltpu.make_async_copy(src, dst.at[z], sems.at[i, z]))
        for load in loads:
            load.start()
        pl.run_scoped(
            functools.partial(
                attention_backward,
                at,
                total,
                collect,
                backward_events,
                cos_ref,
                sin_ref,
                qfeat_ref,
                lse_ref,
                mixed_ref,
                gradt_ref,
                jointt,
                win_hbm,
                feat_hbm,
                qt_hbm,
            ),
            *attend_backward_scratch(keys, lanes, tokens),
            VMEM(win_hbm.shape, BF),
            VMEM(feat_hbm.shape, BF),
            VMEM(qt_hbm.shape, BF),
            DMA((3,)),
        )
        for load in loads:
            load.wait()
        pl.run_scoped(
            functools.partial(
                projection_backward,
                at,
                total,
                collect,
                last_events,
                cos_ref,
                sin_ref,
                jointt,
                hidden_own,
                hidden_give,
                x_hbm,
                middle_grad_hbm,
                attend_hbm,
                grad_hbm,
            ),
            VMEM(attend_hbm.shape, BF),
            VMEM((tokens, width), BF),
            VMEM((tokens, width), F32),
            VMEM((tokens, width), F32),
            VMEM((shard_count, 8, rows), F32),
            VMEM((2, D, PART), F32),
            DMA((5,)),
        )

    pl.run_scoped(
        attention,
        VMEM(win_hbm.shape, BF),
        VMEM(pairs.shape, BF),
        VMEM(pairs.shape, BF),
        VMEM((shard_count // 2, rows, tokens), BF),
        VMEM((shard_count // 2, rows, tokens), BF),
        DMA((2, shard_count // 2)),
    )


def rear(in_hbm, in_vmem, number):
    rest, attend, window, _, qt, _, x = in_hbm[:7]
    _, kv_heads, tokens, lanes = window.shape
    shard_count, rows, _ = rest.shape
    columns = sum(width for _, width in sum_chunks())
    pairs = (kv_heads, tokens, lanes)
    return pl.pallas_call(
        rear_kernel,
        out_shape=(
            jax.ShapeDtypeStruct((rows, columns), BF),
            jax.ShapeDtypeStruct((D, tokens), F32),
            jax.ShapeDtypeStruct((D, tokens), F32),
            jax.ShapeDtypeStruct((tokens, shard_count * rows), F32),
        ),
        in_specs=[pl.BlockSpec(memory_space=VMEM)] * len(in_vmem)
        + [pl.BlockSpec(memory_space=ANY)] * len(in_hbm),
        out_specs=(pl.BlockSpec(memory_space=VMEM),) + (pl.BlockSpec(memory_space=ANY),) * 3,
        scratch_shapes=[VMEM(qt.shape, BF), VMEM((JW, tokens), BF), VMEM(pairs, F32)]
        + [VMEM(pairs, BF)] * 4
        + [DMA((4, kv_heads)), DMA((4, kv_heads))]
        + Reduce.scratch(rows, sum_chunks(), 2),
        compiler_params=pltpu.CompilerParams(
            collective_id=number, has_side_effects=True, vmem_limit_bytes=BIG_VMEM
        ),
        name="rear",
    )(*in_vmem, *in_hbm)


def adam_parts(old_weight, gradient, first, second, decay_factor):
    moment = beta_one * first + (1.0 - beta_one) * gradient
    square = beta_two * second + (1.0 - beta_two) * gradient * gradient
    corrected = moment * (1.0 / (1.0 - beta_one**STEP))
    divisor = jnp.sqrt(square * (1.0 / (1.0 - beta_two**STEP))) + adam_eps
    update = -learn_rate * (corrected / divisor + decay_factor * old_weight)
    return moment, square, update


def adam_kernel(grad_scale, own_rows, *refs):
    sums, attend_planes, rest_planes = refs[:3]
    states, passed_in, results, passed_out = refs[3:11], refs[11:13], refs[13:29], refs[29:31]
    buffers, weights, staged = refs[31:47], refs[47:49], refs[49:51]
    in_sems, out_sems = refs[51], refs[52]
    chunks = sum_chunks()
    shard = lax.axis_index("shard")
    loads = [
        pltpu.make_async_copy(attend_planes.at[shard], weights[0], in_sems.at[8]),
        pltpu.make_async_copy(rest_planes.at[shard], weights[1], in_sems.at[9]),
    ]
    order = (2, 3, 0, 1)
    for n in order:
        for i in range(2):
            loads.append(
                pltpu.make_async_copy(
                    states[2 * n + i], buffers[4 * n + 1 + i], in_sems.at[2 * n + i]
                )
            )
    for i in range(2):
        loads.append(pltpu.make_async_copy(passed_in[i], staged[i], in_sems.at[10 + i]))
    for load in loads:
        load.start()
    loads[0].wait()
    loads[1].wait()
    stores = []

    def update(n, where, total, weight, flip):
        gradient, moment, square, changed = buffers[4 * n : 4 * n + 4]
        total = total.astype(F32)
        weight = weight.astype(F32)
        if flip:
            total, weight = total.T[:, :own_rows], weight.T[:, :own_rows]
        total = total * grad_scale
        new_moment, new_square, step = adam_parts(
            weight, total, moment[where], square[where], decay_rate
        )
        gradient[where] = total
        moment[where] = new_moment
        square[where] = new_square
        changed[where] = weight + step

    everything = slice(None)
    for place, n in enumerate(order):
        loads[2 + 2 * place].wait()
        loads[3 + 2 * place].wait()
        if n == 0:
            for chunk, first, count in ((QUERY_CHUNK, 0, QW), (PAIR_CHUNK, QW, 2 * KW)):
                low, cols = chunks[chunk][0], slice(first, first + count)
                update(
                    0,
                    (everything, cols),
                    sums[:own_rows, low : low + count],
                    weights[0][:own_rows, cols],
                    False,
                )
        elif n == 1:
            low = chunks[OUT_CHUNK][0]
            cols = slice(3 * FF, 3 * FF + QW)
            update(
                1, (everything, everything), sums[:, low : low + QW], weights[1][:, cols], True
            )
        else:
            for c in range(FF // CHUNK):
                for part in (0, 1) if n == 2 else (2,):
                    low = 3 * CHUNK * c + CHUNK * part
                    first = part * FF + CHUNK * c
                    total = sums[:own_rows, low : low + CHUNK]
                    weight = weights[1][:own_rows, first : first + CHUNK]
                    column = first if n == 2 else first - 2 * FF
                    cols = slice(column, column + CHUNK)
                    update(n, (everything, cols), total, weight, False)
        for i in range(4):
            store = pltpu.make_async_copy(
                buffers[4 * n + i], results[4 * n + i], out_sems.at[4 * n + i]
            )
            store.start()
            stores.append(store)
        if place < 2:
            loads[10 + place].wait()
            store = pltpu.make_async_copy(
                staged[place], passed_out[place], out_sems.at[16 + place]
            )
            store.start()
            stores.append(store)
    for store in stores:
        store.wait()


def adam(grad_scale, own_rows, sums, attend_planes, rest_planes, states, passed):
    flat = [array for pair in states for array in pair]
    shapes = [pair[0].shape for pair in states]
    return pl.pallas_call(
        functools.partial(adam_kernel, grad_scale, own_rows),
        out_shape=tuple(jax.ShapeDtypeStruct(shape, F32) for shape in shapes for _ in range(4))
        + tuple(jax.ShapeDtypeStruct(array.shape, array.dtype) for array in passed),
        in_specs=[pl.BlockSpec(memory_space=VMEM)] + [pl.BlockSpec(memory_space=ANY)] * 12,
        out_specs=(pl.BlockSpec(memory_space=ANY),) * 18,
        scratch_shapes=[VMEM(shape, F32) for shape in shapes for _ in range(4)]
        + [VMEM(attend_planes.shape[1:], BF), VMEM(rest_planes.shape[1:], BF)]
        + [VMEM(array.shape, F32) for array in passed]
        + [DMA((12,)), DMA((18,))],
        compiler_params=pltpu.CompilerParams(vmem_limit_bytes=BIG_VMEM),
        name="adam",
    )(sums, attend_planes, rest_planes, *flat, *passed)


def spread_pairs(pairs, reach):
    devices = range(lax.axis_size("shard"))
    blocks = []
    for distance in range(reach, 0, -1):
        route = [(i - distance, i) for i in devices if i - distance in devices]
        blocks.append(lax.ppermute(pairs, "shard", route))
    return jnp.stack(blocks + [pairs])


def collect_pairs(grads, reach):
    devices = range(lax.axis_size("shard"))
    own = grads[reach].astype(F32)
    for distance in range(1, reach + 1):
        route = [(i, i - distance) for i in devices if i - distance in devices]
        own = own + lax.ppermute(grads[reach - distance], "shard", route).astype(F32)
    return own


def angles(positions):
    half_dim = HEAD_DIM // 2
    inverse = rope_base ** (-(2.0 * jnp.arange(half_dim, dtype=F32) / HEAD_DIM))
    phases = positions.astype(F32)[:, None] * inverse[None, :]
    return (jnp.cos(phases)[:, None, :], jnp.sin(phases)[:, None, :])


def rotate(tensor, cosine_table, sine_table):
    half_dim = HEAD_DIM // 2
    front, back = tensor[..., :half_dim], tensor[..., half_dim:]
    return jnp.concatenate(
        [front * cosine_table - back * sine_table, back * cosine_table + front * sine_table],
        axis=-1,
    )


def norm_back(upstream, normed, scale_rows):
    mean = jnp.sum(upstream * normed, axis=-1, keepdims=True) * (1.0 / D)
    return scale_rows * (upstream - normed * mean)


def adam_step(weight_now, gradient, first, second, decay_factor):
    moment, square, update = adam_parts(
        weight_now.astype(F32), gradient, first, second, decay_factor
    )
    return (gradient, moment, square, update)


def shards(
    direct,
    block_input,
    block_cotangent,
    lengths,
    attend_gain,
    attend_weight,
    output_weight,
    expand_gain,
    expand_weight,
    shrink_weight,
    attend_gain_first,
    attend_weight_first,
    output_weight_first,
    expand_gain_first,
    expand_weight_first,
    shrink_weight_first,
    attend_gain_second,
    attend_weight_second,
    output_weight_second,
    expand_gain_second,
    expand_weight_second,
    shrink_weight_second,
):
    tokens = block_input.shape[0]
    shard_count = lax.axis_size("shard")
    token_count = tokens * shard_count * lax.axis_size("rep")
    reach = (MAXLEN - 2) // tokens + 1
    own_rows = attend_weight.shape[0]
    rows = -(-(own_rows + 2) // 16) * 16
    width = shard_count * rows

    def padded(tensor):
        blocks = tensor.reshape(tokens, shard_count, own_rows)
        return jnp.pad(blocks, ((0, 0), (0, 0), (0, rows - own_rows))).reshape(tokens, width)

    def unpadded(tensor):
        return tensor.reshape(tokens, shard_count, rows)[:, :, :own_rows].reshape(tokens, D)

    def with_gain(weight, gain):
        if gain is None:
            return jnp.pad(weight, ((0, rows - own_rows), (0, 0)))
        tail = jnp.pad(gain[None, :], ((0, rows - own_rows - 1), (0, weight.shape[1] - own_rows)))
        return jnp.concatenate([weight, tail], axis=0)

    def gain_of(planes, column):
        return jnp.pad(
            planes[:, own_rows, column : column + own_rows], ((0, 0), (0, rows - own_rows))
        ).reshape(1, width).astype(F32)

    def add_gain(planes, term, column):
        row = term.reshape(shard_count, 1, rows).astype(planes.dtype)
        return lax.dynamic_update_slice(planes, row, (0, own_rows, column))

    def in_chunks(expand, shrink):
        parts = jnp.concatenate([expand, shrink], axis=1).reshape(-1, 3, FF // CHUNK, CHUNK)
        return parts.transpose(0, 2, 1, 3).reshape(-1, 3 * FF)

    if direct:
        weights = (
            attend_gain[None, :],
            attend_weight,
            expand_gain[None, :],
            expand_weight,
            shrink_weight.T,
            output_weight,
        )
        made = front(lengths, block_input.T, block_cotangent.T, weights, shard_count, 0)
        rest_planes, attend_planes = made[:2]
        sums, block_output, input_gradient, _ = rear(made[:12], made[12:], 1)
    else:
        first_row = lax.axis_index("shard") * tokens
        local_index = first_row + jnp.arange(tokens, dtype=jnp.int32)
        key_index = first_row - reach * tokens + jnp.arange((reach + 1) * tokens, dtype=jnp.int32)
        ends = jnp.cumsum(lengths[0], dtype=jnp.int32)
        starts = ends - lengths[0]
        seq_count = lengths.shape[1]
        in_key = (key_index[:, None] >= starts[None, :]) & (key_index[:, None] < ends[None, :])
        in_query = (local_index[None, :] >= starts[:, None]) & (local_index[None, :] < ends[:, None])
        lanes = 2 * HEAD_DIM
        feat = jnp.concatenate(
            [
                in_key.astype(BF),
                (key_index < 0).astype(BF)[:, None],
                jnp.zeros((key_index.shape[0], ONES - seq_count - 1), BF),
                jnp.ones((key_index.shape[0], lanes - ONES), BF),
            ],
            axis=1,
        )
        qfeat = jnp.concatenate(
            [
                jnp.where(in_query, 0.0, NEG).astype(BF),
                jnp.full((1, tokens), NEG, BF),
                jnp.zeros((lanes - seq_count - 1, tokens), BF),
            ],
            axis=0,
        )
        start_index = jnp.sum(in_query * starts[:, None], axis=0, dtype=jnp.int32)
        cosine_table, sine_table = angles(local_index - start_index)
        attend_own = with_gain(attend_weight, attend_gain)
        rest_own = jnp.concatenate(
            [
                with_gain(jnp.concatenate([expand_weight, shrink_weight.T], axis=1), None),
                with_gain(output_weight.T, expand_gain),
            ],
            axis=1,
        )
        attend_planes = lax.all_gather(attend_own, "shard", axis=0)
        rest_planes = lax.all_gather(rest_own, "shard", axis=0)
        gain_one, gain_two = gain_of(attend_planes, 0), gain_of(rest_planes, 3 * FF)
        joint_weight = attend_planes.reshape(width, JW)
        rest = rest_planes.reshape(width, rest_own.shape[1])
        expand_full, shrink_full, out_full = rest[:, : 2 * FF], rest[:, 2 * FF : 3 * FF], rest[:, 3 * FF :]
        real = (jnp.arange(width, dtype=jnp.int32) % rows < own_rows)[None, :]

        inputs = padded(block_input).astype(F32)
        scale_one = lax.rsqrt(jnp.sum(inputs * inputs, axis=-1, keepdims=True) * (1.0 / D) + eps_norm)
        normed_one = inputs * scale_one
        hidden_one = (normed_one * gain_one).astype(BF)
        joint = dot(hidden_one, joint_weight)
        queries = rotate(joint[:, :QW].reshape(tokens, HEADS, HEAD_DIM), cosine_table, sine_table)
        key_rows = rotate(
            joint[:, QW : QW + KW].reshape(tokens, KV_HEADS, HEAD_DIM), cosine_table, sine_table
        )
        values = joint[:, QW + KW :].reshape(tokens, KV_HEADS, HEAD_DIM)
        pairs = jnp.concatenate([key_rows, values], axis=-1).astype(BF).transpose(1, 0, 2)
        qt = queries.astype(BF).reshape(tokens, QW).T
        window = spread_pairs(pairs, reach)
        mixedt, lse = attend_forward(window, feat, qt, qfeat)
        middle = inputs + jnp.where(real, dot(mixedt, out_full, 0, 1), 0.0)
        scale_two = lax.rsqrt(jnp.sum(middle * middle, axis=-1, keepdims=True) * (1.0 / D) + eps_norm)
        normed_two = middle * scale_two
        hidden_two = (normed_two * gain_two).astype(BF)
        gate_up = dot(hidden_two, expand_full)
        gate_value, upper_value = gate_up[:, :FF], gate_up[:, FF:]
        sigmoid_gate = jax.nn.sigmoid(gate_value)
        inner_rows = (gate_value * sigmoid_gate * upper_value).astype(BF)
        block_output = middle + dot(inner_rows, shrink_full, 1, 1)

        cotangent = padded(block_cotangent)
        shrink_term = dot(cotangent, inner_rows, 0, 0)
        inner_grad = dot(cotangent, shrink_full)
        gate_grad = (
            inner_grad * upper_value * sigmoid_gate * (1.0 + gate_value * (1.0 - sigmoid_gate))
        ).astype(BF)
        upper_grad = (inner_grad * gate_value * sigmoid_gate).astype(BF)
        gate_up_grad = jnp.concatenate([gate_grad, upper_grad], axis=1)
        expand_term = dot(hidden_two, gate_up_grad, 0, 0)
        hidden_two_grad = jnp.where(real, dot(gate_up_grad, expand_full, 1, 1), 0.0)
        gain_two_term = jnp.sum(hidden_two_grad * normed_two, axis=0)
        middle_grad = cotangent.astype(F32) + norm_back(
            hidden_two_grad * gain_two, normed_two, scale_two
        )
        branch_grad = middle_grad.astype(BF)
        output_term = dot(branch_grad, mixedt, 0, 1)
        gradt = dot(out_full, branch_grad, 0, 1).astype(BF)
        dqt, dwindow = attend_backward(window, feat, qt, qfeat, gradt, mixedt, lse)
        own_pairs = collect_pairs(dwindow, reach)
        block_output = unpadded(block_output).T
        own_pairs = own_pairs.transpose(1, 0, 2)
        dq = dqt.T.reshape(tokens, HEADS, HEAD_DIM)
        query_raw = rotate(dq, cosine_table, -sine_table).reshape(tokens, QW)
        key_raw = rotate(own_pairs[..., :HEAD_DIM], cosine_table, -sine_table).reshape(tokens, KW)
        value_raw = own_pairs[..., HEAD_DIM:].reshape(tokens, KW)
        joint_grad = jnp.concatenate([query_raw, key_raw, value_raw], axis=1).astype(BF)
        joint_term = dot(hidden_one, joint_grad, 0, 0).astype(BF)
        hidden_one_grad = jnp.where(real, dot(joint_grad, joint_weight, 1, 1), 0.0)
        gain_one_term = jnp.sum(hidden_one_grad * normed_one, axis=0)
        input_gradient = middle_grad + norm_back(hidden_one_grad * gain_one, normed_one, scale_one)
        to_lanes = ((0, 0), (0, up_to_lanes(QW) - QW))
        terms = jnp.concatenate(
            [
                in_chunks(expand_term, shrink_term).astype(BF),
                jnp.pad(output_term.astype(BF), to_lanes),
                jnp.pad(joint_term[:, :QW], to_lanes),
                joint_term[:, QW:],
            ],
            axis=1,
        ).reshape(shard_count, rows, -1)
        terms = add_gain(terms, gain_two_term, sum_chunks()[OUT_CHUNK][0])
        terms = add_gain(terms, gain_one_term, sum_chunks()[PAIR_CHUNK][0])
        sums = lax.psum(lax.psum_scatter(terms, "shard", scatter_dimension=0), "rep")
        input_gradient = unpadded(input_gradient).T

    grad_scale = grad_factor * token_count ** (-0.5)
    def gain_sum(chunk):
        first = sum_chunks()[chunk][0]
        return sums[own_rows, first : first + own_rows]

    first_gain, second_gain = (
        adam_step(weight, total.astype(F32) * grad_scale, first, second, 0.0)
        for weight, total, first, second in (
            (
                attend_gain,
                gain_sum(PAIR_CHUNK),
                attend_gain_first,
                attend_gain_second,
            ),
            (
                expand_gain,
                gain_sum(OUT_CHUNK),
                expand_gain_first,
                expand_gain_second,
            ),
        )
    )
    matrices = adam(
        grad_scale,
        own_rows,
        sums,
        attend_planes,
        rest_planes,
        (
            (attend_weight_first, attend_weight_second),
            (output_weight_first, output_weight_second),
            (expand_weight_first, expand_weight_second),
            (shrink_weight_first.T, shrink_weight_second.T),
        ),
        (block_output, input_gradient),
    )
    first_joint, first_output, second_expand, second_shrink = (
        matrices[4 * n : 4 * n + 4] for n in range(4)
    )
    second_shrink = [result.T for result in second_shrink]
    block_output, input_gradient = (result.T for result in matrices[16:])
    steps = (first_gain, first_joint, first_output, second_gain, second_expand, second_shrink)
    return (block_output, input_gradient, *[step[i] for i in range(4) for step in steps])


def solution(mesh):
    whole_rows = P(("rep", "shard"), None)
    state = (P("shard"), P("shard", None), P(None, "shard")) * 2
    direct = mesh.shape["rep"] == 4 and mesh.shape["shard"] == 8
    return jax.shard_map(
        functools.partial(shards, direct),
        mesh=mesh,
        in_specs=(whole_rows, whole_rows, P("rep", None), *state, *state, *state),
        out_specs=(whole_rows, whole_rows, *state, *state, *state, *state),
        check_vma=False,
    )
```
